32 devices in a mesh: dp: 4 (over y, x), fsdp: 8 (over z, core).
Axes of the slice: x: 2, y: 2, z: 4, core: 2. Of those that a mesh axis runs over, the one named last changes fastest.
Arguments:
- latents: bfloat16 [32, 128, 16, 8], P(('dp', 'fsdp')), may hold values from -6 to 6
- noises: bfloat16 [32, 128, 16, 8], P(('dp', 'fsdp')), may hold values from -6 to 6
- clap_embed: float32 [32, 512], P(('dp', 'fsdp')), may hold values from -6 to 6
- timesteps: int32 [32], P(('dp', 'fsdp')), may hold values from 0 to 999
- lengths: int32 [32], P(('dp', 'fsdp')), may hold values from 32 to 128, as said below
- step_count: int32 [1], replicated, may hold values from 2 to 20
- stem_w: float32 [72, 256], replicated, may hold values from -0.75 to 0.75
- head_w: float32 [2304, 8], replicated, may hold values from -0.125 to 0.125
- time_w: float32 [3, 512, 512], P(None, 'fsdp'), may hold values from -0.25 to 0.25
- vector: float32 [5896], replicated
- conv_w: float32 [2, 2304, 256], P(None, 'fsdp'), may hold values from -0.125 to 0.125
- wide_w: float32 [256, 2048], P('fsdp'), may hold values from -0.375 to 0.375
- down_w: float32 [1024, 256], P('fsdp'), may hold values from -0.1875 to 0.1875
- roots_small: float32 [5, 256, 256], replicated, as said below
- root_wide: float32 [768, 768], replicated, as said below
- roots_large: float32 [2, 1024, 1024], replicated, as said below
- stem_moment: float32 [72, 256], replicated
- stem_square: float32 [72, 256], replicated, as said below
- head_moment: float32 [2304, 8], replicated
- head_square: float32 [2304, 8], replicated, as said below
- time_moment: float32 [3, 512, 512], P(None, 'fsdp')
- time_square: float32 [3, 512, 512], P(None, 'fsdp'), as said below
- vector_moment: float32 [5896], replicated
- vector_square: float32 [5896], replicated, as said below
- conv_moment: float32 [2, 2304, 256], P(None, 'fsdp')
- conv_square: float32 [2, 2304, 256], P(None, 'fsdp'), as said below
- wide_moment: float32 [256, 2048], P('fsdp')
- down_moment: float32 [1024, 256], P('fsdp')
Outputs:
- loss_value: float32 [], replicated
- grad_norm: float32 [], replicated
- stem_new: float32 [72, 256], replicated
- stem_moment_new: float32 [72, 256], replicated
- stem_square_new: float32 [72, 256], replicated
- head_new: float32 [2304, 8], replicated
- head_moment_new: float32 [2304, 8], replicated
- head_square_new: float32 [2304, 8], replicated
- time_new: float32 [3, 512, 512], P(None, 'fsdp')
- time_moment_new: float32 [3, 512, 512], P(None, 'fsdp')
- time_square_new: float32 [3, 512, 512], P(None, 'fsdp')
- vector_grad: float32 [5896], replicated
- vector_moment_new: float32 [5896], replicated
- vector_square_new: float32 [5896], replicated
- conv_new: float32 [2, 2304, 256], P(None, 'fsdp')
- conv_moment_new: float32 [2, 2304, 256], P(None, 'fsdp')
- conv_square_new: float32 [2, 2304, 256], P(None, 'fsdp')
- wide_new: float32 [256, 2048], P('fsdp')
- wide_moment_new: float32 [256, 2048], P('fsdp')
- down_new: float32 [1024, 256], P('fsdp')
- down_moment_new: float32 [1024, 256], P('fsdp')
The draws below stay inside these ranges and needn't reach their ends.
Inputs may be any that keep to these rules, and one draw needn't show every extreme that they name: `lengths`: each clip's live latent frames; clip 0 has 128. `roots_small`: symmetric and positive definite. `root_wide`: symmetric and positive definite. `roots_large`: symmetric and positive definite. `stem_square`: positive. `head_square`: positive. `time_square`: positive. `vector_square`: positive. `conv_square`: positive.
All inputs are finite; a program needn't handle non-finite values.
Results may differ from the reference program's by a relative error of at most 0.013.
Values may be sent and summed in bfloat16 or wider, within the bound.
A program may use at most 320 MiB of HBM per device.

```python
import math
import jax
import jax.numpy as jnp
from jax import lax

C = 256
HEADS = 8
FF = 1024
EMB = 512
GROUPS = 32
LAT = 8
FQ = 16
FRAMES = 128
CLIPS = 32
VEC = 5896
NPARAM = 2795272


clip_limit = 0.002


def grad_scale():
    return clip_limit / math.sqrt(NPARAM)


def first_moment(key, array_shape, factor=1.0):
    return 0.111 * factor * grad_scale() * jax.random.normal(key, array_shape, jnp.float32)


def second_moment(key, array_shape, factor=1.0):
    exponent = jax.random.uniform(key, array_shape, jnp.float32, math.log(0.0005), math.log(0.008))
    return jnp.exp(exponent) * (factor * factor * grad_scale() * grad_scale())


def root_stack(key, stack_count, matrix_order):
    first_key, second_key = jax.random.split(key)
    multiple = jnp.exp(jax.random.uniform(first_key, (stack_count, 1, 1), jnp.float32, math.log(0.5), math.log(2.0))) / math.sqrt(grad_scale())
    drawn = jax.random.normal(second_key, (stack_count, matrix_order, matrix_order), jnp.float32)
    symmetric = (drawn + jnp.swapaxes(drawn, 1, 2)) * (0.4 / math.sqrt(2.0 * matrix_order))
    return multiple * (jnp.eye(matrix_order, dtype=jnp.float32)[None] + symmetric)


def draw_lengths(key, part):
    drawn_len = jax.random.randint(key, (CLIPS,), FRAMES // 4, FRAMES + 1)
    return drawn_len.at[0].set(FRAMES).astype(jnp.int32)


def draw_vector(key, part):
    first_key, second_key = jax.random.split(key)
    base_draw = 0.2 * jax.random.normal(first_key, (VEC,), jnp.float32)
    rough = 1.0 + 0.15 * jax.random.normal(second_key, (VEC,), jnp.float32)
    position = jnp.arange(VEC)
    gain_rows = (position < C) | (position >= 3 * C) & (position < 4 * C) | (position >= 6 * C) & (position < 7 * C) | (position >= 9 * C) & (position < 10 * C)
    fraction = (position % C).astype(jnp.float32) / C
    low_end, high_end = (0.5, 2.0)
    rising = jnp.exp(math.log(low_end) + (math.log(high_end) - math.log(low_end)) * fraction) * rough
    return jnp.where(gain_rows, rising, base_draw)


def draw_roots_small(key, part):
    return root_stack(key, 5, C)


def draw_root_wide(key, part):
    return root_stack(key, 1, 3 * C)[0]


def draw_roots_large(key, part):
    return root_stack(key, 2, FF)


def draw_stem_moment(key, part):
    return first_moment(key, (9 * LAT, C), 0.35)


def draw_stem_square(key, part):
    return second_moment(key, (9 * LAT, C), 0.35)


def draw_head_moment(key, part):
    return first_moment(key, (9 * C, LAT))


def draw_head_square(key, part):
    return second_moment(key, (9 * C, LAT))


def draw_time_moment(key, part):
    return first_moment(key, (3, EMB, EMB))


def draw_time_square(key, part):
    return second_moment(key, (3, EMB, EMB))


def draw_vector_moment(key, part):
    return first_moment(key, (VEC,))


def draw_vector_square(key, part):
    return second_moment(key, (VEC,))


def draw_conv_moment(key, part):
    return first_moment(key, (2, 9 * C, C))


def draw_conv_square(key, part):
    return second_moment(key, (2, 9 * C, C))


def draw_wide_moment(key, part):
    return grad_scale() * jax.random.normal(key, (C, 4 * C + FF), jnp.float32)


def draw_down_moment(key, part):
    return grad_scale() * jax.random.normal(key, (FF, C), jnp.float32)


def touch_ends(array, stream_key, low, largest):
    longest = array.shape.index(max(array.shape))
    spots = []
    for shift in (0, 1):
        where = [jax.random.randint(jax.random.fold_in(stream_key, axis), (), 0, length) for axis, length in enumerate(array.shape)]
        where[longest] = (where[longest] + shift) % array.shape[longest]
        spots.append(tuple(where))
    return array.at[spots[0]].set(low).at[spots[1]].set(largest)


def steps_of(rng, dims, cuts, least, largest):
    factor_of = 1.0
    for dim, parts in cuts:
        heights = jax.random.uniform(jax.random.fold_in(jax.random.fold_in(rng, 6), dim), (parts,), jnp.float32, least / len(cuts), largest / len(cuts))
        factor_of = factor_of * jnp.repeat(jnp.exp(heights), dims[dim] // parts).reshape((-1,) + (1,) * (len(dims) - 1 - dim))
    return factor_of


def normal_values(stream_key, extent, scale, bound, cuts=(), kind=jnp.bfloat16):
    factor_of = steps_of(stream_key, extent, cuts, -0.22, 0.18) if cuts else 1.0
    values = jax.random.normal(stream_key, extent, jnp.float32) * scale * factor_of
    return jnp.minimum(jnp.maximum(values, -bound), bound).astype(kind)


def setup_inputs(seed: int = 0) -> dict:
    key_of = jax.random.split(jax.random.key(seed), 29)
    return {
        "latents": normal_values(key_of[0], (CLIPS, FRAMES, FQ, LAT), 1.0, 6.0, ((0, 32),)),
        "noises": normal_values(key_of[1], (CLIPS, FRAMES, FQ, LAT), 1.0, 6.0, ((0, 32),)),
        "clap_embed": normal_values(key_of[2], (CLIPS, EMB), 1.0, 6.0, ((0, 32),), jnp.float32),
        "timesteps": touch_ends(jax.random.randint(key_of[3], (CLIPS,), 0, 1000), jax.random.fold_in(key_of[3], 1), 0, 999).astype(jnp.int32),
        "lengths": draw_lengths(jax.random.fold_in(key_of[28], 71), 0),
        "step_count": jax.random.randint(key_of[5], (1,), 2, 21).astype(jnp.int32),
        "stem_w": normal_values(key_of[6], (9 * LAT, C), (9 * LAT) ** -0.5, 0.75, (), jnp.float32),
        "head_w": normal_values(key_of[7], (9 * C, LAT), (9 * C) ** -0.5, 0.125, (), jnp.float32),
        "time_w": normal_values(key_of[8], (3, EMB, EMB), EMB ** -0.5, 0.25, ((1, 8),), jnp.float32),
        "vector": draw_vector(jax.random.fold_in(key_of[28], 71), 0),
        "conv_w": normal_values(key_of[10], (2, 9 * C, C), (9 * C) ** -0.5, 0.125, ((1, 8),), jnp.float32),
        "wide_w": normal_values(key_of[11], (C, 4 * C + FF), C ** -0.5, 0.375, ((0, 8),), jnp.float32),
        "down_w": normal_values(key_of[12], (FF, C), FF ** -0.5, 0.1875, ((0, 8),), jnp.float32),
        "roots_small": draw_roots_small(jax.random.fold_in(key_of[28], 71), 0),
        "root_wide": draw_root_wide(jax.random.fold_in(key_of[28], 71), 0),
        "roots_large": draw_roots_large(jax.random.fold_in(key_of[28], 71), 0),
        "stem_moment": draw_stem_moment(jax.random.fold_in(key_of[28], 71), 0),
        "stem_square": draw_stem_square(jax.random.fold_in(key_of[28], 71), 0),
        "head_moment": draw_head_moment(jax.random.fold_in(key_of[28], 71), 0),
        "head_square": draw_head_square(jax.random.fold_in(key_of[28], 71), 0),
        "time_moment": draw_time_moment(jax.random.fold_in(key_of[28], 71), 0),
        "time_square": draw_time_square(jax.random.fold_in(key_of[28], 71), 0),
        "vector_moment": draw_vector_moment(jax.random.fold_in(key_of[28], 71), 0),
        "vector_square": draw_vector_square(jax.random.fold_in(key_of[28], 71), 0),
        "conv_moment": draw_conv_moment(jax.random.fold_in(key_of[28], 71), 0),
        "conv_square": draw_conv_square(jax.random.fold_in(key_of[28], 71), 0),
        "wide_moment": draw_wide_moment(jax.random.fold_in(key_of[28], 71), 0),
        "down_moment": draw_down_moment(jax.random.fold_in(key_of[28], 71), 0),
    }


@jax.custom_vjp
def low(v):
    return lax.optimization_barrier(v.astype(jnp.bfloat16)).astype(jnp.float32)

@jax.custom_vjp
def low_back(v):
    return v

def low_keep(v):
    return (low(v), None)

def low_pass(kept, grad):
    return (grad,)

def back_keep(v):
    return (v, None)

def back_low(kept, grad):
    return (low(grad),)
low.defvjp(low_keep, low_pass)
low_back.defvjp(back_keep, back_low)
highest = lax.Precision.HIGHEST
norm_floor = 1e-05
masked_score = -1e+30
clip_limit = 0.002
adam_rate = 0.05
adam_floor = 1e-08
shampoo_rate = 0.02
decay_rate = 0.01

def split_vector(vector, channels, embed_width, hidden_units, latent_ch):
    lengths_list = [channels] * 13 + [embed_width] * 3 + [hidden_units, latent_ch]
    pieces = []
    offset = 0
    for seg_len in lengths_list:
        pieces.append(vector[offset:offset + seg_len])
        offset = offset + seg_len
    return pieces

def conv(inputs, kernel):
    in_ch = inputs.shape[-1]
    shaped = low(kernel).reshape(3, 3, in_ch, kernel.shape[-1])
    result = lax.conv_general_dilated(low(inputs)[None], shaped, (1, 1), ((1, 1), (1, 1)), dimension_numbers=('NHWC', 'HWIO', 'NHWC'), precision=highest)
    return low_back(result[0])

def linear(inputs, weight):
    return low_back(jnp.dot(low(inputs), low(weight), precision=highest))

def group_norm(field, gain, shift, pix_mask, groups):
    frames_n, freq_bins, channels = field.shape
    grouped = field.reshape(frames_n, freq_bins, groups, channels // groups)
    mask_grid = pix_mask.reshape(frames_n, freq_bins, 1, 1)
    counted = jnp.sum(mask_grid) * (channels // groups)
    center = lax.optimization_barrier(jnp.sum(grouped * mask_grid, axis=(0, 1, 3), keepdims=True)) / counted
    spread = lax.optimization_barrier(jnp.sum(mask_grid * (grouped - center) ** 2, axis=(0, 1, 3), keepdims=True)) / counted
    normed = ((grouped - center) * lax.rsqrt(spread + norm_floor)).reshape(field.shape)
    return normed * gain + shift

def layer_norm(row_field, gain, shift):
    center = lax.optimization_barrier(jnp.mean(row_field, axis=-1, keepdims=True))
    spread = lax.optimization_barrier(jnp.mean((row_field - center) ** 2, axis=-1, keepdims=True))
    return (row_field - center) * lax.rsqrt(spread + norm_floor) * gain + shift

def noise_mix(step_value):
    phase = (step_value.astype(jnp.float32) / 1000.0 + 0.008) / 1.008 * (math.pi / 2)
    keep_part = jnp.cos(phase) ** 2
    return (jnp.sqrt(keep_part), jnp.sqrt(1.0 - keep_part))

def film_terms(time_w, bias_one, bias_two, bias_film, step_value, clap_row):
    half_width = time_w.shape[1] // 2
    frequency = jnp.exp(-math.log(10000.0) * jnp.arange(half_width).astype(jnp.float32) / half_width)
    angles = step_value.astype(jnp.float32) * frequency
    sinusoid = jnp.concatenate([jnp.cos(angles), jnp.sin(angles)])
    hidden = jax.nn.silu(jnp.dot(sinusoid, time_w[0], precision=highest) + bias_one)
    embedding = jnp.dot(hidden, time_w[1], precision=highest) + bias_two + clap_row
    return jnp.dot(jax.nn.silu(embedding), time_w[2], precision=highest) + bias_film

def attention(proj_qkv, key_live):
    rows_n, triple = proj_qkv.shape
    channels = triple // 3
    head_dim = channels // HEADS
    block_rows = min(512, rows_n)
    queries = proj_qkv[:, :channels].reshape(rows_n // block_rows, block_rows, HEADS, head_dim)
    key_heads = proj_qkv[:, channels:2 * channels].reshape(rows_n, HEADS, head_dim)
    value_heads = proj_qkv[:, 2 * channels:].reshape(rows_n, HEADS, head_dim)

    def one_block(query_block):
        raw_scores = jnp.einsum('qhd,khd->hqk', query_block, key_heads, precision=highest)
        scores = low_back(raw_scores) * head_dim ** (-0.5)
        scores = jnp.where(key_live[None, None, :], scores, masked_score)
        soft_weights = jax.nn.softmax(scores, axis=-1)
        mixed_block = jnp.einsum('hqk,khd->qhd', low(soft_weights), value_heads, precision=highest)
        return low_back(mixed_block).reshape(block_rows, channels)
    outputs = lax.map(jax.checkpoint(one_block), queries)
    return outputs.reshape(rows_n, channels)

def clip_error(weights, latent, noise_grid, clap_row, step_value, length):
    stem_w, head_w, time_w, vector, conv_w, wide_w, down_w = weights
    frames_n, freq_bins, latent_ch = latent.shape
    channels = stem_w.shape[1]
    segs = split_vector(vector, channels, time_w.shape[1], down_w.shape[0], latent_ch)
    key_live = jnp.repeat(jnp.arange(frames_n) < length, freq_bins)
    pix_mask = key_live.astype(jnp.float32)[:, None]
    grid_mask = pix_mask.reshape(frames_n, freq_bins, 1)
    keep_root, noise_root = noise_mix(step_value)
    noisy = (keep_root * latent + noise_root * noise_grid) * grid_mask
    stream = conv(noisy, stem_w) + segs[12]
    act_one = jax.nn.silu(group_norm(stream, segs[0], segs[1], pix_mask, GROUPS)) * grid_mask
    inner_out = conv(act_one, conv_w[0]) + segs[2]
    film_out = film_terms(time_w, segs[13], segs[14], segs[15], step_value, clap_row)
    moved = inner_out * (1.0 + film_out[:channels]) + film_out[channels:]
    act_two = jax.nn.silu(group_norm(moved, segs[3], segs[4], pix_mask, GROUPS)) * grid_mask
    stream = stream + conv(act_two, conv_w[1]) + segs[5]
    row_field = stream.reshape(frames_n * freq_bins, channels)
    proj_qkv = low(linear(layer_norm(row_field, segs[6], segs[7]), wide_w[:, :3 * channels]))
    mixed_out = attention(proj_qkv, key_live)
    row_field = row_field + linear(mixed_out, wide_w[:, 3 * channels:4 * channels]) + segs[8]
    pre_act = linear(layer_norm(row_field, segs[9], segs[10]), wide_w[:, 4 * channels:]) + segs[16]
    hidden = jax.nn.gelu(pre_act, approximate=False)
    row_field = row_field + linear(hidden, down_w) + segs[11]
    head_in = (row_field * pix_mask).reshape(frames_n, freq_bins, channels)
    predicted = conv(head_in, head_w) + segs[17]
    errors = (predicted - noise_grid) * grid_mask
    return jnp.sum(errors * errors)

def adam_step(weight, moment_one, moment_two, gradient, decay_on, fix_one, fix_two):
    first_new = 0.9 * moment_one + 0.1 * gradient
    second_new = 0.999 * moment_two + 0.001 * gradient * gradient
    moved = first_new / fix_one / (jnp.sqrt(second_new / fix_two) + adam_floor)
    return (weight - adam_rate * (moved + decay_on * weight), first_new, second_new)

def shampoo_step(weight, moment, gradient, left_root, right_root):
    moment_new = 0.9 * moment + gradient
    direction = jnp.dot(jnp.dot(left_root, moment_new, precision=highest), right_root, precision=highest)
    return (weight * (1.0 - shampoo_rate * decay_rate) - shampoo_rate * direction, moment_new)

def reference(latents, noises, clap_embed, timesteps, lengths, step_count, stem_w, head_w, time_w, vector, conv_w, wide_w, down_w, roots_small, root_wide, roots_large, stem_moment, stem_square, head_moment, head_square, time_moment, time_square, vector_moment, vector_square, conv_moment, conv_square, wide_moment, down_moment):
    weights = (stem_w, head_w, time_w, vector, conv_w, wide_w, down_w)
    live_count = jnp.sum(lengths).astype(jnp.float32) * FQ
    clip_data = (latents.astype(jnp.float32), noises.astype(jnp.float32), clap_embed, timesteps, lengths)
    checked = jax.checkpoint(clip_error)

    def total_loss(params):

        def add_clip(running, item):
            return (running + checked(params, item[0], item[1], item[2], item[3], item[4]), None)
        summed, _ = lax.scan(add_clip, jnp.zeros((), jnp.float32), clip_data)
        return summed / (LAT * live_count)
    loss_value, pullback = jax.vjp(total_loss, weights)
    grads = pullback(jnp.ones((), jnp.float32))[0]
    squares = jnp.zeros((), jnp.float32)
    for gradient in grads:
        squares = squares + jnp.sum(gradient * gradient)
    grad_norm = jnp.sqrt(squares)
    factor = jnp.minimum(1.0, clip_limit / grad_norm)
    clipped = [factor * gradient for gradient in grads]
    step_value = step_count[0].astype(jnp.float32)
    fix_one = 1.0 - jnp.power(0.9, step_value)
    fix_two = 1.0 - jnp.power(0.999, step_value)
    stem_out = adam_step(stem_w, stem_moment, stem_square, clipped[0], decay_rate, fix_one, fix_two)
    head_out = adam_step(head_w, head_moment, head_square, clipped[1], decay_rate, fix_one, fix_two)
    time_out = adam_step(time_w, time_moment, time_square, clipped[2], decay_rate, fix_one, fix_two)
    vector_out = adam_step(vector, vector_moment, vector_square, clipped[3], 0.0, fix_one, fix_two)
    conv_out = adam_step(conv_w, conv_moment, conv_square, clipped[4], decay_rate, fix_one, fix_two)
    bounds = (0, 3 * C, 4 * C, 4 * C + FF)
    lefts = (roots_small[0], roots_small[1], roots_small[2])
    rights = (root_wide, roots_small[3], roots_large[0])
    new_blocks = []
    moment_blocks = []
    for index_block in range(3):
        low_col, high_col = (bounds[index_block], bounds[index_block + 1])
        block_new, block_moment = shampoo_step(wide_w[:, low_col:high_col], wide_moment[:, low_col:high_col], clipped[5][:, low_col:high_col], lefts[index_block], rights[index_block])
        new_blocks.append(block_new)
        moment_blocks.append(block_moment)
    down_new, down_moment_new = shampoo_step(down_w, down_moment, clipped[6], roots_large[1], roots_small[4])
    return (loss_value, grad_norm, stem_out[0], stem_out[1], stem_out[2], head_out[0], head_out[1], head_out[2], time_out[0], time_out[1], time_out[2], clipped[3], vector_out[1], vector_out[2], conv_out[0], conv_out[1], conv_out[2], jnp.concatenate(new_blocks, 1), jnp.concatenate(moment_blocks, 1), down_new, down_moment_new)
```

```python
import functools
import math

import jax
import jax.numpy as jnp
from jax import lax
from jax.experimental import pallas as pl
from jax.experimental.pallas import tpu as pltpu
from jax.sharding import PartitionSpec as P

HEADS = 8
FF = 1024
EMB = 512
GROUPS = 32

norm_floor = 1e-05
masked_score = -1e30
clip_limit = 0.002
adam_rate = 0.05
adam_floor = 1e-08
shampoo_rate = 0.02
decay_rate = 0.01

f32 = jnp.float32
bf16 = jnp.bfloat16
highest = lax.Precision.HIGHEST
LOG2E = math.log2(math.e)
CHUNK = 256


def mm(left_op, right_op):
    return jnp.dot(left_op, right_op, preferred_element_type=f32)


def mm_nt(left_op, right_op):
    return lax.dot_general(
        left_op, right_op, (((1,), (1,)), ((), ())), preferred_element_type=f32
    )


def col_sum(value):
    return jnp.sum(value, axis=0, keepdims=True)


def row_mean(value):
    return jnp.mean(value, axis=-1, keepdims=True)


def loop(count, body, init):
    return lax.fori_loop(0, count, body, init)


def tap_shift(field, a, b, freq_bins):
    length = field.shape[1]
    step = freq_bins * (a - 1) + (b - 1)
    if step == 0:
        return field
    pos = lax.broadcasted_iota(jnp.int32, field.shape, 1)
    bin_pos = lax.rem(pos, freq_bins)
    keep = None
    for wanted, test in (
        (a == 0, lambda: pos >= freq_bins),
        (a == 2, lambda: pos < length - freq_bins),
        (b == 0, lambda: bin_pos >= 1),
        (b == 2, lambda: bin_pos < freq_bins - 1),
    ):
        if wanted:
            keep = test() if keep is None else jnp.logical_and(keep, test())
    return jnp.where(keep, pltpu.roll(field, (-step) % length, 1), 0.0)


def put_shifted(buf, start, value, freq_bins):
    rows, channels = value.shape
    bin_pos = lax.rem(lax.broadcasted_iota(jnp.int32, value.shape, 0), freq_bins)
    before = jnp.where(bin_pos == 0, 0.0, pltpu.roll(value, 1, 0))
    after = jnp.where(bin_pos == freq_bins - 1, 0.0, pltpu.roll(value, rows - 1, 0))
    where = pl.ds(start + freq_bins, rows)
    buf[where, 0:channels] = before.astype(bf16)
    buf[where, channels : 2 * channels] = value.astype(bf16)
    buf[where, 2 * channels : 3 * channels] = after.astype(bf16)


def clear_ends(buf, rows_n, freq_bins):
    blank = jnp.zeros((freq_bins, buf.shape[1]), bf16)
    buf[0:freq_bins, :] = blank
    buf[rows_n + freq_bins : rows_n + 2 * freq_bins, :] = blank


def live_rows(start, shape, live):
    return start + lax.broadcasted_iota(jnp.int32, shape, 0) < live


def group_total(row, groups):
    channels = row.shape[1]
    size = channels // groups
    one = lax.broadcasted_iota(jnp.int32, (channels, channels), 0) // size
    two = lax.broadcasted_iota(jnp.int32, (channels, channels), 1) // size
    same = jnp.where(one == two, 1.0, 0.0).astype(f32)
    wide = jnp.broadcast_to(row, (8, channels))
    return jnp.dot(wide, same, precision=highest, preferred_element_type=f32)[0:1]


def vec_mat(row, weight, transposed=False):
    top = row.astype(bf16).astype(f32)
    rest = row - top
    mid = rest.astype(bf16).astype(f32)
    low = rest - mid
    shape = (16, row.shape[1])
    index = lax.broadcasted_iota(jnp.int32, shape, 0)
    stacked = jnp.where(
        index == 0,
        jnp.broadcast_to(top, shape),
        jnp.where(
            index == 1,
            jnp.broadcast_to(mid, shape),
            jnp.where(index == 2, jnp.broadcast_to(low, shape), 0.0),
        ),
    ).astype(bf16)
    return col_sum(mm_nt(stacked, weight) if transposed else mm(stacked, weight))


def silu_slope(value):
    gate = jax.nn.sigmoid(value)
    return gate * (1.0 + value * (1.0 - gate))


def group_stats(read, rows_n, live, channels, groups, counted):
    count = rows_n // CHUNK

    def add(i, total):
        start = pl.multiple_of(i * CHUNK, CHUNK)
        value = read(start)
        return total + col_sum(jnp.where(live_rows(start, value.shape, live), value, 0.0))

    center = group_total(loop(count, add, jnp.zeros((1, channels), f32)), groups) / counted

    def add_square(i, total):
        start = pl.multiple_of(i * CHUNK, CHUNK)
        value = read(start) - center
        return total + col_sum(jnp.where(live_rows(start, value.shape, live), value * value, 0.0))

    spread = group_total(loop(count, add_square, jnp.zeros((1, channels), f32)), groups) / counted
    return center, lax.rsqrt(spread + norm_floor)


def offsets(channels, embed_width, hidden_units, latent_ch):
    starts = []
    start = 0
    for length in [channels] * 13 + [embed_width] * 3 + [hidden_units, latent_ch]:
        starts.append((start, length))
        start = start + length
    return starts


def fore_kernel(
    freq_bins,
    groups,
    len_ref,
    mix_ref,
    lat_ref,
    noi_ref,
    stem_ref,
    conv_ref,
    wide_ref,
    time_ref,
    vec_ref,
    wave_ref,
    clap_ref,
    zero_ref,
    act_one_ref,
    inner_ref,
    act_two_ref,
    one_ref,
    normed_ref,
    qkv_ref,
    colsT_ref,
    noiT_ref,
    stat_ref,
    film_ref,
    buf,
    cols,
    tall,
):
    rows_n, channels = zero_ref.shape
    latent_ch = lat_ref.shape[1]
    embed = time_ref.shape[1]
    count = rows_n // CHUNK
    live = len_ref[0] * freq_bins
    counted = (live * (channels // groups)).astype(f32)
    segs = offsets(channels, embed, FF, latent_ch)

    def seg(index):
        start, length = segs[index]
        return vec_ref[:, start : start + length]

    wave = wave_ref[...]
    pre_time = vec_mat(wave, time_ref[0]) + seg(13)
    embedding = vec_mat(jax.nn.silu(pre_time), time_ref[1]) + seg(14) + clap_ref[...]
    film = vec_mat(jax.nn.silu(embedding), time_ref[2]) + seg(15)
    film_ref[0:1] = film
    film_ref[1:2] = pre_time
    film_ref[2:3] = embedding
    film_ref[3:8] = jnp.zeros((5, embed), f32)
    lift = 1.0 + film[:, :channels]
    move = film[:, channels:]

    eye = jnp.where(
        lax.broadcasted_iota(jnp.int32, (latent_ch, latent_ch), 0)
        == lax.broadcasted_iota(jnp.int32, (latent_ch, latent_ch), 1),
        1.0,
        0.0,
    ).astype(bf16)
    noise_t = mm_nt(eye, noi_ref[...])
    noiT_ref[...] = noise_t
    mixed = mix_ref[0] * mm_nt(eye, lat_ref[...]) + mix_ref[1] * noise_t
    pos = lax.broadcasted_iota(jnp.int32, mixed.shape, 1)
    noisy = jnp.where(pos < live, mixed, 0.0).astype(bf16).astype(f32)
    taps = 9 * latent_ch
    for a in range(3):
        for b in range(3):
            tap = 3 * a + b
            tall[tap * latent_ch : (tap + 1) * latent_ch] = tap_shift(noisy, a, b, freq_bins)
    tall[taps:] = jnp.zeros((tall.shape[0] - taps, rows_n), f32)
    colsT_ref[...] = tall[0:taps].astype(bf16)
    cols[...] = tall[...].T.astype(bf16)
    stem_low = jnp.concatenate(
        [stem_ref[...], jnp.zeros((cols.shape[1] - taps, channels), f32)], 0
    ).astype(bf16)
    stem_bias = seg(12)

    def stem_part(i, carry):
        rows = pl.ds(pl.multiple_of(i * CHUNK, CHUNK), CHUNK)
        zero_ref[rows, :] = mm(cols[rows, :], stem_low) + stem_bias
        return carry

    loop(count, stem_part, 0)

    clear_ends(buf, rows_n, freq_bins)

    def convolve(which, start):
        total = None
        for a in range(3):
            part = mm(
                buf[pl.ds(start + freq_bins * a, CHUNK), :],
                conv_ref[which, 3 * a * channels : 3 * (a + 1) * channels, :],
            )
            total = part if total is None else total + part
        return total

    def activate(read, center, scale, gain, shift, act_ref):
        factor = scale * gain

        def part(i, carry):
            start = pl.multiple_of(i * CHUNK, CHUNK)
            value = jax.nn.silu((read(start) - center) * factor + shift)
            value = jnp.where(live_rows(start, value.shape, live), value, 0.0)
            low = value.astype(bf16)
            act_ref[pl.ds(start, CHUNK), :] = low
            put_shifted(buf, start, low.astype(f32), freq_bins)
            return carry

        loop(count, part, 0)

    def read_zero(start):
        return zero_ref[pl.ds(start, CHUNK), :]

    center, scale = group_stats(read_zero, rows_n, live, channels, groups, counted)
    stat_ref[0:1] = center
    stat_ref[1:2] = scale
    activate(read_zero, center, scale, seg(0), seg(1), act_one_ref)

    bias_one = seg(2)

    def conv_part(i, carry):
        start = pl.multiple_of(i * CHUNK, CHUNK)
        inner_ref[pl.ds(start, CHUNK), :] = convolve(0, start) + bias_one
        return carry

    loop(count, conv_part, 0)

    def read_moved(start):
        return inner_ref[pl.ds(start, CHUNK), :] * lift + move

    center, scale = group_stats(read_moved, rows_n, live, channels, groups, counted)
    stat_ref[2:3] = center
    stat_ref[3:4] = scale
    stat_ref[4:8] = jnp.zeros((4, channels), f32)
    activate(read_moved, center, scale, seg(3), seg(4), act_two_ref)

    bias_two = seg(5)
    gain, shift = seg(6), seg(7)
    wqkv_t = wide_ref[...].T

    def last_part(i, carry):
        start = pl.multiple_of(i * CHUNK, CHUNK)
        rows = pl.ds(start, CHUNK)
        stream = zero_ref[rows, :] + convolve(1, start) + bias_two
        one_ref[rows, :] = stream
        gap = stream - row_mean(stream)
        normed = gap * lax.rsqrt(row_mean(gap * gap) + norm_floor) * gain + shift
        low = normed.astype(bf16)
        normed_ref[rows, :] = low
        qkv_ref[:, rows] = mm_nt(wqkv_t, low).astype(bf16)
        return carry

    loop(count, last_part, 0)


def fill_query(aug, query, factor, extra):
    dim, length = query.shape
    scaled = query.astype(f32) * (factor * LOG2E)
    high = scaled.astype(bf16)
    aug[0:dim] = high
    aug[dim : 2 * dim] = (scaled - high.astype(f32)).astype(bf16)
    index = lax.broadcasted_iota(jnp.int32, (16, length), 0)
    tile = jnp.where(index == 0, 1.0, 0.0)
    for place, row in enumerate(extra):
        tile = jnp.where(index == place + 1, jnp.broadcast_to(row, tile.shape), tile)
    aug[2 * dim : 2 * dim + 16] = tile.astype(bf16)
    aug[2 * dim + 16 :] = jnp.zeros((aug.shape[0] - 2 * dim - 16, length), bf16)


def fill_keys(aug, keys, live):
    dim, length = keys.shape
    rest = aug.shape[1] - 2 * dim
    index = lax.broadcasted_iota(jnp.int32, (rest, length), 0)
    pos = lax.broadcasted_iota(jnp.int32, (rest, length), 1)
    mask = jnp.where(pos < live, 0.0, masked_score)
    tile = jnp.where(index == 0, mask, jnp.where(index < 4, 1.0, 0.0))
    both = keys.astype(f32)
    aug[...] = jnp.concatenate([both, both, tile], 0).T.astype(bf16)


def three_parts(row):
    top = row.astype(bf16).astype(f32)
    rest = row - top
    mid = rest.astype(bf16).astype(f32)
    return top, mid, rest - mid


def attend_kernel(
    freq_bins, key_block, len_ref, q_ref, k_ref, v_ref, o_ref, lse_ref, kaug, qaug, vaug
):
    dim, length = q_ref.shape
    live = len_ref[0] * freq_bins
    fill_query(qaug, q_ref[...], dim ** (-0.5), ())
    fill_keys(kaug, k_ref[...], live)
    vaug[0:dim] = v_ref[...]
    index = lax.broadcasted_iota(jnp.int32, (16, length), 0)
    vaug[dim : dim + 16] = jnp.where(index == 0, 1.0, 0.0).astype(bf16)
    top = None
    for i in range(length // key_block):
        keys = slice(i * key_block, (i + 1) * key_block)
        scores = mm(kaug[keys, :], qaug[...])
        block_top = jnp.max(scores, axis=0, keepdims=True)
        new_top = block_top if top is None else jnp.maximum(top, block_top)
        weights = jnp.exp2(scores - new_top).astype(bf16)
        part = mm(vaug[:, keys], weights)
        total = part if top is None else total * jnp.exp2(top - new_top) + part
        top = new_top
    summed = total[dim : dim + 1]
    o_ref[...] = total[0:dim] / summed
    lse_ref[0] = top + jnp.log2(summed)


def attend_back_kernel(
    freq_bins,
    key_block,
    len_ref,
    q_ref,
    k_ref,
    v_ref,
    lse_ref,
    o_ref,
    do_ref,
    dq_ref,
    dk_ref,
    dv_ref,
    kaug,
    qaug,
    vaug,
    daug,
    acc,
):
    dim, length = q_ref.shape
    step = pl.program_id(1)
    factor = dim ** (-0.5)

    @pl.when(step == 0)
    def _():
        live = len_ref[0] * freq_bins
        fill_query(qaug, q_ref[...], factor, three_parts(-lse_ref[0]))
        fill_keys(kaug, k_ref[...], live)
        values = v_ref[...].astype(f32)
        rest = vaug.shape[1] - dim
        index = lax.broadcasted_iota(jnp.int32, (rest, length), 0)
        tile = jnp.where(index < 3, -1.0, 0.0)
        vaug[...] = jnp.concatenate([values, tile], 0).T.astype(bf16)
        back = do_ref[...]
        delta = col_sum(back.astype(f32) * o_ref[...])
        daug[0:dim] = back
        index = lax.broadcasted_iota(jnp.int32, (16, length), 0)
        tile = jnp.zeros((16, length), f32)
        for place, row in enumerate(three_parts(delta)):
            tile = jnp.where(index == place, jnp.broadcast_to(row, tile.shape), tile)
        daug[dim : dim + 16] = tile.astype(bf16)
        daug[dim + 16 :] = jnp.zeros((daug.shape[0] - dim - 16, length), bf16)
        acc[...] = jnp.zeros(acc.shape, f32)

    keys = pl.ds(pl.multiple_of(step * key_block, key_block), key_block)
    weights = jnp.exp2(mm(kaug[keys, :], qaug[...]))
    raw = (weights * mm(vaug[keys, :], daug[...])).astype(bf16)
    dv_ref[...] = mm_nt(do_ref[...], weights.astype(bf16)).astype(bf16)
    dk_ref[...] = (mm_nt(q_ref[...], raw) * factor).astype(bf16)
    acc[...] += mm(k_ref[:, keys], raw)

    @pl.when(step == pl.num_programs(1) - 1)
    def _():
        dq_ref[...] = (acc[...] * factor).astype(bf16)


def middle_kernel(
    freq_bins,
    len_ref,
    mixed_ref,
    one_ref,
    wide_ref,
    down_ref,
    vec_ref,
    head_ref,
    head_bias_ref,
    noiT_ref,
    two_grad_ref,
    do_ref,
    gdown_ref,
    gup_ref,
    gproj_ref,
    ghead_ref,
    gvec_ref,
    small_ref,
    hidden,
    slope,
    xhat,
    spread,
    three,
    prod,
    gcols,
    normed_t,
    three_t,
    gpre,
    glow,
):
    rows_n, channels = one_ref.shape
    units = down_ref.shape[0]
    latent_ch = noiT_ref.shape[0]
    count = rows_n // CHUNK
    live = len_ref[0] * freq_bins
    segs = offsets(channels, EMB, units, latent_ch)

    def seg(index):
        start, length = segs[index]
        return vec_ref[:, start : start + length]

    w_out = wide_ref[:, 3 * channels : 4 * channels]
    proj_bias, gain, shift, up_bias, down_bias = seg(8), seg(9), seg(10), seg(16), seg(11)

    def fore(i, carry):
        start = pl.multiple_of(i * CHUNK, CHUNK)
        rows = pl.ds(start, CHUNK)
        mixed = mixed_ref[:, rows].T.astype(bf16)
        stream = one_ref[rows, :] + mm(mixed, w_out) + proj_bias
        gap = stream - row_mean(stream)
        scale = lax.rsqrt(row_mean(gap * gap) + norm_floor)
        hat = gap * scale
        xhat[rows, :] = hat
        spread[rows, :] = jnp.broadcast_to(scale, (CHUNK, spread.shape[1]))
        normed = (hat * gain + shift).astype(bf16)
        normed_t[:, rows] = normed.T
        pre = mm(normed, wide_ref[:, 4 * channels :]) + up_bias
        phi = 0.5 * (1.0 + lax.erf(pre * (0.5**0.5)))
        slope[rows, :] = phi + pre * jnp.exp(-0.5 * pre * pre) * (0.5 / math.pi) ** 0.5
        low = (pre * phi).astype(bf16)
        hidden[rows, :] = low
        stream = stream + mm(low, down_ref[...]) + down_bias
        stream = jnp.where(live_rows(start, stream.shape, live), stream, 0.0).astype(bf16)
        three[rows, :] = stream
        prod[:, rows] = mm_nt(head_ref[...], stream)
        return carry

    loop(count, fore, 0)

    taps = 9 * latent_ch
    predicted = jnp.zeros((latent_ch, rows_n), f32) + head_bias_ref[...]
    for a in range(3):
        for b in range(3):
            tap = 3 * a + b
            predicted = predicted + tap_shift(
                prod[tap * latent_ch : (tap + 1) * latent_ch], a, b, freq_bins
            )
    pos = lax.broadcasted_iota(jnp.int32, predicted.shape, 1)
    errors = jnp.where(pos < live, predicted - noiT_ref[...], 0.0)
    small_ref[:, 0:128] = jnp.broadcast_to(
        jnp.sum(errors, axis=1, keepdims=True), (latent_ch, 128)
    )
    small_ref[:, 128:256] = jnp.broadcast_to(
        jnp.sum(errors * errors, axis=1, keepdims=True), (latent_ch, 128)
    )
    errors = errors.astype(bf16).astype(f32)
    for a in range(3):
        for b in range(3):
            tap = 3 * a + b
            prod[tap * latent_ch : (tap + 1) * latent_ch] = tap_shift(
                errors, 2 - a, 2 - b, freq_bins
            )
    prod[taps:] = jnp.zeros((prod.shape[0] - taps, rows_n), f32)
    gcols[...] = prod[...].T.astype(bf16)
    ghead_ref[...] = mm(prod[0:taps].astype(bf16), three[...])

    def back(i, carry):
        g_down, g_up, g_gain, g_shift, g_proj = carry
        start = pl.multiple_of(i * CHUNK, CHUNK)
        rows = pl.ds(start, CHUNK)
        grad = mm(gcols[rows, :], head_ref[...])
        grad = jnp.where(live_rows(start, grad.shape, live), grad, 0.0)
        low = grad.astype(bf16)
        three_t[:, rows] = low.T
        pre = mm_nt(low, down_ref[...]) * slope[rows, :]
        pre_low = pre.astype(bf16)
        gpre[rows, :] = pre_low
        dnormed = mm_nt(pre_low, wide_ref[:, 4 * channels :])
        hat = xhat[rows, :]
        dhat = dnormed * gain
        dstream = (dhat - row_mean(dhat) - hat * row_mean(dhat * hat)) * spread[rows, 0:1]
        two = grad + dstream
        two_grad_ref[rows, :] = two
        two_low = two.astype(bf16)
        glow[rows, :] = two_low
        do_ref[:, rows] = mm_nt(w_out, two_low).astype(bf16)
        return (
            g_down + col_sum(grad),
            g_up + col_sum(pre),
            g_gain + col_sum(dnormed * hat),
            g_shift + col_sum(dnormed),
            g_proj + col_sum(two),
        )

    blank = jnp.zeros((1, channels), f32)
    sums = loop(count, back, (blank, jnp.zeros((1, units), f32), blank, blank, blank))
    gvec_ref[...] = jnp.zeros(gvec_ref.shape, f32)
    for index, value in zip((11, 16, 9, 10, 8), sums):
        start, length = segs[index]
        gvec_ref[:, start : start + length] = value
    gproj_ref[...] = mm(mixed_ref[...].astype(bf16), glow[...]).astype(bf16)
    for part in range(units // channels):
        columns = slice(part * channels, (part + 1) * channels)
        gdown_ref[columns, :] = mm(three_t[...], hidden[:, columns]).T.astype(bf16)
        gup_ref[:, columns] = mm(normed_t[...], gpre[:, columns]).astype(bf16)


def hind_kernel(
    freq_bins,
    groups,
    len_ref,
    dq_ref,
    dk_ref,
    dv_ref,
    two_grad_ref,
    normed_ref,
    one_ref,
    act_two_ref,
    inner_ref,
    act_one_ref,
    zero_ref,
    colsT_ref,
    stat_ref,
    film_ref,
    conv_ref,
    wide_ref,
    time_ref,
    vec_ref,
    wave_ref,
    gqkv_ref,
    gconv_ref,
    gstem_ref,
    gvec_ref,
    factor_ref,
    buf,
    field,
    other,
    act_t,
):
    rows_n, channels = one_ref.shape
    embed = time_ref.shape[1]
    latent_ch = colsT_ref.shape[0] // 9
    count = rows_n // CHUNK
    live = len_ref[0] * freq_bins
    counted = (live * (channels // groups)).astype(f32)
    segs = offsets(channels, embed, FF, latent_ch)
    blank = jnp.zeros((1, channels), f32)
    gvec_ref[...] = jnp.zeros(gvec_ref.shape, f32)

    def seg(index):
        start, length = segs[index]
        return vec_ref[:, start : start + length]

    def put_vec(index, value):
        start, length = segs[index]
        gvec_ref[:, start : start + length] = value

    for part, ref in enumerate((dq_ref, dk_ref, dv_ref)):
        columns = slice(part * channels, (part + 1) * channels)
        gqkv_ref[:, columns] = mm(ref[...], normed_ref[...]).T.astype(bf16)

    gain_one = seg(6)
    clear_ends(buf, rows_n, freq_bins)

    def norm_part(i, carry):
        g_gain, g_shift, g_bias = carry
        start = pl.multiple_of(i * CHUNK, CHUNK)
        rows = pl.ds(start, CHUNK)
        dnormed_t = None
        for part, ref in enumerate((dq_ref, dk_ref, dv_ref)):
            term = mm(wide_ref[:, part * channels : (part + 1) * channels], ref[:, rows])
            dnormed_t = term if dnormed_t is None else dnormed_t + term
        dnormed = dnormed_t.T
        stream = one_ref[rows, :]
        gap = stream - row_mean(stream)
        scale = lax.rsqrt(row_mean(gap * gap) + norm_floor)
        hat = gap * scale
        dhat = dnormed * gain_one
        grad = two_grad_ref[rows, :] + scale * (
            dhat - row_mean(dhat) - hat * row_mean(dhat * hat)
        )
        field[rows, :] = grad
        put_shifted(buf, start, grad.astype(bf16).astype(f32), freq_bins)
        return (
            g_gain + col_sum(dnormed * hat),
            g_shift + col_sum(dnormed),
            g_bias + col_sum(grad),
        )

    sums = loop(count, norm_part, (blank, blank, blank))
    for index, value in zip((6, 7, 5), sums):
        put_vec(index, value)

    def weight_grad(which, act_ref):
        act_t[...] = act_ref[...].T
        for a in range(3):
            full = buf[freq_bins * (2 - a) : freq_bins * (2 - a) + rows_n, :]
            for b in range(3):
                shifted = full[:, (2 - b) * channels : (3 - b) * channels]
                first = (3 * a + b) * channels
                gconv_ref[which, first : first + channels, :] = mm(act_t[...], shifted).astype(
                    bf16
                )

    def input_grad(which, start):
        total = None
        for a in range(3):
            for b in range(3):
                first = (3 * (2 - a) + 2 - b) * channels
                part = mm_nt(
                    buf[
                        pl.ds(start + freq_bins * a, CHUNK),
                        b * channels : (b + 1) * channels,
                    ],
                    conv_ref[which, first : first + channels, :],
                )
                total = part if total is None else total + part
        return total

    def norm_back(which, read, center, scale, gain, shift, g_refs):
        def part(i, carry):
            g_gain, g_shift = carry
            start = pl.multiple_of(i * CHUNK, CHUNK)
            rows = pl.ds(start, CHUNK)
            hat = (read(start) - center) * scale
            slope = silu_slope(hat * gain + shift)
            grad = input_grad(which, start) * slope
            grad = jnp.where(live_rows(start, grad.shape, live), grad, 0.0)
            other[rows, :] = grad
            return (g_gain + col_sum(grad * hat), g_shift + col_sum(grad))

        g_gain, g_shift = loop(count, part, (blank, blank))
        put_vec(g_refs[0], g_gain)
        put_vec(g_refs[1], g_shift)
        mean_grad = group_total(g_shift * gain, groups) / counted
        mean_hat = group_total(g_gain * gain, groups) / counted

        def finish(start):
            hat = (read(start) - center) * scale
            grad = (other[pl.ds(start, CHUNK), :] * gain - mean_grad - hat * mean_hat) * scale
            return jnp.where(live_rows(start, grad.shape, live), grad, 0.0)

        return finish

    film = film_ref[0:1]
    lift = 1.0 + film[:, :channels]
    move = film[:, channels:]

    weight_grad(1, act_two_ref)
    finish = norm_back(
        1,
        lambda start: inner_ref[pl.ds(start, CHUNK), :] * lift + move,
        stat_ref[2:3],
        stat_ref[3:4],
        seg(3),
        seg(4),
        (3, 4),
    )

    def inner_part(i, carry):
        g_lift, g_move, g_bias = carry
        start = pl.multiple_of(i * CHUNK, CHUNK)
        moved = finish(start)
        grad = moved * lift
        put_shifted(buf, start, grad.astype(bf16).astype(f32), freq_bins)
        return (
            g_lift + col_sum(moved * inner_ref[pl.ds(start, CHUNK), :]),
            g_move + col_sum(moved),
            g_bias + col_sum(grad),
        )

    g_lift, g_move, g_bias = loop(count, inner_part, (blank, blank, blank))
    put_vec(2, g_bias)

    weight_grad(0, act_one_ref)
    finish_zero = norm_back(
        0,
        lambda start: zero_ref[pl.ds(start, CHUNK), :],
        stat_ref[0:1],
        stat_ref[1:2],
        seg(0),
        seg(1),
        (0, 1),
    )

    def zero_part(i, carry):
        g_stem, g_bias = carry
        start = pl.multiple_of(i * CHUNK, CHUNK)
        rows = pl.ds(start, CHUNK)
        grad = field[rows, :] + finish_zero(start)
        return (g_stem + mm(colsT_ref[:, rows], grad.astype(bf16)), g_bias + col_sum(grad))

    g_stem, g_bias = loop(
        count, zero_part, (jnp.zeros((colsT_ref.shape[0], channels), f32), blank)
    )
    gstem_ref[...] = g_stem
    put_vec(12, g_bias)

    pre_time = film_ref[1:2]
    embedding = film_ref[2:3]
    g_film = jnp.concatenate([g_lift, g_move], 1)
    g_embed = vec_mat(g_film, time_ref[2], True) * silu_slope(embedding)
    g_time = vec_mat(g_embed, time_ref[1], True) * silu_slope(pre_time)
    put_vec(13, g_time)
    put_vec(14, g_embed)
    put_vec(15, g_film)
    factor_ref[0:1] = wave_ref[...]
    factor_ref[1:2] = jax.nn.silu(pre_time)
    factor_ref[2:3] = jax.nn.silu(embedding)
    factor_ref[3:4] = g_time
    factor_ref[4:5] = g_embed
    factor_ref[5:6] = g_film
    factor_ref[6:8] = jnp.zeros((2, embed), f32)


def sized(shape, dtype=f32):
    return jax.ShapeDtypeStruct(shape, dtype)


VM = pl.BlockSpec(memory_space=pltpu.VMEM)
SM = pl.BlockSpec(memory_space=pltpu.SMEM)


def params(mib):
    return pltpu.CompilerParams(vmem_limit_bytes=mib * 2**20)


def run_fore(freq_bins, length, mix, lat, noi, stem_w, conv, wide_qkv, time_low, vec, wave, clap):
    rows_n, latent_ch = lat.shape
    channels = stem_w.shape[1]
    embed = time_low.shape[1]
    field = sized((rows_n, channels))
    field_low = sized((rows_n, channels), bf16)
    return pl.pallas_call(
        functools.partial(fore_kernel, freq_bins, GROUPS),
        in_specs=[SM, SM] + [VM] * 9,
        out_specs=[VM] * 11,
        out_shape=[
            field,
            field_low,
            field,
            field_low,
            field,
            field_low,
            sized((3 * channels, rows_n), bf16),
            sized((9 * latent_ch, rows_n), bf16),
            sized((latent_ch, rows_n)),
            sized((8, channels)),
            sized((8, embed)),
        ],
        scratch_shapes=[
            pltpu.VMEM((rows_n + 2 * freq_bins, 3 * channels), bf16),
            pltpu.VMEM((rows_n, 128), bf16),
            pltpu.VMEM((128, rows_n), f32),
        ],
        compiler_params=params(48),
        name="fore",
    )(length, mix, lat, noi, stem_w, conv, wide_qkv, time_low, vec, wave, clap)


def run_attend(freq_bins, length, qkv_t, key_block=256):
    triple, rows_n = qkv_t.shape
    channels = triple // 3
    dim = channels // HEADS
    return pl.pallas_call(
        functools.partial(attend_kernel, freq_bins, key_block),
        grid=(HEADS,),
        in_specs=[SM]
        + [pl.BlockSpec((dim, rows_n), lambda h, t=t: (t * HEADS + h, 0)) for t in range(3)],
        out_specs=[
            pl.BlockSpec((dim, rows_n), lambda h: (h, 0)),
            pl.BlockSpec((1, 1, rows_n), lambda h: (h, 0, 0)),
        ],
        out_shape=[sized((channels, rows_n)), sized((HEADS, 1, rows_n))],
        scratch_shapes=[
            pltpu.VMEM((rows_n, 128), bf16),
            pltpu.VMEM((128, rows_n), bf16),
            pltpu.VMEM((dim + 16, rows_n), bf16),
        ],
        compiler_params=params(48),
        name="attend",
    )(length, qkv_t, qkv_t, qkv_t)


def run_attend_back(freq_bins, length, qkv_t, lse, mixed_t, grad_t, key_block=512):
    triple, rows_n = qkv_t.shape
    channels = triple // 3
    dim = channels // HEADS
    whole = pl.BlockSpec((dim, rows_n), lambda h, j: (h, 0))
    block = pl.BlockSpec((dim, key_block), lambda h, j: (h, j))
    return pl.pallas_call(
        functools.partial(attend_back_kernel, freq_bins, key_block),
        grid=(HEADS, rows_n // key_block),
        in_specs=[SM]
        + [pl.BlockSpec((dim, rows_n), lambda h, j, t=t: (t * HEADS + h, 0)) for t in range(3)]
        + [pl.BlockSpec((1, 1, rows_n), lambda h, j: (h, 0, 0)), whole, whole],
        out_specs=[whole, block, block],
        out_shape=[sized((channels, rows_n), bf16)] * 3,
        scratch_shapes=[
            pltpu.VMEM((rows_n, 128), bf16),
            pltpu.VMEM((128, rows_n), bf16),
            pltpu.VMEM((rows_n, 128), bf16),
            pltpu.VMEM((128, rows_n), bf16),
            pltpu.VMEM((dim, rows_n), f32),
        ],
        compiler_params=params(48),
        name="attend_back",
    )(length, qkv_t, qkv_t, qkv_t, lse, mixed_t, grad_t)


def run_middle(freq_bins, length, mixed_t, one, wide, down, vec, head_t, head_bias, noi_t):
    rows_n, channels = one.shape
    units = down.shape[0]
    latent_ch = noi_t.shape[0]
    return pl.pallas_call(
        functools.partial(middle_kernel, freq_bins),
        in_specs=[SM] + [VM] * 8,
        out_specs=[VM] * 8,
        out_shape=[
            sized((rows_n, channels)),
            sized((channels, rows_n), bf16),
            sized((units, channels), bf16),
            sized((channels, units), bf16),
            sized((channels, channels), bf16),
            sized((9 * latent_ch, channels)),
            sized(vec.shape),
            sized((latent_ch, 256)),
        ],
        scratch_shapes=[
            pltpu.VMEM((rows_n, units), bf16),
            pltpu.VMEM((rows_n, units), f32),
            pltpu.VMEM((rows_n, channels), f32),
            pltpu.VMEM((rows_n, 128), f32),
            pltpu.VMEM((rows_n, channels), bf16),
            pltpu.VMEM((128, rows_n), f32),
            pltpu.VMEM((rows_n, 128), bf16),
            pltpu.VMEM((channels, rows_n), bf16),
            pltpu.VMEM((channels, rows_n), bf16),
            pltpu.VMEM((rows_n, units), bf16),
            pltpu.VMEM((rows_n, channels), bf16),
        ],
        compiler_params=params(56),
        name="middle",
    )(length, mixed_t, one, wide, down, vec, head_t, head_bias, noi_t)


def run_hind(freq_bins, length, *arrays):
    one = arrays[5]
    rows_n, channels = one.shape
    cols_t = arrays[10]
    vec = arrays[16]
    embed = arrays[15].shape[1]
    return pl.pallas_call(
        functools.partial(hind_kernel, freq_bins, GROUPS),
        in_specs=[SM] + [VM] * len(arrays),
        out_specs=[VM] * 5,
        out_shape=[
            sized((channels, 3 * channels), bf16),
            sized((2, 9 * channels, channels), bf16),
            sized((cols_t.shape[0], channels)),
            sized(vec.shape),
            sized((8, embed)),
        ],
        scratch_shapes=[
            pltpu.VMEM((rows_n + 2 * freq_bins, 3 * channels), bf16),
            pltpu.VMEM((rows_n, channels), f32),
            pltpu.VMEM((rows_n, channels), f32),
            pltpu.VMEM((channels, rows_n), bf16),
        ],
        compiler_params=params(56),
        name="hind",
    )(length, *arrays)


def noise_mix(step_value):
    phase = (step_value.astype(f32) / 1000.0 + 0.008) / 1.008 * (math.pi / 2)
    keep_part = jnp.cos(phase) ** 2
    return jnp.stack([jnp.sqrt(keep_part), jnp.sqrt(1.0 - keep_part)])


def adam_step(weight, moment_one, moment_two, gradient, decay_on, fix_one, fix_two):
    first_new = 0.9 * moment_one + 0.1 * gradient
    second_new = 0.999 * moment_two + 0.001 * gradient * gradient
    moved = first_new / fix_one / (jnp.sqrt(second_new / fix_two) + adam_floor)
    return (weight - adam_rate * (moved + decay_on * weight), first_new, second_new)


def local(
    latents,
    noises,
    clap_embed,
    timesteps,
    lengths,
    step_count,
    stem_w,
    head_w,
    time_w,
    vector,
    conv_w,
    wide_w,
    down_w,
    roots_small,
    root_wide,
    roots_large,
    stem_moment,
    stem_square,
    head_moment,
    head_square,
    time_moment,
    time_square,
    vector_moment,
    vector_square,
    conv_moment,
    conv_square,
    wide_moment,
    down_moment,
):
    frames_n, freq_bins, latent_ch = (latents.shape[1], latents.shape[2], latents.shape[3])
    channels = stem_w.shape[1]
    embed = time_w.shape[2]
    rows_n = frames_n * freq_bins
    both = ("dp", "fsdp")
    here = lax.axis_index("fsdp")

    def gather(value, dim):
        return lax.all_gather(value.astype(bf16), "fsdp", axis=dim, tiled=True)

    conv_full = gather(conv_w, 1)
    time_full = gather(time_w, 1)
    wide_full = gather(wide_w, 0)
    down_full = gather(down_w, 0)
    wide_moment_full = gather(wide_moment, 0)
    down_moment_full = gather(down_moment, 0)

    half_width = embed // 2
    frequency = jnp.exp(-math.log(10000.0) * jnp.arange(half_width).astype(f32) / half_width)
    angles = timesteps[0].astype(f32) * frequency
    wave = jnp.concatenate([jnp.cos(angles), jnp.sin(angles)])[None]
    vec = vector[None]
    head_t = jnp.pad(
        head_w.reshape(9, channels, latent_ch).transpose(0, 2, 1).reshape(-1, channels),
        ((0, 128 - 9 * latent_ch), (0, 0)),
    ).astype(bf16)
    head_bias = vector[-latent_ch:][:, None]

    (
        zero,
        act_one,
        inner,
        act_two,
        one,
        normed,
        qkv_t,
        cols_t,
        noi_t,
        stat,
        film,
    ) = run_fore(
        freq_bins,
        lengths,
        noise_mix(timesteps[0]),
        latents.reshape(rows_n, latent_ch),
        noises.reshape(rows_n, latent_ch),
        stem_w,
        conv_full,
        wide_full[:, : 3 * channels],
        time_full,
        vec,
        wave,
        clap_embed,
    )
    mixed_t, lse = run_attend(freq_bins, lengths, qkv_t)
    two_grad, do_t, gdown, gup, gproj, ghead_t, gvec_mid, small = run_middle(
        freq_bins, lengths, mixed_t, one, wide_full, down_full, vec, head_t, head_bias, noi_t
    )
    gdown, gup, gproj = lax.psum((gdown, gup, gproj), both)
    dq, dk, dv = run_attend_back(freq_bins, lengths, qkv_t, lse, mixed_t, do_t)
    gqkv, gconv, gstem, gvec_hind, factors = run_hind(
        freq_bins,
        lengths,
        dq,
        dk,
        dv,
        two_grad,
        normed,
        one,
        act_two,
        inner,
        act_one,
        zero,
        cols_t,
        stat,
        film,
        conv_full,
        wide_full,
        time_full,
        vec,
        wave,
    )

    conv_shard = lax.psum_scatter(gconv, "fsdp", scatter_dimension=1, tiled=True)
    conv_shard = lax.psum(conv_shard, "dp").astype(f32)
    gqkv = lax.psum(gqkv, both)
    gvec_head = jnp.pad(small[:, 0], (vector.shape[0] - latent_ch, 0))
    gvec = gvec_mid[0] + gvec_hind[0] + gvec_head
    loss_local = jnp.sum(small[:, 128])
    live_local = lengths[0].astype(f32) * freq_bins
    loss_sum, live_count, gstem, ghead_t, gvec = lax.psum(
        (loss_local, live_local, gstem, ghead_t, gvec), both
    )
    ghead = ghead_t.reshape(9, latent_ch, channels).transpose(0, 2, 1).reshape(-1, latent_ch)
    everyone = lax.all_gather(factors, both, axis=0)
    rows_here = time_w.shape[1]
    sides = lax.dynamic_slice_in_dim(everyone[:, 0:3], here * rows_here, rows_here, 2)
    time_shard = jnp.einsum("niw,niv->iwv", sides, everyone[:, 3:6], precision=highest)

    def squares(value):
        value = value.astype(f32)
        return jnp.sum(value * value)

    shard_total = lax.psum(squares(conv_shard) + squares(time_shard), "fsdp")
    total = (
        shard_total
        + squares(gstem)
        + squares(ghead)
        + squares(gvec)
        + squares(gdown)
        + squares(gup)
        + squares(gproj)
        + squares(gqkv)
    )
    unit = 2.0 / (latent_ch * live_count)
    loss_value = loss_sum / (latent_ch * live_count)
    grad_norm = unit * jnp.sqrt(total)
    factor = jnp.minimum(1.0, clip_limit / grad_norm) * unit
    step_value = step_count[0].astype(f32)
    fix_one = 1.0 - jnp.power(0.9, step_value)
    fix_two = 1.0 - jnp.power(0.999, step_value)
    vector_clipped = factor * gvec

    def adam(weight, first, second, grad, decay_on):
        return adam_step(weight, first, second, grad, decay_on, fix_one, fix_two)

    stem_out = adam(stem_w, stem_moment, stem_square, factor * gstem, decay_rate)
    head_out = adam(head_w, head_moment, head_square, factor * ghead, decay_rate)
    time_out = adam(time_w, time_moment, time_square, factor * time_shard, decay_rate)
    vector_out = adam(vector, vector_moment, vector_square, vector_clipped, 0.0)
    conv_out = adam(conv_w, conv_moment, conv_square, factor * conv_shard, decay_rate)

    wide_rows = wide_w.shape[0]
    down_rows = down_w.shape[0]
    gwide = jnp.concatenate([gqkv, gproj, gup], 1)
    wide_mine = lax.dynamic_slice_in_dim(gwide, here * wide_rows, wide_rows, 0)
    down_mine = lax.dynamic_slice_in_dim(gdown, here * down_rows, down_rows, 0)
    wide_moment_new = 0.9 * wide_moment + factor * wide_mine.astype(f32)
    down_moment_new = 0.9 * down_moment + factor * down_mine.astype(f32)

    def direction(left_root, moment_full, grad_full, right_root, rows):
        left = lax.dynamic_slice_in_dim(left_root, here * rows, rows, 0).astype(bf16)
        moment_now = 0.9 * moment_full.astype(f32) + factor * grad_full.astype(f32)
        left_done = mm(left, moment_now.astype(bf16))
        return mm(left_done.astype(bf16), right_root.astype(bf16))

    bounds = (0, 3 * channels, 4 * channels, 4 * channels + FF)
    rights = (root_wide, roots_small[3], roots_large[0])
    directions = []
    for index in range(3):
        columns = slice(bounds[index], bounds[index + 1])
        directions.append(
            direction(
                roots_small[index],
                wide_moment_full[:, columns],
                gwide[:, columns],
                rights[index],
                wide_rows,
            )
        )
    wide_new = wide_w * (1.0 - shampoo_rate * decay_rate) - shampoo_rate * jnp.concatenate(
        directions, 1
    )
    down_direction = direction(
        roots_large[1], down_moment_full, gdown, roots_small[4], down_rows
    )
    down_new = down_w * (1.0 - shampoo_rate * decay_rate) - shampoo_rate * down_direction
    return (
        loss_value,
        grad_norm,
        stem_out[0],
        stem_out[1],
        stem_out[2],
        head_out[0],
        head_out[1],
        head_out[2],
        time_out[0],
        time_out[1],
        time_out[2],
        vector_clipped,
        vector_out[1],
        vector_out[2],
        conv_out[0],
        conv_out[1],
        conv_out[2],
        wide_new,
        wide_moment_new,
        down_new,
        down_moment_new,
    )


def solution(mesh):
    in_specs = (
        P(("dp", "fsdp"), None, None, None),
        P(("dp", "fsdp"), None, None, None),
        P(("dp", "fsdp"), None),
        P(("dp", "fsdp")),
        P(("dp", "fsdp")),
        P(),
        P(),
        P(),
        P(None, "fsdp", None),
        P(),
        P(None, "fsdp", None),
        P("fsdp", None),
        P("fsdp", None),
        P(),
        P(),
        P(),
        P(),
        P(),
        P(),
        P(),
        P(None, "fsdp", None),
        P(None, "fsdp", None),
        P(),
        P(),
        P(None, "fsdp", None),
        P(None, "fsdp", None),
        P("fsdp", None),
        P("fsdp", None),
    )
    out_specs = (
        P(),
        P(),
        P(),
        P(),
        P(),
        P(),
        P(),
        P(),
        P(None, "fsdp", None),
        P(None, "fsdp", None),
        P(None, "fsdp", None),
        P(),
        P(),
        P(),
        P(None, "fsdp", None),
        P(None, "fsdp", None),
        P(None, "fsdp", None),
        P("fsdp", None),
        P("fsdp", None),
        P("fsdp", None),
        P("fsdp", None),
    )
    return jax.shard_map(local, mesh=mesh, in_specs=in_specs, out_specs=out_specs, check_vma=False)
```

```python
import functools
import math

import jax
import jax.numpy as jnp
from jax import lax
from jax.experimental import pallas as pl
from jax.experimental.pallas import tpu as pltpu
from jax.sharding import PartitionSpec as P

HEADS = 8
FF = 1024
EMB = 512
GROUPS = 32

norm_floor = 1e-05
masked_score = -1e30
clip_limit = 0.002
adam_rate = 0.05
adam_floor = 1e-08
shampoo_rate = 0.02
decay_rate = 0.01

f32 = jnp.float32
bf16 = jnp.bfloat16
highest = lax.Precision.HIGHEST
LOG2E = math.log2(math.e)
CHUNK = 256


def mm(left_op, right_op):
    return jnp.dot(left_op, right_op, preferred_element_type=f32)


def mm_nt(left_op, right_op):
    return lax.dot_general(
        left_op, right_op, (((1,), (1,)), ((), ())), preferred_element_type=f32
    )


def col_sum(value):
    return jnp.sum(value, axis=0, keepdims=True)


def row_mean(value):
    return jnp.mean(value, axis=-1, keepdims=True)


def loop(count, body, init):
    return lax.fori_loop(0, count, body, init)


def tap_shift(field, a, b, freq_bins):
    length = field.shape[1]
    step = freq_bins * (a - 1) + (b - 1)
    if step == 0:
        return field
    pos = lax.broadcasted_iota(jnp.int32, field.shape, 1)
    bin_pos = lax.rem(pos, freq_bins)
    keep = None
    for wanted, test in (
        (a == 0, lambda: pos >= freq_bins),
        (a == 2, lambda: pos < length - freq_bins),
        (b == 0, lambda: bin_pos >= 1),
        (b == 2, lambda: bin_pos < freq_bins - 1),
    ):
        if wanted:
            keep = test() if keep is None else jnp.logical_and(keep, test())
    return jnp.where(keep, pltpu.roll(field, (-step) % length, 1), 0.0)


def put_shifted(buf, start, value, freq_bins):
    rows, channels = value.shape
    bin_pos = lax.rem(lax.broadcasted_iota(jnp.int32, value.shape, 0), freq_bins)
    before = jnp.where(bin_pos == 0, 0.0, pltpu.roll(value, 1, 0))
    after = jnp.where(bin_pos == freq_bins - 1, 0.0, pltpu.roll(value, rows - 1, 0))
    where = pl.ds(start + freq_bins, rows)
    buf[where, 0:channels] = before.astype(bf16)
    buf[where, channels : 2 * channels] = value.astype(bf16)
    buf[where, 2 * channels : 3 * channels] = after.astype(bf16)


def clear_ends(buf, rows_n, freq_bins):
    blank = jnp.zeros((freq_bins, buf.shape[1]), bf16)
    buf[0:freq_bins, :] = blank
    buf[rows_n + freq_bins : rows_n + 2 * freq_bins, :] = blank


def live_rows(start, shape, live):
    return start + lax.broadcasted_iota(jnp.int32, shape, 0) < live


def group_total(row, groups):
    channels = row.shape[1]
    size = channels // groups
    one = lax.broadcasted_iota(jnp.int32, (channels, channels), 0) // size
    two = lax.broadcasted_iota(jnp.int32, (channels, channels), 1) // size
    same = jnp.where(one == two, 1.0, 0.0).astype(f32)
    wide = jnp.broadcast_to(row, (8, channels))
    return jnp.dot(wide, same, precision=highest, preferred_element_type=f32)[0:1]


def vec_mat(row, weight, transposed=False):
    top = row.astype(bf16).astype(f32)
    rest = row - top
    mid = rest.astype(bf16).astype(f32)
    low = rest - mid
    shape = (16, row.shape[1])
    index = lax.broadcasted_iota(jnp.int32, shape, 0)
    stacked = jnp.where(
        index == 0,
        jnp.broadcast_to(top, shape),
        jnp.where(
            index == 1,
            jnp.broadcast_to(mid, shape),
            jnp.where(index == 2, jnp.broadcast_to(low, shape), 0.0),
        ),
    ).astype(bf16)
    return col_sum(mm_nt(stacked, weight) if transposed else mm(stacked, weight))


def silu_slope(value):
    gate = jax.nn.sigmoid(value)
    return gate * (1.0 + value * (1.0 - gate))


def group_stats(read, rows_n, live, channels, groups, counted):
    count = rows_n // CHUNK

    def add(i, total):
        start = pl.multiple_of(i * CHUNK, CHUNK)
        value = read(start)
        return total + col_sum(jnp.where(live_rows(start, value.shape, live), value, 0.0))

    center = group_total(loop(count, add, jnp.zeros((1, channels), f32)), groups) / counted

    def add_square(i, total):
        start = pl.multiple_of(i * CHUNK, CHUNK)
        value = read(start) - center
        return total + col_sum(jnp.where(live_rows(start, value.shape, live), value * value, 0.0))

    spread = group_total(loop(count, add_square, jnp.zeros((1, channels), f32)), groups) / counted
    return center, lax.rsqrt(spread + norm_floor)


def offsets(channels, embed_width, hidden_units, latent_ch):
    starts = []
    start = 0
    for length in [channels] * 13 + [embed_width] * 3 + [hidden_units, latent_ch]:
        starts.append((start, length))
        start = start + length
    return starts


def put_small(ref, index, value):
    if index < 13:
        half = value.shape[1]
        ref[index // 2 : index // 2 + 1, (index % 2) * half : (index % 2 + 1) * half] = value
    elif index < 16:
        ref[index - 6 : index - 5, :] = value
    elif index == 16:
        half = value.shape[1] // 2
        ref[10:11, :] = value[:, :half]
        ref[11:12, :] = value[:, half:]
    else:
        ref[index - 5 : index - 4, 0 : value.shape[1]] = value


def take_small(rows, latent_ch):
    return jnp.concatenate(
        [
            rows[0:6].reshape(-1),
            rows[6, : rows.shape[1] // 2],
            rows[7:12].reshape(-1),
            rows[12, :latent_ch],
        ]
    )


def fore_kernel(
    freq_bins,
    groups,
    len_ref,
    mix_ref,
    lat_ref,
    noi_ref,
    stem_ref,
    conv_ref,
    wide_ref,
    time_ref,
    vec_ref,
    wave_ref,
    clap_ref,
    zero_ref,
    act_one_ref,
    inner_ref,
    act_two_ref,
    one_ref,
    normed_ref,
    qkv_ref,
    colsT_ref,
    noiT_ref,
    stat_ref,
    film_ref,
    buf,
    cols,
    tall,
):
    rows_n, channels = zero_ref.shape
    latent_ch = lat_ref.shape[1]
    embed = time_ref.shape[1]
    count = rows_n // CHUNK
    live = len_ref[0] * freq_bins
    counted = (live * (channels // groups)).astype(f32)
    segs = offsets(channels, embed, FF, latent_ch)

    def seg(index):
        start, length = segs[index]
        return vec_ref[:, start : start + length]

    wave = wave_ref[...]
    pre_time = vec_mat(wave, time_ref[0]) + seg(13)
    embedding = vec_mat(jax.nn.silu(pre_time), time_ref[1]) + seg(14) + clap_ref[...]
    film = vec_mat(jax.nn.silu(embedding), time_ref[2]) + seg(15)
    film_ref[0:1] = film
    film_ref[1:2] = pre_time
    film_ref[2:3] = embedding
    film_ref[3:8] = jnp.zeros((5, embed), f32)
    lift = 1.0 + film[:, :channels]
    move = film[:, channels:]

    eye = jnp.where(
        lax.broadcasted_iota(jnp.int32, (latent_ch, latent_ch), 0)
        == lax.broadcasted_iota(jnp.int32, (latent_ch, latent_ch), 1),
        1.0,
        0.0,
    ).astype(bf16)
    noise_t = mm_nt(eye, noi_ref[...])
    noiT_ref[...] = noise_t
    mixed = mix_ref[0] * mm_nt(eye, lat_ref[...]) + mix_ref[1] * noise_t
    pos = lax.broadcasted_iota(jnp.int32, mixed.shape, 1)
    noisy = jnp.where(pos < live, mixed, 0.0).astype(bf16).astype(f32)
    taps = 9 * latent_ch
    for a in range(3):
        for b in range(3):
            tap = 3 * a + b
            tall[tap * latent_ch : (tap + 1) * latent_ch] = tap_shift(noisy, a, b, freq_bins)
    tall[taps:] = jnp.zeros((tall.shape[0] - taps, rows_n), f32)
    colsT_ref[...] = tall[0:taps].astype(bf16)
    cols[...] = tall[...].T.astype(bf16)
    stem_low = jnp.concatenate(
        [stem_ref[...], jnp.zeros((cols.shape[1] - taps, channels), f32)], 0
    ).astype(bf16)
    stem_bias = seg(12)

    def stem_part(i, carry):
        rows = pl.ds(pl.multiple_of(i * CHUNK, CHUNK), CHUNK)
        zero_ref[rows, :] = mm(cols[rows, :], stem_low) + stem_bias
        return carry

    loop(count, stem_part, 0)

    clear_ends(buf, rows_n, freq_bins)

    def convolve(which, start):
        total = None
        for a in range(3):
            part = mm(
                buf[pl.ds(start + freq_bins * a, CHUNK), :],
                conv_ref[which, 3 * a * channels : 3 * (a + 1) * channels, :],
            )
            total = part if total is None else total + part
        return total

    def activate(read, center, scale, gain, shift, act_ref):
        factor = scale * gain

        def part(i, carry):
            start = pl.multiple_of(i * CHUNK, CHUNK)
            value = jax.nn.silu((read(start) - center) * factor + shift)
            value = jnp.where(live_rows(start, value.shape, live), value, 0.0)
            low = value.astype(bf16)
            act_ref[pl.ds(start, CHUNK), :] = low
            put_shifted(buf, start, low.astype(f32), freq_bins)
            return carry

        loop(count, part, 0)

    def read_zero(start):
        return zero_ref[pl.ds(start, CHUNK), :]

    center, scale = group_stats(read_zero, rows_n, live, channels, groups, counted)
    stat_ref[0:1] = center
    stat_ref[1:2] = scale
    activate(read_zero, center, scale, seg(0), seg(1), act_one_ref)

    bias_one = seg(2)

    def conv_part(i, carry):
        start = pl.multiple_of(i * CHUNK, CHUNK)
        inner_ref[pl.ds(start, CHUNK), :] = convolve(0, start) + bias_one
        return carry

    loop(count, conv_part, 0)

    def read_moved(start):
        return inner_ref[pl.ds(start, CHUNK), :] * lift + move

    center, scale = group_stats(read_moved, rows_n, live, channels, groups, counted)
    stat_ref[2:3] = center
    stat_ref[3:4] = scale
    stat_ref[4:8] = jnp.zeros((4, channels), f32)
    activate(read_moved, center, scale, seg(3), seg(4), act_two_ref)

    bias_two = seg(5)
    gain, shift = seg(6), seg(7)
    wqkv_t = wide_ref[...].T

    def last_part(i, carry):
        start = pl.multiple_of(i * CHUNK, CHUNK)
        rows = pl.ds(start, CHUNK)
        stream = zero_ref[rows, :] + convolve(1, start) + bias_two
        one_ref[rows, :] = stream
        gap = stream - row_mean(stream)
        normed = gap * lax.rsqrt(row_mean(gap * gap) + norm_floor) * gain + shift
        low = normed.astype(bf16)
        normed_ref[rows, :] = low
        qkv_ref[:, rows] = mm_nt(wqkv_t, low).astype(bf16)
        return carry

    loop(count, last_part, 0)


MESH = pl.DeviceIdType.MESH


def places():
    n_d, n_f = lax.axis_size("dp"), lax.axis_size("fsdp")
    me = lax.axis_index("fsdp")
    return n_d, n_f // 2, lax.axis_index("dp"), me // 2, lax.rem(me, 2)


def push(src, dst, sends, recvs, target):
    copy = pltpu.make_async_remote_copy(
        src_ref=src,
        dst_ref=dst,
        send_sem=sends,
        recv_sem=recvs,
        device_id=target,
        device_id_type=MESH,
    )
    copy.start()
    return copy


def greet(n_d, n_z, d, z, c):
    barrier = pltpu.get_barrier_semaphore()
    for j in range(1, n_d):
        pl.semaphore_signal(
            barrier, inc=1, device_id={"dp": lax.rem(d + j, n_d)}, device_id_type=MESH
        )
    for k in range(1, n_z):
        pl.semaphore_signal(
            barrier,
            inc=1,
            device_id={"fsdp": 2 * lax.rem(z + k, n_z) + c},
            device_id_type=MESH,
        )
    pl.semaphore_signal(
        barrier, inc=1, device_id={"fsdp": 2 * z + 1 - c}, device_id_type=MESH
    )
    pl.semaphore_wait(barrier, n_d + n_z - 1)


def conv_piece(d, n_d, channels):
    width = 2 * channels // n_d
    return (d * width) // channels, pl.ds(
        pl.multiple_of(lax.rem(d * width, channels), 128), width
    )


def lane_piece(d, n_d, lanes):
    width = lanes // n_d
    return pl.ds(pl.multiple_of(d * width, 128), width)


def plan_gather(here, parts, wholes, sems):
    n_d, n_z, d, z, c = here
    s1, r1, s2, r2, s3, r3 = sems
    sibling = {"fsdp": 2 * z + 1 - c}

    def copy(ref, sends, recvs, target):
        return pltpu.make_async_remote_copy(
            src_ref=ref,
            dst_ref=ref,
            send_sem=sends,
            recv_sem=recvs,
            device_id=target,
            device_id_type=MESH,
        )

    def source(k):
        return lax.rem(z - k + n_z, n_z)

    def first(k):
        target = {"fsdp": 2 * lax.rem(z + k, n_z) + c}
        return [copy(r, s1.at[k, i], r1.at[k, i], target) for i, r in enumerate(parts(z))]

    def second(k, j):
        target = {"dp": lax.rem(d + j, n_d)}
        refs = parts(source(k))
        return [copy(r, s2.at[k, j, i], r2.at[k, j, i], target) for i, r in enumerate(refs)]

    def last(k):
        refs = wholes(source(k))
        return [copy(r, s3.at[k, i], r3.at[k, i], sibling) for i, r in enumerate(refs)]

    def start(group):
        for item in group:
            item.start()

    def arrive(group):
        for item in group:
            item.wait_recv()

    def leave(group):
        for item in group:
            item.wait_send()

    far = range(1, n_z)
    peers = range(1, n_d)

    def step_one():
        for k in far:
            start(first(k))
        start(last(0))

    def step_two():
        for k in far:
            arrive(first(k))
            for j in peers:
                start(second(k, j))

    def step_three():
        for k in far:
            for j in peers:
                arrive(second(k, j))
            start(last(k))

    def step_four():
        for k in range(n_z):
            arrive(last(k))
        for k in far:
            leave(first(k))
            for j in peers:
                leave(second(k, j))
        for k in range(n_z):
            leave(last(k))

    return step_one, step_two, step_three, step_four


def gather_sems(count):
    n_d, n_z = lax.axis_size("dp"), lax.axis_size("fsdp") // 2
    dma = pltpu.SemaphoreType.DMA
    return [
        dma((n_z, count)),
        dma((n_z, count)),
        dma((n_z, n_d, count)),
        dma((n_z, n_d, count)),
        dma((n_z, count)),
        dma((n_z, count)),
    ]


def plan_total(here, value_ref, out, pair, other, from_dp, summed, from_z, sems):
    n_d, n_z, d, z, c = here
    lanes_n = out.shape[3]
    mine = lane_piece(d, n_d, lanes_n)
    sibling = {"fsdp": 2 * z + 1 - c}
    send, recv = sems

    def copy(src, dst, index, target):
        return pltpu.make_async_remote_copy(
            src_ref=src,
            dst_ref=dst,
            send_sem=send.at[index],
            recv_sem=recv.at[index],
            device_id=target,
            device_id_type=MESH,
        )

    def replica(j):
        return lax.rem(d + j, n_d)

    def chip(k):
        return lax.rem(z + k, n_z)

    def one():
        return [copy(value_ref.at[:, 1 - c], other, 0, sibling)]

    def two():
        return [
            copy(
                pair.at[:, :, lane_piece(replica(j), n_d, lanes_n)],
                from_dp.at[j],
                j,
                {"dp": replica(j)},
            )
            for j in range(1, n_d)
        ]

    def three():
        return [
            copy(summed.at[chip(k)], from_z.at[k], n_d + k, {"fsdp": 2 * chip(k) + c})
            for k in range(1, n_z)
        ]

    def four():
        ref = out.at[z, c, :, mine]
        return [
            copy(ref, ref, n_d + n_z + j, {"dp": replica(j)}) for j in range(1, n_d)
        ]

    def five():
        ref = out.at[z, c]
        return [
            copy(ref, ref, 2 * n_d + n_z + k, {"fsdp": 2 * chip(k) + c}) for k in range(1, n_z)
        ]

    def six():
        ref = out.at[:, c]
        return [copy(ref, ref, 2 * n_d + 2 * n_z, sibling)]

    def start(group):
        for item in group:
            item.start()

    def arrive(group):
        for item in group:
            item.wait_recv()

    def step_one():
        start(one())

    def step_two():
        arrive(one())
        for i in range(n_z):
            pair[i] = (
                value_ref[i, pl.ds(c, 1)][0].astype(f32) + other[i].astype(f32)
            ).astype(pair.dtype)
        start(two())

    def step_three():
        arrive(two())
        for i in range(n_z):
            value = pair[i, :, mine].astype(f32)
            for j in range(1, n_d):
                value = value + from_dp[j, i].astype(f32)
            summed[i] = value.astype(summed.dtype)
        start(three())

    def step_four():
        arrive(three())
        value = summed[pl.ds(z, 1)][0].astype(f32)
        for k in range(1, n_z):
            value = value + from_z[k].astype(f32)
        out[pl.ds(z, 1), pl.ds(c, 1), :, mine] = value.astype(out.dtype)[None, None]
        start(four())

    def step_five():
        arrive(four())
        start(five())

    def step_six():
        arrive(five())
        start(six())

    def step_seven():
        arrive(six())
        for group in (one(), two(), three(), four(), five(), six()):
            for item in group:
                item.wait_send()

    return step_one, step_two, step_three, step_four, step_five, step_six, step_seven


def total_scratch(rows, lanes, dtype):
    n_d, n_z = lax.axis_size("dp"), lax.axis_size("fsdp") // 2
    part = lanes // n_d
    dma = pltpu.SemaphoreType.DMA
    count = 2 * n_d + 2 * n_z + 1
    return [
        pltpu.VMEM((n_z, 2, rows, lanes), dtype),
        pltpu.VMEM((n_z, rows, lanes), dtype),
        pltpu.VMEM((n_z, rows, lanes), dtype),
        pltpu.VMEM((n_d, n_z, rows, part), dtype),
        pltpu.VMEM((n_z, rows, part), dtype),
        pltpu.VMEM((n_z, rows, part), dtype),
        dma((count,)),
        dma((count,)),
    ]


def fold_rows(value):
    half = value.shape[0] // 2
    return jnp.concatenate([value[:half], value[half:]], 1)


def shard_gather(here, wide_land, down_land, sems):
    n_d, n_z, d, z, c = here
    lanes_w = lane_piece(d, n_d, wide_land.shape[3])
    lanes_d = lane_piece(d, n_d, down_land.shape[3])

    def parts(source):
        return [
            wide_land.at[source, c, :, lanes_w],
            down_land.at[source, c, :, lanes_d],
        ]

    def wholes(source):
        return [wide_land.at[source, c], down_land.at[source, c]]

    return plan_gather(here, parts, wholes, sems)


def place_shards(here, wide_ref, down_ref, wide_land, down_land):
    z, c = here[3], here[4]
    wide_land[pl.ds(z, 1), pl.ds(c, 1)] = wide_ref[...].astype(bf16)[None, None]
    down_land[pl.ds(z, 1), pl.ds(c, 1)] = fold_rows(down_ref[...]).astype(bf16)[None, None]


def land_out(wide_land, down_land, wide_out, down_out):
    n_z = wide_land.shape[0]
    lanes = down_out.shape[1]
    rows_w, rows_d = wide_land.shape[2], down_land.shape[2]
    for i in range(n_z):
        for j in range(2):
            shard = 2 * i + j
            wide_out[shard * rows_w : (shard + 1) * rows_w, :] = wide_land[i, j]
            first = 2 * shard * rows_d
            down_out[first : first + rows_d, :] = down_land[i, j, :, :lanes]
            down_out[first + rows_d : first + 2 * rows_d, :] = down_land[i, j, :, lanes:]


def land_scratch(wide_shape, down_shape):
    n_z = lax.axis_size("fsdp") // 2
    return [
        pltpu.VMEM((n_z, 2) + wide_shape, bf16),
        pltpu.VMEM((n_z, 2, down_shape[0] // 2, 2 * down_shape[1]), bf16),
    ] + gather_sems(2)


def fill_query(aug, query, factor, extra):
    dim, length = query.shape
    scaled = query.astype(f32) * (factor * LOG2E)
    high = scaled.astype(bf16)
    aug[0:dim] = high
    aug[dim : 2 * dim] = (scaled - high.astype(f32)).astype(bf16)
    index = lax.broadcasted_iota(jnp.int32, (16, length), 0)
    tile = jnp.where(index == 0, 1.0, 0.0)
    for place, row in enumerate(extra):
        tile = jnp.where(index == place + 1, jnp.broadcast_to(row, tile.shape), tile)
    aug[2 * dim : 2 * dim + 16] = tile.astype(bf16)
    aug[2 * dim + 16 :] = jnp.zeros((aug.shape[0] - 2 * dim - 16, length), bf16)


def fill_keys(aug, keys, live):
    dim, length = keys.shape
    rest = aug.shape[1] - 2 * dim
    index = lax.broadcasted_iota(jnp.int32, (rest, length), 0)
    pos = lax.broadcasted_iota(jnp.int32, (rest, length), 1)
    mask = jnp.where(pos < live, 0.0, masked_score)
    tile = jnp.where(index == 0, mask, jnp.where(index < 4, 1.0, 0.0))
    both = keys.astype(f32)
    aug[...] = jnp.concatenate([both, both, tile], 0).T.astype(bf16)


def three_parts(row):
    top = row.astype(bf16).astype(f32)
    rest = row - top
    mid = rest.astype(bf16).astype(f32)
    return top, mid, rest - mid


def attend_kernel(
    freq_bins,
    key_block,
    len_ref,
    q_ref,
    k_ref,
    v_ref,
    up_ref,
    down_ref,
    o_ref,
    lse_ref,
    up_out,
    down_out,
    kaug,
    qaug,
    vaug,
    up_land,
    down_land,
    *sems,
):
    dim, length = q_ref.shape
    here = places()
    steps = shard_gather(here, up_land, down_land, sems)
    head = pl.program_id(0)

    @pl.when(head == 0)
    def _():
        place_shards(here, up_ref, down_ref, up_land, down_land)
        greet(*here)
        steps[0]()

    pl.when(head == 1)(steps[1])
    pl.when(head == 3)(steps[2])

    @pl.when(head == 5)
    def _():
        steps[3]()
        land_out(up_land, down_land, up_out, down_out)

    live = len_ref[0] * freq_bins
    fill_query(qaug, q_ref[...], dim ** (-0.5), ())
    fill_keys(kaug, k_ref[...], live)
    vaug[0:dim] = v_ref[...]
    index = lax.broadcasted_iota(jnp.int32, (16, length), 0)
    vaug[dim : dim + 16] = jnp.where(index == 0, 1.0, 0.0).astype(bf16)
    top = None
    for i in range(length // key_block):
        keys = slice(i * key_block, (i + 1) * key_block)
        scores = mm(kaug[keys, :], qaug[...])
        block_top = jnp.max(scores, axis=0, keepdims=True)
        new_top = block_top if top is None else jnp.maximum(top, block_top)
        weights = jnp.exp2(scores - new_top).astype(bf16)
        part = mm(vaug[:, keys], weights)
        total = part if top is None else total * jnp.exp2(top - new_top) + part
        top = new_top
    summed = total[dim : dim + 1]
    o_ref[...] = total[0:dim] / summed
    lse_ref[0] = top + jnp.log2(summed)


def attend_back_kernel(
    freq_bins,
    key_block,
    len_ref,
    q_ref,
    k_ref,
    v_ref,
    lse_ref,
    o_ref,
    do_ref,
    early_ref,
    wide_ref,
    down_ref,
    dq_ref,
    dk_ref,
    dv_ref,
    early_out,
    wide_out,
    down_out,
    kaug,
    qaug,
    vaug,
    daug,
    acc,
    early_land,
    pair,
    other,
    from_dp,
    summed,
    from_z,
    send,
    recv,
    wide_land,
    down_land,
    *sems,
):
    dim, length = q_ref.shape
    step = pl.program_id(1)
    here = places()
    now = pl.program_id(0) * pl.num_programs(1) + step
    gathers = shard_gather(here, wide_land, down_land, sems)
    totals = plan_total(
        here, early_ref, early_land, pair, other, from_dp, summed, from_z, (send, recv)
    )

    @pl.when(now == 0)
    def _():
        place_shards(here, wide_ref, down_ref, wide_land, down_land)
        greet(*here)
        totals[0]()

    for place, action in (
        (2, totals[1]),
        (6, totals[2]),
        (9, totals[3]),
        (11, totals[4]),
        (13, totals[5]),
        (16, totals[6]),
        (17, gathers[0]),
        (19, gathers[1]),
        (23, gathers[2]),
        (27, gathers[3]),
    ):
        pl.when(now == place)(action)

    @pl.when(now == 28)
    def _():
        early_out[...] = early_land[...]
        land_out(wide_land, down_land, wide_out, down_out)

    factor = dim ** (-0.5)

    @pl.when(step == 0)
    def _():
        live = len_ref[0] * freq_bins
        fill_query(qaug, q_ref[...], factor, three_parts(-lse_ref[0]))
        fill_keys(kaug, k_ref[...], live)
        values = v_ref[...].astype(f32)
        rest = vaug.shape[1] - dim
        index = lax.broadcasted_iota(jnp.int32, (rest, length), 0)
        tile = jnp.where(index < 3, -1.0, 0.0)
        vaug[...] = jnp.concatenate([values, tile], 0).T.astype(bf16)
        back = do_ref[...]
        delta = col_sum(back.astype(f32) * o_ref[...])
        daug[0:dim] = back
        index = lax.broadcasted_iota(jnp.int32, (16, length), 0)
        tile = jnp.zeros((16, length), f32)
        for place, row in enumerate(three_parts(delta)):
            tile = jnp.where(index == place, jnp.broadcast_to(row, tile.shape), tile)
        daug[dim : dim + 16] = tile.astype(bf16)
        daug[dim + 16 :] = jnp.zeros((daug.shape[0] - dim - 16, length), bf16)
        acc[...] = jnp.zeros(acc.shape, f32)

    keys = pl.ds(pl.multiple_of(step * key_block, key_block), key_block)
    weights = jnp.exp2(mm(kaug[keys, :], qaug[...]))
    raw = (weights * mm(vaug[keys, :], daug[...])).astype(bf16)
    dv_ref[...] = mm_nt(do_ref[...], weights.astype(bf16)).astype(bf16)
    dk_ref[...] = (mm_nt(q_ref[...], raw) * factor).astype(bf16)
    acc[...] += mm(k_ref[:, keys], raw)

    @pl.when(step == pl.num_programs(1) - 1)
    def _():
        dq_ref[...] = (acc[...] * factor).astype(bf16)


def middle_kernel(
    freq_bins,
    len_ref,
    mixed_ref,
    one_ref,
    out_ref,
    up_ref,
    down_ref,
    vec_ref,
    head_ref,
    head_bias_ref,
    noiT_ref,
    two_grad_ref,
    do_ref,
    early_ref,
    ghead_ref,
    small_ref,
    hidden,
    slope,
    xhat,
    spread,
    three,
    prod,
    gcols,
    normed_t,
    three_t,
    gpre,
    glow,
):
    rows_n, channels = one_ref.shape
    units = down_ref.shape[0]
    latent_ch = noiT_ref.shape[0]
    count = rows_n // CHUNK
    live = len_ref[0] * freq_bins
    segs = offsets(channels, EMB, units, latent_ch)

    def seg(index):
        start, length = segs[index]
        return vec_ref[:, start : start + length]

    w_out = out_ref[...]
    proj_bias, gain, shift, up_bias, down_bias = seg(8), seg(9), seg(10), seg(16), seg(11)

    def fore(i, carry):
        start = pl.multiple_of(i * CHUNK, CHUNK)
        rows = pl.ds(start, CHUNK)
        mixed = mixed_ref[:, rows].T.astype(bf16)
        stream = one_ref[rows, :] + mm(mixed, w_out) + proj_bias
        gap = stream - row_mean(stream)
        scale = lax.rsqrt(row_mean(gap * gap) + norm_floor)
        hat = gap * scale
        xhat[rows, :] = hat
        spread[rows, :] = jnp.broadcast_to(scale, (CHUNK, spread.shape[1]))
        normed = (hat * gain + shift).astype(bf16)
        normed_t[:, rows] = normed.T
        pre = mm(normed, up_ref[...]) + up_bias
        phi = 0.5 * (1.0 + lax.erf(pre * (0.5**0.5)))
        slope[rows, :] = phi + pre * jnp.exp(-0.5 * pre * pre) * (0.5 / math.pi) ** 0.5
        low = (pre * phi).astype(bf16)
        hidden[rows, :] = low
        stream = stream + mm(low, down_ref[...]) + down_bias
        stream = jnp.where(live_rows(start, stream.shape, live), stream, 0.0).astype(bf16)
        three[rows, :] = stream
        prod[:, rows] = mm_nt(head_ref[...], stream)
        return carry

    loop(count, fore, 0)

    taps = 9 * latent_ch
    predicted = jnp.zeros((latent_ch, rows_n), f32) + head_bias_ref[...]
    for a in range(3):
        for b in range(3):
            tap = 3 * a + b
            predicted = predicted + tap_shift(
                prod[tap * latent_ch : (tap + 1) * latent_ch], a, b, freq_bins
            )
    pos = lax.broadcasted_iota(jnp.int32, predicted.shape, 1)
    errors = jnp.where(pos < live, predicted - noiT_ref[...], 0.0)
    small_ref[...] = jnp.zeros(small_ref.shape, f32)
    tile = (latent_ch, 128)
    sums = jnp.broadcast_to(jnp.sum(errors, axis=1, keepdims=True), tile)
    same = lax.broadcasted_iota(jnp.int32, tile, 0) == lax.broadcasted_iota(jnp.int32, tile, 1)
    put_small(small_ref, 17, col_sum(jnp.where(same, sums, 0.0)))
    sums = jnp.broadcast_to(jnp.sum(errors * errors, axis=1, keepdims=True), tile)
    put_small(small_ref, 18, col_sum(sums))
    put_small(small_ref, 19, jnp.zeros((1, 128), f32) + live.astype(f32))
    errors = errors.astype(bf16).astype(f32)
    for a in range(3):
        for b in range(3):
            tap = 3 * a + b
            prod[tap * latent_ch : (tap + 1) * latent_ch] = tap_shift(
                errors, 2 - a, 2 - b, freq_bins
            )
    prod[taps:] = jnp.zeros((prod.shape[0] - taps, rows_n), f32)
    gcols[...] = prod[...].T.astype(bf16)
    ghead_ref[...] = mm(prod[0:taps].astype(bf16), three[...])

    def back(i, carry):
        g_down, g_up, g_gain, g_shift, g_proj = carry
        start = pl.multiple_of(i * CHUNK, CHUNK)
        rows = pl.ds(start, CHUNK)
        grad = mm(gcols[rows, :], head_ref[...])
        grad = jnp.where(live_rows(start, grad.shape, live), grad, 0.0)
        low = grad.astype(bf16)
        three_t[:, rows] = low.T
        pre = mm_nt(low, down_ref[...]) * slope[rows, :]
        pre_low = pre.astype(bf16)
        gpre[rows, :] = pre_low
        dnormed = mm_nt(pre_low, up_ref[...])
        hat = xhat[rows, :]
        dhat = dnormed * gain
        dstream = (dhat - row_mean(dhat) - hat * row_mean(dhat * hat)) * spread[rows, 0:1]
        two = grad + dstream
        two_grad_ref[rows, :] = two
        two_low = two.astype(bf16)
        glow[rows, :] = two_low
        do_ref[:, rows] = mm_nt(w_out, two_low).astype(bf16)
        return (
            g_down + col_sum(grad),
            g_up + col_sum(pre),
            g_gain + col_sum(dnormed * hat),
            g_shift + col_sum(dnormed),
            g_proj + col_sum(two),
        )

    blank = jnp.zeros((1, channels), f32)
    sums = loop(count, back, (blank, jnp.zeros((1, units), f32), blank, blank, blank))
    for index, value in zip((11, 16, 9, 10, 8), sums):
        put_small(small_ref, index, value)
    half = units // 2
    for part in range(units // channels):
        columns = slice(part * channels, (part + 1) * channels)
        first = (part * channels) % half
        lanes = slice((part * channels) // half * channels, (part * channels) // half * channels + channels)
        early_ref[first : first + channels, lanes] = mm(three_t[...], hidden[:, columns]).T.astype(
            bf16
        )
        first = half + (part // 2) * channels
        lanes = slice((part % 2) * channels, (part % 2 + 1) * channels)
        early_ref[first : first + channels, lanes] = mm(normed_t[...], gpre[:, columns]).astype(
            bf16
        )
    gproj = mm(mixed_ref[...].astype(bf16), glow[...]).astype(bf16)
    first = half + (units // channels // 2) * channels
    early_ref[first:, 0:channels] = gproj[: channels // 2]
    early_ref[first:, channels:] = gproj[channels // 2 :]


def hind_kernel(
    freq_bins,
    groups,
    len_ref,
    dq_ref,
    dk_ref,
    dv_ref,
    two_grad_ref,
    normed_ref,
    one_ref,
    act_two_ref,
    inner_ref,
    act_one_ref,
    zero_ref,
    colsT_ref,
    stat_ref,
    film_ref,
    conv_ref,
    wide_ref,
    time_ref,
    vec_ref,
    wave_ref,
    mid_ref,
    ghead_ref,
    gqkv_ref,
    gconv_ref,
    gsmall_ref,
    factor_ref,
    buf,
    field,
    other,
    act_t,
    small,
):
    rows_n, channels = one_ref.shape
    embed = time_ref.shape[1]
    latent_ch = colsT_ref.shape[0] // 9
    count = rows_n // CHUNK
    live = len_ref[0] * freq_bins
    counted = (live * (channels // groups)).astype(f32)
    segs = offsets(channels, embed, FF, latent_ch)
    blank = jnp.zeros((1, channels), f32)
    small[...] = jnp.zeros(small.shape, f32)

    def seg(index):
        start, length = segs[index]
        return vec_ref[:, start : start + length]

    def put_vec(index, value):
        put_small(small, index, value)

    half = channels // 2
    gqkv_ref[0:channels, 0:channels] = mm(dq_ref[...], normed_ref[...]).T.astype(bf16)
    gqkv_ref[0:channels, channels:] = mm(dk_ref[...], normed_ref[...]).T.astype(bf16)
    values_grad = mm(dv_ref[...], normed_ref[...]).T.astype(bf16)
    gqkv_ref[channels:, 0:channels] = values_grad[:half]
    gqkv_ref[channels:, channels:] = values_grad[half:]

    gain_one = seg(6)
    clear_ends(buf, rows_n, freq_bins)

    def norm_part(i, carry):
        g_gain, g_shift, g_bias = carry
        start = pl.multiple_of(i * CHUNK, CHUNK)
        rows = pl.ds(start, CHUNK)
        dnormed_t = None
        for part, ref in enumerate((dq_ref, dk_ref, dv_ref)):
            term = mm(wide_ref[:, part * channels : (part + 1) * channels], ref[:, rows])
            dnormed_t = term if dnormed_t is None else dnormed_t + term
        dnormed = dnormed_t.T
        stream = one_ref[rows, :]
        gap = stream - row_mean(stream)
        scale = lax.rsqrt(row_mean(gap * gap) + norm_floor)
        hat = gap * scale
        dhat = dnormed * gain_one
        grad = two_grad_ref[rows, :] + scale * (
            dhat - row_mean(dhat) - hat * row_mean(dhat * hat)
        )
        field[rows, :] = grad
        put_shifted(buf, start, grad.astype(bf16).astype(f32), freq_bins)
        return (
            g_gain + col_sum(dnormed * hat),
            g_shift + col_sum(dnormed),
            g_bias + col_sum(grad),
        )

    sums = loop(count, norm_part, (blank, blank, blank))
    for index, value in zip((6, 7, 5), sums):
        put_vec(index, value)

    def weight_grad(which, act_ref):
        act_t[...] = act_ref[...].T
        for a in range(3):
            full = buf[freq_bins * (2 - a) : freq_bins * (2 - a) + rows_n, :]
            for b in range(3):
                shifted = full[:, (2 - b) * channels : (3 - b) * channels]
                first = (3 * a + b) * channels
                gconv_ref[which, first : first + channels, :] = mm(act_t[...], shifted).astype(
                    bf16
                )

    def input_grad(which, start):
        total = None
        for a in range(3):
            for b in range(3):
                first = (3 * (2 - a) + 2 - b) * channels
                part = mm_nt(
                    buf[
                        pl.ds(start + freq_bins * a, CHUNK),
                        b * channels : (b + 1) * channels,
                    ],
                    conv_ref[which, first : first + channels, :],
                )
                total = part if total is None else total + part
        return total

    def norm_back(which, read, center, scale, gain, shift, g_refs):
        def part(i, carry):
            g_gain, g_shift = carry
            start = pl.multiple_of(i * CHUNK, CHUNK)
            rows = pl.ds(start, CHUNK)
            hat = (read(start) - center) * scale
            slope = silu_slope(hat * gain + shift)
            grad = input_grad(which, start) * slope
            grad = jnp.where(live_rows(start, grad.shape, live), grad, 0.0)
            other[rows, :] = grad
            return (g_gain + col_sum(grad * hat), g_shift + col_sum(grad))

        g_gain, g_shift = loop(count, part, (blank, blank))
        put_vec(g_refs[0], g_gain)
        put_vec(g_refs[1], g_shift)
        mean_grad = group_total(g_shift * gain, groups) / counted
        mean_hat = group_total(g_gain * gain, groups) / counted

        def finish(start):
            hat = (read(start) - center) * scale
            grad = (other[pl.ds(start, CHUNK), :] * gain - mean_grad - hat * mean_hat) * scale
            return jnp.where(live_rows(start, grad.shape, live), grad, 0.0)

        return finish

    film = film_ref[0:1]
    lift = 1.0 + film[:, :channels]
    move = film[:, channels:]

    weight_grad(1, act_two_ref)
    finish = norm_back(
        1,
        lambda start: inner_ref[pl.ds(start, CHUNK), :] * lift + move,
        stat_ref[2:3],
        stat_ref[3:4],
        seg(3),
        seg(4),
        (3, 4),
    )

    def inner_part(i, carry):
        g_lift, g_move, g_bias = carry
        start = pl.multiple_of(i * CHUNK, CHUNK)
        moved = finish(start)
        grad = moved * lift
        put_shifted(buf, start, grad.astype(bf16).astype(f32), freq_bins)
        return (
            g_lift + col_sum(moved * inner_ref[pl.ds(start, CHUNK), :]),
            g_move + col_sum(moved),
            g_bias + col_sum(grad),
        )

    g_lift, g_move, g_bias = loop(count, inner_part, (blank, blank, blank))
    put_vec(2, g_bias)

    weight_grad(0, act_one_ref)
    finish_zero = norm_back(
        0,
        lambda start: zero_ref[pl.ds(start, CHUNK), :],
        stat_ref[0:1],
        stat_ref[1:2],
        seg(0),
        seg(1),
        (0, 1),
    )

    def zero_part(i, carry):
        g_stem, g_bias = carry
        start = pl.multiple_of(i * CHUNK, CHUNK)
        rows = pl.ds(start, CHUNK)
        grad = field[rows, :] + finish_zero(start)
        return (g_stem + mm(colsT_ref[:, rows], grad.astype(bf16)), g_bias + col_sum(grad))

    g_stem, g_bias = loop(
        count, zero_part, (jnp.zeros((colsT_ref.shape[0], channels), f32), blank)
    )
    taps = colsT_ref.shape[0]
    gsmall_ref[0:taps, 0:channels] = g_stem
    gsmall_ref[0:taps, channels:] = ghead_ref[...]
    put_vec(12, g_bias)

    pre_time = film_ref[1:2]
    embedding = film_ref[2:3]
    g_film = jnp.concatenate([g_lift, g_move], 1)
    g_embed = vec_mat(g_film, time_ref[2], True) * silu_slope(embedding)
    g_time = vec_mat(g_embed, time_ref[1], True) * silu_slope(pre_time)
    put_vec(13, g_time)
    put_vec(14, g_embed)
    put_vec(15, g_film)
    gsmall_ref[taps : taps + 16, :] = small[...] + mid_ref[...]
    gsmall_ref[taps + 16 :, :] = jnp.zeros(
        (gsmall_ref.shape[0] - taps - 16, gsmall_ref.shape[1]), f32
    )
    factor_ref[0:1] = wave_ref[...]
    factor_ref[1:2] = jax.nn.silu(pre_time)
    factor_ref[2:3] = jax.nn.silu(embedding)
    factor_ref[3:4] = g_time
    factor_ref[4:5] = g_embed
    factor_ref[5:6] = g_film
    factor_ref[6:8] = jnp.zeros((2, embed), f32)


def sized(shape, dtype=f32):
    return jax.ShapeDtypeStruct(shape, dtype)


VM = pl.BlockSpec(memory_space=pltpu.VMEM)
SM = pl.BlockSpec(memory_space=pltpu.SMEM)


def params(mib):
    return pltpu.CompilerParams(vmem_limit_bytes=mib * 2**20)


def remote_params(number, mib):
    return pltpu.CompilerParams(
        collective_id=number, has_side_effects=True, vmem_limit_bytes=mib * 2**20
    )


def run_fore(freq_bins, length, mix, lat, noi, stem_w, conv, wide_qkv, time_low, vec, wave, clap):
    rows_n, latent_ch = lat.shape
    channels = stem_w.shape[1]
    embed = time_low.shape[1]
    field = sized((rows_n, channels))
    field_low = sized((rows_n, channels), bf16)
    return pl.pallas_call(
        functools.partial(fore_kernel, freq_bins, GROUPS),
        in_specs=[SM, SM] + [VM] * 9,
        out_specs=[VM] * 11,
        out_shape=[
            field,
            field_low,
            field,
            field_low,
            field,
            field_low,
            sized((3 * channels, rows_n), bf16),
            sized((9 * latent_ch, rows_n), bf16),
            sized((latent_ch, rows_n)),
            sized((8, channels)),
            sized((8, embed)),
        ],
        scratch_shapes=[
            pltpu.VMEM((rows_n + 2 * freq_bins, 3 * channels), bf16),
            pltpu.VMEM((rows_n, 128), bf16),
            pltpu.VMEM((128, rows_n), f32),
        ],
        compiler_params=params(48),
        name="fore",
    )(length, mix, lat, noi, stem_w, conv, wide_qkv, time_low, vec, wave, clap)


def run_attend(freq_bins, length, qkv_t, up, down, key_block=256):
    n_f = lax.axis_size("fsdp")
    triple, rows_n = qkv_t.shape
    channels = triple // 3
    dim = channels // HEADS
    return pl.pallas_call(
        functools.partial(attend_kernel, freq_bins, key_block),
        grid=(HEADS,),
        in_specs=[SM]
        + [pl.BlockSpec((dim, rows_n), lambda h, t=t: (t * HEADS + h, 0)) for t in range(3)]
        + [VM] * 2,
        out_specs=[
            pl.BlockSpec((dim, rows_n), lambda h: (h, 0)),
            pl.BlockSpec((1, 1, rows_n), lambda h: (h, 0, 0)),
            VM,
            VM,
        ],
        out_shape=[
            sized((channels, rows_n)),
            sized((HEADS, 1, rows_n)),
            sized((up.shape[0] * n_f, up.shape[1]), bf16),
            sized((down.shape[0] * n_f, down.shape[1]), bf16),
        ],
        scratch_shapes=[
            pltpu.VMEM((rows_n, 128), bf16),
            pltpu.VMEM((128, rows_n), bf16),
            pltpu.VMEM((dim + 16, rows_n), bf16),
        ]
        + land_scratch(up.shape, down.shape),
        compiler_params=remote_params(3, 48),
        name="attend",
    )(length, qkv_t, qkv_t, qkv_t, up, down)


def run_attend_back(
    freq_bins, length, qkv_t, lse, mixed_t, grad_t, early, wide, down, key_block=512
):
    n_f = lax.axis_size("fsdp")
    early = early.reshape(n_f // 2, 2, early.shape[0] // n_f, early.shape[1])
    triple, rows_n = qkv_t.shape
    channels = triple // 3
    dim = channels // HEADS
    whole = pl.BlockSpec((dim, rows_n), lambda h, j: (h, 0))
    block = pl.BlockSpec((dim, key_block), lambda h, j: (h, j))
    return pl.pallas_call(
        functools.partial(attend_back_kernel, freq_bins, key_block),
        grid=(HEADS, rows_n // key_block),
        in_specs=[SM]
        + [pl.BlockSpec((dim, rows_n), lambda h, j, t=t: (t * HEADS + h, 0)) for t in range(3)]
        + [pl.BlockSpec((1, 1, rows_n), lambda h, j: (h, 0, 0)), whole, whole]
        + [VM] * 3,
        out_specs=[whole, block, block] + [VM] * 3,
        out_shape=[sized((channels, rows_n), bf16)] * 3
        + [
            sized(early.shape, bf16),
            sized((wide.shape[0] * n_f, wide.shape[1]), bf16),
            sized((down.shape[0] * n_f, down.shape[1]), bf16),
        ],
        scratch_shapes=[
            pltpu.VMEM((rows_n, 128), bf16),
            pltpu.VMEM((128, rows_n), bf16),
            pltpu.VMEM((rows_n, 128), bf16),
            pltpu.VMEM((128, rows_n), bf16),
            pltpu.VMEM((dim, rows_n), f32),
        ]
        + total_scratch(early.shape[2], early.shape[3], bf16)
        + land_scratch(wide.shape, down.shape),
        compiler_params=remote_params(4, 56),
        name="attend_back",
    )(length, qkv_t, qkv_t, qkv_t, lse, mixed_t, grad_t, early, wide, down)


def run_middle(freq_bins, length, mixed_t, one, out, up, down, vec, head_t, head_bias, noi_t):
    rows_n, channels = one.shape
    units = down.shape[0]
    latent_ch = noi_t.shape[0]
    return pl.pallas_call(
        functools.partial(middle_kernel, freq_bins),
        in_specs=[SM] + [VM] * 9,
        out_specs=[VM] * 5,
        out_shape=[
            sized((rows_n, channels)),
            sized((channels, rows_n), bf16),
            sized((units + channels // 2, 2 * channels), bf16),
            sized((9 * latent_ch, channels)),
            sized((16, 2 * channels)),
        ],
        scratch_shapes=[
            pltpu.VMEM((rows_n, units), bf16),
            pltpu.VMEM((rows_n, units), f32),
            pltpu.VMEM((rows_n, channels), f32),
            pltpu.VMEM((rows_n, 128), f32),
            pltpu.VMEM((rows_n, channels), bf16),
            pltpu.VMEM((128, rows_n), f32),
            pltpu.VMEM((rows_n, 128), bf16),
            pltpu.VMEM((channels, rows_n), bf16),
            pltpu.VMEM((channels, rows_n), bf16),
            pltpu.VMEM((rows_n, units), bf16),
            pltpu.VMEM((rows_n, channels), bf16),
        ],
        compiler_params=params(56),
        name="middle",
    )(length, mixed_t, one, out, up, down, vec, head_t, head_bias, noi_t)


def run_hind(freq_bins, length, *arrays):
    one = arrays[5]
    rows_n, channels = one.shape
    embed = arrays[15].shape[1]
    return pl.pallas_call(
        functools.partial(hind_kernel, freq_bins, GROUPS),
        in_specs=[SM] + [VM] * len(arrays),
        out_specs=[VM] * 4,
        out_shape=[
            sized((channels + channels // 2, 2 * channels), bf16),
            sized((2, 9 * channels, channels), bf16),
            sized((128, 2 * channels)),
            sized((8, embed)),
        ],
        scratch_shapes=[
            pltpu.VMEM((rows_n + 2 * freq_bins, 3 * channels), bf16),
            pltpu.VMEM((rows_n, channels), f32),
            pltpu.VMEM((rows_n, channels), f32),
            pltpu.VMEM((channels, rows_n), bf16),
            pltpu.VMEM((16, 2 * channels), f32),
        ],
        compiler_params=params(56),
        name="hind",
    )(length, *arrays)


def gather_kernel(conv_ref, time_ref, wide_ref, conv_out, time_out, wide_out, *sems):
    here = places()
    n_d, n_z, d, z, c = here
    channels, embed = conv_ref.shape[2], time_ref.shape[2]
    which, lanes = conv_piece(d, n_d, channels)
    t_lanes = lane_piece(d, n_d, embed)
    w_lanes = lane_piece(d, n_d, wide_out.shape[3])
    conv_out[:, pl.ds(z, 1), pl.ds(c, 1)] = conv_ref[...].astype(bf16)[:, None, None]
    time_out[:, pl.ds(z, 1), pl.ds(c, 1)] = time_ref[...].astype(bf16)[:, None, None]
    wide_out[pl.ds(z, 1), pl.ds(c, 1)] = wide_ref[...].astype(bf16)[None, None]

    def parts(source):
        return [
            conv_out.at[which, source, c, :, lanes],
            time_out.at[:, source, c, :, t_lanes],
            wide_out.at[source, c, :, w_lanes],
        ]

    def wholes(source):
        return [
            conv_out.at[:, source, c],
            time_out.at[:, source, c],
            wide_out.at[source, c],
        ]

    steps = plan_gather(here, parts, wholes, sems)
    greet(*here)
    for step in steps:
        step()


def run_gather(conv_w, time_w, wide):
    n_z = lax.axis_size("fsdp") // 2
    conv, time, wide_full = pl.pallas_call(
        gather_kernel,
        in_specs=[VM] * 3,
        out_specs=[VM] * 3,
        out_shape=[
            sized((2, n_z, 2) + conv_w.shape[1:], bf16),
            sized((3, n_z, 2) + time_w.shape[1:], bf16),
            sized((n_z, 2) + wide.shape, bf16),
        ],
        scratch_shapes=gather_sems(3),
        compiler_params=remote_params(1, 32),
        name="gather",
    )(conv_w, time_w, wide)
    return (
        conv.reshape(2, -1, conv_w.shape[2]),
        time.reshape(3, -1, time_w.shape[2]),
        wide_full.reshape(-1, wide.shape[1]),
    )


def reduce_kernel(
    gconv_ref,
    ga_ref,
    gs_ref,
    factor_ref,
    conv_out,
    a_out,
    s_out,
    time_out,
    square_out,
    shard,
    pair_c,
    pair_a,
    pair_s,
    sib_c,
    sib_a,
    sib_s,
    dp_c,
    dp_a,
    dp_s,
    sum_c,
    sum_a,
    sum_s,
    z_c,
    z_a,
    z_s,
    everyone,
    squares,
    product,
    s1,
    r1,
    s2,
    r2,
    s3,
    r3,
    s4,
    r4,
    s5,
    r5,
    s6,
    r6,
):
    n_d, n_z, d, z, c = places()
    rows_here, channels = conv_out.shape[1:]
    wide = a_out.shape[3]
    embed = factor_ref.shape[1]
    which, lanes = conv_piece(d, n_d, channels)
    a_lanes = lane_piece(d, n_d, wide)
    sibling = {"fsdp": 2 * z + 1 - c}
    everyone[pl.ds(d, 1), pl.ds(z, 1), pl.ds(c, 1)] = factor_ref[...][None, None, None]
    greet(n_d, n_z, d, z, c)
    copies = []

    def send(pairs, sends, recvs, target):
        group = []
        for index, (src, dst) in enumerate(pairs):
            group.append(push(src, dst, sends.at[index], recvs.at[index], target))
        copies.extend(group)
        return group

    def arrive(groups):
        for group in groups:
            for copy in group:
                copy.wait_recv()

    one = send(
        (
            (gconv_ref.at[:, :, 1 - c], sib_c),
            (ga_ref.at[:, 1 - c], sib_a),
            (gs_ref.at[:, 1 - c], sib_s),
        ),
        s1,
        r1,
        sibling,
    )
    mine = everyone.at[d, z, c]
    two_f = [
        send(((mine, mine),), s2.at[j, 3:4], r2.at[j, 3:4], {"dp": lax.rem(d + j, n_d)})
        for j in range(1, n_d)
    ]
    arrive([one])
    for i in range(n_z):
        for part in range(2):
            pair_c[part, i] = (
                gconv_ref[part, i, pl.ds(c, 1)][0].astype(f32) + sib_c[part, i].astype(f32)
            ).astype(bf16)
        pair_a[i] = (ga_ref[i, pl.ds(c, 1)][0].astype(f32) + sib_a[i].astype(f32)).astype(bf16)
        pair_s[i] = gs_ref[i, pl.ds(c, 1)][0] + sib_s[i]

    two = []
    for j in range(1, n_d):
        other = lax.rem(d + j, n_d)
        other_which, other_lanes = conv_piece(other, n_d, channels)
        other_a = lane_piece(other, n_d, wide)
        two.append(
            send(
                (
                    (pair_c.at[other_which, :, :, other_lanes], dp_c.at[j]),
                    (pair_a.at[:, :, other_a], dp_a.at[j]),
                    (pair_s.at[:, :, other_a], dp_s.at[j]),
                ),
                s2.at[j],
                r2.at[j],
                {"dp": other},
            )
        )
    arrive(two_f)
    column = everyone.at[:, z, c]
    three_f = [
        send(
            ((column, column),),
            s3.at[k, 3:4],
            r3.at[k, 3:4],
            {"fsdp": 2 * lax.rem(z + k, n_z) + c},
        )
        for k in range(1, n_z)
    ]
    arrive(two)

    def total(first, rest):
        value = first.astype(f32)
        for term in rest:
            value = value + term.astype(f32)
        return value

    for i in range(n_z):
        rest = range(1, n_d)
        sum_c[i] = total(
            pair_c[pl.ds(which, 1), i, :, lanes][0], [dp_c[j, i] for j in rest]
        ).astype(bf16)
        sum_a[i] = total(pair_a[i, :, a_lanes], [dp_a[j, i] for j in rest]).astype(bf16)
        sum_s[i] = total(pair_s[i, :, a_lanes], [dp_s[j, i] for j in rest])

    three = []
    for k in range(1, n_z):
        other = lax.rem(z + k, n_z)
        three.append(
            send(
                (
                    (sum_c.at[other], z_c.at[k]),
                    (sum_a.at[other], z_a.at[k]),
                    (sum_s.at[other], z_s.at[k]),
                ),
                s3.at[k],
                r3.at[k],
                {"fsdp": 2 * other + c},
            )
        )
    arrive(three_f)
    row = everyone.at[:, :, c]
    four_f = send(((row, row),), s4.at[0], r4.at[0], sibling)
    arrive(three)
    rest = range(1, n_z)
    shard[pl.ds(which, 1), :, lanes] = total(
        sum_c[pl.ds(z, 1)][0], [z_c[k] for k in rest]
    ).astype(bf16)[None]
    a_out[pl.ds(z, 1), pl.ds(c, 1), :, a_lanes] = total(
        sum_a[pl.ds(z, 1)][0], [z_a[k] for k in rest]
    ).astype(bf16)[None, None]
    s_out[pl.ds(z, 1), pl.ds(c, 1), :, a_lanes] = total(
        sum_s[pl.ds(z, 1)][0], [z_s[k] for k in rest]
    )[None, None]

    four = []
    for j in range(1, n_d):
        refs = (
            shard.at[which, :, lanes],
            a_out.at[z, c, :, a_lanes],
            s_out.at[z, c, :, a_lanes],
        )
        four.append(
            send(
                [(ref, ref) for ref in refs],
                s4.at[j],
                r4.at[j],
                {"dp": lax.rem(d + j, n_d)},
            )
        )
    arrive([four_f])
    clips = 2 * n_d * n_z
    depth = time_out.shape[1]
    first = (2 * z + c) * depth
    block = pl.ds(pl.multiple_of(first // 128 * 128, 128), 128)
    offset = pl.multiple_of(lax.rem(first, 128), 8)
    square = jnp.zeros((), f32)
    for i in range(3):
        left = everyone[:, :, :, i, block].reshape(clips, 128)
        right = everyone[:, :, :, i + 3, :].reshape(clips, embed)
        product[...] = jnp.dot(
            left.T, right, precision=highest, preferred_element_type=f32
        )
        value = product[pl.ds(offset, depth), :]
        time_out[i] = value
        square = square + jnp.sum(value * value)
    arrive(four)
    value = shard[...].astype(f32)
    conv_out[...] = value
    square = square + jnp.sum(value * value)
    squares[pl.ds(z, 1), pl.ds(c, 1)] = jnp.zeros((1, 1) + squares.shape[2:], f32) + square

    five = []
    for k in range(1, n_z):
        refs = (a_out.at[z, c], s_out.at[z, c], squares.at[z, c])
        five.append(
            send(
                [(ref, ref) for ref in refs],
                s5.at[k],
                r5.at[k],
                {"fsdp": 2 * lax.rem(z + k, n_z) + c},
            )
        )
    arrive(five)
    refs = (a_out.at[:, c], s_out.at[:, c], squares.at[:, c])
    six = send([(ref, ref) for ref in refs], s6, r6, sibling)
    arrive([six])
    value = jnp.zeros(squares.shape[2:], f32)
    for i in range(n_z):
        for j in range(2):
            value = value + squares[i, j]
    square_out[...] = value
    for copy in copies:
        copy.wait_send()


def run_reduce(gconv, ga, gs, factors, time_rows):
    n_d, n_f = lax.axis_size("dp"), lax.axis_size("fsdp")
    n_z = n_f // 2
    channels = gconv.shape[2]
    embed = factors.shape[1]
    rows_c = gconv.shape[1] // n_f
    rows_a = ga.shape[0] // n_f
    rows_s = gs.shape[0] // n_f
    wide = ga.shape[1]
    part = wide // n_d
    part_c = 2 * channels // n_d
    dma = pltpu.SemaphoreType.DMA
    vmem = pltpu.VMEM
    conv, a_full, s_full, time, square = pl.pallas_call(
        reduce_kernel,
        in_specs=[VM] * 4,
        out_specs=[VM] * 5,
        out_shape=[
            sized((2, rows_c, channels)),
            sized((n_z, 2, rows_a, wide), bf16),
            sized((n_z, 2, rows_s, wide)),
            sized((3, time_rows, embed)),
            sized((8, 128)),
        ],
        scratch_shapes=[
            vmem((2, rows_c, channels), bf16),
            vmem((2, n_z, rows_c, channels), bf16),
            vmem((n_z, rows_a, wide), bf16),
            vmem((n_z, rows_s, wide), f32),
            vmem((2, n_z, rows_c, channels), bf16),
            vmem((n_z, rows_a, wide), bf16),
            vmem((n_z, rows_s, wide), f32),
            vmem((n_d, n_z, rows_c, part_c), bf16),
            vmem((n_d, n_z, rows_a, part), bf16),
            vmem((n_d, n_z, rows_s, part), f32),
            vmem((n_z, rows_c, part_c), bf16),
            vmem((n_z, rows_a, part), bf16),
            vmem((n_z, rows_s, part), f32),
            vmem((n_z, rows_c, part_c), bf16),
            vmem((n_z, rows_a, part), bf16),
            vmem((n_z, rows_s, part), f32),
            vmem((n_d, n_z, 2, 8, embed), f32),
            vmem((n_z, 2, 8, 128), f32),
            vmem((128, embed), f32),
            dma((3,)),
            dma((3,)),
            dma((n_d, 4)),
            dma((n_d, 4)),
            dma((n_z, 4)),
            dma((n_z, 4)),
            dma((n_d, 3)),
            dma((n_d, 3)),
            dma((n_z, 3)),
            dma((n_z, 3)),
            dma((3,)),
            dma((3,)),
        ],
        compiler_params=pltpu.CompilerParams(
            collective_id=2, has_side_effects=True, vmem_limit_bytes=48 * 2**20
        ),
        name="reduce",
    )(
        gconv.reshape(2, n_z, 2, rows_c, channels),
        ga.reshape(n_z, 2, rows_a, wide),
        gs.reshape(n_z, 2, rows_s, wide),
        factors,
    )
    return (
        conv,
        a_full.reshape(ga.shape),
        s_full.reshape(gs.shape),
        time,
        square[0, 0],
    )


def noise_mix(step_value):
    phase = (step_value.astype(f32) / 1000.0 + 0.008) / 1.008 * (math.pi / 2)
    keep_part = jnp.cos(phase) ** 2
    return jnp.stack([jnp.sqrt(keep_part), jnp.sqrt(1.0 - keep_part)])


def adam_step(weight, moment_one, moment_two, gradient, decay_on, fix_one, fix_two):
    first_new = 0.9 * moment_one + 0.1 * gradient
    second_new = 0.999 * moment_two + 0.001 * gradient * gradient
    moved = first_new / fix_one / (jnp.sqrt(second_new / fix_two) + adam_floor)
    return (weight - adam_rate * (moved + decay_on * weight), first_new, second_new)


def local(
    latents,
    noises,
    clap_embed,
    timesteps,
    lengths,
    step_count,
    stem_w,
    head_w,
    time_w,
    vector,
    conv_w,
    wide_w,
    down_w,
    roots_small,
    root_wide,
    roots_large,
    stem_moment,
    stem_square,
    head_moment,
    head_square,
    time_moment,
    time_square,
    vector_moment,
    vector_square,
    conv_moment,
    conv_square,
    wide_moment,
    down_moment,
):
    frames_n, freq_bins, latent_ch = (latents.shape[1], latents.shape[2], latents.shape[3])
    channels = stem_w.shape[1]
    embed = time_w.shape[2]
    rows_n = frames_n * freq_bins
    both = ("dp", "fsdp")
    here = lax.axis_index("fsdp")

    conv_full, time_full, first_full = run_gather(conv_w, time_w, wide_w[:, : 4 * channels])

    half_width = embed // 2
    frequency = jnp.exp(-math.log(10000.0) * jnp.arange(half_width).astype(f32) / half_width)
    angles = timesteps[0].astype(f32) * frequency
    wave = jnp.concatenate([jnp.cos(angles), jnp.sin(angles)])[None]
    vec = vector[None]
    head_t = jnp.pad(
        head_w.reshape(9, channels, latent_ch).transpose(0, 2, 1).reshape(-1, channels),
        ((0, 128 - 9 * latent_ch), (0, 0)),
    ).astype(bf16)
    head_bias = vector[-latent_ch:][:, None]

    (
        zero,
        act_one,
        inner,
        act_two,
        one,
        normed,
        qkv_t,
        cols_t,
        noi_t,
        stat,
        film,
    ) = run_fore(
        freq_bins,
        lengths,
        noise_mix(timesteps[0]),
        latents.reshape(rows_n, latent_ch),
        noises.reshape(rows_n, latent_ch),
        stem_w,
        conv_full,
        first_full[:, : 3 * channels],
        time_full,
        vec,
        wave,
        clap_embed,
    )
    mixed_t, lse, up_full, down_full = run_attend(
        freq_bins, lengths, qkv_t, wide_w[:, 4 * channels :], down_w
    )
    two_grad, do_t, early, ghead_t, small = run_middle(
        freq_bins,
        lengths,
        mixed_t,
        one,
        first_full[:, 3 * channels :],
        up_full,
        down_full,
        vec,
        head_t,
        head_bias,
        noi_t,
    )
    dq, dk, dv, early, wide_moment_full, down_moment_full = run_attend_back(
        freq_bins, lengths, qkv_t, lse, mixed_t, do_t, early, wide_moment, down_moment
    )
    early = early.reshape(-1, early.shape[3])
    half = FF // 2
    gdown = jnp.concatenate([early[:half, :channels], early[:half, channels:]], 0)
    gup = jnp.concatenate(
        [early[half : half + channels], early[half + channels : half + 2 * channels]], 1
    )
    gproj = jnp.concatenate(
        [early[half + 2 * channels :, :channels], early[half + 2 * channels :, channels:]], 0
    )
    ga, gconv, gs, factors = run_hind(
        freq_bins,
        lengths,
        dq,
        dk,
        dv,
        two_grad,
        normed,
        one,
        act_two,
        inner,
        act_one,
        zero,
        cols_t,
        stat,
        film,
        conv_full,
        first_full,
        time_full,
        vec,
        wave,
        small,
        ghead_t,
    )
    conv_shard, ga, gs, time_shard, shard_total = run_reduce(
        gconv, ga, gs, factors, time_w.shape[1]
    )
    gqkv = jnp.concatenate(
        [
            ga[:channels],
            jnp.concatenate([ga[channels:, :channels], ga[channels:, channels:]], 0),
        ],
        1,
    )
    taps = stem_w.shape[0]
    gstem = gs[:taps, :channels]
    ghead = (
        gs[:taps, channels:]
        .reshape(9, latent_ch, channels)
        .transpose(0, 2, 1)
        .reshape(-1, latent_ch)
    )
    gvec = take_small(gs[taps:], latent_ch)
    loss_sum = gs[taps + 13, 0]
    live_count = gs[taps + 14, 0]

    def squares(value):
        value = value.astype(f32)
        return jnp.sum(value * value)

    total = (
        shard_total
        + squares(gstem)
        + squares(ghead)
        + squares(gvec)
        + squares(gdown)
        + squares(gup)
        + squares(gproj)
        + squares(gqkv)
    )
    unit = 2.0 / (latent_ch * live_count)
    loss_value = loss_sum / (latent_ch * live_count)
    grad_norm = unit * jnp.sqrt(total)
    factor = jnp.minimum(1.0, clip_limit / grad_norm) * unit
    step_value = step_count[0].astype(f32)
    fix_one = 1.0 - jnp.power(0.9, step_value)
    fix_two = 1.0 - jnp.power(0.999, step_value)
    vector_clipped = factor * gvec

    def adam(weight, first, second, grad, decay_on):
        return adam_step(weight, first, second, grad, decay_on, fix_one, fix_two)

    stem_out = adam(stem_w, stem_moment, stem_square, factor * gstem, decay_rate)
    head_out = adam(head_w, head_moment, head_square, factor * ghead, decay_rate)
    time_out = adam(time_w, time_moment, time_square, factor * time_shard, decay_rate)
    vector_out = adam(vector, vector_moment, vector_square, vector_clipped, 0.0)
    conv_out = adam(conv_w, conv_moment, conv_square, factor * conv_shard, decay_rate)

    wide_rows = wide_w.shape[0]
    down_rows = down_w.shape[0]
    gwide = jnp.concatenate([gqkv, gproj, gup], 1)
    wide_mine = lax.dynamic_slice_in_dim(gwide, here * wide_rows, wide_rows, 0)
    down_mine = lax.dynamic_slice_in_dim(gdown, here * down_rows, down_rows, 0)
    wide_moment_new = 0.9 * wide_moment + factor * wide_mine.astype(f32)
    down_moment_new = 0.9 * down_moment + factor * down_mine.astype(f32)

    def direction(left_root, moment_full, grad_full, right_root, rows):
        left = lax.dynamic_slice_in_dim(left_root, here * rows, rows, 0).astype(bf16)
        moment_now = 0.9 * moment_full.astype(f32) + factor * grad_full.astype(f32)
        left_done = mm(left, moment_now.astype(bf16))
        return mm(left_done.astype(bf16), right_root.astype(bf16))

    bounds = (0, 3 * channels, 4 * channels, 4 * channels + FF)
    rights = (root_wide, roots_small[3], roots_large[0])
    directions = []
    for index in range(3):
        columns = slice(bounds[index], bounds[index + 1])
        directions.append(
            direction(
                roots_small[index],
                wide_moment_full[:, columns],
                gwide[:, columns],
                rights[index],
                wide_rows,
            )
        )
    wide_new = wide_w * (1.0 - shampoo_rate * decay_rate) - shampoo_rate * jnp.concatenate(
        directions, 1
    )
    down_direction = direction(
        roots_large[1], down_moment_full, gdown, roots_small[4], down_rows
    )
    down_new = down_w * (1.0 - shampoo_rate * decay_rate) - shampoo_rate * down_direction
    return (
        loss_value,
        grad_norm,
        stem_out[0],
        stem_out[1],
        stem_out[2],
        head_out[0],
        head_out[1],
        head_out[2],
        time_out[0],
        time_out[1],
        time_out[2],
        vector_clipped,
        vector_out[1],
        vector_out[2],
        conv_out[0],
        conv_out[1],
        conv_out[2],
        wide_new,
        wide_moment_new,
        down_new,
        down_moment_new,
    )


def solution(mesh):
    in_specs = (
        P(("dp", "fsdp"), None, None, None),
        P(("dp", "fsdp"), None, None, None),
        P(("dp", "fsdp"), None),
        P(("dp", "fsdp")),
        P(("dp", "fsdp")),
        P(),
        P(),
        P(),
        P(None, "fsdp", None),
        P(),
        P(None, "fsdp", None),
        P("fsdp", None),
        P("fsdp", None),
        P(),
        P(),
        P(),
        P(),
        P(),
        P(),
        P(),
        P(None, "fsdp", None),
        P(None, "fsdp", None),
        P(),
        P(),
        P(None, "fsdp", None),
        P(None, "fsdp", None),
        P("fsdp", None),
        P("fsdp", None),
    )
    out_specs = (
        P(),
        P(),
        P(),
        P(),
        P(),
        P(),
        P(),
        P(),
        P(None, "fsdp", None),
        P(None, "fsdp", None),
        P(None, "fsdp", None),
        P(),
        P(),
        P(),
        P(None, "fsdp", None),
        P(None, "fsdp", None),
        P(None, "fsdp", None),
        P("fsdp", None),
        P("fsdp", None),
        P("fsdp", None),
        P("fsdp", None),
    )
    return jax.shard_map(local, mesh=mesh, in_specs=in_specs, out_specs=out_specs, check_vma=False)
```

```python
import functools
import math

import jax
import jax.numpy as jnp
from jax import lax
from jax.experimental import pallas as pl
from jax.experimental.pallas import tpu as pltpu
from jax.sharding import PartitionSpec as P

HEADS = 8
FF = 1024
EMB = 512
GROUPS = 32

norm_floor = 1e-05
masked_score = -1e30
clip_limit = 0.002
adam_rate = 0.05
adam_floor = 1e-08
shampoo_rate = 0.02
decay_rate = 0.01

f32 = jnp.float32
bf16 = jnp.bfloat16
highest = lax.Precision.HIGHEST
LOG2E = math.log2(math.e)
CHUNK = 1024


def mm(left_op, right_op):
    return jnp.dot(left_op, right_op, preferred_element_type=f32)


def mm_nt(left_op, right_op):
    return lax.dot_general(
        left_op, right_op, (((1,), (1,)), ((), ())), preferred_element_type=f32
    )


def col_sum(value):
    return jnp.sum(value, axis=0, keepdims=True)


def row_mean(value):
    return jnp.mean(value, axis=-1, keepdims=True)


def loop(count, body, init, hooks=()):
    if not hooks:
        return lax.fori_loop(0, count, body, init)

    def step(i, carry):
        for place, action in hooks:
            pl.when(i == place)(action)
        return body(i, carry)

    return lax.fori_loop(0, count, step, init)


def tap_shift(field, a, b, run):
    length = field.shape[1]
    step = run * (a - 1) + (b - 1)
    if step == 0:
        return field
    pos = lax.broadcasted_iota(jnp.int32, field.shape, 1)
    bin_pos = lax.rem(pos, run)
    keep = None
    for wanted, test in (
        (a == 0, lambda: pos >= run),
        (a == 2, lambda: pos < length - run),
        (b == 0, lambda: bin_pos >= 1),
        (b == 2, lambda: bin_pos < run - 1),
    ):
        if wanted:
            keep = test() if keep is None else jnp.logical_and(keep, test())
    return jnp.where(keep, pltpu.roll(field, (-step) % length, 1), 0.0)


def put_shifted(buf, start, value, run):
    rows, channels = value.shape
    bin_pos = lax.rem(lax.broadcasted_iota(jnp.int32, value.shape, 0), run)
    before = jnp.where(bin_pos == 0, 0.0, pltpu.roll(value, 1, 0))
    after = jnp.where(bin_pos == run - 1, 0.0, pltpu.roll(value, rows - 1, 0))
    where = pl.ds(start + run, rows)
    buf[where, 0:channels] = before.astype(bf16)
    buf[where, channels : 2 * channels] = value.astype(bf16)
    buf[where, 2 * channels : 3 * channels] = after.astype(bf16)


def clear_ends(buf, rows_n, run):
    blank = jnp.zeros((run, buf.shape[1]), bf16)
    buf[0:run, :] = blank
    buf[rows_n + run : rows_n + 2 * run, :] = blank


def live_rows(shape, live, run):
    return lax.rem(lax.broadcasted_iota(jnp.int32, shape, 0), run) < live


def swap_tap(tap):
    return tap % 3 * 3 + tap // 3


def swap_taps(value, axis=0):
    size = value.shape[axis] // 9
    pieces = [
        lax.slice_in_dim(value, swap_tap(t) * size, (swap_tap(t) + 1) * size, axis=axis)
        for t in range(9)
    ]
    return jnp.concatenate(pieces, axis)


def group_total(row, groups):
    channels = row.shape[1]
    size = channels // groups
    one = lax.broadcasted_iota(jnp.int32, (channels, channels), 0) // size
    two = lax.broadcasted_iota(jnp.int32, (channels, channels), 1) // size
    same = jnp.where(one == two, 1.0, 0.0).astype(f32)
    wide = jnp.broadcast_to(row, (8, channels))
    return jnp.dot(wide, same, precision=highest, preferred_element_type=f32)[0:1]


def vec_mat(row, weight, transposed=False):
    top = row.astype(bf16).astype(f32)
    rest = row - top
    mid = rest.astype(bf16).astype(f32)
    low = rest - mid
    shape = (16, row.shape[1])
    index = lax.broadcasted_iota(jnp.int32, shape, 0)
    stacked = jnp.where(
        index == 0,
        jnp.broadcast_to(top, shape),
        jnp.where(
            index == 1,
            jnp.broadcast_to(mid, shape),
            jnp.where(index == 2, jnp.broadcast_to(low, shape), 0.0),
        ),
    ).astype(bf16)
    return col_sum(mm_nt(stacked, weight) if transposed else mm(stacked, weight))


def silu_slope(value):
    gate = jax.nn.sigmoid(value)
    return gate * (1.0 + value * (1.0 - gate))


def channel_stats(read, rows_n, live, run, channels, average):
    count = rows_n // CHUNK

    def add(i, total):
        start = pl.multiple_of(i * CHUNK, CHUNK)
        value = read(start)
        return total + col_sum(jnp.where(live_rows(value.shape, live, run), value, 0.0))

    center = average(loop(count, add, jnp.zeros((1, channels), f32)))

    def add_square(i, total):
        start = pl.multiple_of(i * CHUNK, CHUNK)
        value = read(start) - center
        return total + col_sum(jnp.where(live_rows(value.shape, live, run), value * value, 0.0))

    return center, average(loop(count, add_square, jnp.zeros((1, channels), f32)))


def group_stats(read, rows_n, live, run, channels, groups, counted):
    center, spread = channel_stats(
        read, rows_n, live, run, channels, lambda row: group_total(row, groups) / counted
    )
    return center, lax.rsqrt(spread + norm_floor)


def time_wave(time_ref, embed):
    half = embed // 2
    index = lax.broadcasted_iota(jnp.int32, (1, half), 1).astype(f32)
    frequency = jnp.exp(-math.log(10000.0) * index / half)
    angles = (jnp.zeros((1, half), f32) + time_ref[0].astype(f32)) * frequency
    return jnp.concatenate([jnp.cos(angles), jnp.sin(angles)], 1)


def offsets(channels, embed_width, hidden_units, latent_ch):
    starts = []
    start = 0
    for length in [channels] * 13 + [embed_width] * 3 + [hidden_units, latent_ch]:
        starts.append((start, length))
        start = start + length
    return starts


def put_small(ref, index, value):
    if index < 13:
        half = value.shape[1]
        ref[index // 2 : index // 2 + 1, (index % 2) * half : (index % 2 + 1) * half] = value
    elif index < 16:
        ref[index - 6 : index - 5, :] = value
    elif index == 16:
        half = value.shape[1] // 2
        ref[10:11, :] = value[:, :half]
        ref[11:12, :] = value[:, half:]
    else:
        ref[index - 5 : index - 4, 0 : value.shape[1]] = value


def take_small(rows, latent_ch):
    return jnp.concatenate(
        [
            rows[0:6].reshape(-1),
            rows[6, : rows.shape[1] // 2],
            rows[7:12].reshape(-1),
            rows[12, :latent_ch],
        ]
    )


MESH = pl.DeviceIdType.MESH


def places():
    n_d, n_f = lax.axis_size("dp"), lax.axis_size("fsdp")
    me = lax.axis_index("fsdp")
    return n_d, n_f // 2, lax.axis_index("dp"), me // 2, lax.rem(me, 2)


def push(src, dst, sends, recvs, target):
    copy = pltpu.make_async_remote_copy(
        src_ref=src,
        dst_ref=dst,
        send_sem=sends,
        recv_sem=recvs,
        device_id=target,
        device_id_type=MESH,
    )
    copy.start()
    return copy


def greet(n_d, n_z, d, z, c):
    barrier = pltpu.get_barrier_semaphore()
    for j in range(1, n_d):
        pl.semaphore_signal(
            barrier, inc=1, device_id={"dp": lax.rem(d + j, n_d)}, device_id_type=MESH
        )
    for k in range(1, n_z):
        pl.semaphore_signal(
            barrier,
            inc=1,
            device_id={"fsdp": 2 * lax.rem(z + k, n_z) + c},
            device_id_type=MESH,
        )
    pl.semaphore_signal(
        barrier, inc=1, device_id={"fsdp": 2 * z + 1 - c}, device_id_type=MESH
    )
    pl.semaphore_wait(barrier, n_d + n_z - 1)


def conv_piece(d, n_d, channels):
    width = 2 * channels // n_d
    return (d * width) // channels, pl.ds(
        pl.multiple_of(lax.rem(d * width, channels), 128), width
    )


def lane_piece(d, n_d, lanes):
    width = lanes // n_d
    return pl.ds(pl.multiple_of(d * width, 128), width)


def plan_gather(here, parts, wholes, sems):
    n_d, n_z, d, z, c = here
    s1, r1, s2, r2, s3, r3 = sems
    sibling = {"fsdp": 2 * z + 1 - c}

    def copy(ref, sends, recvs, target):
        return pltpu.make_async_remote_copy(
            src_ref=ref,
            dst_ref=ref,
            send_sem=sends,
            recv_sem=recvs,
            device_id=target,
            device_id_type=MESH,
        )

    def source(k):
        return lax.rem(z - k + n_z, n_z)

    def first(k):
        target = {"fsdp": 2 * lax.rem(z + k, n_z) + c}
        return [copy(r, s1.at[k, i], r1.at[k, i], target) for i, r in enumerate(parts(z))]

    def second(k, j):
        target = {"dp": lax.rem(d + j, n_d)}
        refs = parts(source(k))
        return [copy(r, s2.at[k, j, i], r2.at[k, j, i], target) for i, r in enumerate(refs)]

    def last(k):
        refs = wholes(source(k))
        return [copy(r, s3.at[k, i], r3.at[k, i], sibling) for i, r in enumerate(refs)]

    def start(group):
        for item in group:
            item.start()

    def arrive(group):
        for item in group:
            item.wait_recv()

    def leave(group):
        for item in group:
            item.wait_send()

    far = range(1, n_z)
    peers = range(1, n_d)

    def step_one():
        for k in far:
            start(first(k))
        start(last(0))

    def step_two():
        for k in far:
            arrive(first(k))
            for j in peers:
                start(second(k, j))

    def step_three():
        for k in far:
            for j in peers:
                arrive(second(k, j))
            start(last(k))

    def step_four():
        for k in range(n_z):
            arrive(last(k))
        for k in far:
            leave(first(k))
            for j in peers:
                leave(second(k, j))
        for k in range(n_z):
            leave(last(k))

    return step_one, step_two, step_three, step_four


def gather_sems(count):
    n_d, n_z = lax.axis_size("dp"), lax.axis_size("fsdp") // 2
    dma = pltpu.SemaphoreType.DMA
    return [
        dma((n_z, count)),
        dma((n_z, count)),
        dma((n_z, n_d, count)),
        dma((n_z, n_d, count)),
        dma((n_z, count)),
        dma((n_z, count)),
    ]


def plan_total(here, value_ref, out, pair, other, from_dp, summed, from_z, sems):
    n_d, n_z, d, z, c = here
    lanes_n = out.shape[3]
    mine = lane_piece(d, n_d, lanes_n)
    sibling = {"fsdp": 2 * z + 1 - c}
    send, recv = sems

    def copy(src, dst, index, target):
        return pltpu.make_async_remote_copy(
            src_ref=src,
            dst_ref=dst,
            send_sem=send.at[index],
            recv_sem=recv.at[index],
            device_id=target,
            device_id_type=MESH,
        )

    def replica(j):
        return lax.rem(d + j, n_d)

    def chip(k):
        return lax.rem(z + k, n_z)

    def one():
        return [copy(value_ref.at[:, 1 - c], other, 0, sibling)]

    def two():
        return [
            copy(
                pair.at[:, :, lane_piece(replica(j), n_d, lanes_n)],
                from_dp.at[j],
                j,
                {"dp": replica(j)},
            )
            for j in range(1, n_d)
        ]

    def three():
        return [
            copy(summed.at[chip(k)], from_z.at[k], n_d + k, {"fsdp": 2 * chip(k) + c})
            for k in range(1, n_z)
        ]

    def four():
        ref = out.at[z, c, :, mine]
        return [
            copy(ref, ref, n_d + n_z + j, {"dp": replica(j)}) for j in range(1, n_d)
        ]

    def five():
        ref = out.at[z, c]
        return [
            copy(ref, ref, 2 * n_d + n_z + k, {"fsdp": 2 * chip(k) + c}) for k in range(1, n_z)
        ]

    def six():
        ref = out.at[:, c]
        return [copy(ref, ref, 2 * n_d + 2 * n_z, sibling)]

    def start(group):
        for item in group:
            item.start()

    def arrive(group):
        for item in group:
            item.wait_recv()

    def step_one():
        start(one())

    def step_two():
        arrive(one())
        for i in range(n_z):
            pair[i] = (
                value_ref[i, pl.ds(c, 1)][0].astype(f32) + other[i].astype(f32)
            ).astype(pair.dtype)
        start(two())

    def step_three():
        arrive(two())
        for i in range(n_z):
            value = pair[i, :, mine].astype(f32)
            for j in range(1, n_d):
                value = value + from_dp[j, i].astype(f32)
            summed[i] = value.astype(summed.dtype)
        start(three())

    def step_four():
        arrive(three())
        value = summed[pl.ds(z, 1)][0].astype(f32)
        for k in range(1, n_z):
            value = value + from_z[k].astype(f32)
        out[pl.ds(z, 1), pl.ds(c, 1), :, mine] = value.astype(out.dtype)[None, None]
        start(four())

    def step_five():
        arrive(four())
        start(five())

    def step_six():
        arrive(five())
        start(six())

    def step_seven():
        arrive(six())
        for group in (one(), two(), three(), four(), five(), six()):
            for item in group:
                item.wait_send()

    return step_one, step_two, step_three, step_four, step_five, step_six, step_seven


def starts(group):
    for item in group:
        item.start()


def arrives(group):
    for item in group:
        item.wait_recv()


def leaves(group):
    for item in group:
        item.wait_send()


def remote(src, dst, send, recv, target):
    return pltpu.make_async_remote_copy(
        src_ref=src,
        dst_ref=dst,
        send_sem=send,
        recv_sem=recv,
        device_id=target,
        device_id_type=MESH,
    )


def plan_owner(here, value, other, pair, from_dp, summed, from_z, out, sems):
    n_d, n_z, d, z, c = here
    lanes_n = out.shape[1]
    mine = lane_piece(d, n_d, lanes_n)
    send, recv = sems

    def one():
        target = {"fsdp": 2 * z + 1 - c}
        return [remote(value.at[:, 1 - c], other, send.at[0], recv.at[0], target)]

    def two():
        group = []
        for j in range(1, n_d):
            peer = lax.rem(d + j, n_d)
            ref = pair.at[:, :, lane_piece(peer, n_d, lanes_n)]
            group.append(remote(ref, from_dp.at[j], send.at[j], recv.at[j], {"dp": peer}))
        return group

    def three():
        group = []
        for k in range(1, n_z):
            chip = lax.rem(z + k, n_z)
            index = n_d + k
            target = {"fsdp": 2 * chip + c}
            group.append(
                remote(summed.at[chip], from_z.at[k], send.at[index], recv.at[index], target)
            )
        return group

    def four():
        group = []
        ref = out.at[:, mine]
        for j in range(1, n_d):
            index = n_d + n_z + j
            target = {"dp": lax.rem(d + j, n_d)}
            group.append(remote(ref, ref, send.at[index], recv.at[index], target))
        return group

    def step_one():
        starts(one())

    def step_two():
        arrives(one())
        for i in range(n_z):
            own = value[i, pl.ds(c, 1)][0].astype(f32)
            pair[i] = (own + other[i].astype(f32)).astype(bf16)
        starts(two())

    def step_three():
        arrives(two())
        for i in range(n_z):
            total = pair[i, :, mine].astype(f32)
            for j in range(1, n_d):
                total = total + from_dp[j, i].astype(f32)
            summed[i] = total.astype(bf16)
        starts(three())

    def step_four():
        arrives(three())
        total = summed[pl.ds(z, 1)][0].astype(f32)
        for k in range(1, n_z):
            total = total + from_z[k].astype(f32)
        out[:, mine] = total.astype(bf16)
        starts(four())

    def finish():
        arrives(four())
        for group in (one(), two(), three(), four()):
            leaves(group)

    return step_one, step_two, step_three, step_four, finish


def owner_scratch(rows, lanes):
    n_d, n_z = lax.axis_size("dp"), lax.axis_size("fsdp") // 2
    part = lanes // n_d
    dma = pltpu.SemaphoreType.DMA
    return [
        pltpu.VMEM((n_z, 2, rows, lanes), bf16),
        pltpu.VMEM((n_z, rows, lanes), bf16),
        pltpu.VMEM((n_z, rows, lanes), bf16),
        pltpu.VMEM((n_d, n_z, rows, part), bf16),
        pltpu.VMEM((n_z, rows, part), bf16),
        pltpu.VMEM((n_z, rows, part), bf16),
        pltpu.VMEM((rows, lanes), bf16),
        dma((2 * n_d + n_z,)),
        dma((2 * n_d + n_z,)),
    ]


def plan_spread(here, out, sems):
    n_d, n_z, d, z, c = here
    send, recv = sems

    def one():
        group = []
        for k in range(1, n_z):
            ref = out.at[z, c]
            target = {"fsdp": 2 * lax.rem(z + k, n_z) + c}
            group.append(remote(ref, ref, send.at[k], recv.at[k], target))
        return group

    def two():
        ref = out.at[:, c]
        return [remote(ref, ref, send.at[0], recv.at[0], {"fsdp": 2 * z + 1 - c})]

    def step_two():
        arrives(one())
        starts(two())

    def finish():
        arrives(two())
        leaves(one())
        leaves(two())

    return (lambda: starts(one())), step_two, finish


def plan_clips(here, everyone, sems):
    n_d, n_z, d, z, c = here
    send, recv = sems

    def one():
        group = []
        for j in range(1, n_d):
            ref = everyone.at[d, z, c]
            target = {"dp": lax.rem(d + j, n_d)}
            group.append(remote(ref, ref, send.at[j], recv.at[j], target))
        return group

    def two():
        group = []
        for k in range(1, n_z):
            ref = everyone.at[:, z, c]
            target = {"fsdp": 2 * lax.rem(z + k, n_z) + c}
            group.append(remote(ref, ref, send.at[n_d + k], recv.at[n_d + k], target))
        return group

    def three():
        ref = everyone.at[:, :, c]
        return [remote(ref, ref, send.at[0], recv.at[0], {"fsdp": 2 * z + 1 - c})]

    def step_two():
        arrives(one())
        starts(two())

    def step_three():
        arrives(two())
        starts(three())

    def finish():
        arrives(three())
        for group in (one(), two(), three()):
            leaves(group)

    return (lambda: starts(one())), step_two, step_three, finish


def all_peers(here):
    n_d, n_z, d, z, c = here
    n_f = 2 * n_z
    me = 2 * z + c
    peers = []
    for j in range(n_d):
        for k in range(n_f):
            if j or k:
                peers.append((j * n_f + k, lax.rem(d + j, n_d), lax.rem(me + k, n_f)))
    return peers


def greet_all(here):
    barrier = pltpu.get_barrier_semaphore()
    peers = all_peers(here)
    for _, other_d, other_f in peers:
        pl.semaphore_signal(
            barrier,
            inc=1,
            device_id={"dp": other_d, "fsdp": other_f},
            device_id_type=MESH,
        )
    pl.semaphore_wait(barrier, len(peers))


def plan_small(here, tiles, terms, out, sems):
    n_d, n_z, d, z, c = here
    n_f = 2 * n_z
    mine = d * n_f + 2 * z + c
    s1, r1, s2, r2 = sems
    peers = all_peers(here)

    def one():
        return [
            remote(
                tiles.at[other_d * n_f + other_f],
                terms.at[mine],
                s1.at[index],
                r1.at[index],
                {"dp": other_d, "fsdp": other_f},
            )
            for index, other_d, other_f in peers
        ]

    def two():
        ref = out.at[mine]
        return [
            remote(
                ref, ref, s2.at[index], r2.at[index], {"dp": other_d, "fsdp": other_f}
            )
            for index, other_d, other_f in peers
        ]

    def step_one():
        terms[pl.ds(mine, 1)] = tiles[pl.ds(mine, 1)]
        starts(one())

    def step_two():
        arrives(one())
        total = terms[0]
        for i in range(1, n_d * n_f):
            total = total + terms[i]
        out[pl.ds(mine, 1)] = total[None]
        starts(two())

    def finish():
        arrives(two())
        leaves(one())
        leaves(two())

    return step_one, step_two, finish


def plan_scalar(here, squares, sems):
    n_d, n_z, d, z, c = here
    n_f = 2 * n_z
    mine = d * n_f + 2 * z + c
    send, recv = sems

    def one():
        ref = squares.at[mine]
        return [
            remote(
                ref, ref, send.at[index], recv.at[index], {"dp": other_d, "fsdp": other_f}
            )
            for index, other_d, other_f in all_peers(here)
        ]

    def finish():
        arrives(one())
        total = squares[0]
        for i in range(1, n_d * n_f):
            total = total + squares[i]
        leaves(one())
        return total

    return (lambda: starts(one())), finish


def store_rows(ref, first, lane, value):
    size = ref.shape[2]
    done = 0
    while done < value.shape[0]:
        shard, offset = divmod(first + done, size)
        count = min(size - offset, value.shape[0] - done)
        ref[shard // 2, shard % 2, offset : offset + count, lane : lane + value.shape[1]] = value[
            done : done + count
        ]
        done = done + count


def store_folded(ref, first, value):
    size = ref.shape[2]
    width = value.shape[1]
    done = 0
    while done < value.shape[0]:
        block, offset = divmod(first + done, size)
        shard, side = divmod(block, 2)
        count = min(size - offset, value.shape[0] - done)
        ref[
            shard // 2, shard % 2, offset : offset + count, side * width : (side + 1) * width
        ] = value[done : done + count]
        done = done + count


def put_tiles(ref, first, value):
    across = value.shape[1] // 128
    for i in range(value.shape[0] // 8):
        for j in range(across):
            ref[first + i * across + j] = value[8 * i : 8 * i + 8, 128 * j : 128 * j + 128]


def take_tiles(ref, first, rows, lanes):
    across = lanes // 128
    return jnp.concatenate(
        [
            jnp.concatenate([ref[first + i * across + j] for j in range(across)], 1)
            for i in range(rows // 8)
        ],
        0,
    )


def total_scratch(rows, lanes, dtype):
    n_d, n_z = lax.axis_size("dp"), lax.axis_size("fsdp") // 2
    part = lanes // n_d
    dma = pltpu.SemaphoreType.DMA
    count = 2 * n_d + 2 * n_z + 1
    return [
        pltpu.VMEM((n_z, 2, rows, lanes), dtype),
        pltpu.VMEM((n_z, rows, lanes), dtype),
        pltpu.VMEM((n_z, rows, lanes), dtype),
        pltpu.VMEM((n_d, n_z, rows, part), dtype),
        pltpu.VMEM((n_z, rows, part), dtype),
        pltpu.VMEM((n_z, rows, part), dtype),
        dma((count,)),
        dma((count,)),
    ]


def fold_rows(value):
    half = value.shape[0] // 2
    return jnp.concatenate([value[:half], value[half:]], 1)


def shard_gather(here, wide_land, down_land, sems):
    n_d, n_z, d, z, c = here
    lanes_w = lane_piece(d, n_d, wide_land.shape[3])
    lanes_d = lane_piece(d, n_d, down_land.shape[3])

    def parts(source):
        return [
            wide_land.at[source, c, :, lanes_w],
            down_land.at[source, c, :, lanes_d],
        ]

    def wholes(source):
        return [wide_land.at[source, c], down_land.at[source, c]]

    return plan_gather(here, parts, wholes, sems)


def place_shards(here, wide, down, wide_land, down_land):
    z, c = here[3], here[4]
    wide_land[pl.ds(z, 1), pl.ds(c, 1)] = wide.astype(bf16)[None, None]
    down_land[pl.ds(z, 1), pl.ds(c, 1)] = fold_rows(down).astype(bf16)[None, None]


def land_out(wide_land, down_land, wide_out, down_out):
    n_z = wide_land.shape[0]
    lanes = down_out.shape[1]
    rows_w, rows_d = wide_land.shape[2], down_land.shape[2]
    for i in range(n_z):
        for j in range(2):
            shard = 2 * i + j
            wide_out[shard * rows_w : (shard + 1) * rows_w, :] = wide_land[i, j]
            first = 2 * shard * rows_d
            down_out[first : first + rows_d, :] = down_land[i, j, :, :lanes]
            down_out[first + rows_d : first + 2 * rows_d, :] = down_land[i, j, :, lanes:]


def land_scratch(wide_shape, down_shape):
    n_z = lax.axis_size("fsdp") // 2
    return [
        pltpu.VMEM((n_z, 2) + wide_shape, bf16),
        pltpu.VMEM((n_z, 2, down_shape[0] // 2, 2 * down_shape[1]), bf16),
    ] + gather_sems(2)


def land_gather(here, land, sems):
    n_d, c = here[0], here[4]
    lanes = lane_piece(here[2], n_d, land.shape[3])
    return plan_gather(
        here,
        lambda source: [land.at[source, c, :, lanes]],
        lambda source: [land.at[source, c]],
        sems,
    )


def unfold_land(land, out, which):
    n_z, _, rows, lanes = land.shape
    width = lanes // 2
    for block in range(n_z * 4):
        shard, side = divmod(block, 2)
        done = 0
        while done < rows:
            tap, offset = divmod(block * rows + done, width)
            count = min(width - offset, rows - done)
            first = swap_tap(tap) * width + offset
            out[which, first : first + count, :] = land[
                shard // 2, shard % 2, done : done + count, side * width : (side + 1) * width
            ]
            done = done + count


def fore_kernel(
    run,
    groups,
    len_ref,
    time_ref,
    lat_ref,
    noi_ref,
    stem_ref,
    conv_own,
    wide_own,
    time_own,
    vec_ref,
    clap_ref,
    zero_any,
    act_one_any,
    inner_any,
    act_two_any,
    one_any,
    normed_any,
    qkv_any,
    colsT_ref,
    noiT_ref,
    stat_ref,
    film_ref,
    conv_any,
    time_any,
    wide_any,
    buf,
    cols,
    tall,
    first_land,
    second_land,
    zero_ref,
    act_one_ref,
    inner_ref,
    act_two_ref,
    one_ref,
    normed_ref,
    qkv_ref,
    conv_ref,
    time_land,
    wide_land,
    out_sems,
    *sems,
):
    rows_n, channels = zero_ref.shape
    latent_ch = lat_ref.shape[0] * run // rows_n
    embed = time_own.shape[2]
    count = rows_n // CHUNK
    here = places()
    n_d, n_z, d, z, c = here
    first_plan = land_gather(here, first_land, sems[0:6])
    second_plan = land_gather(here, second_land, sems[6:12])
    wide_plan = land_gather(here, wide_land, sems[12:18])
    t_lanes = lane_piece(d, n_d, embed)
    time_plan = plan_gather(
        here,
        lambda source: [time_land.at[:, source, c, :, t_lanes]],
        lambda source: [time_land.at[:, source, c]],
        sems[18:24],
    )
    own = (pl.ds(z, 1), pl.ds(c, 1))
    first_land[own] = fold_rows(conv_own[0]).astype(bf16)[None, None]
    second_land[own] = fold_rows(conv_own[1]).astype(bf16)[None, None]
    wide_land[own] = wide_own[:, 0 : wide_land.shape[3]].astype(bf16)[None, None]
    time_land[:, pl.ds(z, 1), pl.ds(c, 1)] = time_own[...].astype(bf16)[:, None, None]
    outs = []

    def save(src, dst):
        copy = pltpu.make_async_copy(src, dst, out_sems.at[len(outs)])
        outs.append(copy)
        copy.start()

    greet(*here)
    first_plan[0]()
    time_plan[0]()
    live = len_ref[0]
    counted = (live * (rows_n // run) * (channels // groups)).astype(f32)
    segs = offsets(channels, embed, FF, latent_ch)

    def seg(index):
        start, length = segs[index]
        return vec_ref[start : start + length].reshape(1, length)

    def by_bins(value):
        return jnp.concatenate(
            [value[i * latent_ch : (i + 1) * latent_ch] for i in range(rows_n // run)], 1
        )

    noise = noi_ref[...].astype(f32)
    noiT_ref[...] = by_bins(noise)
    phase = (jnp.zeros((1, run), f32) + time_ref[0].astype(f32)) / 1000.0
    kept = jnp.cos((phase + 0.008) / 1.008 * (math.pi / 2)) ** 2
    mixed = jnp.sqrt(kept) * lat_ref[...].astype(f32) + jnp.sqrt(1.0 - kept) * noise
    pos = lax.broadcasted_iota(jnp.int32, mixed.shape, 1)
    noisy = by_bins(jnp.where(pos < live, mixed, 0.0).astype(bf16).astype(f32))
    taps = 9 * latent_ch
    for a in range(3):
        for b in range(3):
            tap = 3 * a + b
            tall[tap * latent_ch : (tap + 1) * latent_ch] = tap_shift(noisy, a, b, run)
    tall[taps:] = jnp.zeros((tall.shape[0] - taps, rows_n), f32)
    colsT_ref[...] = tall[0:taps].astype(bf16)
    cols[...] = tall[...].T.astype(bf16)
    stem_low = jnp.concatenate(
        [swap_taps(stem_ref[...]), jnp.zeros((cols.shape[1] - taps, channels), f32)], 0
    ).astype(bf16)
    stem_bias = seg(12)

    def stem_part(i, carry):
        rows = pl.ds(pl.multiple_of(i * CHUNK, CHUNK), CHUNK)
        zero_ref[rows, :] = mm(cols[rows, :], stem_low) + stem_bias
        return carry

    loop(count, stem_part, 0)
    save(zero_ref, zero_any)
    first_plan[1]()

    clear_ends(buf, rows_n, run)

    def convolve(which, start):
        total = None
        for a in range(3):
            part = mm(
                buf[pl.ds(start + run * a, CHUNK), :],
                conv_ref[which, 3 * a * channels : 3 * (a + 1) * channels, :],
            )
            total = part if total is None else total + part
        return total

    def activate(read, center, scale, gain, shift, act_ref, hooks):
        factor = scale * gain

        def part(i, carry):
            start = pl.multiple_of(i * CHUNK, CHUNK)
            value = jax.nn.silu((read(start) - center) * factor + shift)
            value = jnp.where(live_rows(value.shape, live, run), value, 0.0)
            low = value.astype(bf16)
            act_ref[pl.ds(start, CHUNK), :] = low
            put_shifted(buf, start, low.astype(f32), run)
            return carry

        loop(count, part, 0, hooks)

    def read_zero(start):
        return zero_ref[pl.ds(start, CHUNK), :]

    center, scale = group_stats(read_zero, rows_n, live, run, channels, groups, counted)
    stat_ref[0:1] = center
    stat_ref[1:2] = scale
    second_plan[0]()
    wide_plan[0]()
    activate(
        read_zero, center, scale, seg(0), seg(1), act_one_ref, ((1, time_plan[1]),)
    )
    first_plan[2]()
    first_plan[3]()
    unfold_land(first_land, conv_ref, 0)
    save(act_one_ref, act_one_any)
    save(conv_ref.at[0], conv_any.at[0])

    bias_one = seg(2)

    def conv_part(i, carry):
        start = pl.multiple_of(i * CHUNK, CHUNK)
        inner_ref[pl.ds(start, CHUNK), :] = convolve(0, start) + bias_one
        return carry

    loop(count, conv_part, 0, ((1, second_plan[1]),))
    wide_plan[1]()
    save(inner_ref, inner_any)

    def read_inner(start):
        return inner_ref[pl.ds(start, CHUNK), :]

    pixels = (live * (rows_n // run)).astype(f32)
    middle, spread = channel_stats(
        read_inner, rows_n, live, run, channels, lambda row: row / pixels
    )
    time_plan[2]()
    time_plan[3]()
    def time_matrix(index):
        return time_land[index].reshape(embed, embed)

    wave = time_wave(time_ref, embed)
    pre_time = vec_mat(wave, time_matrix(0)) + seg(13)
    embedding = vec_mat(jax.nn.silu(pre_time), time_matrix(1)) + seg(14) + clap_ref[...]
    film = vec_mat(jax.nn.silu(embedding), time_matrix(2)) + seg(15)
    film_ref[0:1] = film
    film_ref[1:2] = pre_time
    film_ref[2:3] = embedding
    film_ref[3:8] = jnp.zeros((5, embed), f32)
    lift = 1.0 + film[:, :channels]
    move = film[:, channels:]


    def read_moved(start):
        return inner_ref[pl.ds(start, CHUNK), :] * lift + move

    size = channels // groups
    middle = middle * lift + move
    center = group_total(middle, groups) / size
    gap = middle - center
    spread = group_total(lift * lift * spread + gap * gap, groups) / size
    scale = lax.rsqrt(spread + norm_floor)
    stat_ref[2:3] = center
    stat_ref[3:4] = scale
    stat_ref[4:8] = jnp.zeros((4, channels), f32)
    second_plan[2]()
    wide_plan[2]()
    activate(read_moved, center, scale, seg(3), seg(4), act_two_ref, ())
    second_plan[3]()
    wide_plan[3]()
    unfold_land(second_land, conv_ref, 1)
    save(act_two_ref, act_two_any)
    save(conv_ref.at[1], conv_any.at[1])
    save(time_land, time_any)
    save(wide_land, wide_any)

    bias_two = seg(5)
    gain, shift = seg(6), seg(7)
    wide_full = wide_land[...].reshape(channels, wide_land.shape[3])
    wqkv_t = wide_full[:, 0 : 3 * channels].T

    def last_part(i, carry):
        start = pl.multiple_of(i * CHUNK, CHUNK)
        rows = pl.ds(start, CHUNK)
        stream = zero_ref[rows, :] + convolve(1, start) + bias_two
        one_ref[rows, :] = stream
        gap = stream - row_mean(stream)
        normed = gap * lax.rsqrt(row_mean(gap * gap) + norm_floor) * gain + shift
        low = normed.astype(bf16)
        normed_ref[rows, :] = low
        qkv_ref[:, rows] = mm_nt(wqkv_t, low).astype(bf16)
        return carry

    for i in range(count):
        last_part(i, 0)
        rows = pl.ds(i * CHUNK, CHUNK)
        save(one_ref.at[rows], one_any.at[rows])
        save(normed_ref.at[rows], normed_any.at[rows])
        save(qkv_ref.at[:, rows], qkv_any.at[:, rows])
    for copy in outs:
        copy.wait()


def fill_query(aug, query, factor, extra):
    dim, length = query.shape
    scaled = query.astype(f32) * (factor * LOG2E)
    high = scaled.astype(bf16)
    aug[0:dim] = high
    aug[dim : 2 * dim] = (scaled - high.astype(f32)).astype(bf16)
    index = lax.broadcasted_iota(jnp.int32, (16, length), 0)
    tile = jnp.where(index == 0, 1.0, 0.0)
    for place, row in enumerate(extra):
        tile = jnp.where(index == place + 1, jnp.broadcast_to(row, tile.shape), tile)
    aug[2 * dim : 2 * dim + 16] = tile.astype(bf16)
    aug[2 * dim + 16 :] = jnp.zeros((aug.shape[0] - 2 * dim - 16, length), bf16)


def fill_keys(aug, keys, live, run):
    dim, length = keys.shape
    rest = aug.shape[1] - 2 * dim
    index = lax.broadcasted_iota(jnp.int32, (rest, length), 0)
    pos = lax.broadcasted_iota(jnp.int32, (rest, length), 1)
    mask = jnp.where(lax.rem(pos, run) < live, 0.0, masked_score)
    tile = jnp.where(index == 0, mask, jnp.where(index < 4, 1.0, 0.0))
    both = keys.astype(f32)
    aug[...] = jnp.concatenate([both, both, tile], 0).T.astype(bf16)


def three_parts(row):
    top = row.astype(bf16).astype(f32)
    rest = row - top
    mid = rest.astype(bf16).astype(f32)
    return top, mid, rest - mid


def attend_kernel(
    run,
    key_block,
    len_ref,
    q_ref,
    k_ref,
    v_ref,
    up_ref,
    down_ref,
    o_ref,
    lse_ref,
    up_out,
    down_out,
    kaug,
    qaug,
    vaug,
    up_land,
    down_land,
    *sems,
):
    dim, length = q_ref.shape
    here = places()
    steps = shard_gather(here, up_land, down_land, sems)
    head = pl.program_id(0)

    @pl.when(head == 0)
    def _():
        place_shards(here, up_ref[:, -up_land.shape[3] :], down_ref[...], up_land, down_land)
        greet(*here)
        steps[0]()

    pl.when(head == 2)(steps[1])
    pl.when(head == 4)(steps[2])

    @pl.when(head == 6)
    def _():
        steps[3]()
        land_out(up_land, down_land, up_out, down_out)

    live = len_ref[0]
    fill_query(qaug, q_ref[...], dim ** (-0.5), ())
    fill_keys(kaug, k_ref[...], live, run)
    vaug[0:dim] = v_ref[...]
    index = lax.broadcasted_iota(jnp.int32, (16, length), 0)
    vaug[dim : dim + 16] = jnp.where(index == 0, 1.0, 0.0).astype(bf16)
    top = None
    for i in range(length // key_block):
        keys = slice(i * key_block, (i + 1) * key_block)
        scores = mm(kaug[keys, :], qaug[...])
        block_top = jnp.max(scores, axis=0, keepdims=True)
        new_top = block_top if top is None else jnp.maximum(top, block_top)
        weights = jnp.exp2(scores - new_top).astype(bf16)
        part = mm(vaug[:, keys], weights)
        total = part if top is None else total * jnp.exp2(top - new_top) + part
        top = new_top
    summed = total[dim : dim + 1]
    o_ref[...] = total[0:dim] / summed
    lse_ref[0] = top + jnp.log2(summed)


def attend_back_kernel(
    run,
    key_block,
    len_ref,
    q_ref,
    k_ref,
    v_ref,
    lse_ref,
    o_ref,
    do_ref,
    early_ref,
    wide_ref,
    down_ref,
    dq_ref,
    dk_ref,
    dv_ref,
    early_out,
    wide_out,
    down_out,
    kaug,
    qaug,
    vaug,
    daug,
    acc,
    early_land,
    pair,
    other,
    from_dp,
    summed,
    from_z,
    send,
    recv,
    wide_land,
    down_land,
    *sems,
):
    dim, length = q_ref.shape
    step = pl.program_id(1)
    here = places()
    now = pl.program_id(0) * pl.num_programs(1) + step
    gathers = shard_gather(here, wide_land, down_land, sems)
    totals = plan_total(
        here, early_ref, early_land, pair, other, from_dp, summed, from_z, (send, recv)
    )

    @pl.when(now == 0)
    def _():
        place_shards(here, wide_ref[...], down_ref[...], wide_land, down_land)
        greet(*here)
        totals[0]()

    for place, action in (
        (2, totals[1]),
        (6, totals[2]),
        (9, totals[3]),
        (12, totals[4]),
        (19, totals[5]),
        (21, totals[6]),
        (21, gathers[0]),
        (24, gathers[1]),
        (28, gathers[2]),
        (31, gathers[3]),
    ):
        pl.when(now == place)(action)

    @pl.when(now == 31)
    def _():
        early_out[...] = early_land[...]
        land_out(wide_land, down_land, wide_out, down_out)

    factor = dim ** (-0.5)

    @pl.when(step == 0)
    def _():
        live = len_ref[0]
        fill_query(qaug, q_ref[...], factor, three_parts(-lse_ref[0]))
        fill_keys(kaug, k_ref[...], live, run)
        values = v_ref[...].astype(f32)
        rest = vaug.shape[1] - dim
        index = lax.broadcasted_iota(jnp.int32, (rest, length), 0)
        tile = jnp.where(index < 3, -1.0, 0.0)
        vaug[...] = jnp.concatenate([values, tile], 0).T.astype(bf16)
        back = do_ref[...]
        delta = col_sum(back.astype(f32) * o_ref[...])
        daug[0:dim] = back
        index = lax.broadcasted_iota(jnp.int32, (16, length), 0)
        tile = jnp.zeros((16, length), f32)
        for place, row in enumerate(three_parts(delta)):
            tile = jnp.where(index == place, jnp.broadcast_to(row, tile.shape), tile)
        daug[dim : dim + 16] = tile.astype(bf16)
        daug[dim + 16 :] = jnp.zeros((daug.shape[0] - dim - 16, length), bf16)
        acc[...] = jnp.zeros(acc.shape, f32)

    keys = pl.ds(pl.multiple_of(step * key_block, key_block), key_block)
    weights = jnp.exp2(mm(kaug[keys, :], qaug[...]))
    raw = (weights * mm(vaug[keys, :], daug[...])).astype(bf16)
    dv_ref[...] = mm_nt(do_ref[...], weights.astype(bf16)).astype(bf16)
    dk_ref[...] = (mm_nt(q_ref[...], raw) * factor).astype(bf16)
    acc[...] += mm(k_ref[:, keys], raw)

    @pl.when(step == pl.num_programs(1) - 1)
    def _():
        dq_ref[...] = (acc[...] * factor).astype(bf16)


def middle_kernel(
    run,
    len_ref,
    mixed_ref,
    one_ref,
    first_ref,
    up_ref,
    down_ref,
    vec_ref,
    headw_ref,
    noiT_ref,
    two_grad_ref,
    do_ref,
    early_ref,
    small_ref,
    hidden,
    slope,
    xhat,
    spread,
    three,
    prod,
    gcols,
    normed_t,
    three_t,
    gpre,
    glow,
    head_ref,
):
    rows_n, channels = one_ref.shape
    units = down_ref.shape[0]
    latent_ch = noiT_ref.shape[0]
    count = rows_n // CHUNK
    live = len_ref[0]
    segs = offsets(channels, EMB, units, latent_ch)

    def seg(index):
        start, length = segs[index]
        return vec_ref[start : start + length].reshape(1, length)

    w_out = first_ref[:, 3 * channels :]
    for tap in range(9):
        first = swap_tap(tap) * channels
        prod[tap * latent_ch : (tap + 1) * latent_ch, 0:channels] = headw_ref[
            :, first : first + channels
        ]
    prod[9 * latent_ch :, 0:channels] = jnp.zeros((prod.shape[0] - 9 * latent_ch, channels), f32)
    head_ref[...] = prod[:, 0:channels].astype(bf16)
    index = lax.broadcasted_iota(jnp.int32, (latent_ch, latent_ch), 0)
    same = index == lax.broadcasted_iota(jnp.int32, (latent_ch, latent_ch), 1)
    head_bias = jnp.sum(jnp.where(same, seg(17), 0.0), axis=1, keepdims=True)
    proj_bias, gain, shift, up_bias, down_bias = seg(8), seg(9), seg(10), seg(16), seg(11)

    def fore(i, carry):
        start = pl.multiple_of(i * CHUNK, CHUNK)
        rows = pl.ds(start, CHUNK)
        mixed = mixed_ref[:, rows].T.astype(bf16)
        stream = one_ref[rows, :] + mm(mixed, w_out) + proj_bias
        gap = stream - row_mean(stream)
        scale = lax.rsqrt(row_mean(gap * gap) + norm_floor)
        hat = gap * scale
        xhat[rows, :] = hat
        spread[rows, :] = jnp.broadcast_to(scale, (CHUNK, spread.shape[1]))
        normed = (hat * gain + shift).astype(bf16)
        normed_t[:, rows] = normed.T
        pre = mm(normed, up_ref[...]) + up_bias
        phi = 0.5 * (1.0 + lax.erf(pre * (0.5**0.5)))
        slope[rows, :] = phi + pre * jnp.exp(-0.5 * pre * pre) * (0.5 / math.pi) ** 0.5
        low = (pre * phi).astype(bf16)
        hidden[rows, :] = low
        stream = stream + mm(low, down_ref[...]) + down_bias
        stream = jnp.where(live_rows(stream.shape, live, run), stream, 0.0).astype(bf16)
        three[rows, :] = stream
        prod[:, rows] = mm_nt(head_ref[...], stream)
        return carry

    loop(count, fore, 0)

    taps = 9 * latent_ch
    predicted = jnp.zeros((latent_ch, rows_n), f32) + head_bias
    for a in range(3):
        for b in range(3):
            tap = 3 * a + b
            predicted = predicted + tap_shift(
                prod[tap * latent_ch : (tap + 1) * latent_ch], a, b, run
            )
    pos = lax.broadcasted_iota(jnp.int32, predicted.shape, 1)
    errors = jnp.where(lax.rem(pos, run) < live, predicted - noiT_ref[...], 0.0)
    small_ref[...] = jnp.zeros(small_ref.shape, f32)
    tile = (latent_ch, 128)
    sums = jnp.broadcast_to(jnp.sum(errors, axis=1, keepdims=True), tile)
    same = lax.broadcasted_iota(jnp.int32, tile, 0) == lax.broadcasted_iota(jnp.int32, tile, 1)
    put_small(small_ref, 17, col_sum(jnp.where(same, sums, 0.0)))
    sums = jnp.broadcast_to(jnp.sum(errors * errors, axis=1, keepdims=True), tile)
    put_small(small_ref, 18, col_sum(sums))
    put_small(small_ref, 19, jnp.zeros((1, 128), f32) + (live * (rows_n // run)).astype(f32))
    errors = errors.astype(bf16).astype(f32)
    for a in range(3):
        for b in range(3):
            tap = 3 * a + b
            prod[tap * latent_ch : (tap + 1) * latent_ch] = tap_shift(
                errors, 2 - a, 2 - b, run
            )
    prod[taps:] = jnp.zeros((prod.shape[0] - taps, rows_n), f32)
    gcols[...] = prod[...].T.astype(bf16)
    ghead = mm(prod[0:taps].astype(bf16), three[...])

    def back(i, carry):
        g_down, g_up, g_gain, g_shift, g_proj = carry
        start = pl.multiple_of(i * CHUNK, CHUNK)
        rows = pl.ds(start, CHUNK)
        grad = mm(gcols[rows, :], head_ref[...])
        grad = jnp.where(live_rows(grad.shape, live, run), grad, 0.0)
        low = grad.astype(bf16)
        three_t[:, rows] = low.T
        pre = mm_nt(low, down_ref[...]) * slope[rows, :]
        pre_low = pre.astype(bf16)
        gpre[rows, :] = pre_low
        dnormed = mm_nt(pre_low, up_ref[...])
        hat = xhat[rows, :]
        dhat = dnormed * gain
        dstream = (dhat - row_mean(dhat) - hat * row_mean(dhat * hat)) * spread[rows, 0:1]
        two = grad + dstream
        two_grad_ref[rows, :] = two
        two_low = two.astype(bf16)
        glow[rows, :] = two_low
        do_ref[:, rows] = mm_nt(w_out, two_low).astype(bf16)
        return (
            g_down + col_sum(grad),
            g_up + col_sum(pre),
            g_gain + col_sum(dnormed * hat),
            g_shift + col_sum(dnormed),
            g_proj + col_sum(two),
        )

    blank = jnp.zeros((1, channels), f32)
    sums = loop(count, back, (blank, jnp.zeros((1, units), f32), blank, blank, blank))
    for index, value in zip((11, 16, 9, 10, 8), sums):
        put_small(small_ref, index, value)
    half = units // 2
    for part in range(units // channels):
        columns = slice(part * channels, (part + 1) * channels)
        first = (part * channels) % half
        lanes = slice((part * channels) // half * channels, (part * channels) // half * channels + channels)
        early_ref[first : first + channels, lanes] = mm(three_t[...], hidden[:, columns]).T.astype(
            bf16
        )
        first = half + (part // 2) * channels
        lanes = slice((part % 2) * channels, (part % 2 + 1) * channels)
        early_ref[first : first + channels, lanes] = mm(normed_t[...], gpre[:, columns]).astype(
            bf16
        )
    gproj = mm(mixed_ref[...].astype(bf16), glow[...]).astype(bf16)
    first = half + (units // channels // 2) * channels
    middle = channels // 2
    early_ref[first : first + middle, 0:channels] = gproj[:middle]
    early_ref[first : first + middle, channels:] = gproj[middle:]
    first = first + middle
    ghead = swap_taps(ghead).astype(bf16)
    middle = taps // 2
    early_ref[first : first + middle, 0:channels] = ghead[:middle]
    early_ref[first : first + middle, channels:] = ghead[middle:]
    early_ref[first + middle :, :] = jnp.zeros(
        (early_ref.shape[0] - first - middle, 2 * channels), bf16
    )


def hind_kernel(
    run,
    groups,
    len_ref,
    step_ref,
    dq_any,
    dk_any,
    dv_any,
    two_grad_any,
    normed_any,
    one_any,
    act_two_any,
    inner_any,
    act_one_any,
    zero_any,
    colsT_any,
    stat_ref,
    film_ref,
    conv_any,
    wide_any_w,
    time_any,
    vec_ref,
    mid_ref,
    early_any,
    wide_any,
    down_any,
    small_any,
    root_any,
    large_any,
    conv_out,
    tile_out,
    time_out,
    scalar_out,
    head_out,
    wide_out,
    wide_dir,
    down_out,
    down_dir,
    buf,
    field,
    other,
    act_t,
    small,
    everyone,
    tiles,
    terms,
    squares,
    product,
    first_g,
    first_o,
    first_p,
    first_d,
    first_f,
    first_z,
    first_t,
    first_s,
    first_r,
    second_g,
    second_o,
    second_p,
    second_d,
    second_f,
    second_z,
    second_t,
    second_s,
    second_r,
    qkv_g,
    qkv_o,
    qkv_p,
    qkv_d,
    qkv_f,
    qkv_z,
    qkv_t,
    qkv_s,
    qkv_r,
    spread_s,
    spread_r,
    clip_s,
    clip_r,
    tile_s1,
    tile_r1,
    tile_s2,
    tile_r2,
    square_s,
    square_r,
    qkv_out,
    early,
    wide_full,
    down_full,
    roots_small,
    root_wide,
    root_large,
    root_rows,
    local_sems,
    dq_ref,
    dk_ref,
    dv_ref,
    normed_ref,
    wide_ref,
    two_grad_ref,
    one_ref,
    act_two_ref,
    inner_ref,
    conv_ref,
    time_ref,
    act_one_ref,
    zero_ref,
    colsT_ref,
    load_sems,
):
    rows_n, channels = one_ref.shape
    embed = time_ref.shape[2]
    latent_ch = colsT_ref.shape[0] // 9
    count = rows_n // CHUNK
    live = len_ref[0]
    counted = (live * (rows_n // run) * (channels // groups)).astype(f32)
    segs = offsets(channels, embed, FF, latent_ch)
    blank = jnp.zeros((1, channels), f32)
    small[...] = jnp.zeros(small.shape, f32)
    here = places()
    n_d, n_z, d, z, c = here
    conv_plans = (
        plan_owner(here, first_g, first_o, first_p, first_d, first_f, first_z, first_t, (first_s, first_r)),
        plan_owner(here, second_g, second_o, second_p, second_d, second_f, second_z, second_t, (second_s, second_r)),
    )
    qkv_plan = plan_owner(here, qkv_g, qkv_o, qkv_p, qkv_d, qkv_f, qkv_z, qkv_t, (qkv_s, qkv_r))
    spread_plan = plan_spread(here, qkv_out, (spread_s, spread_r))
    clip_plan = plan_clips(here, everyone, (clip_s, clip_r))
    tile_plan = plan_small(here, tiles, terms, tile_out, (tile_s1, tile_r1, tile_s2, tile_r2))
    square_plan = plan_scalar(here, squares, (square_s, square_r))
    own_rows = root_rows.shape[0]
    loads = [
        pltpu.make_async_copy(src, dst, local_sems.at[index])
        for index, (src, dst) in enumerate(
            (
                (early_any, early),
                (wide_any, wide_full),
                (down_any, down_full),
                (small_any, roots_small),
                (root_any, root_wide),
                (large_any.at[0], root_large),
                (large_any.at[1, pl.ds(lax.axis_index("fsdp") * own_rows, own_rows)], root_rows),
            )
        )
    ]
    first_loads = {
        id(ref): pltpu.make_async_copy(src, ref, load_sems.at[index])
        for index, (src, ref) in enumerate(
            (
                (dq_any, dq_ref),
                (dk_any, dk_ref),
                (dv_any, dv_ref),
                (normed_any, normed_ref),
                (wide_any_w, wide_ref),
                (two_grad_any, two_grad_ref),
                (one_any, one_ref),
                (act_two_any, act_two_ref),
                (inner_any, inner_ref),
                (conv_any, conv_ref),
                (time_any, time_ref),
                (act_one_any, act_one_ref),
                (zero_any, zero_ref),
                (colsT_any, colsT_ref),
            )
        )
    }
    starts(first_loads.values())
    starts(loads)
    greet_all(here)

    def ready(*refs):
        for ref in refs:
            first_loads[id(ref)].wait()

    ready(dq_ref, dk_ref, dv_ref, normed_ref)

    def seg(index):
        start, length = segs[index]
        return vec_ref[start : start + length].reshape(1, length)

    def put_vec(index, value):
        put_small(small, index, value)

    half = channels // 2
    store_rows(qkv_g, 0, 0, mm(dq_ref[...], normed_ref[...]).T.astype(bf16))
    store_rows(qkv_g, 0, channels, mm(dk_ref[...], normed_ref[...]).T.astype(bf16))
    values_grad = mm(dv_ref[...], normed_ref[...]).T.astype(bf16)
    store_rows(qkv_g, channels, 0, values_grad[:half])
    store_rows(qkv_g, channels, channels, values_grad[half:])
    qkv_plan[0]()

    ready(wide_ref, two_grad_ref, one_ref)
    gain_one = seg(6)
    clear_ends(buf, rows_n, run)

    def norm_part(i, carry):
        g_gain, g_shift, g_bias = carry
        start = pl.multiple_of(i * CHUNK, CHUNK)
        rows = pl.ds(start, CHUNK)
        dnormed_t = None
        for part, ref in enumerate((dq_ref, dk_ref, dv_ref)):
            term = mm(wide_ref[:, part * channels : (part + 1) * channels], ref[:, rows])
            dnormed_t = term if dnormed_t is None else dnormed_t + term
        dnormed = dnormed_t.T
        stream = one_ref[rows, :]
        gap = stream - row_mean(stream)
        scale = lax.rsqrt(row_mean(gap * gap) + norm_floor)
        hat = gap * scale
        dhat = dnormed * gain_one
        grad = two_grad_ref[rows, :] + scale * (
            dhat - row_mean(dhat) - hat * row_mean(dhat * hat)
        )
        field[rows, :] = grad
        put_shifted(buf, start, grad.astype(bf16).astype(f32), run)
        return (
            g_gain + col_sum(dnormed * hat),
            g_shift + col_sum(dnormed),
            g_bias + col_sum(grad),
        )

    sums = loop(count, norm_part, (blank, blank, blank), ((1, qkv_plan[1]),))
    for index, value in zip((6, 7, 5), sums):
        put_vec(index, value)

    def weight_grad(which, act_ref):
        act_t[...] = act_ref[...].T
        for a in range(3):
            full = buf[run * (2 - a) : run * (2 - a) + rows_n, :]
            for b in range(3):
                shifted = full[:, (2 - b) * channels : (3 - b) * channels]
                first = (3 * b + a) * channels
                store_folded(
                    (first_g, second_g)[which], first, mm(act_t[...], shifted).astype(bf16)
                )

    def input_grad(which, start):
        total = None
        for a in range(3):
            for b in range(3):
                first = (3 * (2 - a) + 2 - b) * channels
                part = mm_nt(
                    buf[
                        pl.ds(start + run * a, CHUNK),
                        b * channels : (b + 1) * channels,
                    ],
                    conv_ref[which, first : first + channels, :],
                )
                total = part if total is None else total + part
        return total

    def norm_back(which, read, center, scale, gain, shift, g_refs, hooks):
        def part(i, carry):
            g_gain, g_shift = carry
            start = pl.multiple_of(i * CHUNK, CHUNK)
            rows = pl.ds(start, CHUNK)
            hat = (read(start) - center) * scale
            slope = silu_slope(hat * gain + shift)
            grad = input_grad(which, start) * slope
            grad = jnp.where(live_rows(grad.shape, live, run), grad, 0.0)
            other[rows, :] = grad
            return (g_gain + col_sum(grad * hat), g_shift + col_sum(grad))

        g_gain, g_shift = loop(count, part, (blank, blank), hooks)
        put_vec(g_refs[0], g_gain)
        put_vec(g_refs[1], g_shift)
        mean_grad = group_total(g_shift * gain, groups) / counted
        mean_hat = group_total(g_gain * gain, groups) / counted

        def finish(start):
            hat = (read(start) - center) * scale
            grad = (other[pl.ds(start, CHUNK), :] * gain - mean_grad - hat * mean_hat) * scale
            return jnp.where(live_rows(grad.shape, live, run), grad, 0.0)

        return finish

    film = film_ref[0:1]
    lift = 1.0 + film[:, :channels]
    move = film[:, channels:]

    ready(act_two_ref)
    weight_grad(1, act_two_ref)
    conv_plans[1][0]()
    qkv_plan[2]()
    ready(inner_ref, conv_ref)
    finish = norm_back(
        1,
        lambda start: inner_ref[pl.ds(start, CHUNK), :] * lift + move,
        stat_ref[2:3],
        stat_ref[3:4],
        seg(3),
        seg(4),
        (3, 4),
        ((1, conv_plans[1][1]),),
    )

    qkv_plan[3]()

    def inner_part(i, carry):
        g_lift, g_move, g_bias = carry
        start = pl.multiple_of(i * CHUNK, CHUNK)
        moved = finish(start)
        grad = moved * lift
        put_shifted(buf, start, grad.astype(bf16).astype(f32), run)
        return (
            g_lift + col_sum(moved * inner_ref[pl.ds(start, CHUNK), :]),
            g_move + col_sum(moved),
            g_bias + col_sum(grad),
        )

    g_lift, g_move, g_bias = loop(count, inner_part, (blank, blank, blank))
    put_vec(2, g_bias)

    ready(time_ref, act_one_ref, zero_ref, colsT_ref)
    pre_time = film_ref[1:2]
    embedding = film_ref[2:3]
    g_film = jnp.concatenate([g_lift, g_move], 1)
    g_embed = vec_mat(g_film, time_ref[2], True) * silu_slope(embedding)
    g_time = vec_mat(g_embed, time_ref[1], True) * silu_slope(pre_time)
    put_vec(13, g_time)
    put_vec(14, g_embed)
    put_vec(15, g_film)
    factors = jnp.concatenate(
        [
            time_wave(step_ref, embed),
            jax.nn.silu(pre_time),
            jax.nn.silu(embedding),
            g_time,
            g_embed,
            g_film,
            jnp.zeros((2, embed), f32),
        ],
        0,
    )
    factors = jnp.concatenate([factors[:, : embed // 2], factors[:, embed // 2 :]], 0)
    everyone[pl.ds(d, 1), pl.ds(z, 1), pl.ds(c, 1)] = factors.astype(bf16)[None, None, None]
    clip_plan[0]()

    weight_grad(0, act_one_ref)
    conv_plans[0][0]()
    conv_plans[1][2]()
    qkv_plan[4]()
    qkv_out[pl.ds(z, 1), pl.ds(c, 1)] = qkv_t[...][None, None]
    spread_plan[0]()
    finish_zero = norm_back(
        0,
        lambda start: zero_ref[pl.ds(start, CHUNK), :],
        stat_ref[0:1],
        stat_ref[1:2],
        seg(0),
        seg(1),
        (0, 1),
        ((0, clip_plan[1]), (1, conv_plans[0][1])),
    )
    conv_plans[1][3]()
    spread_plan[1]()

    def zero_part(i, carry):
        g_stem, g_bias = carry
        start = pl.multiple_of(i * CHUNK, CHUNK)
        rows = pl.ds(start, CHUNK)
        grad = field[rows, :] + finish_zero(start)
        return (g_stem + mm(colsT_ref[:, rows], grad.astype(bf16)), g_bias + col_sum(grad))

    taps = colsT_ref.shape[0]
    g_stem, g_bias = loop(count, zero_part, (jnp.zeros((taps, channels), f32), blank))
    put_vec(12, g_bias)
    used = taps // 8 * (channels // 128)
    put_tiles(tiles, 0, swap_taps(g_stem))
    put_tiles(tiles, used, small[...] + mid_ref[...])
    used = used + 2 * (small.shape[1] // 128)
    for i in range(used, tiles.shape[0]):
        tiles[i] = jnp.zeros((8, 128), f32)
    tile_plan[0]()
    conv_plans[0][2]()
    clip_plan[2]()
    conv_plans[1][4]()
    mine = lane_piece(d, n_d, 2 * channels)
    rows_c = second_t.shape[0]

    def squared(value):
        return jnp.sum(value * value)

    def unfold(which, ref):
        value = ref[...].astype(f32)
        conv_out[which, 0:rows_c] = value[:, 0:channels]
        conv_out[which, rows_c:] = value[:, channels:]

    unfold(1, second_t)
    square = squared(second_t[:, mine].astype(f32))

    for copy in loads:
        copy.wait()
    width = 2 * channels
    early_rows = early.shape[0] * 2 * early.shape[2]
    sums = early[...].reshape(early_rows, width)
    units = down_full.shape[0]
    half = units // 2
    shared = squared(sums.astype(f32))

    def choose(rows, order):
        own = lax.broadcasted_iota(jnp.int32, (rows, order), 0) + (2 * z + c) * rows
        return jnp.where(
            own == lax.broadcasted_iota(jnp.int32, (rows, order), 1), 1.0, 0.0
        ).astype(bf16)

    pick = choose(wide_out.shape[0], channels)

    def apply(left, value, right_root):
        return mm(mm(left, value).astype(bf16), right_root.astype(bf16))

    def side_by_side(first, rows):
        return jnp.concatenate([sums[first : first + rows], sums[first + rows : first + 2 * rows]], 1)

    def stacked(first, rows):
        block = sums[first : first + rows]
        return jnp.concatenate([block[:, :channels], block[:, channels:]], 0)

    first = half + 2 * channels
    head_first = first + channels // 2
    head_out[...] = stacked(head_first, taps // 2).astype(f32)
    lefts = [mm(pick, roots_small[i].astype(bf16)).astype(bf16) for i in range(3)]
    q_end, o_end = 3 * channels, 4 * channels
    momentum = {}
    later = {}
    for index, (grad, right_root, start, end) in enumerate(
        (
            (None, root_wide, 0, q_end),
            (stacked(first, channels // 2), roots_small.at[3], q_end, o_end),
            (side_by_side(half, channels), root_large, o_end, o_end + units),
        )
    ):
        wide_dir[:, start:end] = 0.9 * apply(
            lefts[index], wide_full[:, start:end], right_root[...]
        )
        if grad is not None:
            wide_out[:, start:end] = mm(pick, grad)
            later[start, end] = apply(lefts[index], grad, right_root[...])
    grad = stacked(0, half)
    rows = root_rows[...].astype(bf16)
    down_out[...] = mm(choose(down_out.shape[0], units), grad)
    later_down = apply(rows, grad, roots_small[4])
    down_dir[...] = 0.9 * apply(rows, down_full[...], roots_small[4])

    tile_plan[1]()
    spread_plan[2]()
    qkv_sum = qkv_out[...].reshape(channels + channels // 2, width)
    shared = shared + squared(qkv_sum.astype(f32))
    tail = qkv_sum[channels:]
    grad = jnp.concatenate(
        [qkv_sum[:channels], jnp.concatenate([tail[:, :channels], tail[:, channels:]], 0)], 1
    )
    wide_out[:, 0:q_end] = mm(pick, grad)
    later[0, q_end] = apply(lefts[0], grad, root_wide[...])
    conv_plans[0][3]()
    square = square + squared(first_t[:, mine].astype(f32))
    clip_plan[3]()
    clips = 2 * n_d * n_z
    depth = time_out.shape[1]
    first = (2 * z + c) * depth
    block = pl.ds(pl.multiple_of(lax.rem(first, embed // 2) // 128 * 128, 128), 128)
    offset = pl.multiple_of(lax.rem(first, 128), 8)
    upper = first >= embed // 2
    time_square = jnp.zeros((), f32)
    for i in range(3):
        sides = [
            everyone[:, :, :, :, block].astype(f32).reshape(clips, 16, 128)[:, part + i]
            for part in (0, 8)
        ]
        left = jnp.where(upper, sides[1], sides[0])
        full = everyone[...].astype(f32).reshape(clips, 16, embed // 2)
        right = jnp.concatenate([full[:, i + 3], full[:, i + 11]], 1)
        product[...] = mm(left.T.astype(bf16), right.astype(bf16))
        value = product[pl.ds(offset, depth), :]
        time_out[i] = value
        time_square = time_square + squared(value)
    square = square + time_square / n_d
    squares[pl.ds(d * 2 * n_z + 2 * z + c, 1)] = jnp.zeros((1, 8, 128), f32) + square
    square_plan[0]()
    tile_plan[2]()
    g_stem = take_tiles(tile_out, 0, taps, channels)
    total = take_tiles(tile_out, taps // 8 * (channels // 128), 16, width)
    index = lax.broadcasted_iota(jnp.int32, total.shape, 0)
    shared = shared + squared(g_stem) + squared(jnp.where(index < 13, total, 0.0))
    conv_plans[0][4]()
    unfold(0, first_t)
    shared = square_plan[1]() + shared
    unit = 2.0 / (latent_ch * total[14:15, 0:1])
    norm = unit * jnp.sqrt(shared)
    factor = jnp.minimum(1.0, clip_limit / norm) * unit
    row = lax.broadcasted_iota(jnp.int32, scalar_out.shape, 0)
    loss = total[13:14, 0:1] * (0.5 * unit)
    scalar_out[...] = jnp.where(row == 0, loss, jnp.where(row == 1, norm, factor))
    factor = factor[0:1, 0:1]
    for (start, end), value in later.items():
        wide_dir[:, start:end] += factor * value
    down_dir[...] += factor * later_down


def sized(shape, dtype=f32):
    return jax.ShapeDtypeStruct(shape, dtype)


VM = pl.BlockSpec(memory_space=pltpu.VMEM)
SM = pl.BlockSpec(memory_space=pltpu.SMEM)
ANY = pl.BlockSpec(memory_space=pl.ANY)


def params(mib):
    return pltpu.CompilerParams(vmem_limit_bytes=mib * 2**20)


def remote_params(number, mib):
    return pltpu.CompilerParams(
        collective_id=number, has_side_effects=True, vmem_limit_bytes=mib * 2**20
    )


def run_fore(run, length, step, lat, noi, stem_w, conv_w, wide_w, time_w, vec, clap):
    channels = stem_w.shape[1]
    latent_ch = stem_w.shape[0] // 9
    rows_n = lat.shape[1] * (lat.shape[0] // latent_ch)
    embed = time_w.shape[2]
    n_z = lax.axis_size("fsdp") // 2
    field = (rows_n, channels)
    land = pltpu.VMEM((n_z, 2, conv_w.shape[1] // 2, 2 * channels), bf16)
    large = [
        sized(field),
        sized(field, bf16),
        sized(field),
        sized(field, bf16),
        sized(field),
        sized(field, bf16),
        sized((3 * channels, rows_n), bf16),
    ]
    weights = [
        sized((2, 9 * channels, channels), bf16),
        sized((3, n_z, 2) + time_w.shape[1:], bf16),
        sized((n_z, 2, wide_w.shape[0], 4 * channels), bf16),
    ]
    outs = pl.pallas_call(
        functools.partial(fore_kernel, run, GROUPS),
        in_specs=[SM, SM] + [VM] * 8,
        out_specs=[ANY] * 7 + [VM] * 4 + [ANY] * 3,
        out_shape=large
        + [
            sized((9 * latent_ch, rows_n), bf16),
            sized((latent_ch, rows_n)),
            sized((8, channels)),
            sized((8, embed)),
        ]
        + weights,
        scratch_shapes=[
            pltpu.VMEM((rows_n + 2 * run, 3 * channels), bf16),
            pltpu.VMEM((rows_n, 128), bf16),
            pltpu.VMEM((128, rows_n), f32),
            land,
            land,
        ]
        + [pltpu.VMEM(item.shape, item.dtype) for item in large + weights]
        + [pltpu.SemaphoreType.DMA((8 + 3 * max(1, rows_n // CHUNK),))]
        + gather_sems(1) * 4,
        compiler_params=remote_params(1, 62),
        name="fore",
    )(length, step, lat, noi, stem_w, conv_w, wide_w, time_w, vec, clap)
    time_full = outs[12].reshape(3, -1, embed)
    first_full = outs[13].reshape(-1, 4 * channels)
    return (*outs[:12], time_full, first_full)


def run_attend(run, length, qkv_t, up, down, key_block=256):
    n_f = lax.axis_size("fsdp")
    triple, rows_n = qkv_t.shape
    channels = triple // 3
    dim = channels // HEADS
    return pl.pallas_call(
        functools.partial(attend_kernel, run, key_block),
        grid=(HEADS,),
        in_specs=[SM]
        + [pl.BlockSpec((dim, rows_n), lambda h, t=t: (t * HEADS + h, 0)) for t in range(3)]
        + [VM] * 2,
        out_specs=[
            pl.BlockSpec((dim, rows_n), lambda h: (h, 0)),
            pl.BlockSpec((1, 1, rows_n), lambda h: (h, 0, 0)),
            VM,
            VM,
        ],
        out_shape=[
            sized((channels, rows_n)),
            sized((HEADS, 1, rows_n)),
            sized((up.shape[0] * n_f, FF), bf16),
            sized((down.shape[0] * n_f, down.shape[1]), bf16),
        ],
        scratch_shapes=[
            pltpu.VMEM((rows_n, 128), bf16),
            pltpu.VMEM((128, rows_n), bf16),
            pltpu.VMEM((dim + 16, rows_n), bf16),
        ]
        + land_scratch((up.shape[0], FF), down.shape),
        compiler_params=remote_params(3, 62),
        name="attend",
    )(length, qkv_t, qkv_t, qkv_t, up, down)


def run_attend_back(
    run, length, qkv_t, lse, mixed_t, grad_t, early, wide, down, key_block=512
):
    n_f = lax.axis_size("fsdp")
    early = early.reshape(n_f // 2, 2, early.shape[0] // n_f, early.shape[1])
    triple, rows_n = qkv_t.shape
    channels = triple // 3
    dim = channels // HEADS
    whole = pl.BlockSpec((dim, rows_n), lambda h, j: (h, 0))
    block = pl.BlockSpec((dim, key_block), lambda h, j: (h, j))
    return pl.pallas_call(
        functools.partial(attend_back_kernel, run, key_block),
        grid=(HEADS, rows_n // key_block),
        in_specs=[SM]
        + [pl.BlockSpec((dim, rows_n), lambda h, j, t=t: (t * HEADS + h, 0)) for t in range(3)]
        + [pl.BlockSpec((1, 1, rows_n), lambda h, j: (h, 0, 0)), whole, whole]
        + [VM] * 3,
        out_specs=[whole, block, block] + [VM] * 3,
        out_shape=[sized((channels, rows_n), bf16)] * 3
        + [
            sized(early.shape, bf16),
            sized((wide.shape[0] * n_f, wide.shape[1]), bf16),
            sized((down.shape[0] * n_f, down.shape[1]), bf16),
        ],
        scratch_shapes=[
            pltpu.VMEM((rows_n, 128), bf16),
            pltpu.VMEM((128, rows_n), bf16),
            pltpu.VMEM((rows_n, 128), bf16),
            pltpu.VMEM((128, rows_n), bf16),
            pltpu.VMEM((dim, rows_n), f32),
        ]
        + total_scratch(early.shape[2], early.shape[3], bf16)
        + land_scratch(wide.shape, down.shape),
        compiler_params=remote_params(4, 62),
        name="attend_back",
    )(length, qkv_t, qkv_t, qkv_t, lse, mixed_t, grad_t, early, wide, down)


def run_middle(run, length, mixed_t, one, first, up, down, vec, head_w, noi_t):
    rows_n, channels = one.shape
    units = down.shape[0]
    latent_ch = noi_t.shape[0]
    return pl.pallas_call(
        functools.partial(middle_kernel, run),
        in_specs=[SM] + [VM] * 8,
        out_specs=[VM] * 4,
        out_shape=[
            sized((rows_n, channels)),
            sized((channels, rows_n), bf16),
            sized((units + channels, 2 * channels), bf16),
            sized((16, 2 * channels)),
        ],
        scratch_shapes=[
            pltpu.VMEM((rows_n, units), bf16),
            pltpu.VMEM((rows_n, units), f32),
            pltpu.VMEM((rows_n, channels), f32),
            pltpu.VMEM((rows_n, 128), f32),
            pltpu.VMEM((rows_n, channels), bf16),
            pltpu.VMEM((128, rows_n), f32),
            pltpu.VMEM((rows_n, 128), bf16),
            pltpu.VMEM((channels, rows_n), bf16),
            pltpu.VMEM((channels, rows_n), bf16),
            pltpu.VMEM((rows_n, units), bf16),
            pltpu.VMEM((rows_n, channels), bf16),
            pltpu.VMEM((128, channels), bf16),
        ],
        compiler_params=params(62),
        name="middle",
    )(length, mixed_t, one, first, up, down, vec, head_w, noi_t)


def run_hind(run, length, step, *arrays):
    one = arrays[5]
    rows_n, channels = one.shape
    embed = arrays[15].shape[2]
    n_d, n_f = lax.axis_size("dp"), lax.axis_size("fsdp")
    n_z = n_f // 2
    count = n_d * n_f
    tile_count = max(count, 32)
    rows_c = arrays[13].shape[1] // n_f
    rows_a = (channels + channels // 2) // n_f
    dma = pltpu.SemaphoreType.DMA
    return pl.pallas_call(
        functools.partial(hind_kernel, run, GROUPS),
        in_specs=[SM, SM]
        + [ANY] * 11
        + [VM] * 2
        + [ANY] * 3
        + [VM] * 2
        + [ANY] * 6,
        out_specs=[VM] * 9,
        out_shape=[
            sized((2, rows_c, channels)),
            sized((tile_count, 8, 128)),
            sized((3, embed // n_f, embed)),
            sized((8, 128)),
            sized((arrays[10].shape[0], channels)),
            sized((channels // n_f, 4 * channels + FF)),
            sized((channels // n_f, 4 * channels + FF)),
            sized((FF // n_f, channels)),
            sized((FF // n_f, channels)),
        ],
        scratch_shapes=[
            pltpu.VMEM((rows_n + 2 * run, 3 * channels), bf16),
            pltpu.VMEM((rows_n, channels), f32),
            pltpu.VMEM((rows_n, channels), f32),
            pltpu.VMEM((channels, rows_n), bf16),
            pltpu.VMEM((16, 2 * channels), f32),
            pltpu.VMEM((n_d, n_z, 2, 16, embed // 2), bf16),
            pltpu.VMEM((tile_count, 8, 128), f32),
            pltpu.VMEM((count, 8, 128), f32),
            pltpu.VMEM((count, 8, 128), f32),
            pltpu.VMEM((128, embed), f32),
        ]
        + owner_scratch(rows_c // 2, 2 * channels)
        + owner_scratch(rows_c // 2, 2 * channels)
        + owner_scratch(rows_a, 2 * channels)
        + [
            dma((n_z,)),
            dma((n_z,)),
            dma((n_d + n_z,)),
            dma((n_d + n_z,)),
            dma((count,)),
            dma((count,)),
            dma((count,)),
            dma((count,)),
            dma((count,)),
            dma((count,)),
            pltpu.VMEM((n_z, 2, rows_a, 2 * channels), bf16),
            pltpu.VMEM(arrays[-6].shape, bf16),
            pltpu.VMEM(arrays[-5].shape, bf16),
            pltpu.VMEM(arrays[-4].shape, bf16),
            pltpu.VMEM(arrays[-3].shape, f32),
            pltpu.VMEM(arrays[-2].shape, f32),
            pltpu.VMEM(arrays[-1].shape[1:], f32),
            pltpu.VMEM((FF // n_f, FF), f32),
            dma((7,)),
        ]
        + [pltpu.VMEM(arrays[i].shape, arrays[i].dtype) for i in (0, 1, 2, 4, 14, 3, 5)]
        + [pltpu.VMEM(arrays[i].shape, arrays[i].dtype) for i in (6, 7, 13, 15, 8, 9, 10)]
        + [dma((14,))],
        compiler_params=remote_params(2, 63),
        name="hind",
    )(length, step, *arrays)


def update_kernel(
    latent_ch,
    units,
    step_ref,
    scalar_ref,
    conv_g,
    time_g,
    tiles,
    head_g,
    wide_g,
    wide_dir,
    down_g,
    down_dir,
    stem_w,
    stem_m,
    stem_s,
    head_w,
    head_m,
    head_s,
    time_w,
    time_m,
    time_s,
    vec_m,
    vec_s,
    conv_w,
    conv_m,
    conv_s,
    wide_w,
    wide_m,
    down_w,
    down_m,
    loss_out,
    norm_out,
    stem_out,
    stem_m_out,
    stem_s_out,
    head_out,
    head_m_out,
    head_s_out,
    time_out,
    time_m_out,
    time_s_out,
    vec_out,
    vec_m_out,
    vec_s_out,
    conv_out,
    conv_m_out,
    conv_s_out,
    wide_out,
    wide_m_out,
    down_out,
    down_m_out,
):
    taps, channels = stem_w.shape
    stem_tiles = taps // 8 * (channels // 128)
    small = take_tiles(tiles, stem_tiles, 16, 2 * channels)
    factor = scalar_ref[2:3, 0:1]
    loss_out[0] = scalar_ref[0, 0]
    norm_out[0] = scalar_ref[1, 0]
    step = jnp.zeros((1, 1), f32) + step_ref[0].astype(f32)
    one_over = 1.0 / (1.0 - jnp.exp(step * math.log(0.9)))
    two_over = 1.0 / (1.0 - jnp.exp(step * math.log(0.999)))

    def adam(outs, where, weight, first, second, grad):
        grad = factor * grad
        first_new = 0.9 * first + 0.1 * grad
        second_new = 0.999 * second + 0.001 * grad * grad
        moved = first_new * one_over / (jnp.sqrt(second_new * two_over) + adam_floor)
        outs[0][where] = weight - adam_rate * (moved + decay_rate * weight)
        outs[1][where] = first_new
        outs[2][where] = second_new

    whole = slice(None)
    adam(
        (stem_out, stem_m_out, stem_s_out),
        whole,
        stem_w[...],
        stem_m[...],
        stem_s[...],
        take_tiles(tiles, 0, taps, channels),
    )
    outs = (time_out, time_m_out, time_s_out)
    for i in range(time_w.shape[0]):
        adam(outs, i, time_w[i], time_m[i], time_s[i], time_g[i])
    outs = (conv_out, conv_m_out, conv_s_out)
    for i in range(conv_w.shape[0]):
        adam(outs, i, conv_w[i], conv_m[i], conv_s[i], conv_g[i])
    outs = (head_out, head_m_out, head_s_out)
    for tap in range(9):
        where = (whole, slice(tap * channels, (tap + 1) * channels))
        grad = head_g[tap * latent_ch : (tap + 1) * latent_ch]
        adam(outs, where, head_w[where], head_m[where], head_s[where], grad)

    def vec_grad(which):
        if which < 13:
            lane = (which % 2) * channels
            return small[which // 2 : which // 2 + 1, lane : lane + channels]
        if which < 16:
            return small[which - 6 : which - 5]
        if which == 16:
            return jnp.concatenate([small[10:11], small[11:12]], 1)
        return small[12:13, 0:latent_ch]

    for which, (first, length) in enumerate(
        offsets(channels, 2 * channels, units, latent_ch)
    ):
        where = slice(first, first + length)
        grad = (factor * vec_grad(which)).reshape(length)
        vec_out[where] = grad
        vec_m_out[where] = 0.9 * vec_m[where] + 0.1 * grad
        vec_s_out[where] = 0.999 * vec_s[where] + 0.001 * grad * grad

    kept = 1.0 - shampoo_rate * decay_rate
    wide_m_out[...] = 0.9 * wide_m[...] + factor * wide_g[...]
    wide_out[...] = wide_w[...] * kept - shampoo_rate * wide_dir[...]
    down_m_out[...] = 0.9 * down_m[...] + factor * down_g[...]
    down_out[...] = down_w[...] * kept - shampoo_rate * down_dir[...]


def run_update(latent_ch, step, *arrays):
    stem_w, head_w, time_w, vec_m = arrays[9], arrays[12], arrays[15], arrays[18]
    conv_w, wide_w, down_w = arrays[20], arrays[23], arrays[25]
    shapes = [(1,)] * 2 + [stem_w.shape] * 3 + [head_w.shape] * 3 + [time_w.shape] * 3
    shapes += [vec_m.shape] * 3 + [conv_w.shape] * 3 + [wide_w.shape] * 2 + [down_w.shape] * 2
    return pl.pallas_call(
        functools.partial(update_kernel, latent_ch, FF),
        in_specs=[SM] + [VM] * len(arrays),
        out_specs=[SM] * 2 + [VM] * (len(shapes) - 2),
        out_shape=[sized(shape) for shape in shapes],
        compiler_params=params(62),
        name="update",
    )(step, *arrays)


def local(
    latents,
    noises,
    clap_embed,
    timesteps,
    lengths,
    step_count,
    stem_w,
    head_w,
    time_w,
    vector,
    conv_w,
    wide_w,
    down_w,
    roots_small,
    root_wide,
    roots_large,
    stem_moment,
    stem_square,
    head_moment,
    head_square,
    time_moment,
    time_square,
    vector_moment,
    vector_square,
    conv_moment,
    conv_square,
    wide_moment,
    down_moment,
):
    frames_n, freq_bins, latent_ch = (latents.shape[1], latents.shape[2], latents.shape[3])
    channels = stem_w.shape[1]
    def by_bins(value):
        return value[0].transpose(1, 2, 0).reshape(freq_bins * latent_ch, frames_n)

    head_t = head_w.T
    (
        zero,
        act_one,
        inner,
        act_two,
        one,
        normed,
        qkv_t,
        cols_t,
        noi_t,
        stat,
        film,
        conv_full,
        time_full,
        first_full,
    ) = run_fore(
        frames_n,
        lengths,
        timesteps,
        by_bins(latents),
        by_bins(noises),
        stem_w,
        conv_w,
        wide_w,
        time_w,
        vector,
        clap_embed,
    )
    mixed_t, lse, up_full, down_full = run_attend(
        frames_n, lengths, qkv_t, wide_w, down_w
    )
    two_grad, do_t, early, small = run_middle(
        frames_n,
        lengths,
        mixed_t,
        one,
        first_full,
        up_full,
        down_full,
        vector,
        head_t,
        noi_t,
    )
    dq, dk, dv, early, wide_moment_full, down_moment_full = run_attend_back(
        frames_n, lengths, qkv_t, lse, mixed_t, do_t, early, wide_moment, down_moment
    )
    outs = run_hind(
        frames_n,
        lengths,
        timesteps,
        dq,
        dk,
        dv,
        two_grad,
        normed,
        one,
        act_two,
        inner,
        act_one,
        zero,
        cols_t,
        stat,
        film,
        conv_full,
        first_full,
        time_full,
        vector,
        small,
        early,
        wide_moment_full,
        down_moment_full,
        roots_small,
        root_wide,
        roots_large,
    )
    conv_sum, tiles, time_sum, scalars, head_sum, wide_sum, wide_dir, down_sum, down_dir = outs
    outs = run_update(
        latent_ch,
        step_count,
        scalars,
        conv_sum,
        time_sum,
        tiles,
        head_sum,
        wide_sum,
        wide_dir,
        down_sum,
        down_dir,
        stem_w,
        stem_moment,
        stem_square,
        head_t,
        head_moment.T,
        head_square.T,
        time_w,
        time_moment,
        time_square,
        vector_moment,
        vector_square,
        conv_w,
        conv_moment,
        conv_square,
        wide_w,
        wide_moment,
        down_w,
        down_moment,
    )
    outs = list(outs)
    for index in (5, 6, 7):
        outs[index] = outs[index].T
    return (outs[0][0], outs[1][0], *outs[2:])


def solution(mesh):
    in_specs = (
        P(("dp", "fsdp"), None, None, None),
        P(("dp", "fsdp"), None, None, None),
        P(("dp", "fsdp"), None),
        P(("dp", "fsdp")),
        P(("dp", "fsdp")),
        P(),
        P(),
        P(),
        P(None, "fsdp", None),
        P(),
        P(None, "fsdp", None),
        P("fsdp", None),
        P("fsdp", None),
        P(),
        P(),
        P(),
        P(),
        P(),
        P(),
        P(),
        P(None, "fsdp", None),
        P(None, "fsdp", None),
        P(),
        P(),
        P(None, "fsdp", None),
        P(None, "fsdp", None),
        P("fsdp", None),
        P("fsdp", None),
    )
    out_specs = (
        P(),
        P(),
        P(),
        P(),
        P(),
        P(),
        P(),
        P(),
        P(None, "fsdp", None),
        P(None, "fsdp", None),
        P(None, "fsdp", None),
        P(),
        P(),
        P(),
        P(None, "fsdp", None),
        P(None, "fsdp", None),
        P(None, "fsdp", None),
        P("fsdp", None),
        P("fsdp", None),
        P("fsdp", None),
        P("fsdp", None),
    )
    return jax.shard_map(local, mesh=mesh, in_specs=in_specs, out_specs=out_specs, check_vma=False)
```

```python
import functools
import math

import jax
import jax.numpy as jnp
from jax import lax
from jax.experimental import pallas as pl
from jax.experimental.pallas import tpu as pltpu
from jax.sharding import PartitionSpec as P

HEADS = 8
FF = 1024
EMB = 512
GROUPS = 32

norm_floor = 1e-05
masked_score = -1e30
clip_limit = 0.002
adam_rate = 0.05
adam_floor = 1e-08
shampoo_rate = 0.02
decay_rate = 0.01

f32 = jnp.float32
bf16 = jnp.bfloat16
highest = lax.Precision.HIGHEST
LOG2E = math.log2(math.e)
CHUNK = 1024


def mm(left_op, right_op):
    return jnp.dot(left_op, right_op, preferred_element_type=f32)


def mm_nt(left_op, right_op):
    return lax.dot_general(
        left_op, right_op, (((1,), (1,)), ((), ())), preferred_element_type=f32
    )


def col_sum(value):
    return jnp.sum(value, axis=0, keepdims=True)


def row_mean(value):
    return jnp.mean(value, axis=-1, keepdims=True)


def loop(count, body, init, hooks=()):
    if not hooks:
        return lax.fori_loop(0, count, body, init)

    def step(i, carry):
        for place, action in hooks:
            pl.when(i == place)(action)
        return body(i, carry)

    return lax.fori_loop(0, count, step, init)


def tap_shift(field, a, b, run):
    length = field.shape[1]
    step = run * (a - 1) + (b - 1)
    if step == 0:
        return field
    pos = lax.broadcasted_iota(jnp.int32, field.shape, 1)
    bin_pos = lax.rem(pos, run)
    keep = None
    for wanted, test in (
        (a == 0, lambda: pos >= run),
        (a == 2, lambda: pos < length - run),
        (b == 0, lambda: bin_pos >= 1),
        (b == 2, lambda: bin_pos < run - 1),
    ):
        if wanted:
            keep = test() if keep is None else jnp.logical_and(keep, test())
    return jnp.where(keep, pltpu.roll(field, (-step) % length, 1), 0.0)


def put_shifted(buf, start, value, run):
    rows, channels = value.shape
    bin_pos = lax.rem(lax.broadcasted_iota(jnp.int32, value.shape, 0), run)
    before = jnp.where(bin_pos == 0, 0.0, pltpu.roll(value, 1, 0))
    after = jnp.where(bin_pos == run - 1, 0.0, pltpu.roll(value, rows - 1, 0))
    where = pl.ds(start + run, rows)
    buf[where, 0:channels] = before.astype(bf16)
    buf[where, channels : 2 * channels] = value.astype(bf16)
    buf[where, 2 * channels : 3 * channels] = after.astype(bf16)


def clear_ends(buf, rows_n, run):
    blank = jnp.zeros((run, buf.shape[1]), bf16)
    buf[0:run, :] = blank
    buf[rows_n + run : rows_n + 2 * run, :] = blank


def live_rows(shape, live, run):
    return lax.rem(lax.broadcasted_iota(jnp.int32, shape, 0), run) < live


def swap_tap(tap):
    return tap % 3 * 3 + tap // 3


def swap_taps(value, axis=0):
    size = value.shape[axis] // 9
    pieces = [
        lax.slice_in_dim(value, swap_tap(t) * size, (swap_tap(t) + 1) * size, axis=axis)
        for t in range(9)
    ]
    return jnp.concatenate(pieces, axis)


def group_total(row, groups):
    channels = row.shape[1]
    size = channels // groups
    one = lax.broadcasted_iota(jnp.int32, (channels, channels), 0) // size
    two = lax.broadcasted_iota(jnp.int32, (channels, channels), 1) // size
    same = jnp.where(one == two, 1.0, 0.0).astype(f32)
    wide = jnp.broadcast_to(row, (8, channels))
    return jnp.dot(wide, same, precision=highest, preferred_element_type=f32)[0:1]


def vec_mat(row, weight, transposed=False):
    top = row.astype(bf16).astype(f32)
    rest = row - top
    mid = rest.astype(bf16).astype(f32)
    low = rest - mid
    shape = (16, row.shape[1])
    index = lax.broadcasted_iota(jnp.int32, shape, 0)
    stacked = jnp.where(
        index == 0,
        jnp.broadcast_to(top, shape),
        jnp.where(
            index == 1,
            jnp.broadcast_to(mid, shape),
            jnp.where(index == 2, jnp.broadcast_to(low, shape), 0.0),
        ),
    ).astype(bf16)
    return col_sum(mm_nt(stacked, weight) if transposed else mm(stacked, weight))


def silu_slope(value):
    gate = jax.nn.sigmoid(value)
    return gate * (1.0 + value * (1.0 - gate))


def channel_stats(read, rows_n, live, run, channels, average):
    count = rows_n // CHUNK

    def add(i, total):
        start = pl.multiple_of(i * CHUNK, CHUNK)
        value = read(start)
        return total + col_sum(jnp.where(live_rows(value.shape, live, run), value, 0.0))

    center = average(loop(count, add, jnp.zeros((1, channels), f32)))

    def add_square(i, total):
        start = pl.multiple_of(i * CHUNK, CHUNK)
        value = read(start) - center
        return total + col_sum(jnp.where(live_rows(value.shape, live, run), value * value, 0.0))

    return center, average(loop(count, add_square, jnp.zeros((1, channels), f32)))


def group_stats(read, rows_n, live, run, channels, groups, counted):
    center, spread = channel_stats(
        read, rows_n, live, run, channels, lambda row: group_total(row, groups) / counted
    )
    return center, lax.rsqrt(spread + norm_floor)


def time_wave(time_ref, embed):
    half = embed // 2
    index = lax.broadcasted_iota(jnp.int32, (1, half), 1).astype(f32)
    frequency = jnp.exp(-math.log(10000.0) * index / half)
    angles = (jnp.zeros((1, half), f32) + time_ref[0].astype(f32)) * frequency
    return jnp.concatenate([jnp.cos(angles), jnp.sin(angles)], 1)


def offsets(channels, embed_width, hidden_units, latent_ch):
    starts = []
    start = 0
    for length in [channels] * 13 + [embed_width] * 3 + [hidden_units, latent_ch]:
        starts.append((start, length))
        start = start + length
    return starts


def put_small(ref, index, value):
    if index < 13:
        half = value.shape[1]
        ref[index // 2 : index // 2 + 1, (index % 2) * half : (index % 2 + 1) * half] = value
    elif index < 16:
        ref[index - 6 : index - 5, :] = value
    elif index == 16:
        half = value.shape[1] // 2
        ref[10:11, :] = value[:, :half]
        ref[11:12, :] = value[:, half:]
    else:
        ref[index - 5 : index - 4, 0 : value.shape[1]] = value


def take_small(rows, latent_ch):
    return jnp.concatenate(
        [
            rows[0:6].reshape(-1),
            rows[6, : rows.shape[1] // 2],
            rows[7:12].reshape(-1),
            rows[12, :latent_ch],
        ]
    )


MESH = pl.DeviceIdType.MESH


def places():
    n_d, n_f = lax.axis_size("dp"), lax.axis_size("fsdp")
    me = lax.axis_index("fsdp")
    return n_d, n_f // 2, lax.axis_index("dp"), me // 2, lax.rem(me, 2)


def push(src, dst, sends, recvs, target):
    copy = pltpu.make_async_remote_copy(
        src_ref=src,
        dst_ref=dst,
        send_sem=sends,
        recv_sem=recvs,
        device_id=target,
        device_id_type=MESH,
    )
    copy.start()
    return copy


def greet(n_d, n_z, d, z, c):
    barrier = pltpu.get_barrier_semaphore()
    for j in range(1, n_d):
        pl.semaphore_signal(
            barrier, inc=1, device_id={"dp": lax.rem(d + j, n_d)}, device_id_type=MESH
        )
    for k in range(1, n_z):
        pl.semaphore_signal(
            barrier,
            inc=1,
            device_id={"fsdp": 2 * lax.rem(z + k, n_z) + c},
            device_id_type=MESH,
        )
    pl.semaphore_signal(
        barrier, inc=1, device_id={"fsdp": 2 * z + 1 - c}, device_id_type=MESH
    )


def met(n_d, n_z, d, z, c):
    pl.semaphore_wait(pltpu.get_barrier_semaphore(), n_d + n_z - 1)


def conv_piece(d, n_d, channels):
    width = 2 * channels // n_d
    return (d * width) // channels, pl.ds(
        pl.multiple_of(lax.rem(d * width, channels), 128), width
    )


def lane_piece(d, n_d, lanes):
    width = lanes // n_d
    return pl.ds(pl.multiple_of(d * width, 128), width)


def plan_gather(here, parts, wholes, sems):
    n_d, n_z, d, z, c = here
    s1, r1, s2, r2, s3, r3 = sems
    sibling = {"fsdp": 2 * z + 1 - c}

    def copy(ref, sends, recvs, target):
        return pltpu.make_async_remote_copy(
            src_ref=ref,
            dst_ref=ref,
            send_sem=sends,
            recv_sem=recvs,
            device_id=target,
            device_id_type=MESH,
        )

    def source(k):
        return lax.rem(z - k + n_z, n_z)

    def first(k):
        target = {"fsdp": 2 * lax.rem(z + k, n_z) + c}
        return [copy(r, s1.at[k, i], r1.at[k, i], target) for i, r in enumerate(parts(z))]

    def second(k, j):
        target = {"dp": lax.rem(d + j, n_d)}
        refs = parts(source(k))
        return [copy(r, s2.at[k, j, i], r2.at[k, j, i], target) for i, r in enumerate(refs)]

    def last(k):
        refs = wholes(source(k))
        return [copy(r, s3.at[k, i], r3.at[k, i], sibling) for i, r in enumerate(refs)]

    def start(group):
        for item in group:
            item.start()

    def arrive(group):
        for item in group:
            item.wait_recv()

    def leave(group):
        for item in group:
            item.wait_send()

    far = range(1, n_z)
    peers = range(1, n_d)

    def step_one():
        for k in far:
            start(first(k))
        start(last(0))

    def step_two():
        for k in far:
            arrive(first(k))
            for j in peers:
                start(second(k, j))

    def step_three():
        for k in far:
            for j in peers:
                arrive(second(k, j))
            start(last(k))

    def step_four():
        for k in range(n_z):
            arrive(last(k))
        for k in far:
            leave(first(k))
            for j in peers:
                leave(second(k, j))
        for k in range(n_z):
            leave(last(k))

    return step_one, step_two, step_three, step_four


def gather_sems(count):
    n_d, n_z = lax.axis_size("dp"), lax.axis_size("fsdp") // 2
    dma = pltpu.SemaphoreType.DMA
    return [
        dma((n_z, count)),
        dma((n_z, count)),
        dma((n_z, n_d, count)),
        dma((n_z, n_d, count)),
        dma((n_z, count)),
        dma((n_z, count)),
    ]


def plan_total(here, value_ref, out, pair, other, from_dp, summed, from_z, sems):
    n_d, n_z, d, z, c = here
    lanes_n = out.shape[3]
    mine = lane_piece(d, n_d, lanes_n)
    sibling = {"fsdp": 2 * z + 1 - c}
    send, recv = sems

    def copy(src, dst, index, target):
        return pltpu.make_async_remote_copy(
            src_ref=src,
            dst_ref=dst,
            send_sem=send.at[index],
            recv_sem=recv.at[index],
            device_id=target,
            device_id_type=MESH,
        )

    def replica(j):
        return lax.rem(d + j, n_d)

    def chip(k):
        return lax.rem(z + k, n_z)

    def one():
        return [copy(value_ref.at[:, 1 - c], other, 0, sibling)]

    def two():
        return [
            copy(
                pair.at[:, :, lane_piece(replica(j), n_d, lanes_n)],
                from_dp.at[j],
                j,
                {"dp": replica(j)},
            )
            for j in range(1, n_d)
        ]

    def three():
        return [
            copy(summed.at[chip(k)], from_z.at[k], n_d + k, {"fsdp": 2 * chip(k) + c})
            for k in range(1, n_z)
        ]

    def four():
        ref = out.at[z, c, :, mine]
        return [
            copy(ref, ref, n_d + n_z + j, {"dp": replica(j)}) for j in range(1, n_d)
        ]

    def five():
        ref = out.at[z, c]
        return [
            copy(ref, ref, 2 * n_d + n_z + k, {"fsdp": 2 * chip(k) + c}) for k in range(1, n_z)
        ]

    def six():
        ref = out.at[:, c]
        return [copy(ref, ref, 2 * n_d + 2 * n_z, sibling)]

    def start(group):
        for item in group:
            item.start()

    def arrive(group):
        for item in group:
            item.wait_recv()

    def step_one():
        start(one())

    def step_two():
        arrive(one())
        for i in range(n_z):
            pair[i] = (
                value_ref[i, pl.ds(c, 1)][0].astype(f32) + other[i].astype(f32)
            ).astype(pair.dtype)
        start(two())

    def step_three():
        arrive(two())
        for i in range(n_z):
            value = pair[i, :, mine].astype(f32)
            for j in range(1, n_d):
                value = value + from_dp[j, i].astype(f32)
            summed[i] = value.astype(summed.dtype)
        start(three())

    def step_four():
        arrive(three())
        value = summed[pl.ds(z, 1)][0].astype(f32)
        for k in range(1, n_z):
            value = value + from_z[k].astype(f32)
        out[pl.ds(z, 1), pl.ds(c, 1), :, mine] = value.astype(out.dtype)[None, None]
        start(four())

    def step_five():
        arrive(four())
        start(five())

    def step_six():
        arrive(five())
        start(six())

    def step_seven():
        arrive(six())
        for group in (one(), two(), three(), four(), five(), six()):
            for item in group:
                item.wait_send()

    return step_one, step_two, step_three, step_four, step_five, step_six, step_seven


def starts(group):
    for item in group:
        item.start()


def arrives(group):
    for item in group:
        item.wait_recv()


def leaves(group):
    for item in group:
        item.wait_send()


def remote(src, dst, send, recv, target):
    return pltpu.make_async_remote_copy(
        src_ref=src,
        dst_ref=dst,
        send_sem=send,
        recv_sem=recv,
        device_id=target,
        device_id_type=MESH,
    )


def plan_owner(here, value, other, pair, from_dp, summed, from_z, out, sems):
    n_d, n_z, d, z, c = here
    lanes_n = out.shape[1]
    mine = lane_piece(d, n_d, lanes_n)
    send, recv = sems

    def one():
        target = {"fsdp": 2 * z + 1 - c}
        return [remote(value.at[:, 1 - c], other, send.at[0], recv.at[0], target)]

    def two():
        group = []
        for j in range(1, n_d):
            peer = lax.rem(d + j, n_d)
            ref = pair.at[:, :, lane_piece(peer, n_d, lanes_n)]
            group.append(remote(ref, from_dp.at[j], send.at[j], recv.at[j], {"dp": peer}))
        return group

    def three():
        group = []
        for k in range(1, n_z):
            chip = lax.rem(z + k, n_z)
            index = n_d + k
            target = {"fsdp": 2 * chip + c}
            group.append(
                remote(summed.at[chip], from_z.at[k], send.at[index], recv.at[index], target)
            )
        return group

    def four():
        group = []
        ref = out.at[:, mine]
        for j in range(1, n_d):
            index = n_d + n_z + j
            target = {"dp": lax.rem(d + j, n_d)}
            group.append(remote(ref, ref, send.at[index], recv.at[index], target))
        return group

    def step_one():
        starts(one())

    def step_two():
        arrives(one())
        for i in range(n_z):
            own = value[i, pl.ds(c, 1)][0].astype(f32)
            pair[i] = (own + other[i].astype(f32)).astype(bf16)
        starts(two())

    def step_three():
        arrives(two())
        for i in range(n_z):
            total = pair[i, :, mine].astype(f32)
            for j in range(1, n_d):
                total = total + from_dp[j, i].astype(f32)
            summed[i] = total.astype(bf16)
        starts(three())

    def step_four():
        arrives(three())
        total = summed[pl.ds(z, 1)][0].astype(f32)
        for k in range(1, n_z):
            total = total + from_z[k].astype(f32)
        out[:, mine] = total.astype(bf16)
        starts(four())

    def finish():
        arrives(four())
        for group in (one(), two(), three(), four()):
            leaves(group)

    return step_one, step_two, step_three, step_four, finish


def owner_scratch(rows, lanes):
    n_d, n_z = lax.axis_size("dp"), lax.axis_size("fsdp") // 2
    part = lanes // n_d
    dma = pltpu.SemaphoreType.DMA
    return [
        pltpu.VMEM((n_z, 2, rows, lanes), bf16),
        pltpu.VMEM((n_z, rows, lanes), bf16),
        pltpu.VMEM((n_z, rows, lanes), bf16),
        pltpu.VMEM((n_d, n_z, rows, part), bf16),
        pltpu.VMEM((n_z, rows, part), bf16),
        pltpu.VMEM((n_z, rows, part), bf16),
        pltpu.VMEM((rows, lanes), bf16),
        dma((2 * n_d + n_z,)),
        dma((2 * n_d + n_z,)),
    ]


def plan_spread(here, out, sems):
    n_d, n_z, d, z, c = here
    send, recv = sems

    def one():
        group = []
        for k in range(1, n_z):
            ref = out.at[z, c]
            target = {"fsdp": 2 * lax.rem(z + k, n_z) + c}
            group.append(remote(ref, ref, send.at[k], recv.at[k], target))
        return group

    def two():
        ref = out.at[:, c]
        return [remote(ref, ref, send.at[0], recv.at[0], {"fsdp": 2 * z + 1 - c})]

    def step_two():
        arrives(one())
        starts(two())

    def finish():
        arrives(two())
        leaves(one())
        leaves(two())

    return (lambda: starts(one())), step_two, finish


def plan_clips(here, everyone, sems):
    n_d, n_z, d, z, c = here
    send, recv = sems

    def one():
        group = []
        for j in range(1, n_d):
            ref = everyone.at[d, z, c]
            target = {"dp": lax.rem(d + j, n_d)}
            group.append(remote(ref, ref, send.at[j], recv.at[j], target))
        return group

    def two():
        group = []
        for k in range(1, n_z):
            ref = everyone.at[:, z, c]
            target = {"fsdp": 2 * lax.rem(z + k, n_z) + c}
            group.append(remote(ref, ref, send.at[n_d + k], recv.at[n_d + k], target))
        return group

    def three():
        ref = everyone.at[:, :, c]
        return [remote(ref, ref, send.at[0], recv.at[0], {"fsdp": 2 * z + 1 - c})]

    def step_two():
        arrives(one())
        starts(two())

    def step_three():
        arrives(two())
        starts(three())

    def finish():
        arrives(three())
        for group in (one(), two(), three()):
            leaves(group)

    return (lambda: starts(one())), step_two, step_three, finish


def all_peers(here):
    n_d, n_z, d, z, c = here
    n_f = 2 * n_z
    me = 2 * z + c
    peers = []
    for j in range(n_d):
        for k in range(n_f):
            if j or k:
                peers.append((j * n_f + k, lax.rem(d + j, n_d), lax.rem(me + k, n_f)))
    return peers


def greet_all(here):
    barrier = pltpu.get_barrier_semaphore()
    peers = all_peers(here)
    for _, other_d, other_f in peers:
        pl.semaphore_signal(
            barrier,
            inc=1,
            device_id={"dp": other_d, "fsdp": other_f},
            device_id_type=MESH,
        )


def met_all(here):
    pl.semaphore_wait(pltpu.get_barrier_semaphore(), len(all_peers(here)))


def plan_small(here, value, out, other, pair, from_dp, summed, from_z, sems):
    n_d, n_z, d, z, c = here
    lanes_n = out.shape[3]
    mine = lane_piece(d, n_d, lanes_n)
    send, recv, all_send, all_recv = sems

    def one():
        target = {"fsdp": 2 * z + 1 - c}
        return [remote(value.at[:, 1 - c], other, send.at[0], recv.at[0], target)]

    def two():
        group = []
        for j in range(1, n_d):
            peer = lax.rem(d + j, n_d)
            ref = pair.at[:, :, lane_piece(peer, n_d, lanes_n)]
            group.append(remote(ref, from_dp.at[j], send.at[j], recv.at[j], {"dp": peer}))
        return group

    def three():
        group = []
        for k in range(1, n_z):
            chip = lax.rem(z + k, n_z)
            index = n_d + k
            target = {"fsdp": 2 * chip + c}
            group.append(
                remote(summed.at[chip], from_z.at[k], send.at[index], recv.at[index], target)
            )
        return group

    def four():
        ref = out.at[z, c, :, mine]
        return [
            remote(
                ref,
                ref,
                all_send.at[index],
                all_recv.at[index],
                {"dp": other_d, "fsdp": other_f},
            )
            for index, other_d, other_f in all_peers(here)
        ]

    def step_one():
        starts(one())

    def step_two():
        arrives(one())
        for i in range(n_z):
            pair[i] = value[i, pl.ds(c, 1)][0] + other[i]
        starts(two())

    def step_three():
        arrives(two())
        for i in range(n_z):
            total = pair[i, :, mine]
            for j in range(1, n_d):
                total = total + from_dp[j, i]
            summed[i] = total
        starts(three())

    def step_four():
        arrives(three())
        total = summed[pl.ds(z, 1)][0]
        for k in range(1, n_z):
            total = total + from_z[k]
        out[pl.ds(z, 1), pl.ds(c, 1), :, mine] = total[None, None]
        starts(four())

    def finish():
        arrives(four())
        for group in (one(), two(), three(), four()):
            leaves(group)

    return step_one, step_two, step_three, step_four, finish


def small_scratch(lanes):
    n_d, n_z = lax.axis_size("dp"), lax.axis_size("fsdp") // 2
    part = lanes // n_d
    dma = pltpu.SemaphoreType.DMA
    return [
        pltpu.VMEM((n_z, 2, 8, lanes), f32),
        pltpu.VMEM((n_z, 8, lanes), f32),
        pltpu.VMEM((n_z, 8, lanes), f32),
        pltpu.VMEM((n_d, n_z, 8, part), f32),
        pltpu.VMEM((n_z, 8, part), f32),
        pltpu.VMEM((n_z, 8, part), f32),
        dma((n_d + n_z,)),
        dma((n_d + n_z,)),
        dma((n_d * n_z * 2,)),
        dma((n_d * n_z * 2,)),
    ]


def plan_scalar(here, squares, sems):
    n_d, n_z, d, z, c = here
    n_f = 2 * n_z
    mine = d * n_f + 2 * z + c
    send, recv = sems

    def one():
        ref = squares.at[mine]
        return [
            remote(
                ref, ref, send.at[index], recv.at[index], {"dp": other_d, "fsdp": other_f}
            )
            for index, other_d, other_f in all_peers(here)
        ]

    def finish():
        arrives(one())
        total = squares[0]
        for i in range(1, n_d * n_f):
            total = total + squares[i]
        leaves(one())
        return total

    return (lambda: starts(one())), finish


def store_rows(ref, first, lane, value):
    size = ref.shape[2]
    done = 0
    while done < value.shape[0]:
        shard, offset = divmod(first + done, size)
        count = min(size - offset, value.shape[0] - done)
        ref[shard // 2, shard % 2, offset : offset + count, lane : lane + value.shape[1]] = value[
            done : done + count
        ]
        done = done + count


def store_folded(ref, first, value):
    size = ref.shape[2]
    width = value.shape[1]
    done = 0
    while done < value.shape[0]:
        block, offset = divmod(first + done, size)
        shard, side = divmod(block, 2)
        count = min(size - offset, value.shape[0] - done)
        ref[
            shard // 2, shard % 2, offset : offset + count, side * width : (side + 1) * width
        ] = value[done : done + count]
        done = done + count


def tile_place(ref, tile):
    across = ref.shape[3] // 128
    shard, lane = divmod(tile, across)
    return (shard // 2, shard % 2, slice(None), slice(128 * lane, 128 * lane + 128))


def put_tiles(ref, first, value):
    across = value.shape[1] // 128
    for i in range(value.shape[0] // 8):
        for j in range(across):
            ref[tile_place(ref, first + i * across + j)] = value[
                8 * i : 8 * i + 8, 128 * j : 128 * j + 128
            ]


def take_tiles(ref, first, rows, lanes):
    across = lanes // 128
    return jnp.concatenate(
        [
            jnp.concatenate(
                [ref[tile_place(ref, first + i * across + j)] for j in range(across)], 1
            )
            for i in range(rows // 8)
        ],
        0,
    )


def total_scratch(rows, lanes, dtype):
    n_d, n_z = lax.axis_size("dp"), lax.axis_size("fsdp") // 2
    part = lanes // n_d
    dma = pltpu.SemaphoreType.DMA
    count = 2 * n_d + 2 * n_z + 1
    return [
        pltpu.VMEM((n_z, 2, rows, lanes), dtype),
        pltpu.VMEM((n_z, rows, lanes), dtype),
        pltpu.VMEM((n_z, rows, lanes), dtype),
        pltpu.VMEM((n_d, n_z, rows, part), dtype),
        pltpu.VMEM((n_z, rows, part), dtype),
        pltpu.VMEM((n_z, rows, part), dtype),
        dma((count,)),
        dma((count,)),
    ]


def fold_rows(value):
    half = value.shape[0] // 2
    return jnp.concatenate([value[:half], value[half:]], 1)


def shard_gather(here, wide_land, down_land, sems):
    n_d, n_z, d, z, c = here
    lanes_w = lane_piece(d, n_d, wide_land.shape[3])
    lanes_d = lane_piece(d, n_d, down_land.shape[3])

    def parts(source):
        return [
            wide_land.at[source, c, :, lanes_w],
            down_land.at[source, c, :, lanes_d],
        ]

    def wholes(source):
        return [wide_land.at[source, c], down_land.at[source, c]]

    return plan_gather(here, parts, wholes, sems)


def place_shards(here, wide, down, wide_land, down_land):
    z, c = here[3], here[4]
    wide_land[pl.ds(z, 1), pl.ds(c, 1)] = wide.astype(bf16)[None, None]
    down_land[pl.ds(z, 1), pl.ds(c, 1)] = fold_rows(down).astype(bf16)[None, None]


def land_out(wide_land, down_land, wide_out, down_out):
    n_z = wide_land.shape[0]
    lanes = down_out.shape[1]
    rows_w, rows_d = wide_land.shape[2], down_land.shape[2]
    for i in range(n_z):
        for j in range(2):
            shard = 2 * i + j
            wide_out[shard * rows_w : (shard + 1) * rows_w, :] = wide_land[i, j]
            first = 2 * shard * rows_d
            down_out[first : first + rows_d, :] = down_land[i, j, :, :lanes]
            down_out[first + rows_d : first + 2 * rows_d, :] = down_land[i, j, :, lanes:]


def land_scratch(wide_shape, down_shape):
    n_z = lax.axis_size("fsdp") // 2
    return [
        pltpu.VMEM((n_z, 2) + wide_shape, bf16),
        pltpu.VMEM((n_z, 2, down_shape[0] // 2, 2 * down_shape[1]), bf16),
    ] + gather_sems(2)


def land_gather(here, land, sems):
    n_d, c = here[0], here[4]
    lanes = lane_piece(here[2], n_d, land.shape[3])
    return plan_gather(
        here,
        lambda source: [land.at[source, c, :, lanes]],
        lambda source: [land.at[source, c]],
        sems,
    )


def unfold_land(land, out, which):
    n_z, _, rows, lanes = land.shape
    width = lanes // 2
    for block in range(n_z * 4):
        shard, side = divmod(block, 2)
        done = 0
        while done < rows:
            tap, offset = divmod(block * rows + done, width)
            count = min(width - offset, rows - done)
            first = swap_tap(tap) * width + offset
            out[which, first : first + count, :] = land[
                shard // 2, shard % 2, done : done + count, side * width : (side + 1) * width
            ]
            done = done + count


def fore_kernel(
    run,
    groups,
    len_ref,
    time_ref,
    lat_ref,
    noi_ref,
    stem_ref,
    conv_own,
    wide_own,
    time_own,
    vec_ref,
    clap_ref,
    zero_any,
    act_one_any,
    inner_any,
    act_two_any,
    one_any,
    normed_any,
    qkv_any,
    colsT_ref,
    noiT_ref,
    stat_ref,
    film_ref,
    conv_any,
    time_any,
    wide_any,
    buf,
    cols,
    tall,
    first_land,
    second_land,
    zero_ref,
    act_one_ref,
    inner_ref,
    act_two_ref,
    one_ref,
    normed_ref,
    qkv_ref,
    conv_ref,
    time_land,
    wide_land,
    out_sems,
    *sems,
):
    rows_n, channels = zero_ref.shape
    latent_ch = lat_ref.shape[0] * run // rows_n
    embed = time_own.shape[2]
    count = rows_n // CHUNK
    here = places()
    n_d, n_z, d, z, c = here
    greet(*here)
    first_plan = land_gather(here, first_land, sems[0:6])
    second_plan = land_gather(here, second_land, sems[6:12])
    wide_plan = land_gather(here, wide_land, sems[12:18])
    t_lanes = lane_piece(d, n_d, embed)
    time_plan = plan_gather(
        here,
        lambda source: [time_land.at[:, source, c, :, t_lanes]],
        lambda source: [time_land.at[:, source, c]],
        sems[18:24],
    )
    own = (pl.ds(z, 1), pl.ds(c, 1))
    first_land[own] = fold_rows(conv_own[0]).astype(bf16)[None, None]
    second_land[own] = fold_rows(conv_own[1]).astype(bf16)[None, None]
    wide_land[own] = wide_own[:, 0 : wide_land.shape[3]].astype(bf16)[None, None]
    time_land[:, pl.ds(z, 1), pl.ds(c, 1)] = time_own[...].astype(bf16)[:, None, None]
    outs = []

    def save(src, dst):
        copy = pltpu.make_async_copy(src, dst, out_sems.at[len(outs)])
        outs.append(copy)
        copy.start()

    met(*here)
    first_plan[0]()
    time_plan[0]()
    live = len_ref[0]
    counted = (live * (rows_n // run) * (channels // groups)).astype(f32)
    segs = offsets(channels, embed, FF, latent_ch)

    def seg(index):
        start, length = segs[index]
        return vec_ref[start : start + length].reshape(1, length)

    def by_bins(value):
        return jnp.concatenate(
            [value[i * latent_ch : (i + 1) * latent_ch] for i in range(rows_n // run)], 1
        )

    noise = noi_ref[...].astype(f32)
    noiT_ref[...] = by_bins(noise)
    phase = (jnp.zeros((1, run), f32) + time_ref[0].astype(f32)) / 1000.0
    kept = jnp.cos((phase + 0.008) / 1.008 * (math.pi / 2)) ** 2
    mixed = jnp.sqrt(kept) * lat_ref[...].astype(f32) + jnp.sqrt(1.0 - kept) * noise
    pos = lax.broadcasted_iota(jnp.int32, mixed.shape, 1)
    noisy = by_bins(jnp.where(pos < live, mixed, 0.0).astype(bf16).astype(f32))
    taps = 9 * latent_ch
    for a in range(3):
        for b in range(3):
            tap = 3 * a + b
            tall[tap * latent_ch : (tap + 1) * latent_ch] = tap_shift(noisy, a, b, run)
    tall[taps:] = jnp.zeros((tall.shape[0] - taps, rows_n), f32)
    colsT_ref[...] = tall[0:taps].astype(bf16)
    cols[...] = tall[...].T.astype(bf16)
    stem_low = jnp.concatenate(
        [swap_taps(stem_ref[...]), jnp.zeros((cols.shape[1] - taps, channels), f32)], 0
    ).astype(bf16)
    stem_bias = seg(12)

    def stem_part(i, carry):
        rows = pl.ds(pl.multiple_of(i * CHUNK, CHUNK), CHUNK)
        zero_ref[rows, :] = mm(cols[rows, :], stem_low) + stem_bias
        return carry

    loop(count, stem_part, 0)
    save(zero_ref, zero_any)
    first_plan[1]()

    clear_ends(buf, rows_n, run)

    def convolve(which, start):
        total = None
        for a in range(3):
            part = mm(
                buf[pl.ds(start + run * a, CHUNK), :],
                conv_ref[which, 3 * a * channels : 3 * (a + 1) * channels, :],
            )
            total = part if total is None else total + part
        return total

    def activate(read, center, scale, gain, shift, act_ref, hooks):
        factor = scale * gain

        def part(i, carry):
            start = pl.multiple_of(i * CHUNK, CHUNK)
            value = jax.nn.silu((read(start) - center) * factor + shift)
            value = jnp.where(live_rows(value.shape, live, run), value, 0.0)
            low = value.astype(bf16)
            act_ref[pl.ds(start, CHUNK), :] = low
            put_shifted(buf, start, low.astype(f32), run)
            return carry

        loop(count, part, 0, hooks)

    def read_zero(start):
        return zero_ref[pl.ds(start, CHUNK), :]

    center, scale = group_stats(read_zero, rows_n, live, run, channels, groups, counted)
    stat_ref[0:1] = center
    stat_ref[1:2] = scale
    second_plan[0]()
    wide_plan[0]()
    activate(
        read_zero, center, scale, seg(0), seg(1), act_one_ref, ((1, time_plan[1]),)
    )
    first_plan[2]()
    first_plan[3]()
    unfold_land(first_land, conv_ref, 0)
    save(act_one_ref, act_one_any)
    save(conv_ref.at[0], conv_any.at[0])

    bias_one = seg(2)

    def conv_part(i, carry):
        start = pl.multiple_of(i * CHUNK, CHUNK)
        inner_ref[pl.ds(start, CHUNK), :] = convolve(0, start) + bias_one
        return carry

    loop(count, conv_part, 0, ((1, second_plan[1]),))
    wide_plan[1]()
    save(inner_ref, inner_any)

    def read_inner(start):
        return inner_ref[pl.ds(start, CHUNK), :]

    pixels = (live * (rows_n // run)).astype(f32)
    middle, spread = channel_stats(
        read_inner, rows_n, live, run, channels, lambda row: row / pixels
    )
    time_plan[2]()
    time_plan[3]()
    def time_matrix(index):
        return time_land[index].reshape(embed, embed)

    wave = time_wave(time_ref, embed)
    pre_time = vec_mat(wave, time_matrix(0)) + seg(13)
    embedding = vec_mat(jax.nn.silu(pre_time), time_matrix(1)) + seg(14) + clap_ref[...]
    film = vec_mat(jax.nn.silu(embedding), time_matrix(2)) + seg(15)
    film_ref[0:1] = film
    film_ref[1:2] = pre_time
    film_ref[2:3] = embedding
    film_ref[3:8] = jnp.zeros((5, embed), f32)
    lift = 1.0 + film[:, :channels]
    move = film[:, channels:]


    def read_moved(start):
        return inner_ref[pl.ds(start, CHUNK), :] * lift + move

    size = channels // groups
    middle = middle * lift + move
    center = group_total(middle, groups) / size
    gap = middle - center
    spread = group_total(lift * lift * spread + gap * gap, groups) / size
    scale = lax.rsqrt(spread + norm_floor)
    stat_ref[2:3] = center
    stat_ref[3:4] = scale
    stat_ref[4:8] = jnp.zeros((4, channels), f32)
    second_plan[2]()
    wide_plan[2]()
    activate(read_moved, center, scale, seg(3), seg(4), act_two_ref, ())
    second_plan[3]()
    wide_plan[3]()
    unfold_land(second_land, conv_ref, 1)
    save(act_two_ref, act_two_any)
    save(conv_ref.at[1], conv_any.at[1])
    save(time_land, time_any)
    save(wide_land, wide_any)

    bias_two = seg(5)
    gain, shift = seg(6), seg(7)
    wide_full = wide_land[...].reshape(channels, wide_land.shape[3])
    wqkv_t = wide_full[:, 0 : 3 * channels].T

    def last_part(i, carry):
        start = pl.multiple_of(i * CHUNK, CHUNK)
        rows = pl.ds(start, CHUNK)
        stream = zero_ref[rows, :] + convolve(1, start) + bias_two
        one_ref[rows, :] = stream
        gap = stream - row_mean(stream)
        normed = gap * lax.rsqrt(row_mean(gap * gap) + norm_floor) * gain + shift
        low = normed.astype(bf16)
        normed_ref[rows, :] = low
        qkv_ref[:, rows] = mm_nt(wqkv_t, low).astype(bf16)
        return carry

    for i in range(count):
        last_part(i, 0)
        rows = pl.ds(i * CHUNK, CHUNK)
        save(one_ref.at[rows], one_any.at[rows])
        save(normed_ref.at[rows], normed_any.at[rows])
        save(qkv_ref.at[:, rows], qkv_any.at[:, rows])
    for copy in outs:
        copy.wait()


def query_rows(query, factor, extra):
    dim, length = query.shape
    scaled = query.astype(f32) * (factor * LOG2E)
    high = scaled.astype(bf16).astype(f32)
    index = lax.broadcasted_iota(jnp.int32, (128 - 2 * dim, length), 0)
    tile = jnp.where(index == 0, 1.0, 0.0)
    for place, row in enumerate(extra):
        tile = jnp.where(index == place + 1, jnp.broadcast_to(row, tile.shape), tile)
    return jnp.concatenate([high, scaled - high, tile], 0)


def key_rows(keys, live, run):
    dim, length = keys.shape
    shape = (128 - 2 * dim, length)
    index = lax.broadcasted_iota(jnp.int32, shape, 0)
    pos = lax.broadcasted_iota(jnp.int32, shape, 1)
    mask = jnp.where(lax.rem(pos, run) < live, 0.0, masked_score)
    tile = jnp.where(index == 0, mask, jnp.where(index < 4, 1.0, 0.0))
    both = keys.astype(f32)
    return jnp.concatenate([both, both, tile], 0)


def three_parts(row):
    top = row.astype(bf16).astype(f32)
    rest = row - top
    mid = rest.astype(bf16).astype(f32)
    return top, mid, rest - mid


def attend_kernel(
    run,
    key_block,
    len_ref,
    q_ref,
    k_ref,
    v_ref,
    up_ref,
    down_ref,
    o_ref,
    lse_ref,
    up_out,
    down_out,
    kaug,
    qaug,
    vaug,
    up_land,
    down_land,
    *sems,
):
    dim, length = q_ref.shape
    here = places()
    steps = shard_gather(here, up_land, down_land, sems)
    head = pl.program_id(0)

    @pl.when(head == 0)
    def _():
        greet(*here)
        place_shards(here, up_ref[:, -up_land.shape[3] :], down_ref[...], up_land, down_land)

    @pl.when(head == 1)
    def _():
        met(*here)
        steps[0]()

    pl.when(head == 3)(steps[1])
    pl.when(head == 5)(steps[2])

    @pl.when(head == 7)
    def _():
        steps[3]()
        land_out(up_land, down_land, up_out, down_out)

    live = len_ref[0]
    qaug[...] = query_rows(q_ref[...], dim ** (-0.5), ()).astype(bf16)
    kaug[...] = key_rows(k_ref[...], live, run).T.astype(bf16)
    vaug[0:dim] = v_ref[...]
    index = lax.broadcasted_iota(jnp.int32, (16, length), 0)
    vaug[dim : dim + 16] = jnp.where(index == 0, 1.0, 0.0).astype(bf16)
    top = None
    for i in range(length // key_block):
        keys = slice(i * key_block, (i + 1) * key_block)
        scores = mm(kaug[keys, :], qaug[...])
        block_top = jnp.max(scores, axis=0, keepdims=True)
        new_top = block_top if top is None else jnp.maximum(top, block_top)
        weights = jnp.exp2(scores - new_top).astype(bf16)
        part = mm(vaug[:, keys], weights)
        total = part if top is None else total * jnp.exp2(top - new_top) + part
        top = new_top
    summed = total[dim : dim + 1]
    o_ref[...] = total[0:dim] / summed
    lse_ref[0] = top + jnp.log2(summed)


def attend_back_kernel(
    run,
    block,
    len_ref,
    q_ref,
    k_ref,
    v_ref,
    lse_ref,
    o_ref,
    do_ref,
    early_ref,
    wide_ref,
    down_ref,
    dq_ref,
    dk_ref,
    dv_ref,
    early_out,
    wide_out,
    down_out,
    kaug,
    qaug,
    vaug,
    daug,
    early_land,
    pair,
    other,
    from_dp,
    summed,
    from_z,
    send,
    recv,
    wide_land,
    down_land,
    *sems,
):
    dim, length = q_ref.shape
    here = places()
    head = pl.program_id(0)
    gathers = shard_gather(here, wide_land, down_land, sems)
    totals = plan_total(
        here, early_ref, early_land, pair, other, from_dp, summed, from_z, (send, recv)
    )

    @pl.when(head == 0)
    def _():
        greet(*here)
        place_shards(here, wide_ref[...], down_ref[...], wide_land, down_land)

    @pl.when(head == 1)
    def _():
        met(*here)
        totals[0]()

    for place in range(2, 5):

        @pl.when(head == place)
        def _(place=place):
            totals[place - 1]()
            gathers[place - 2]()

    @pl.when(head == 5)
    def _():
        totals[4]()
        gathers[3]()
        land_out(wide_land, down_land, wide_out, down_out)

    pl.when(head == 7)(totals[5])

    factor = dim ** (-0.5)
    qaug[...] = query_rows(q_ref[...], factor, three_parts(-lse_ref[0])).T.astype(bf16)
    kaug[...] = key_rows(k_ref[...], len_ref[0], run).astype(bf16)
    index = lax.broadcasted_iota(jnp.int32, (128 - dim, length), 0)
    tile = jnp.where(index < 3, -1.0, 0.0)
    vaug[...] = jnp.concatenate([v_ref[...].astype(f32), tile], 0).astype(bf16)
    back = do_ref[...].astype(f32)
    tile = jnp.zeros((128 - dim, length), f32)
    for place, row in enumerate(three_parts(col_sum(back * o_ref[...]))):
        tile = jnp.where(index == place, jnp.broadcast_to(row, tile.shape), tile)
    daug[...] = jnp.concatenate([back, tile], 0).T.astype(bf16)

    dk = dv = None
    for i in range(length // block):
        rows = slice(i * block, (i + 1) * block)
        weights = jnp.exp2(mm(qaug[rows, :], kaug[...]))
        raw = (weights * mm(daug[rows, :], vaug[...])).astype(bf16)
        dv_part = mm(do_ref[:, rows], weights.astype(bf16))
        dk_part = mm(q_ref[:, rows], raw)
        dv = dv_part if dv is None else dv + dv_part
        dk = dk_part if dk is None else dk + dk_part
        dq_ref[:, rows] = (mm_nt(k_ref[...], raw) * factor).astype(bf16)
    dk_ref[...] = (dk * factor).astype(bf16)
    dv_ref[...] = dv.astype(bf16)

    @pl.when(head == HEADS - 1)
    def _():
        totals[6]()
        early_out[...] = early_land[...]


def middle_kernel(
    run,
    len_ref,
    mixed_ref,
    one_ref,
    first_ref,
    up_ref,
    down_ref,
    vec_ref,
    headw_ref,
    noiT_ref,
    two_grad_ref,
    do_ref,
    early_ref,
    small_ref,
    hidden,
    slope,
    xhat,
    spread,
    three,
    prod,
    gcols,
    normed_t,
    three_t,
    gpre,
    glow,
    head_ref,
):
    rows_n, channels = one_ref.shape
    units = down_ref.shape[0]
    latent_ch = noiT_ref.shape[0]
    count = rows_n // CHUNK
    live = len_ref[0]
    segs = offsets(channels, EMB, units, latent_ch)

    def seg(index):
        start, length = segs[index]
        return vec_ref[start : start + length].reshape(1, length)

    w_out = first_ref[:, 3 * channels :]
    for tap in range(9):
        first = swap_tap(tap) * channels
        prod[tap * latent_ch : (tap + 1) * latent_ch, 0:channels] = headw_ref[
            :, first : first + channels
        ]
    prod[9 * latent_ch :, 0:channels] = jnp.zeros((prod.shape[0] - 9 * latent_ch, channels), f32)
    head_ref[...] = prod[:, 0:channels].astype(bf16)
    index = lax.broadcasted_iota(jnp.int32, (latent_ch, latent_ch), 0)
    same = index == lax.broadcasted_iota(jnp.int32, (latent_ch, latent_ch), 1)
    head_bias = jnp.sum(jnp.where(same, seg(17), 0.0), axis=1, keepdims=True)
    proj_bias, gain, shift, up_bias, down_bias = seg(8), seg(9), seg(10), seg(16), seg(11)

    def fore(i, carry):
        start = pl.multiple_of(i * CHUNK, CHUNK)
        rows = pl.ds(start, CHUNK)
        mixed = mixed_ref[:, rows].T.astype(bf16)
        stream = one_ref[rows, :] + mm(mixed, w_out) + proj_bias
        gap = stream - row_mean(stream)
        scale = lax.rsqrt(row_mean(gap * gap) + norm_floor)
        hat = gap * scale
        xhat[rows, :] = hat
        spread[rows, :] = jnp.broadcast_to(scale, (CHUNK, spread.shape[1]))
        normed = (hat * gain + shift).astype(bf16)
        normed_t[:, rows] = normed.T
        pre = mm(normed, up_ref[...]) + up_bias
        phi = 0.5 * (1.0 + lax.erf(pre * (0.5**0.5)))
        slope[rows, :] = phi + pre * jnp.exp(-0.5 * pre * pre) * (0.5 / math.pi) ** 0.5
        low = (pre * phi).astype(bf16)
        hidden[rows, :] = low
        stream = stream + mm(low, down_ref[...]) + down_bias
        stream = jnp.where(live_rows(stream.shape, live, run), stream, 0.0).astype(bf16)
        three[rows, :] = stream
        prod[:, rows] = mm_nt(head_ref[...], stream)
        return carry

    loop(count, fore, 0)

    taps = 9 * latent_ch
    predicted = jnp.zeros((latent_ch, rows_n), f32) + head_bias
    for a in range(3):
        for b in range(3):
            tap = 3 * a + b
            predicted = predicted + tap_shift(
                prod[tap * latent_ch : (tap + 1) * latent_ch], a, b, run
            )
    pos = lax.broadcasted_iota(jnp.int32, predicted.shape, 1)
    errors = jnp.where(lax.rem(pos, run) < live, predicted - noiT_ref[...], 0.0)
    small_ref[...] = jnp.zeros(small_ref.shape, f32)
    tile = (latent_ch, 128)
    sums = jnp.broadcast_to(jnp.sum(errors, axis=1, keepdims=True), tile)
    same = lax.broadcasted_iota(jnp.int32, tile, 0) == lax.broadcasted_iota(jnp.int32, tile, 1)
    put_small(small_ref, 17, col_sum(jnp.where(same, sums, 0.0)))
    sums = jnp.broadcast_to(jnp.sum(errors * errors, axis=1, keepdims=True), tile)
    put_small(small_ref, 18, col_sum(sums))
    put_small(small_ref, 19, jnp.zeros((1, 128), f32) + (live * (rows_n // run)).astype(f32))
    errors = errors.astype(bf16).astype(f32)
    for a in range(3):
        for b in range(3):
            tap = 3 * a + b
            prod[tap * latent_ch : (tap + 1) * latent_ch] = tap_shift(
                errors, 2 - a, 2 - b, run
            )
    prod[taps:] = jnp.zeros((prod.shape[0] - taps, rows_n), f32)
    gcols[...] = prod[...].T.astype(bf16)
    ghead = mm(prod[0:taps].astype(bf16), three[...])

    def back(i, carry):
        g_down, g_up, g_gain, g_shift, g_proj = carry
        start = pl.multiple_of(i * CHUNK, CHUNK)
        rows = pl.ds(start, CHUNK)
        grad = mm(gcols[rows, :], head_ref[...])
        grad = jnp.where(live_rows(grad.shape, live, run), grad, 0.0)
        low = grad.astype(bf16)
        three_t[:, rows] = low.T
        pre = mm_nt(low, down_ref[...]) * slope[rows, :]
        pre_low = pre.astype(bf16)
        gpre[rows, :] = pre_low
        dnormed = mm_nt(pre_low, up_ref[...])
        hat = xhat[rows, :]
        dhat = dnormed * gain
        dstream = (dhat - row_mean(dhat) - hat * row_mean(dhat * hat)) * spread[rows, 0:1]
        two = grad + dstream
        two_grad_ref[rows, :] = two
        two_low = two.astype(bf16)
        glow[rows, :] = two_low
        do_ref[:, rows] = mm_nt(w_out, two_low).astype(bf16)
        return (
            g_down + col_sum(grad),
            g_up + col_sum(pre),
            g_gain + col_sum(dnormed * hat),
            g_shift + col_sum(dnormed),
            g_proj + col_sum(two),
        )

    blank = jnp.zeros((1, channels), f32)
    sums = loop(count, back, (blank, jnp.zeros((1, units), f32), blank, blank, blank))
    for index, value in zip((11, 16, 9, 10, 8), sums):
        put_small(small_ref, index, value)
    half = units // 2
    for part in range(units // channels):
        columns = slice(part * channels, (part + 1) * channels)
        first = (part * channels) % half
        lanes = slice((part * channels) // half * channels, (part * channels) // half * channels + channels)
        early_ref[first : first + channels, lanes] = mm(three_t[...], hidden[:, columns]).T.astype(
            bf16
        )
        first = half + (part // 2) * channels
        lanes = slice((part % 2) * channels, (part % 2 + 1) * channels)
        early_ref[first : first + channels, lanes] = mm(normed_t[...], gpre[:, columns]).astype(
            bf16
        )
    gproj = mm(mixed_ref[...].astype(bf16), glow[...]).astype(bf16)
    first = half + (units // channels // 2) * channels
    middle = channels // 2
    early_ref[first : first + middle, 0:channels] = gproj[:middle]
    early_ref[first : first + middle, channels:] = gproj[middle:]
    first = first + middle
    ghead = swap_taps(ghead).astype(bf16)
    middle = taps // 2
    early_ref[first : first + middle, 0:channels] = ghead[:middle]
    early_ref[first : first + middle, channels:] = ghead[middle:]
    early_ref[first + middle :, :] = jnp.zeros(
        (early_ref.shape[0] - first - middle, 2 * channels), bf16
    )


def hind_kernel(
    run,
    groups,
    len_ref,
    step_ref,
    dq_any,
    dk_any,
    dv_any,
    two_grad_any,
    normed_any,
    one_any,
    act_two_any,
    inner_any,
    act_one_any,
    zero_any,
    colsT_any,
    stat_ref,
    film_ref,
    conv_any,
    wide_any_w,
    time_any,
    vec_ref,
    mid_ref,
    early_any,
    wide_any,
    down_any,
    small_any,
    root_any,
    large_any,
    conv_out,
    tile_out,
    time_out,
    scalar_out,
    head_out,
    wide_out,
    wide_dir,
    down_out,
    down_dir,
    buf,
    field,
    other,
    act_t,
    small,
    everyone,
    tiles,
    tile_o,
    tile_p,
    tile_d,
    tile_f,
    tile_z,
    tile_s,
    tile_r,
    tile_as,
    tile_ar,
    squares,
    product,
    first_g,
    first_o,
    first_p,
    first_d,
    first_f,
    first_z,
    first_t,
    first_s,
    first_r,
    second_g,
    second_o,
    second_p,
    second_d,
    second_f,
    second_z,
    second_t,
    second_s,
    second_r,
    qkv_g,
    qkv_o,
    qkv_p,
    qkv_d,
    qkv_f,
    qkv_z,
    qkv_t,
    qkv_s,
    qkv_r,
    spread_s,
    spread_r,
    clip_s,
    clip_r,
    square_s,
    square_r,
    qkv_out,
    early,
    wide_full,
    down_full,
    roots_small,
    root_wide,
    root_large,
    root_rows,
    local_sems,
    dq_ref,
    dk_ref,
    dv_ref,
    normed_ref,
    wide_ref,
    two_grad_ref,
    one_ref,
    act_two_ref,
    inner_ref,
    conv_ref,
    time_ref,
    act_one_ref,
    zero_ref,
    colsT_ref,
    load_sems,
):
    rows_n, channels = one_ref.shape
    embed = time_ref.shape[2]
    latent_ch = colsT_ref.shape[0] // 9
    count = rows_n // CHUNK
    live = len_ref[0]
    counted = (live * (rows_n // run) * (channels // groups)).astype(f32)
    segs = offsets(channels, embed, FF, latent_ch)
    blank = jnp.zeros((1, channels), f32)
    small[...] = jnp.zeros(small.shape, f32)
    here = places()
    n_d, n_z, d, z, c = here
    conv_plans = (
        plan_owner(here, first_g, first_o, first_p, first_d, first_f, first_z, first_t, (first_s, first_r)),
        plan_owner(here, second_g, second_o, second_p, second_d, second_f, second_z, second_t, (second_s, second_r)),
    )
    qkv_plan = plan_owner(here, qkv_g, qkv_o, qkv_p, qkv_d, qkv_f, qkv_z, qkv_t, (qkv_s, qkv_r))
    spread_plan = plan_spread(here, qkv_out, (spread_s, spread_r))
    clip_plan = plan_clips(here, everyone, (clip_s, clip_r))
    tile_plan = plan_small(
        here,
        tiles,
        tile_out,
        tile_o,
        tile_p,
        tile_d,
        tile_f,
        tile_z,
        (tile_s, tile_r, tile_as, tile_ar),
    )
    square_plan = plan_scalar(here, squares, (square_s, square_r))
    own_rows = root_rows.shape[0]
    loads = [
        pltpu.make_async_copy(src, dst, local_sems.at[index])
        for index, (src, dst) in enumerate(
            (
                (early_any, early),
                (wide_any, wide_full),
                (down_any, down_full),
                (small_any, roots_small),
                (root_any, root_wide),
                (large_any.at[0], root_large),
                (large_any.at[1, pl.ds(lax.axis_index("fsdp") * own_rows, own_rows)], root_rows),
            )
        )
    ]
    first_loads = {
        id(ref): pltpu.make_async_copy(src, ref, load_sems.at[index])
        for index, (src, ref) in enumerate(
            (
                (dq_any, dq_ref),
                (dk_any, dk_ref),
                (dv_any, dv_ref),
                (normed_any, normed_ref),
                (wide_any_w, wide_ref),
                (two_grad_any, two_grad_ref),
                (one_any, one_ref),
                (act_two_any, act_two_ref),
                (inner_any, inner_ref),
                (conv_any, conv_ref),
                (time_any, time_ref),
                (act_one_any, act_one_ref),
                (zero_any, zero_ref),
                (colsT_any, colsT_ref),
            )
        )
    }
    greet_all(here)
    starts(first_loads.values())
    starts(loads)

    def ready(*refs):
        for ref in refs:
            first_loads[id(ref)].wait()

    ready(dq_ref, dk_ref, dv_ref, normed_ref)

    def seg(index):
        start, length = segs[index]
        return vec_ref[start : start + length].reshape(1, length)

    def put_vec(index, value):
        put_small(small, index, value)

    half = channels // 2
    store_rows(qkv_g, 0, 0, mm(dq_ref[...], normed_ref[...]).T.astype(bf16))
    store_rows(qkv_g, 0, channels, mm(dk_ref[...], normed_ref[...]).T.astype(bf16))
    values_grad = mm(dv_ref[...], normed_ref[...]).T.astype(bf16)
    store_rows(qkv_g, channels, 0, values_grad[:half])
    store_rows(qkv_g, channels, channels, values_grad[half:])
    met_all(here)
    qkv_plan[0]()

    ready(wide_ref, two_grad_ref, one_ref)
    gain_one = seg(6)
    clear_ends(buf, rows_n, run)

    def norm_part(i, carry):
        g_gain, g_shift, g_bias = carry
        start = pl.multiple_of(i * CHUNK, CHUNK)
        rows = pl.ds(start, CHUNK)
        dnormed_t = None
        for part, ref in enumerate((dq_ref, dk_ref, dv_ref)):
            term = mm(wide_ref[:, part * channels : (part + 1) * channels], ref[:, rows])
            dnormed_t = term if dnormed_t is None else dnormed_t + term
        dnormed = dnormed_t.T
        stream = one_ref[rows, :]
        gap = stream - row_mean(stream)
        scale = lax.rsqrt(row_mean(gap * gap) + norm_floor)
        hat = gap * scale
        dhat = dnormed * gain_one
        grad = two_grad_ref[rows, :] + scale * (
            dhat - row_mean(dhat) - hat * row_mean(dhat * hat)
        )
        field[rows, :] = grad
        put_shifted(buf, start, grad.astype(bf16).astype(f32), run)
        return (
            g_gain + col_sum(dnormed * hat),
            g_shift + col_sum(dnormed),
            g_bias + col_sum(grad),
        )

    sums = loop(count, norm_part, (blank, blank, blank), ((1, qkv_plan[1]),))
    for index, value in zip((6, 7, 5), sums):
        put_vec(index, value)

    def weight_grad(which, act_ref):
        act_t[...] = act_ref[...].T
        for a in range(3):
            full = buf[run * (2 - a) : run * (2 - a) + rows_n, :]
            for b in range(3):
                shifted = full[:, (2 - b) * channels : (3 - b) * channels]
                first = (3 * b + a) * channels
                store_folded(
                    (first_g, second_g)[which], first, mm(act_t[...], shifted).astype(bf16)
                )

    def input_grad(which, start):
        total = None
        for a in range(3):
            for b in range(3):
                first = (3 * (2 - a) + 2 - b) * channels
                part = mm_nt(
                    buf[
                        pl.ds(start + run * a, CHUNK),
                        b * channels : (b + 1) * channels,
                    ],
                    conv_ref[which, first : first + channels, :],
                )
                total = part if total is None else total + part
        return total

    def norm_back(which, read, center, scale, gain, shift, g_refs, hooks):
        def part(i, carry):
            g_gain, g_shift = carry
            start = pl.multiple_of(i * CHUNK, CHUNK)
            rows = pl.ds(start, CHUNK)
            hat = (read(start) - center) * scale
            slope = silu_slope(hat * gain + shift)
            grad = input_grad(which, start) * slope
            grad = jnp.where(live_rows(grad.shape, live, run), grad, 0.0)
            other[rows, :] = grad
            return (g_gain + col_sum(grad * hat), g_shift + col_sum(grad))

        g_gain, g_shift = loop(count, part, (blank, blank), hooks)
        put_vec(g_refs[0], g_gain)
        put_vec(g_refs[1], g_shift)
        mean_grad = group_total(g_shift * gain, groups) / counted
        mean_hat = group_total(g_gain * gain, groups) / counted

        def finish(start):
            hat = (read(start) - center) * scale
            grad = (other[pl.ds(start, CHUNK), :] * gain - mean_grad - hat * mean_hat) * scale
            return jnp.where(live_rows(grad.shape, live, run), grad, 0.0)

        return finish

    film = film_ref[0:1]
    lift = 1.0 + film[:, :channels]
    move = film[:, channels:]

    ready(act_two_ref)
    weight_grad(1, act_two_ref)
    conv_plans[1][0]()
    qkv_plan[2]()
    ready(inner_ref, conv_ref)
    finish = norm_back(
        1,
        lambda start: inner_ref[pl.ds(start, CHUNK), :] * lift + move,
        stat_ref[2:3],
        stat_ref[3:4],
        seg(3),
        seg(4),
        (3, 4),
        ((1, conv_plans[1][1]),),
    )

    qkv_plan[3]()

    def inner_part(i, carry):
        g_lift, g_move, g_bias = carry
        start = pl.multiple_of(i * CHUNK, CHUNK)
        moved = finish(start)
        grad = moved * lift
        put_shifted(buf, start, grad.astype(bf16).astype(f32), run)
        return (
            g_lift + col_sum(moved * inner_ref[pl.ds(start, CHUNK), :]),
            g_move + col_sum(moved),
            g_bias + col_sum(grad),
        )

    g_lift, g_move, g_bias = loop(count, inner_part, (blank, blank, blank))
    put_vec(2, g_bias)

    ready(act_one_ref)
    weight_grad(0, act_one_ref)
    conv_plans[0][0]()
    ready(time_ref, zero_ref, colsT_ref)
    pre_time = film_ref[1:2]
    embedding = film_ref[2:3]
    g_film = jnp.concatenate([g_lift, g_move], 1)
    g_embed = vec_mat(g_film, time_ref[2], True) * silu_slope(embedding)
    g_time = vec_mat(g_embed, time_ref[1], True) * silu_slope(pre_time)
    put_vec(13, g_time)
    put_vec(14, g_embed)
    put_vec(15, g_film)
    factors = jnp.concatenate(
        [
            time_wave(step_ref, embed),
            jax.nn.silu(pre_time),
            jax.nn.silu(embedding),
            g_time,
            g_embed,
            g_film,
            jnp.zeros((2, embed), f32),
        ],
        0,
    )
    factors = jnp.concatenate([factors[:, : embed // 2], factors[:, embed // 2 :]], 0)
    everyone[pl.ds(d, 1), pl.ds(z, 1), pl.ds(c, 1)] = factors.astype(bf16)[None, None, None]
    clip_plan[0]()
    conv_plans[1][2]()
    qkv_plan[4]()
    qkv_out[pl.ds(z, 1), pl.ds(c, 1)] = qkv_t[...][None, None]
    spread_plan[0]()
    finish_zero = norm_back(
        0,
        lambda start: zero_ref[pl.ds(start, CHUNK), :],
        stat_ref[0:1],
        stat_ref[1:2],
        seg(0),
        seg(1),
        (0, 1),
        ((0, conv_plans[0][1]), (1, clip_plan[1])),
    )
    conv_plans[1][3]()
    spread_plan[1]()

    def zero_part(i, carry):
        g_stem, g_bias = carry
        start = pl.multiple_of(i * CHUNK, CHUNK)
        rows = pl.ds(start, CHUNK)
        grad = field[rows, :] + finish_zero(start)
        return (g_stem + mm(colsT_ref[:, rows], grad.astype(bf16)), g_bias + col_sum(grad))

    taps = colsT_ref.shape[0]
    g_stem, g_bias = loop(count, zero_part, (jnp.zeros((taps, channels), f32), blank))
    put_vec(12, g_bias)
    used = taps // 8 * (channels // 128)
    put_tiles(tiles, 0, swap_taps(g_stem))
    put_tiles(tiles, used, small[...] + mid_ref[...])
    used = used + 2 * (small.shape[1] // 128)
    for i in range(used, n_z * 2 * (tiles.shape[3] // 128)):
        tiles[tile_place(tiles, i)] = jnp.zeros((8, 128), f32)
    tile_plan[0]()
    clip_plan[2]()
    conv_plans[0][2]()
    tile_plan[1]()
    conv_plans[1][4]()
    mine = lane_piece(d, n_d, 2 * channels)
    rows_c = second_t.shape[0]

    def squared(value):
        return jnp.sum(value * value)

    def unfold(which, ref):
        value = ref[...].astype(f32)
        conv_out[which, 0:rows_c] = value[:, 0:channels]
        conv_out[which, rows_c:] = value[:, channels:]

    unfold(1, second_t)
    square = squared(second_t[:, mine].astype(f32))

    for copy in loads:
        copy.wait()
    width = 2 * channels
    early_rows = early.shape[0] * 2 * early.shape[2]
    sums = early[...].reshape(early_rows, width)
    units = down_full.shape[0]
    half = units // 2
    shared = squared(sums.astype(f32))

    def choose(rows, order):
        own = lax.broadcasted_iota(jnp.int32, (rows, order), 0) + (2 * z + c) * rows
        return jnp.where(
            own == lax.broadcasted_iota(jnp.int32, (rows, order), 1), 1.0, 0.0
        ).astype(bf16)

    pick = choose(wide_out.shape[0], channels)

    def apply(left, value, right_root):
        return mm(mm(left, value).astype(bf16), right_root.astype(bf16))

    def side_by_side(first, rows):
        return jnp.concatenate([sums[first : first + rows], sums[first + rows : first + 2 * rows]], 1)

    def stacked(first, rows):
        block = sums[first : first + rows]
        return jnp.concatenate([block[:, :channels], block[:, channels:]], 0)

    first = half + 2 * channels
    head_first = first + channels // 2
    head_out[...] = stacked(head_first, taps // 2).astype(f32)
    lefts = [mm(pick, roots_small[i].astype(bf16)).astype(bf16) for i in range(3)]
    q_end, o_end = 3 * channels, 4 * channels
    momentum = {}
    later = {}
    for index, (grad, right_root, start, end) in enumerate(
        (
            (None, root_wide, 0, q_end),
            (stacked(first, channels // 2), roots_small.at[3], q_end, o_end),
            (side_by_side(half, channels), root_large, o_end, o_end + units),
        )
    ):
        wide_dir[:, start:end] = 0.9 * apply(
            lefts[index], wide_full[:, start:end], right_root[...]
        )
        if grad is not None:
            wide_out[:, start:end] = mm(pick, grad)
            later[start, end] = apply(lefts[index], grad, right_root[...])
    grad = stacked(0, half)
    rows = root_rows[...].astype(bf16)
    down_out[...] = mm(choose(down_out.shape[0], units), grad)
    later_down = apply(rows, grad, roots_small[4])
    down_dir[...] = 0.9 * apply(rows, down_full[...], roots_small[4])

    tile_plan[2]()
    spread_plan[2]()
    qkv_sum = qkv_out[...].reshape(channels + channels // 2, width)
    shared = shared + squared(qkv_sum.astype(f32))
    tail = qkv_sum[channels:]
    grad = jnp.concatenate(
        [qkv_sum[:channels], jnp.concatenate([tail[:, :channels], tail[:, channels:]], 0)], 1
    )
    wide_out[:, 0:q_end] = mm(pick, grad)
    later[0, q_end] = apply(lefts[0], grad, root_wide[...])
    clip_plan[3]()
    clips = 2 * n_d * n_z
    depth = time_out.shape[1]
    first = (2 * z + c) * depth
    block = pl.ds(pl.multiple_of(lax.rem(first, embed // 2) // 128 * 128, 128), 128)
    offset = pl.multiple_of(lax.rem(first, 128), 8)
    upper = first >= embed // 2
    time_square = jnp.zeros((), f32)
    for i in range(3):
        sides = [
            everyone[:, :, :, :, block].astype(f32).reshape(clips, 16, 128)[:, part + i]
            for part in (0, 8)
        ]
        left = jnp.where(upper, sides[1], sides[0])
        full = everyone[...].astype(f32).reshape(clips, 16, embed // 2)
        right = jnp.concatenate([full[:, i + 3], full[:, i + 11]], 1)
        product[...] = mm(left.T.astype(bf16), right.astype(bf16))
        value = product[pl.ds(offset, depth), :]
        time_out[i] = value
        time_square = time_square + squared(value)
    square = square + time_square / n_d
    conv_plans[0][3]()
    square = square + squared(first_t[:, mine].astype(f32))
    tile_plan[3]()
    own = tile_out[pl.ds(z, 1), pl.ds(c, 1), :, mine][0, 0]
    row = lax.broadcasted_iota(jnp.int32, own.shape, 0)
    tile_number = (2 * z + c) * n_d + d
    second = tile_number - taps // 8 * (channels // 128) >= width // 128
    square = square + squared(
        jnp.where(jnp.logical_and(second, row >= 13 - 8), 0.0, own)
    )
    lane = lax.broadcasted_iota(jnp.int32, (1, 1, 128), 2)
    loss_live = mid_ref[13:15, 0:1]
    message = jnp.where(
        lane == 0, square, jnp.where(lane == 1, loss_live[0:1][None], loss_live[1:2][None])
    )
    squares[pl.ds(d * 2 * n_z + 2 * z + c, 1)] = message
    square_plan[0]()
    conv_plans[0][4]()
    unfold(0, first_t)
    total = square_plan[1]()
    unit = 2.0 / (latent_ch * total[:, 2:3])
    norm = unit * jnp.sqrt(total[:, 0:1] + shared)
    factor = jnp.minimum(1.0, clip_limit / norm) * unit
    row = lax.broadcasted_iota(jnp.int32, scalar_out.shape, 0)
    loss = total[:, 1:2] * (0.5 * unit)
    scalar_out[...] = jnp.where(row == 0, loss, jnp.where(row == 1, norm, factor))
    factor = factor[0:1, 0:1]
    tile_plan[4]()
    for (start, end), value in later.items():
        wide_dir[:, start:end] += factor * value
    down_dir[...] += factor * later_down


def sized(shape, dtype=f32):
    return jax.ShapeDtypeStruct(shape, dtype)


VM = pl.BlockSpec(memory_space=pltpu.VMEM)
SM = pl.BlockSpec(memory_space=pltpu.SMEM)
ANY = pl.BlockSpec(memory_space=pl.ANY)


def params(mib):
    return pltpu.CompilerParams(vmem_limit_bytes=mib * 2**20)


def remote_params(number, mib):
    return pltpu.CompilerParams(
        collective_id=number, has_side_effects=True, vmem_limit_bytes=mib * 2**20
    )


def run_fore(run, length, step, lat, noi, stem_w, conv_w, wide_w, time_w, vec, clap):
    channels = stem_w.shape[1]
    latent_ch = stem_w.shape[0] // 9
    rows_n = lat.shape[1] * (lat.shape[0] // latent_ch)
    embed = time_w.shape[2]
    n_z = lax.axis_size("fsdp") // 2
    field = (rows_n, channels)
    land = pltpu.VMEM((n_z, 2, conv_w.shape[1] // 2, 2 * channels), bf16)
    large = [
        sized(field),
        sized(field, bf16),
        sized(field),
        sized(field, bf16),
        sized(field),
        sized(field, bf16),
        sized((3 * channels, rows_n), bf16),
    ]
    weights = [
        sized((2, 9 * channels, channels), bf16),
        sized((3, n_z, 2) + time_w.shape[1:], bf16),
        sized((n_z, 2, wide_w.shape[0], 4 * channels), bf16),
    ]
    outs = pl.pallas_call(
        functools.partial(fore_kernel, run, GROUPS),
        in_specs=[SM, SM] + [VM] * 8,
        out_specs=[ANY] * 7 + [VM] * 4 + [ANY] * 3,
        out_shape=large
        + [
            sized((9 * latent_ch, rows_n), bf16),
            sized((latent_ch, rows_n)),
            sized((8, channels)),
            sized((8, embed)),
        ]
        + weights,
        scratch_shapes=[
            pltpu.VMEM((rows_n + 2 * run, 3 * channels), bf16),
            pltpu.VMEM((rows_n, 128), bf16),
            pltpu.VMEM((128, rows_n), f32),
            land,
            land,
        ]
        + [pltpu.VMEM(item.shape, item.dtype) for item in large + weights]
        + [pltpu.SemaphoreType.DMA((8 + 3 * max(1, rows_n // CHUNK),))]
        + gather_sems(1) * 4,
        compiler_params=remote_params(1, 62),
        name="fore",
    )(length, step, lat, noi, stem_w, conv_w, wide_w, time_w, vec, clap)
    time_full = outs[12].reshape(3, -1, embed)
    first_full = outs[13].reshape(-1, 4 * channels)
    return (*outs[:12], time_full, first_full)


def run_attend(run, length, qkv_t, up, down, key_block=256):
    n_f = lax.axis_size("fsdp")
    triple, rows_n = qkv_t.shape
    channels = triple // 3
    dim = channels // HEADS
    return pl.pallas_call(
        functools.partial(attend_kernel, run, key_block),
        grid=(HEADS,),
        in_specs=[SM]
        + [pl.BlockSpec((dim, rows_n), lambda h, t=t: (t * HEADS + h, 0)) for t in range(3)]
        + [VM] * 2,
        out_specs=[
            pl.BlockSpec((dim, rows_n), lambda h: (h, 0)),
            pl.BlockSpec((1, 1, rows_n), lambda h: (h, 0, 0)),
            VM,
            VM,
        ],
        out_shape=[
            sized((channels, rows_n)),
            sized((HEADS, 1, rows_n)),
            sized((up.shape[0] * n_f, FF), bf16),
            sized((down.shape[0] * n_f, down.shape[1]), bf16),
        ],
        scratch_shapes=[
            pltpu.VMEM((rows_n, 128), bf16),
            pltpu.VMEM((128, rows_n), bf16),
            pltpu.VMEM((dim + 16, rows_n), bf16),
        ]
        + land_scratch((up.shape[0], FF), down.shape),
        compiler_params=remote_params(3, 62),
        name="attend",
    )(length, qkv_t, qkv_t, qkv_t, up, down)


def run_attend_back(
    run, length, qkv_t, lse, mixed_t, grad_t, early, wide, down, block=256
):
    n_f = lax.axis_size("fsdp")
    early = early.reshape(n_f // 2, 2, early.shape[0] // n_f, early.shape[1])
    triple, rows_n = qkv_t.shape
    channels = triple // 3
    dim = channels // HEADS
    whole = pl.BlockSpec((dim, rows_n), lambda h: (h, 0))
    return pl.pallas_call(
        functools.partial(attend_back_kernel, run, block),
        grid=(HEADS,),
        in_specs=[SM]
        + [pl.BlockSpec((dim, rows_n), lambda h, t=t: (t * HEADS + h, 0)) for t in range(3)]
        + [pl.BlockSpec((1, 1, rows_n), lambda h: (h, 0, 0)), whole, whole]
        + [VM] * 3,
        out_specs=[whole] * 3 + [VM] * 3,
        out_shape=[sized((channels, rows_n), bf16)] * 3
        + [
            sized(early.shape, bf16),
            sized((wide.shape[0] * n_f, wide.shape[1]), bf16),
            sized((down.shape[0] * n_f, down.shape[1]), bf16),
        ],
        scratch_shapes=[
            pltpu.VMEM((128, rows_n), bf16),
            pltpu.VMEM((rows_n, 128), bf16),
            pltpu.VMEM((128, rows_n), bf16),
            pltpu.VMEM((rows_n, 128), bf16),
        ]
        + total_scratch(early.shape[2], early.shape[3], bf16)
        + land_scratch(wide.shape, down.shape),
        compiler_params=remote_params(4, 62),
        name="attend_back",
    )(length, qkv_t, qkv_t, qkv_t, lse, mixed_t, grad_t, early, wide, down)


def run_middle(run, length, mixed_t, one, first, up, down, vec, head_w, noi_t):
    rows_n, channels = one.shape
    units = down.shape[0]
    latent_ch = noi_t.shape[0]
    return pl.pallas_call(
        functools.partial(middle_kernel, run),
        in_specs=[SM] + [VM] * 8,
        out_specs=[VM] * 4,
        out_shape=[
            sized((rows_n, channels)),
            sized((channels, rows_n), bf16),
            sized((units + channels, 2 * channels), bf16),
            sized((16, 2 * channels)),
        ],
        scratch_shapes=[
            pltpu.VMEM((rows_n, units), bf16),
            pltpu.VMEM((rows_n, units), f32),
            pltpu.VMEM((rows_n, channels), f32),
            pltpu.VMEM((rows_n, 128), f32),
            pltpu.VMEM((rows_n, channels), bf16),
            pltpu.VMEM((128, rows_n), f32),
            pltpu.VMEM((rows_n, 128), bf16),
            pltpu.VMEM((channels, rows_n), bf16),
            pltpu.VMEM((channels, rows_n), bf16),
            pltpu.VMEM((rows_n, units), bf16),
            pltpu.VMEM((rows_n, channels), bf16),
            pltpu.VMEM((128, channels), bf16),
        ],
        compiler_params=params(62),
        name="middle",
    )(length, mixed_t, one, first, up, down, vec, head_w, noi_t)


def run_hind(run, length, step, *arrays):
    one = arrays[5]
    rows_n, channels = one.shape
    embed = arrays[15].shape[2]
    n_d, n_f = lax.axis_size("dp"), lax.axis_size("fsdp")
    n_z = n_f // 2
    count = n_d * n_f
    rows_c = arrays[13].shape[1] // n_f
    rows_a = (channels + channels // 2) // n_f
    dma = pltpu.SemaphoreType.DMA
    return pl.pallas_call(
        functools.partial(hind_kernel, run, GROUPS),
        in_specs=[SM, SM]
        + [ANY] * 11
        + [VM] * 2
        + [ANY] * 3
        + [VM] * 2
        + [ANY] * 6,
        out_specs=[VM] * 9,
        out_shape=[
            sized((2, rows_c, channels)),
            sized((n_z, 2, 8, 2 * channels)),
            sized((3, embed // n_f, embed)),
            sized((8, 128)),
            sized((arrays[10].shape[0], channels)),
            sized((channels // n_f, 4 * channels + FF)),
            sized((channels // n_f, 4 * channels + FF)),
            sized((FF // n_f, channels)),
            sized((FF // n_f, channels)),
        ],
        scratch_shapes=[
            pltpu.VMEM((rows_n + 2 * run, 3 * channels), bf16),
            pltpu.VMEM((rows_n, channels), f32),
            pltpu.VMEM((rows_n, channels), f32),
            pltpu.VMEM((channels, rows_n), bf16),
            pltpu.VMEM((16, 2 * channels), f32),
            pltpu.VMEM((n_d, n_z, 2, 16, embed // 2), bf16),
        ]
        + small_scratch(2 * channels)
        + [
            pltpu.VMEM((count, 1, 128), f32),
            pltpu.VMEM((128, embed), f32),
        ]
        + owner_scratch(rows_c // 2, 2 * channels)
        + owner_scratch(rows_c // 2, 2 * channels)
        + owner_scratch(rows_a, 2 * channels)
        + [
            dma((n_z,)),
            dma((n_z,)),
            dma((n_d + n_z,)),
            dma((n_d + n_z,)),
            dma((count,)),
            dma((count,)),
            pltpu.VMEM((n_z, 2, rows_a, 2 * channels), bf16),
            pltpu.VMEM(arrays[-6].shape, bf16),
            pltpu.VMEM(arrays[-5].shape, bf16),
            pltpu.VMEM(arrays[-4].shape, bf16),
            pltpu.VMEM(arrays[-3].shape, f32),
            pltpu.VMEM(arrays[-2].shape, f32),
            pltpu.VMEM(arrays[-1].shape[1:], f32),
            pltpu.VMEM((FF // n_f, FF), f32),
            dma((7,)),
        ]
        + [pltpu.VMEM(arrays[i].shape, arrays[i].dtype) for i in (0, 1, 2, 4, 14, 3, 5)]
        + [pltpu.VMEM(arrays[i].shape, arrays[i].dtype) for i in (6, 7, 13, 15, 8, 9, 10)]
        + [dma((14,))],
        compiler_params=remote_params(2, 63),
        name="hind",
    )(length, step, *arrays)


def update_kernel(
    latent_ch,
    units,
    step_ref,
    scalar_ref,
    conv_g,
    time_g,
    tiles,
    head_g,
    wide_g,
    wide_dir,
    down_g,
    down_dir,
    stem_w,
    stem_m,
    stem_s,
    head_w,
    head_m,
    head_s,
    time_w,
    time_m,
    time_s,
    vec_m,
    vec_s,
    conv_w,
    conv_m,
    conv_s,
    wide_w,
    wide_m,
    down_w,
    down_m,
    loss_out,
    norm_out,
    stem_out,
    stem_m_out,
    stem_s_out,
    head_out,
    head_m_out,
    head_s_out,
    time_out,
    time_m_out,
    time_s_out,
    vec_out,
    vec_m_out,
    vec_s_out,
    conv_out,
    conv_m_out,
    conv_s_out,
    wide_out,
    wide_m_out,
    down_out,
    down_m_out,
):
    taps, channels = stem_w.shape
    stem_tiles = taps // 8 * (channels // 128)
    small = take_tiles(tiles, stem_tiles, 16, 2 * channels)
    factor = scalar_ref[2:3, 0:1]
    loss_out[0] = scalar_ref[0, 0]
    norm_out[0] = scalar_ref[1, 0]
    step = jnp.zeros((1, 1), f32) + step_ref[0].astype(f32)
    one_over = 1.0 / (1.0 - jnp.exp(step * math.log(0.9)))
    two_over = 1.0 / (1.0 - jnp.exp(step * math.log(0.999)))

    def adam(outs, where, weight, first, second, grad):
        grad = factor * grad
        first_new = 0.9 * first + 0.1 * grad
        second_new = 0.999 * second + 0.001 * grad * grad
        moved = first_new * one_over / (jnp.sqrt(second_new * two_over) + adam_floor)
        outs[0][where] = weight - adam_rate * (moved + decay_rate * weight)
        outs[1][where] = first_new
        outs[2][where] = second_new

    whole = slice(None)
    adam(
        (stem_out, stem_m_out, stem_s_out),
        whole,
        stem_w[...],
        stem_m[...],
        stem_s[...],
        take_tiles(tiles, 0, taps, channels),
    )
    outs = (time_out, time_m_out, time_s_out)
    for i in range(time_w.shape[0]):
        adam(outs, i, time_w[i], time_m[i], time_s[i], time_g[i])
    outs = (conv_out, conv_m_out, conv_s_out)
    for i in range(conv_w.shape[0]):
        adam(outs, i, conv_w[i], conv_m[i], conv_s[i], conv_g[i])
    outs = (head_out, head_m_out, head_s_out)
    for tap in range(9):
        where = (whole, slice(tap * channels, (tap + 1) * channels))
        grad = head_g[tap * latent_ch : (tap + 1) * latent_ch]
        adam(outs, where, head_w[where], head_m[where], head_s[where], grad)

    def vec_grad(which):
        if which < 13:
            lane = (which % 2) * channels
            return small[which // 2 : which // 2 + 1, lane : lane + channels]
        if which < 16:
            return small[which - 6 : which - 5]
        if which == 16:
            return jnp.concatenate([small[10:11], small[11:12]], 1)
        return small[12:13, 0:latent_ch]

    for which, (first, length) in enumerate(
        offsets(channels, 2 * channels, units, latent_ch)
    ):
        where = slice(first, first + length)
        grad = (factor * vec_grad(which)).reshape(length)
        vec_out[where] = grad
        vec_m_out[where] = 0.9 * vec_m[where] + 0.1 * grad
        vec_s_out[where] = 0.999 * vec_s[where] + 0.001 * grad * grad

    kept = 1.0 - shampoo_rate * decay_rate
    wide_m_out[...] = 0.9 * wide_m[...] + factor * wide_g[...]
    wide_out[...] = wide_w[...] * kept - shampoo_rate * wide_dir[...]
    down_m_out[...] = 0.9 * down_m[...] + factor * down_g[...]
    down_out[...] = down_w[...] * kept - shampoo_rate * down_dir[...]


def run_update(latent_ch, step, *arrays):
    stem_w, head_w, time_w, vec_m = arrays[9], arrays[12], arrays[15], arrays[18]
    conv_w, wide_w, down_w = arrays[20], arrays[23], arrays[25]
    shapes = [(1,)] * 2 + [stem_w.shape] * 3 + [head_w.shape] * 3 + [time_w.shape] * 3
    shapes += [vec_m.shape] * 3 + [conv_w.shape] * 3 + [wide_w.shape] * 2 + [down_w.shape] * 2
    return pl.pallas_call(
        functools.partial(update_kernel, latent_ch, FF),
        in_specs=[SM] + [VM] * len(arrays),
        out_specs=[SM] * 2 + [VM] * (len(shapes) - 2),
        out_shape=[sized(shape) for shape in shapes],
        compiler_params=params(62),
        name="update",
    )(step, *arrays)


def local(
    latents,
    noises,
    clap_embed,
    timesteps,
    lengths,
    step_count,
    stem_w,
    head_w,
    time_w,
    vector,
    conv_w,
    wide_w,
    down_w,
    roots_small,
    root_wide,
    roots_large,
    stem_moment,
    stem_square,
    head_moment,
    head_square,
    time_moment,
    time_square,
    vector_moment,
    vector_square,
    conv_moment,
    conv_square,
    wide_moment,
    down_moment,
):
    frames_n, freq_bins, latent_ch = (latents.shape[1], latents.shape[2], latents.shape[3])
    channels = stem_w.shape[1]
    def by_bins(value):
        return value[0].transpose(1, 2, 0).reshape(freq_bins * latent_ch, frames_n)

    head_t = head_w.T
    (
        zero,
        act_one,
        inner,
        act_two,
        one,
        normed,
        qkv_t,
        cols_t,
        noi_t,
        stat,
        film,
        conv_full,
        time_full,
        first_full,
    ) = run_fore(
        frames_n,
        lengths,
        timesteps,
        by_bins(latents),
        by_bins(noises),
        stem_w,
        conv_w,
        wide_w,
        time_w,
        vector,
        clap_embed,
    )
    mixed_t, lse, up_full, down_full = run_attend(
        frames_n, lengths, qkv_t, wide_w, down_w
    )
    two_grad, do_t, early, small = run_middle(
        frames_n,
        lengths,
        mixed_t,
        one,
        first_full,
        up_full,
        down_full,
        vector,
        head_t,
        noi_t,
    )
    dq, dk, dv, early, wide_moment_full, down_moment_full = run_attend_back(
        frames_n, lengths, qkv_t, lse, mixed_t, do_t, early, wide_moment, down_moment
    )
    outs = run_hind(
        frames_n,
        lengths,
        timesteps,
        dq,
        dk,
        dv,
        two_grad,
        normed,
        one,
        act_two,
        inner,
        act_one,
        zero,
        cols_t,
        stat,
        film,
        conv_full,
        first_full,
        time_full,
        vector,
        small,
        early,
        wide_moment_full,
        down_moment_full,
        roots_small,
        root_wide,
        roots_large,
    )
    conv_sum, tiles, time_sum, scalars, head_sum, wide_sum, wide_dir, down_sum, down_dir = outs
    outs = run_update(
        latent_ch,
        step_count,
        scalars,
        conv_sum,
        time_sum,
        tiles,
        head_sum,
        wide_sum,
        wide_dir,
        down_sum,
        down_dir,
        stem_w,
        stem_moment,
        stem_square,
        head_t,
        head_moment.T,
        head_square.T,
        time_w,
        time_moment,
        time_square,
        vector_moment,
        vector_square,
        conv_w,
        conv_moment,
        conv_square,
        wide_w,
        wide_moment,
        down_w,
        down_moment,
    )
    outs = list(outs)
    for index in (5, 6, 7):
        outs[index] = outs[index].T
    return (outs[0][0], outs[1][0], *outs[2:])


def solution(mesh):
    in_specs = (
        P(("dp", "fsdp"), None, None, None),
        P(("dp", "fsdp"), None, None, None),
        P(("dp", "fsdp"), None),
        P(("dp", "fsdp")),
        P(("dp", "fsdp")),
        P(),
        P(),
        P(),
        P(None, "fsdp", None),
        P(),
        P(None, "fsdp", None),
        P("fsdp", None),
        P("fsdp", None),
        P(),
        P(),
        P(),
        P(),
        P(),
        P(),
        P(),
        P(None, "fsdp", None),
        P(None, "fsdp", None),
        P(),
        P(),
        P(None, "fsdp", None),
        P(None, "fsdp", None),
        P("fsdp", None),
        P("fsdp", None),
    )
    out_specs = (
        P(),
        P(),
        P(),
        P(),
        P(),
        P(),
        P(),
        P(),
        P(None, "fsdp", None),
        P(None, "fsdp", None),
        P(None, "fsdp", None),
        P(),
        P(),
        P(),
        P(None, "fsdp", None),
        P(None, "fsdp", None),
        P(None, "fsdp", None),
        P("fsdp", None),
        P("fsdp", None),
        P("fsdp", None),
        P("fsdp", None),
    )
    return jax.shard_map(local, mesh=mesh, in_specs=in_specs, out_specs=out_specs, check_vma=False)
```

```python
import functools
import math

import jax
import jax.numpy as jnp
from jax import lax
from jax.experimental import pallas as pl
from jax.experimental.pallas import tpu as pltpu
from jax.sharding import PartitionSpec as P

HEADS = 8
FF = 1024
EMB = 512
GROUPS = 32

norm_floor = 1e-05
masked_score = -1e30
clip_limit = 0.002
adam_rate = 0.05
adam_floor = 1e-08
shampoo_rate = 0.02
decay_rate = 0.01

f32 = jnp.float32
bf16 = jnp.bfloat16
highest = lax.Precision.HIGHEST
LOG2E = math.log2(math.e)
CHUNK = 1024


def mm(left_op, right_op):
    return jnp.dot(left_op, right_op, preferred_element_type=f32)


def mm_nt(left_op, right_op):
    return lax.dot_general(
        left_op, right_op, (((1,), (1,)), ((), ())), preferred_element_type=f32
    )


def col_sum(value):
    return jnp.sum(value, axis=0, keepdims=True)


def row_mean(value):
    return jnp.mean(value, axis=-1, keepdims=True)


def loop(count, body, init, hooks=()):
    if not hooks:
        return lax.fori_loop(0, count, body, init)

    def step(i, carry):
        for place, action in hooks:
            pl.when(i == place)(action)
        return body(i, carry)

    return lax.fori_loop(0, count, step, init)


def tap_shift(field, a, b, run):
    length = field.shape[1]
    step = run * (a - 1) + (b - 1)
    if step == 0:
        return field
    pos = lax.broadcasted_iota(jnp.int32, field.shape, 1)
    bin_pos = lax.rem(pos, run)
    keep = None
    for wanted, test in (
        (a == 0, lambda: pos >= run),
        (a == 2, lambda: pos < length - run),
        (b == 0, lambda: bin_pos >= 1),
        (b == 2, lambda: bin_pos < run - 1),
    ):
        if wanted:
            keep = test() if keep is None else jnp.logical_and(keep, test())
    return jnp.where(keep, pltpu.roll(field, (-step) % length, 1), 0.0)


def put_shifted(buf, start, value, run):
    rows, channels = value.shape
    bin_pos = lax.rem(lax.broadcasted_iota(jnp.int32, value.shape, 0), run)
    before = jnp.where(bin_pos == 0, 0.0, pltpu.roll(value, 1, 0))
    after = jnp.where(bin_pos == run - 1, 0.0, pltpu.roll(value, rows - 1, 0))
    where = pl.ds(start + run, rows)
    buf[where, 0:channels] = before.astype(bf16)
    buf[where, channels : 2 * channels] = value.astype(bf16)
    buf[where, 2 * channels : 3 * channels] = after.astype(bf16)


def clear_ends(buf, rows_n, run):
    blank = jnp.zeros((run, buf.shape[1]), bf16)
    buf[0:run, :] = blank
    buf[rows_n + run : rows_n + 2 * run, :] = blank


def live_rows(shape, live, run):
    return lax.rem(lax.broadcasted_iota(jnp.int32, shape, 0), run) < live


def swap_tap(tap):
    return tap % 3 * 3 + tap // 3


def swap_taps(value, axis=0):
    size = value.shape[axis] // 9
    pieces = [
        lax.slice_in_dim(value, swap_tap(t) * size, (swap_tap(t) + 1) * size, axis=axis)
        for t in range(9)
    ]
    return jnp.concatenate(pieces, axis)


def group_total(row, groups):
    channels = row.shape[1]
    size = channels // groups
    one = lax.broadcasted_iota(jnp.int32, (channels, channels), 0) // size
    two = lax.broadcasted_iota(jnp.int32, (channels, channels), 1) // size
    same = jnp.where(one == two, 1.0, 0.0).astype(f32)
    wide = jnp.broadcast_to(row, (8, channels))
    return jnp.dot(wide, same, precision=highest, preferred_element_type=f32)[0:1]


def vec_mat(row, weight, transposed=False):
    top = row.astype(bf16).astype(f32)
    rest = row - top
    mid = rest.astype(bf16).astype(f32)
    low = rest - mid
    shape = (16, row.shape[1])
    index = lax.broadcasted_iota(jnp.int32, shape, 0)
    stacked = jnp.where(
        index == 0,
        jnp.broadcast_to(top, shape),
        jnp.where(
            index == 1,
            jnp.broadcast_to(mid, shape),
            jnp.where(index == 2, jnp.broadcast_to(low, shape), 0.0),
        ),
    ).astype(bf16)
    return col_sum(mm_nt(stacked, weight) if transposed else mm(stacked, weight))


def silu_slope(value):
    gate = jax.nn.sigmoid(value)
    return gate * (1.0 + value * (1.0 - gate))


def channel_stats(read, rows_n, live, run, channels, average):
    count = rows_n // CHUNK

    def add(i, total):
        start = pl.multiple_of(i * CHUNK, CHUNK)
        value = read(start)
        return total + col_sum(jnp.where(live_rows(value.shape, live, run), value, 0.0))

    center = average(loop(count, add, jnp.zeros((1, channels), f32)))

    def add_square(i, total):
        start = pl.multiple_of(i * CHUNK, CHUNK)
        value = read(start) - center
        return total + col_sum(jnp.where(live_rows(value.shape, live, run), value * value, 0.0))

    return center, average(loop(count, add_square, jnp.zeros((1, channels), f32)))


def group_stats(read, rows_n, live, run, channels, groups, counted):
    center, spread = channel_stats(
        read, rows_n, live, run, channels, lambda row: group_total(row, groups) / counted
    )
    return center, lax.rsqrt(spread + norm_floor)


def time_wave(time_ref, embed):
    half = embed // 2
    index = lax.broadcasted_iota(jnp.int32, (1, half), 1).astype(f32)
    frequency = jnp.exp(-math.log(10000.0) * index / half)
    angles = (jnp.zeros((1, half), f32) + time_ref[0].astype(f32)) * frequency
    return jnp.concatenate([jnp.cos(angles), jnp.sin(angles)], 1)


def offsets(channels, embed_width, hidden_units, latent_ch):
    starts = []
    start = 0
    for length in [channels] * 13 + [embed_width] * 3 + [hidden_units, latent_ch]:
        starts.append((start, length))
        start = start + length
    return starts


def put_small(ref, index, value):
    if index < 13:
        half = value.shape[1]
        ref[index // 2 : index // 2 + 1, (index % 2) * half : (index % 2 + 1) * half] = value
    elif index < 16:
        ref[index - 6 : index - 5, :] = value
    elif index == 16:
        half = value.shape[1] // 2
        ref[10:11, :] = value[:, :half]
        ref[11:12, :] = value[:, half:]
    else:
        ref[index - 5 : index - 4, 0 : value.shape[1]] = value


def take_small(rows, latent_ch):
    return jnp.concatenate(
        [
            rows[0:6].reshape(-1),
            rows[6, : rows.shape[1] // 2],
            rows[7:12].reshape(-1),
            rows[12, :latent_ch],
        ]
    )


MESH = pl.DeviceIdType.MESH


def places():
    n_d, n_f = lax.axis_size("dp"), lax.axis_size("fsdp")
    me = lax.axis_index("fsdp")
    return n_d, n_f // 2, lax.axis_index("dp"), me // 2, lax.rem(me, 2)


def push(src, dst, sends, recvs, target):
    copy = pltpu.make_async_remote_copy(
        src_ref=src,
        dst_ref=dst,
        send_sem=sends,
        recv_sem=recvs,
        device_id=target,
        device_id_type=MESH,
    )
    copy.start()
    return copy


def greet(n_d, n_z, d, z, c):
    barrier = pltpu.get_barrier_semaphore()
    for j in range(1, n_d):
        pl.semaphore_signal(
            barrier, inc=1, device_id={"dp": lax.rem(d + j, n_d)}, device_id_type=MESH
        )
    for k in range(1, n_z):
        pl.semaphore_signal(
            barrier,
            inc=1,
            device_id={"fsdp": 2 * lax.rem(z + k, n_z) + c},
            device_id_type=MESH,
        )
    pl.semaphore_signal(
        barrier, inc=1, device_id={"fsdp": 2 * z + 1 - c}, device_id_type=MESH
    )


def met(n_d, n_z, d, z, c):
    pl.semaphore_wait(pltpu.get_barrier_semaphore(), n_d + n_z - 1)


def conv_piece(d, n_d, channels):
    width = 2 * channels // n_d
    return (d * width) // channels, pl.ds(
        pl.multiple_of(lax.rem(d * width, channels), 128), width
    )


def lane_piece(d, n_d, lanes):
    width = lanes // n_d
    return pl.ds(pl.multiple_of(d * width, 128), width)


def plan_gather(here, parts, wholes, sems, across=True):
    n_d, n_z, d, z, c = here
    s1, r1, s2, r2, s3, r3 = sems
    sibling = {"fsdp": 2 * z + 1 - c}

    def copy(ref, sends, recvs, target):
        return pltpu.make_async_remote_copy(
            src_ref=ref,
            dst_ref=ref,
            send_sem=sends,
            recv_sem=recvs,
            device_id=target,
            device_id_type=MESH,
        )

    def source(k):
        return lax.rem(z - k + n_z, n_z)

    def first(k):
        target = {"fsdp": 2 * lax.rem(z + k, n_z) + c}
        return [copy(r, s1.at[k, i], r1.at[k, i], target) for i, r in enumerate(parts(z))]

    def second(k, j):
        target = {"dp": lax.rem(d + j, n_d)}
        refs = parts(source(k))
        return [copy(r, s2.at[k, j, i], r2.at[k, j, i], target) for i, r in enumerate(refs)]

    def last(k):
        refs = wholes(source(k))
        return [copy(r, s3.at[k, i], r3.at[k, i], sibling) for i, r in enumerate(refs)]

    def start(group):
        for item in group:
            item.start()

    def arrive(group):
        for item in group:
            item.wait_recv()

    def leave(group):
        for item in group:
            item.wait_send()

    far = range(1, n_z)
    peers = range(1, n_d) if across else ()

    def step_one():
        for k in far:
            start(first(k))
        start(last(0))

    def step_two():
        for k in far:
            arrive(first(k))
            for j in peers:
                start(second(k, j))
            if not across:
                start(last(k))

    def step_three():
        if across:
            for k in far:
                for j in peers:
                    arrive(second(k, j))
                start(last(k))

    def step_four():
        for k in range(n_z):
            arrive(last(k))
        for k in far:
            leave(first(k))
            for j in peers:
                leave(second(k, j))
        for k in range(n_z):
            leave(last(k))

    return step_one, step_two, step_three, step_four


def gather_sems(count):
    n_d, n_z = lax.axis_size("dp"), lax.axis_size("fsdp") // 2
    dma = pltpu.SemaphoreType.DMA
    return [
        dma((n_z, count)),
        dma((n_z, count)),
        dma((n_z, n_d, count)),
        dma((n_z, n_d, count)),
        dma((n_z, count)),
        dma((n_z, count)),
    ]


def plan_total(here, value_ref, out, pair, other, from_dp, summed, from_z, sems):
    n_d, n_z, d, z, c = here
    lanes_n = out.shape[3]
    mine = lane_piece(d, n_d, lanes_n)
    sibling = {"fsdp": 2 * z + 1 - c}
    send, recv = sems

    def copy(src, dst, index, target):
        return pltpu.make_async_remote_copy(
            src_ref=src,
            dst_ref=dst,
            send_sem=send.at[index],
            recv_sem=recv.at[index],
            device_id=target,
            device_id_type=MESH,
        )

    def replica(j):
        return lax.rem(d + j, n_d)

    def chip(k):
        return lax.rem(z + k, n_z)

    def one():
        return [copy(value_ref.at[:, 1 - c], other, 0, sibling)]

    def two():
        return [
            copy(
                pair.at[:, :, lane_piece(replica(j), n_d, lanes_n)],
                from_dp.at[j],
                j,
                {"dp": replica(j)},
            )
            for j in range(1, n_d)
        ]

    def three():
        return [
            copy(summed.at[chip(k)], from_z.at[k], n_d + k, {"fsdp": 2 * chip(k) + c})
            for k in range(1, n_z)
        ]

    def four():
        ref = out.at[z, c, :, mine]
        return [
            copy(ref, ref, n_d + n_z + j, {"dp": replica(j)}) for j in range(1, n_d)
        ]

    def five():
        ref = out.at[z, c]
        return [
            copy(ref, ref, 2 * n_d + n_z + k, {"fsdp": 2 * chip(k) + c}) for k in range(1, n_z)
        ]

    def six():
        ref = out.at[:, c]
        return [copy(ref, ref, 2 * n_d + 2 * n_z, sibling)]

    def start(group):
        for item in group:
            item.start()

    def arrive(group):
        for item in group:
            item.wait_recv()

    def step_one():
        start(one())

    def step_two():
        arrive(one())
        for i in range(n_z):
            pair[i] = (
                value_ref[i, pl.ds(c, 1)][0].astype(f32) + other[i].astype(f32)
            ).astype(pair.dtype)
        start(two())

    def step_three():
        arrive(two())
        for i in range(n_z):
            value = pair[i, :, mine].astype(f32)
            for j in range(1, n_d):
                value = value + from_dp[j, i].astype(f32)
            summed[i] = value.astype(summed.dtype)
        start(three())

    def step_four():
        arrive(three())
        value = summed[pl.ds(z, 1)][0].astype(f32)
        for k in range(1, n_z):
            value = value + from_z[k].astype(f32)
        out[pl.ds(z, 1), pl.ds(c, 1), :, mine] = value.astype(out.dtype)[None, None]
        start(four())

    def step_five():
        arrive(four())
        start(five())

    def step_six():
        arrive(five())
        start(six())

    def step_seven():
        arrive(six())
        for group in (one(), two(), three(), four(), five(), six()):
            for item in group:
                item.wait_send()

    return step_one, step_two, step_three, step_four, step_five, step_six, step_seven


def starts(group):
    for item in group:
        item.start()


def arrives(group):
    for item in group:
        item.wait_recv()


def leaves(group):
    for item in group:
        item.wait_send()


def remote(src, dst, send, recv, target):
    return pltpu.make_async_remote_copy(
        src_ref=src,
        dst_ref=dst,
        send_sem=send,
        recv_sem=recv,
        device_id=target,
        device_id_type=MESH,
    )


def plan_owner(here, value, other, pair, from_dp, summed, from_z, out, sems):
    n_d, n_z, d, z, c = here
    lanes_n = out.shape[1]
    mine = lane_piece(d, n_d, lanes_n)
    send, recv = sems

    def one():
        target = {"fsdp": 2 * z + 1 - c}
        return [remote(value.at[:, 1 - c], other, send.at[0], recv.at[0], target)]

    def two():
        group = []
        for j in range(1, n_d):
            peer = lax.rem(d + j, n_d)
            ref = pair.at[:, :, lane_piece(peer, n_d, lanes_n)]
            group.append(remote(ref, from_dp.at[j], send.at[j], recv.at[j], {"dp": peer}))
        return group

    def three():
        group = []
        for k in range(1, n_z):
            chip = lax.rem(z + k, n_z)
            index = n_d + k
            target = {"fsdp": 2 * chip + c}
            group.append(
                remote(summed.at[chip], from_z.at[k], send.at[index], recv.at[index], target)
            )
        return group

    def four():
        group = []
        ref = out.at[:, mine]
        for j in range(1, n_d):
            index = n_d + n_z + j
            target = {"dp": lax.rem(d + j, n_d)}
            group.append(remote(ref, ref, send.at[index], recv.at[index], target))
        return group

    def step_one():
        starts(one())

    def step_two():
        arrives(one())
        for i in range(n_z):
            own = value[i, pl.ds(c, 1)][0].astype(f32)
            pair[i] = (own + other[i].astype(f32)).astype(bf16)
        starts(two())

    def step_three():
        arrives(two())
        for i in range(n_z):
            total = pair[i, :, mine].astype(f32)
            for j in range(1, n_d):
                total = total + from_dp[j, i].astype(f32)
            summed[i] = total.astype(bf16)
        starts(three())

    def step_four():
        arrives(three())
        total = summed[pl.ds(z, 1)][0].astype(f32)
        for k in range(1, n_z):
            total = total + from_z[k].astype(f32)
        out[:, mine] = total.astype(bf16)
        starts(four())

    def finish():
        arrives(four())
        for group in (one(), two(), three(), four()):
            leaves(group)

    return step_one, step_two, step_three, step_four, finish


def owner_scratch(rows, lanes):
    n_d, n_z = lax.axis_size("dp"), lax.axis_size("fsdp") // 2
    part = lanes // n_d
    dma = pltpu.SemaphoreType.DMA
    return [
        pltpu.VMEM((n_z, 2, rows, lanes), bf16),
        pltpu.VMEM((n_z, rows, lanes), bf16),
        pltpu.VMEM((n_z, rows, lanes), bf16),
        pltpu.VMEM((n_d, n_z, rows, part), bf16),
        pltpu.VMEM((n_z, rows, part), bf16),
        pltpu.VMEM((n_z, rows, part), bf16),
        pltpu.VMEM((rows, lanes), bf16),
        dma((2 * n_d + n_z,)),
        dma((2 * n_d + n_z,)),
    ]


def plan_spread(here, out, sems):
    n_d, n_z, d, z, c = here
    send, recv = sems

    def one():
        group = []
        for k in range(1, n_z):
            ref = out.at[z, c]
            target = {"fsdp": 2 * lax.rem(z + k, n_z) + c}
            group.append(remote(ref, ref, send.at[k], recv.at[k], target))
        return group

    def two():
        ref = out.at[:, c]
        return [remote(ref, ref, send.at[0], recv.at[0], {"fsdp": 2 * z + 1 - c})]

    def step_two():
        arrives(one())
        starts(two())

    def finish():
        arrives(two())
        leaves(one())
        leaves(two())

    return (lambda: starts(one())), step_two, finish


def plan_clips(here, everyone, sems):
    n_d, n_z, d, z, c = here
    send, recv = sems

    def one():
        group = []
        for j in range(1, n_d):
            ref = everyone.at[d, z, c]
            target = {"dp": lax.rem(d + j, n_d)}
            group.append(remote(ref, ref, send.at[j], recv.at[j], target))
        return group

    def two():
        group = []
        for k in range(1, n_z):
            ref = everyone.at[:, z, c]
            target = {"fsdp": 2 * lax.rem(z + k, n_z) + c}
            group.append(remote(ref, ref, send.at[n_d + k], recv.at[n_d + k], target))
        return group

    def three():
        ref = everyone.at[:, :, c]
        return [remote(ref, ref, send.at[0], recv.at[0], {"fsdp": 2 * z + 1 - c})]

    def step_two():
        arrives(one())
        starts(two())

    def step_three():
        arrives(two())
        starts(three())

    def finish():
        arrives(three())
        for group in (one(), two(), three()):
            leaves(group)

    return (lambda: starts(one())), step_two, step_three, finish


def all_peers(here):
    n_d, n_z, d, z, c = here
    n_f = 2 * n_z
    me = 2 * z + c
    peers = []
    for j in range(n_d):
        for k in range(n_f):
            if j or k:
                peers.append((j * n_f + k, lax.rem(d + j, n_d), lax.rem(me + k, n_f)))
    return peers


def greet_all(here):
    barrier = pltpu.get_barrier_semaphore()
    peers = all_peers(here)
    for _, other_d, other_f in peers:
        pl.semaphore_signal(
            barrier,
            inc=1,
            device_id={"dp": other_d, "fsdp": other_f},
            device_id_type=MESH,
        )


def met_all(here):
    pl.semaphore_wait(pltpu.get_barrier_semaphore(), len(all_peers(here)))


def plan_small(here, value, out, other, pair, from_dp, summed, from_z, sems):
    n_d, n_z, d, z, c = here
    lanes_n = out.shape[3]
    mine = lane_piece(d, n_d, lanes_n)
    send, recv, all_send, all_recv = sems

    def one():
        target = {"fsdp": 2 * z + 1 - c}
        return [remote(value.at[:, 1 - c], other, send.at[0], recv.at[0], target)]

    def two():
        group = []
        for j in range(1, n_d):
            peer = lax.rem(d + j, n_d)
            ref = pair.at[:, :, lane_piece(peer, n_d, lanes_n)]
            group.append(remote(ref, from_dp.at[j], send.at[j], recv.at[j], {"dp": peer}))
        return group

    def three():
        group = []
        for k in range(1, n_z):
            chip = lax.rem(z + k, n_z)
            index = n_d + k
            target = {"fsdp": 2 * chip + c}
            group.append(
                remote(summed.at[chip], from_z.at[k], send.at[index], recv.at[index], target)
            )
        return group

    def four():
        ref = out.at[z, c, :, mine]
        return [
            remote(
                ref,
                ref,
                all_send.at[index],
                all_recv.at[index],
                {"dp": other_d, "fsdp": other_f},
            )
            for index, other_d, other_f in all_peers(here)
        ]

    def step_one():
        starts(one())

    def step_two():
        arrives(one())
        for i in range(n_z):
            pair[i] = value[i, pl.ds(c, 1)][0] + other[i]
        starts(two())

    def step_three():
        arrives(two())
        for i in range(n_z):
            total = pair[i, :, mine]
            for j in range(1, n_d):
                total = total + from_dp[j, i]
            summed[i] = total
        starts(three())

    def step_four():
        arrives(three())
        total = summed[pl.ds(z, 1)][0]
        for k in range(1, n_z):
            total = total + from_z[k]
        out[pl.ds(z, 1), pl.ds(c, 1), :, mine] = total[None, None]
        starts(four())

    def finish():
        arrives(four())
        for group in (one(), two(), three(), four()):
            leaves(group)

    return step_one, step_two, step_three, step_four, finish


def small_scratch(lanes):
    n_d, n_z = lax.axis_size("dp"), lax.axis_size("fsdp") // 2
    part = lanes // n_d
    dma = pltpu.SemaphoreType.DMA
    return [
        pltpu.VMEM((n_z, 2, 8, lanes), f32),
        pltpu.VMEM((n_z, 8, lanes), f32),
        pltpu.VMEM((n_z, 8, lanes), f32),
        pltpu.VMEM((n_d, n_z, 8, part), f32),
        pltpu.VMEM((n_z, 8, part), f32),
        pltpu.VMEM((n_z, 8, part), f32),
        dma((n_d + n_z,)),
        dma((n_d + n_z,)),
        dma((n_d * n_z * 2,)),
        dma((n_d * n_z * 2,)),
    ]


def plan_scalar(here, squares, sems):
    n_d, n_z, d, z, c = here
    n_f = 2 * n_z
    mine = d * n_f + 2 * z + c
    send, recv = sems

    def one():
        ref = squares.at[mine]
        return [
            remote(
                ref, ref, send.at[index], recv.at[index], {"dp": other_d, "fsdp": other_f}
            )
            for index, other_d, other_f in all_peers(here)
        ]

    def finish():
        arrives(one())
        total = squares[0]
        for i in range(1, n_d * n_f):
            total = total + squares[i]
        leaves(one())
        return total

    return (lambda: starts(one())), finish


def store_rows(ref, first, lane, value):
    size = ref.shape[2]
    done = 0
    while done < value.shape[0]:
        shard, offset = divmod(first + done, size)
        count = min(size - offset, value.shape[0] - done)
        ref[shard // 2, shard % 2, offset : offset + count, lane : lane + value.shape[1]] = value[
            done : done + count
        ]
        done = done + count


def store_folded(ref, first, value):
    size = ref.shape[2]
    width = value.shape[1]
    done = 0
    while done < value.shape[0]:
        block, offset = divmod(first + done, size)
        shard, side = divmod(block, 2)
        count = min(size - offset, value.shape[0] - done)
        ref[
            shard // 2, shard % 2, offset : offset + count, side * width : (side + 1) * width
        ] = value[done : done + count]
        done = done + count


def tile_place(ref, tile):
    across = ref.shape[3] // 128
    shard, lane = divmod(tile, across)
    return (shard // 2, shard % 2, slice(None), slice(128 * lane, 128 * lane + 128))


def put_tiles(ref, first, value):
    across = value.shape[1] // 128
    for i in range(value.shape[0] // 8):
        for j in range(across):
            ref[tile_place(ref, first + i * across + j)] = value[
                8 * i : 8 * i + 8, 128 * j : 128 * j + 128
            ]


def take_tiles(ref, first, rows, lanes):
    across = lanes // 128
    return jnp.concatenate(
        [
            jnp.concatenate(
                [ref[tile_place(ref, first + i * across + j)] for j in range(across)], 1
            )
            for i in range(rows // 8)
        ],
        0,
    )


def total_scratch(rows, lanes, dtype):
    n_d, n_z = lax.axis_size("dp"), lax.axis_size("fsdp") // 2
    part = lanes // n_d
    dma = pltpu.SemaphoreType.DMA
    count = 2 * n_d + 2 * n_z + 1
    return [
        pltpu.VMEM((n_z, 2, rows, lanes), dtype),
        pltpu.VMEM((n_z, rows, lanes), dtype),
        pltpu.VMEM((n_z, rows, lanes), dtype),
        pltpu.VMEM((n_d, n_z, rows, part), dtype),
        pltpu.VMEM((n_z, rows, part), dtype),
        pltpu.VMEM((n_z, rows, part), dtype),
        dma((count,)),
        dma((count,)),
    ]


def fold_rows(value):
    half = value.shape[0] // 2
    return jnp.concatenate([value[:half], value[half:]], 1)


def shard_gather(here, wide_land, down_land, sems):
    n_d, n_z, d, z, c = here
    lanes_w = lane_piece(d, n_d, wide_land.shape[3])
    lanes_d = lane_piece(d, n_d, down_land.shape[3])

    def parts(source):
        return [
            wide_land.at[source, c, :, lanes_w],
            down_land.at[source, c, :, lanes_d],
        ]

    def wholes(source):
        return [wide_land.at[source, c], down_land.at[source, c]]

    return plan_gather(here, parts, wholes, sems)


def place_shards(here, wide, down, wide_land, down_land):
    z, c = here[3], here[4]
    wide_land[pl.ds(z, 1), pl.ds(c, 1)] = wide.astype(bf16)[None, None]
    down_land[pl.ds(z, 1), pl.ds(c, 1)] = fold_rows(down).astype(bf16)[None, None]


def land_out(wide_land, down_land, wide_out, down_out):
    n_z = wide_land.shape[0]
    lanes = down_out.shape[1]
    rows_w, rows_d = wide_land.shape[2], down_land.shape[2]
    for i in range(n_z):
        for j in range(2):
            shard = 2 * i + j
            wide_out[shard * rows_w : (shard + 1) * rows_w, :] = wide_land[i, j]
            first = 2 * shard * rows_d
            down_out[first : first + rows_d, :] = down_land[i, j, :, :lanes]
            down_out[first + rows_d : first + 2 * rows_d, :] = down_land[i, j, :, lanes:]


def land_scratch(wide_shape, down_shape):
    n_z = lax.axis_size("fsdp") // 2
    return [
        pltpu.VMEM((n_z, 2) + wide_shape, bf16),
        pltpu.VMEM((n_z, 2, down_shape[0] // 2, 2 * down_shape[1]), bf16),
    ] + gather_sems(2)


def land_gather(here, land, sems):
    n_d, c = here[0], here[4]
    lanes = lane_piece(here[2], n_d, land.shape[3])
    return plan_gather(
        here,
        lambda source: [land.at[source, c, :, lanes]],
        lambda source: [land.at[source, c]],
        sems,
    )


def unfold_land(land, out, which):
    n_z, _, rows, lanes = land.shape
    width = lanes // 2
    for block in range(n_z * 4):
        shard, side = divmod(block, 2)
        done = 0
        while done < rows:
            tap, offset = divmod(block * rows + done, width)
            count = min(width - offset, rows - done)
            first = swap_tap(tap) * width + offset
            out[which, first : first + count, :] = land[
                shard // 2, shard % 2, done : done + count, side * width : (side + 1) * width
            ]
            done = done + count


def fore_kernel(
    run,
    groups,
    len_ref,
    time_ref,
    lat_ref,
    noi_ref,
    stem_ref,
    conv_own,
    wide_own,
    time_own,
    vec_ref,
    clap_ref,
    zero_any,
    act_one_any,
    inner_any,
    act_two_any,
    one_any,
    normed_any,
    qkv_any,
    colsT_ref,
    noiT_ref,
    stat_ref,
    film_ref,
    conv_any,
    time_any,
    wide_any,
    buf,
    cols,
    tall,
    first_land,
    second_land,
    zero_ref,
    act_one_ref,
    inner_ref,
    act_two_ref,
    one_ref,
    normed_ref,
    qkv_ref,
    conv_ref,
    time_land,
    wide_land,
    out_sems,
    *sems,
):
    rows_n, channels = zero_ref.shape
    latent_ch = lat_ref.shape[0] * run // rows_n
    embed = time_own.shape[2]
    count = rows_n // CHUNK
    here = places()
    n_d, n_z, d, z, c = here
    greet(*here)
    first_plan = land_gather(here, first_land, sems[0:6])
    second_plan = land_gather(here, second_land, sems[6:12])
    wide_plan = plan_gather(
        here,
        lambda source: [wide_land.at[source, c]],
        lambda source: [wide_land.at[source, c]],
        sems[12:18],
        False,
    )
    t_lanes = lane_piece(d, n_d, embed)
    time_plan = plan_gather(
        here,
        lambda source: [time_land.at[:, source, c, :, t_lanes]],
        lambda source: [time_land.at[:, source, c]],
        sems[18:24],
    )
    own = (pl.ds(z, 1), pl.ds(c, 1))
    first_land[own] = fold_rows(conv_own[0]).astype(bf16)[None, None]
    second_land[own] = fold_rows(conv_own[1]).astype(bf16)[None, None]
    wide_land[own] = wide_own[:, 0 : wide_land.shape[3]].astype(bf16)[None, None]
    time_land[:, pl.ds(z, 1), pl.ds(c, 1)] = time_own[...].astype(bf16)[:, None, None]
    outs = []

    def save(src, dst):
        copy = pltpu.make_async_copy(src, dst, out_sems.at[len(outs)])
        outs.append(copy)
        copy.start()

    met(*here)
    first_plan[0]()
    time_plan[0]()
    live = len_ref[0]
    counted = (live * (rows_n // run) * (channels // groups)).astype(f32)
    segs = offsets(channels, embed, FF, latent_ch)

    def seg(index):
        start, length = segs[index]
        return vec_ref[start : start + length].reshape(1, length)

    def by_bins(value):
        return jnp.concatenate(
            [value[i * latent_ch : (i + 1) * latent_ch] for i in range(rows_n // run)], 1
        )

    noise = noi_ref[...].astype(f32)
    noiT_ref[...] = by_bins(noise)
    phase = (jnp.zeros((1, run), f32) + time_ref[0].astype(f32)) / 1000.0
    kept = jnp.cos((phase + 0.008) / 1.008 * (math.pi / 2)) ** 2
    mixed = jnp.sqrt(kept) * lat_ref[...].astype(f32) + jnp.sqrt(1.0 - kept) * noise
    pos = lax.broadcasted_iota(jnp.int32, mixed.shape, 1)
    noisy = by_bins(jnp.where(pos < live, mixed, 0.0).astype(bf16).astype(f32))
    taps = 9 * latent_ch
    for a in range(3):
        for b in range(3):
            tap = 3 * a + b
            tall[tap * latent_ch : (tap + 1) * latent_ch] = tap_shift(noisy, a, b, run)
    tall[taps:] = jnp.zeros((tall.shape[0] - taps, rows_n), f32)
    colsT_ref[...] = tall[0:taps].astype(bf16)
    cols[...] = tall[...].T.astype(bf16)
    stem_low = jnp.concatenate(
        [swap_taps(stem_ref[...]), jnp.zeros((cols.shape[1] - taps, channels), f32)], 0
    ).astype(bf16)
    stem_bias = seg(12)

    def stem_part(i, carry):
        rows = pl.ds(pl.multiple_of(i * CHUNK, CHUNK), CHUNK)
        zero_ref[rows, :] = mm(cols[rows, :], stem_low) + stem_bias
        return carry

    loop(count, stem_part, 0)
    save(zero_ref, zero_any)
    first_plan[1]()

    clear_ends(buf, rows_n, run)

    def convolve(which, start):
        total = None
        for a in range(3):
            part = mm(
                buf[pl.ds(start + run * a, CHUNK), :],
                conv_ref[which, 3 * a * channels : 3 * (a + 1) * channels, :],
            )
            total = part if total is None else total + part
        return total

    def activate(read, center, scale, gain, shift, act_ref, hooks):
        factor = scale * gain

        def part(i, carry):
            start = pl.multiple_of(i * CHUNK, CHUNK)
            value = jax.nn.silu((read(start) - center) * factor + shift)
            value = jnp.where(live_rows(value.shape, live, run), value, 0.0)
            low = value.astype(bf16)
            act_ref[pl.ds(start, CHUNK), :] = low
            put_shifted(buf, start, low.astype(f32), run)
            return carry

        loop(count, part, 0, hooks)

    def read_zero(start):
        return zero_ref[pl.ds(start, CHUNK), :]

    center, scale = group_stats(read_zero, rows_n, live, run, channels, groups, counted)
    stat_ref[0:1] = center
    stat_ref[1:2] = scale
    second_plan[0]()
    wide_plan[0]()
    activate(
        read_zero, center, scale, seg(0), seg(1), act_one_ref, ((1, time_plan[1]),)
    )
    first_plan[2]()
    second_plan[1]()
    first_plan[3]()
    unfold_land(first_land, conv_ref, 0)
    save(act_one_ref, act_one_any)
    save(conv_ref.at[0], conv_any.at[0])

    bias_one = seg(2)

    def conv_part(i, carry):
        start = pl.multiple_of(i * CHUNK, CHUNK)
        inner_ref[pl.ds(start, CHUNK), :] = convolve(0, start) + bias_one
        return carry

    loop(count, conv_part, 0)
    wide_plan[1]()
    save(inner_ref, inner_any)

    def read_inner(start):
        return inner_ref[pl.ds(start, CHUNK), :]

    pixels = (live * (rows_n // run)).astype(f32)
    middle, spread = channel_stats(
        read_inner, rows_n, live, run, channels, lambda row: row / pixels
    )
    time_plan[2]()
    time_plan[3]()
    def time_matrix(index):
        return time_land[index].reshape(embed, embed)

    wave = time_wave(time_ref, embed)
    pre_time = vec_mat(wave, time_matrix(0)) + seg(13)
    embedding = vec_mat(jax.nn.silu(pre_time), time_matrix(1)) + seg(14) + clap_ref[...]
    film = vec_mat(jax.nn.silu(embedding), time_matrix(2)) + seg(15)
    film_ref[0:1] = film
    film_ref[1:2] = pre_time
    film_ref[2:3] = embedding
    film_ref[3:8] = jnp.zeros((5, embed), f32)
    lift = 1.0 + film[:, :channels]
    move = film[:, channels:]


    def read_moved(start):
        return inner_ref[pl.ds(start, CHUNK), :] * lift + move

    size = channels // groups
    middle = middle * lift + move
    center = group_total(middle, groups) / size
    gap = middle - center
    spread = group_total(lift * lift * spread + gap * gap, groups) / size
    scale = lax.rsqrt(spread + norm_floor)
    stat_ref[2:3] = center
    stat_ref[3:4] = scale
    stat_ref[4:8] = jnp.zeros((4, channels), f32)
    second_plan[2]()
    wide_plan[2]()
    activate(read_moved, center, scale, seg(3), seg(4), act_two_ref, ())
    second_plan[3]()
    wide_plan[3]()
    unfold_land(second_land, conv_ref, 1)
    save(act_two_ref, act_two_any)
    save(conv_ref.at[1], conv_any.at[1])
    save(time_land, time_any)
    save(wide_land, wide_any)

    bias_two = seg(5)
    gain, shift = seg(6), seg(7)
    wide_full = wide_land[...].reshape(channels, wide_land.shape[3])
    wqkv_t = wide_full[:, 0 : 3 * channels].T

    def last_part(i, carry):
        start = pl.multiple_of(i * CHUNK, CHUNK)
        rows = pl.ds(start, CHUNK)
        stream = zero_ref[rows, :] + convolve(1, start) + bias_two
        one_ref[rows, :] = stream
        gap = stream - row_mean(stream)
        normed = gap * lax.rsqrt(row_mean(gap * gap) + norm_floor) * gain + shift
        low = normed.astype(bf16)
        normed_ref[rows, :] = low
        qkv_ref[:, rows] = mm_nt(wqkv_t, low).astype(bf16)
        return carry

    for i in range(count):
        last_part(i, 0)
        rows = pl.ds(i * CHUNK, CHUNK)
        save(one_ref.at[rows], one_any.at[rows])
        save(normed_ref.at[rows], normed_any.at[rows])
        save(qkv_ref.at[:, rows], qkv_any.at[:, rows])
    for copy in outs:
        copy.wait()


def query_rows(query, factor, extra):
    dim, length = query.shape
    scaled = query.astype(f32) * (factor * LOG2E)
    high = scaled.astype(bf16).astype(f32)
    index = lax.broadcasted_iota(jnp.int32, (128 - 2 * dim, length), 0)
    tile = jnp.where(index == 0, 1.0, 0.0)
    for place, row in enumerate(extra):
        tile = jnp.where(index == place + 1, jnp.broadcast_to(row, tile.shape), tile)
    return jnp.concatenate([high, scaled - high, tile], 0)


def key_rows(keys, live, run):
    dim, length = keys.shape
    shape = (128 - 2 * dim, length)
    index = lax.broadcasted_iota(jnp.int32, shape, 0)
    pos = lax.broadcasted_iota(jnp.int32, shape, 1)
    mask = jnp.where(lax.rem(pos, run) < live, 0.0, masked_score)
    tile = jnp.where(index == 0, mask, jnp.where(index < 4, 1.0, 0.0))
    both = keys.astype(f32)
    return jnp.concatenate([both, both, tile], 0)


def three_parts(row):
    top = row.astype(bf16).astype(f32)
    rest = row - top
    mid = rest.astype(bf16).astype(f32)
    return top, mid, rest - mid


def attend_kernel(
    run,
    key_block,
    len_ref,
    q_ref,
    k_ref,
    v_ref,
    up_ref,
    down_ref,
    o_ref,
    lse_ref,
    up_out,
    down_out,
    kaug,
    qaug,
    vaug,
    up_land,
    down_land,
    *sems,
):
    dim, length = q_ref.shape
    here = places()
    steps = shard_gather(here, up_land, down_land, sems)
    head = pl.program_id(0)

    @pl.when(head == 0)
    def _():
        greet(*here)
        place_shards(here, up_ref[:, -up_land.shape[3] :], down_ref[...], up_land, down_land)

    @pl.when(head == 1)
    def _():
        met(*here)
        steps[0]()

    pl.when(head == 3)(steps[1])
    pl.when(head == 5)(steps[2])

    @pl.when(head == 7)
    def _():
        steps[3]()
        land_out(up_land, down_land, up_out, down_out)

    live = len_ref[0]
    qaug[...] = query_rows(q_ref[...], dim ** (-0.5), ()).astype(bf16)
    kaug[...] = key_rows(k_ref[...], live, run).T.astype(bf16)
    vaug[0:dim] = v_ref[...]
    index = lax.broadcasted_iota(jnp.int32, (16, length), 0)
    vaug[dim : dim + 16] = jnp.where(index == 0, 1.0, 0.0).astype(bf16)
    top = None
    for i in range(length // key_block):
        keys = slice(i * key_block, (i + 1) * key_block)
        scores = mm(kaug[keys, :], qaug[...])
        block_top = jnp.max(scores, axis=0, keepdims=True)
        new_top = block_top if top is None else jnp.maximum(top, block_top)
        weights = jnp.exp2(scores - new_top).astype(bf16)
        part = mm(vaug[:, keys], weights)
        total = part if top is None else total * jnp.exp2(top - new_top) + part
        top = new_top
    summed = total[dim : dim + 1]
    o_ref[...] = total[0:dim] / summed
    lse_ref[0] = top + jnp.log2(summed)


def attend_back_kernel(
    run,
    block,
    len_ref,
    q_ref,
    k_ref,
    v_ref,
    lse_ref,
    o_ref,
    do_ref,
    early_ref,
    wide_ref,
    down_ref,
    dq_ref,
    dk_ref,
    dv_ref,
    early_out,
    wide_out,
    down_out,
    kaug,
    qaug,
    vaug,
    daug,
    early_land,
    pair,
    other,
    from_dp,
    summed,
    from_z,
    send,
    recv,
    wide_land,
    down_land,
    *sems,
):
    dim, length = q_ref.shape
    here = places()
    head = pl.program_id(0)
    gathers = shard_gather(here, wide_land, down_land, sems)
    totals = plan_total(
        here, early_ref, early_land, pair, other, from_dp, summed, from_z, (send, recv)
    )

    @pl.when(head == 0)
    def _():
        greet(*here)
        place_shards(here, wide_ref[...], down_ref[...], wide_land, down_land)

    @pl.when(head == 1)
    def _():
        met(*here)
        totals[0]()

    for place in range(2, 5):

        @pl.when(head == place)
        def _(place=place):
            totals[place - 1]()
            gathers[place - 2]()

    @pl.when(head == 5)
    def _():
        totals[4]()
        gathers[3]()
        land_out(wide_land, down_land, wide_out, down_out)

    pl.when(head == 7)(totals[5])

    factor = dim ** (-0.5)
    qaug[...] = query_rows(q_ref[...], factor, three_parts(-lse_ref[0])).T.astype(bf16)
    kaug[...] = key_rows(k_ref[...], len_ref[0], run).astype(bf16)
    index = lax.broadcasted_iota(jnp.int32, (128 - dim, length), 0)
    tile = jnp.where(index < 3, -1.0, 0.0)
    vaug[...] = jnp.concatenate([v_ref[...].astype(f32), tile], 0).astype(bf16)
    back = do_ref[...].astype(f32)
    tile = jnp.zeros((128 - dim, length), f32)
    for place, row in enumerate(three_parts(col_sum(back * o_ref[...]))):
        tile = jnp.where(index == place, jnp.broadcast_to(row, tile.shape), tile)
    daug[...] = jnp.concatenate([back, tile], 0).T.astype(bf16)

    dk = dv = None
    for i in range(length // block):
        rows = slice(i * block, (i + 1) * block)
        weights = jnp.exp2(mm(qaug[rows, :], kaug[...]))
        raw = (weights * mm(daug[rows, :], vaug[...])).astype(bf16)
        dv_part = mm(do_ref[:, rows], weights.astype(bf16))
        dk_part = mm(q_ref[:, rows], raw)
        dv = dv_part if dv is None else dv + dv_part
        dk = dk_part if dk is None else dk + dk_part
        dq_ref[:, rows] = (mm_nt(k_ref[...], raw) * factor).astype(bf16)
    dk_ref[...] = (dk * factor).astype(bf16)
    dv_ref[...] = dv.astype(bf16)

    @pl.when(head == HEADS - 1)
    def _():
        totals[6]()
        early_out[...] = early_land[...]


def middle_kernel(
    run,
    len_ref,
    mixed_ref,
    one_ref,
    first_ref,
    up_ref,
    down_ref,
    vec_ref,
    headw_ref,
    noiT_ref,
    two_grad_ref,
    do_ref,
    early_ref,
    small_ref,
    hidden,
    slope,
    xhat,
    spread,
    three,
    prod,
    gcols,
    normed_t,
    three_t,
    gpre,
    glow,
    head_ref,
):
    rows_n, channels = one_ref.shape
    units = down_ref.shape[0]
    latent_ch = noiT_ref.shape[0]
    count = rows_n // CHUNK
    live = len_ref[0]
    segs = offsets(channels, EMB, units, latent_ch)

    def seg(index):
        start, length = segs[index]
        return vec_ref[start : start + length].reshape(1, length)

    w_out = first_ref[:, 3 * channels :]
    for tap in range(9):
        first = swap_tap(tap) * channels
        prod[tap * latent_ch : (tap + 1) * latent_ch, 0:channels] = headw_ref[
            :, first : first + channels
        ]
    prod[9 * latent_ch :, 0:channels] = jnp.zeros((prod.shape[0] - 9 * latent_ch, channels), f32)
    head_ref[...] = prod[:, 0:channels].astype(bf16)
    index = lax.broadcasted_iota(jnp.int32, (latent_ch, latent_ch), 0)
    same = index == lax.broadcasted_iota(jnp.int32, (latent_ch, latent_ch), 1)
    head_bias = jnp.sum(jnp.where(same, seg(17), 0.0), axis=1, keepdims=True)
    proj_bias, gain, shift, up_bias, down_bias = seg(8), seg(9), seg(10), seg(16), seg(11)

    def fore(i, carry):
        start = pl.multiple_of(i * CHUNK, CHUNK)
        rows = pl.ds(start, CHUNK)
        mixed = mixed_ref[:, rows].T.astype(bf16)
        stream = one_ref[rows, :] + mm(mixed, w_out) + proj_bias
        gap = stream - row_mean(stream)
        scale = lax.rsqrt(row_mean(gap * gap) + norm_floor)
        hat = gap * scale
        xhat[rows, :] = hat
        spread[rows, :] = jnp.broadcast_to(scale, (CHUNK, spread.shape[1]))
        normed = (hat * gain + shift).astype(bf16)
        normed_t[:, rows] = normed.T
        pre = mm(normed, up_ref[...]) + up_bias
        phi = 0.5 * lax.erf(pre * (0.5**0.5)) + 0.5
        slope[rows, :] = phi + pre * jnp.exp2(
            pre * pre * (-0.5 * LOG2E) + 0.5 * math.log2(0.5 / math.pi)
        )
        low = (pre * phi).astype(bf16)
        hidden[rows, :] = low
        stream = stream + mm(low, down_ref[...]) + down_bias
        stream = jnp.where(live_rows(stream.shape, live, run), stream, 0.0).astype(bf16)
        three[rows, :] = stream
        prod[:, rows] = mm_nt(head_ref[...], stream)
        return carry

    loop(count, fore, 0)

    taps = 9 * latent_ch
    predicted = jnp.zeros((latent_ch, rows_n), f32) + head_bias
    for a in range(3):
        for b in range(3):
            tap = 3 * a + b
            predicted = predicted + tap_shift(
                prod[tap * latent_ch : (tap + 1) * latent_ch], a, b, run
            )
    pos = lax.broadcasted_iota(jnp.int32, predicted.shape, 1)
    errors = jnp.where(lax.rem(pos, run) < live, predicted - noiT_ref[...], 0.0)
    small_ref[...] = jnp.zeros(small_ref.shape, f32)
    tile = (latent_ch, 128)
    sums = jnp.broadcast_to(jnp.sum(errors, axis=1, keepdims=True), tile)
    same = lax.broadcasted_iota(jnp.int32, tile, 0) == lax.broadcasted_iota(jnp.int32, tile, 1)
    put_small(small_ref, 17, col_sum(jnp.where(same, sums, 0.0)))
    sums = jnp.broadcast_to(jnp.sum(errors * errors, axis=1, keepdims=True), tile)
    put_small(small_ref, 18, col_sum(sums))
    put_small(small_ref, 19, jnp.zeros((1, 128), f32) + (live * (rows_n // run)).astype(f32))
    errors = errors.astype(bf16).astype(f32)
    for a in range(3):
        for b in range(3):
            tap = 3 * a + b
            prod[tap * latent_ch : (tap + 1) * latent_ch] = tap_shift(
                errors, 2 - a, 2 - b, run
            )
    prod[taps:] = jnp.zeros((prod.shape[0] - taps, rows_n), f32)
    gcols[...] = prod[...].T.astype(bf16)
    ghead = mm(prod[0:taps].astype(bf16), three[...])

    def back(i, carry):
        g_down, g_up, g_gain, g_shift, g_proj = carry
        start = pl.multiple_of(i * CHUNK, CHUNK)
        rows = pl.ds(start, CHUNK)
        grad = mm(gcols[rows, :], head_ref[...])
        grad = jnp.where(live_rows(grad.shape, live, run), grad, 0.0)
        low = grad.astype(bf16)
        three_t[:, rows] = low.T
        pre = mm_nt(low, down_ref[...]) * slope[rows, :]
        pre_low = pre.astype(bf16)
        gpre[rows, :] = pre_low
        dnormed = mm_nt(pre_low, up_ref[...])
        hat = xhat[rows, :]
        dhat = dnormed * gain
        dstream = (dhat - row_mean(dhat) - hat * row_mean(dhat * hat)) * spread[rows, 0:1]
        two = grad + dstream
        two_grad_ref[rows, :] = two
        two_low = two.astype(bf16)
        glow[rows, :] = two_low
        do_ref[:, rows] = mm_nt(w_out, two_low).astype(bf16)
        return (
            g_down + col_sum(grad),
            g_up + col_sum(pre),
            g_gain + col_sum(dnormed * hat),
            g_shift + col_sum(dnormed),
            g_proj + col_sum(two),
        )

    blank = jnp.zeros((1, channels), f32)
    sums = loop(count, back, (blank, jnp.zeros((1, units), f32), blank, blank, blank))
    for index, value in zip((11, 16, 9, 10, 8), sums):
        put_small(small_ref, index, value)
    half = units // 2
    for part in range(units // channels):
        columns = slice(part * channels, (part + 1) * channels)
        first = (part * channels) % half
        lanes = slice((part * channels) // half * channels, (part * channels) // half * channels + channels)
        early_ref[first : first + channels, lanes] = mm(three_t[...], hidden[:, columns]).T.astype(
            bf16
        )
        first = half + (part // 2) * channels
        lanes = slice((part % 2) * channels, (part % 2 + 1) * channels)
        early_ref[first : first + channels, lanes] = mm(normed_t[...], gpre[:, columns]).astype(
            bf16
        )
    gproj = mm(mixed_ref[...].astype(bf16), glow[...]).astype(bf16)
    first = half + (units // channels // 2) * channels
    middle = channels // 2
    early_ref[first : first + middle, 0:channels] = gproj[:middle]
    early_ref[first : first + middle, channels:] = gproj[middle:]
    first = first + middle
    ghead = swap_taps(ghead).astype(bf16)
    middle = taps // 2
    early_ref[first : first + middle, 0:channels] = ghead[:middle]
    early_ref[first : first + middle, channels:] = ghead[middle:]
    early_ref[first + middle :, :] = jnp.zeros(
        (early_ref.shape[0] - first - middle, 2 * channels), bf16
    )


def hind_kernel(
    run,
    groups,
    len_ref,
    step_ref,
    dq_any,
    dk_any,
    dv_any,
    two_grad_any,
    normed_any,
    one_any,
    act_two_any,
    inner_any,
    act_one_any,
    zero_any,
    colsT_any,
    stat_ref,
    film_ref,
    conv_any,
    wide_any_w,
    time_any,
    vec_ref,
    mid_ref,
    early_any,
    wide_any,
    down_any,
    small_any,
    root_any,
    large_any,
    conv_out,
    tile_out,
    time_out,
    scalar_out,
    head_out,
    wide_out,
    wide_dir,
    down_out,
    down_dir,
    buf,
    field,
    other,
    act_t,
    small,
    everyone,
    tiles,
    tile_o,
    tile_p,
    tile_d,
    tile_f,
    tile_z,
    tile_s,
    tile_r,
    tile_as,
    tile_ar,
    squares,
    product,
    first_g,
    first_o,
    first_p,
    first_d,
    first_f,
    first_z,
    first_t,
    first_s,
    first_r,
    second_g,
    second_o,
    second_p,
    second_d,
    second_f,
    second_z,
    second_t,
    second_s,
    second_r,
    qkv_g,
    qkv_o,
    qkv_p,
    qkv_d,
    qkv_f,
    qkv_z,
    qkv_t,
    qkv_s,
    qkv_r,
    spread_s,
    spread_r,
    clip_s,
    clip_r,
    square_s,
    square_r,
    qkv_out,
    early,
    wide_full,
    down_full,
    roots_small,
    root_wide,
    root_large,
    root_rows,
    local_sems,
    dq_ref,
    dk_ref,
    dv_ref,
    normed_ref,
    wide_ref,
    two_grad_ref,
    one_ref,
    act_two_ref,
    inner_ref,
    conv_ref,
    time_ref,
    act_one_ref,
    zero_ref,
    colsT_ref,
    load_sems,
):
    rows_n, channels = one_ref.shape
    embed = time_ref.shape[2]
    latent_ch = colsT_ref.shape[0] // 9
    count = rows_n // CHUNK
    live = len_ref[0]
    counted = (live * (rows_n // run) * (channels // groups)).astype(f32)
    segs = offsets(channels, embed, FF, latent_ch)
    blank = jnp.zeros((1, channels), f32)
    small[...] = jnp.zeros(small.shape, f32)
    here = places()
    n_d, n_z, d, z, c = here
    conv_plans = (
        plan_owner(here, first_g, first_o, first_p, first_d, first_f, first_z, first_t, (first_s, first_r)),
        plan_owner(here, second_g, second_o, second_p, second_d, second_f, second_z, second_t, (second_s, second_r)),
    )
    qkv_plan = plan_owner(here, qkv_g, qkv_o, qkv_p, qkv_d, qkv_f, qkv_z, qkv_t, (qkv_s, qkv_r))
    spread_plan = plan_spread(here, qkv_out, (spread_s, spread_r))
    clip_plan = plan_clips(here, everyone, (clip_s, clip_r))
    tile_plan = plan_small(
        here,
        tiles,
        tile_out,
        tile_o,
        tile_p,
        tile_d,
        tile_f,
        tile_z,
        (tile_s, tile_r, tile_as, tile_ar),
    )
    square_plan = plan_scalar(here, squares, (square_s, square_r))
    own_rows = root_rows.shape[0]
    loads = [
        pltpu.make_async_copy(src, dst, local_sems.at[index])
        for index, (src, dst) in enumerate(
            (
                (early_any, early),
                (wide_any, wide_full),
                (down_any, down_full),
                (small_any, roots_small),
                (root_any, root_wide),
                (large_any.at[0], root_large),
                (large_any.at[1, pl.ds(lax.axis_index("fsdp") * own_rows, own_rows)], root_rows),
            )
        )
    ]
    first_loads = {
        id(ref): pltpu.make_async_copy(src, ref, load_sems.at[index])
        for index, (src, ref) in enumerate(
            (
                (dq_any, dq_ref),
                (dk_any, dk_ref),
                (dv_any, dv_ref),
                (normed_any, normed_ref),
                (wide_any_w, wide_ref),
                (two_grad_any, two_grad_ref),
                (one_any, one_ref),
                (act_two_any, act_two_ref),
                (inner_any, inner_ref),
                (conv_any, conv_ref),
                (time_any, time_ref),
                (act_one_any, act_one_ref),
                (zero_any, zero_ref),
                (colsT_any, colsT_ref),
            )
        )
    }
    greet_all(here)
    starts(first_loads.values())
    starts(loads)

    def ready(*refs):
        for ref in refs:
            first_loads[id(ref)].wait()

    ready(dq_ref, dk_ref, dv_ref, normed_ref)

    def seg(index):
        start, length = segs[index]
        return vec_ref[start : start + length].reshape(1, length)

    def put_vec(index, value):
        put_small(small, index, value)

    half = channels // 2
    store_rows(qkv_g, 0, 0, mm(dq_ref[...], normed_ref[...]).T.astype(bf16))
    store_rows(qkv_g, 0, channels, mm(dk_ref[...], normed_ref[...]).T.astype(bf16))
    values_grad = mm(dv_ref[...], normed_ref[...]).T.astype(bf16)
    store_rows(qkv_g, channels, 0, values_grad[:half])
    store_rows(qkv_g, channels, channels, values_grad[half:])
    met_all(here)
    qkv_plan[0]()

    ready(wide_ref, two_grad_ref, one_ref)
    gain_one = seg(6)
    clear_ends(buf, rows_n, run)

    def norm_part(i, carry):
        g_gain, g_shift, g_bias = carry
        start = pl.multiple_of(i * CHUNK, CHUNK)
        rows = pl.ds(start, CHUNK)
        dnormed_t = None
        for part, ref in enumerate((dq_ref, dk_ref, dv_ref)):
            term = mm(wide_ref[:, part * channels : (part + 1) * channels], ref[:, rows])
            dnormed_t = term if dnormed_t is None else dnormed_t + term
        dnormed = dnormed_t.T
        stream = one_ref[rows, :]
        gap = stream - row_mean(stream)
        scale = lax.rsqrt(row_mean(gap * gap) + norm_floor)
        hat = gap * scale
        dhat = dnormed * gain_one
        grad = two_grad_ref[rows, :] + scale * (
            dhat - row_mean(dhat) - hat * row_mean(dhat * hat)
        )
        field[rows, :] = grad
        put_shifted(buf, start, grad.astype(bf16).astype(f32), run)
        return (
            g_gain + col_sum(dnormed * hat),
            g_shift + col_sum(dnormed),
            g_bias + col_sum(grad),
        )

    sums = loop(count, norm_part, (blank, blank, blank), ((1, qkv_plan[1]),))
    for index, value in zip((6, 7, 5), sums):
        put_vec(index, value)

    def weight_grad(which, act_ref):
        act_t[...] = act_ref[...].T
        for a in range(3):
            full = buf[run * (2 - a) : run * (2 - a) + rows_n, :]
            for b in range(3):
                shifted = full[:, (2 - b) * channels : (3 - b) * channels]
                first = (3 * b + a) * channels
                store_folded(
                    (first_g, second_g)[which], first, mm(act_t[...], shifted).astype(bf16)
                )

    def input_grad(which, start):
        total = None
        for a in range(3):
            for b in range(3):
                first = (3 * (2 - a) + 2 - b) * channels
                part = mm_nt(
                    buf[
                        pl.ds(start + run * a, CHUNK),
                        b * channels : (b + 1) * channels,
                    ],
                    conv_ref[which, first : first + channels, :],
                )
                total = part if total is None else total + part
        return total

    def norm_back(which, read, center, scale, gain, shift, g_refs, hooks):
        def part(i, carry):
            g_gain, g_shift = carry
            start = pl.multiple_of(i * CHUNK, CHUNK)
            rows = pl.ds(start, CHUNK)
            hat = (read(start) - center) * scale
            slope = silu_slope(hat * gain + shift)
            grad = input_grad(which, start) * slope
            grad = jnp.where(live_rows(grad.shape, live, run), grad, 0.0)
            other[rows, :] = grad
            return (g_gain + col_sum(grad * hat), g_shift + col_sum(grad))

        g_gain, g_shift = loop(count, part, (blank, blank), hooks)
        put_vec(g_refs[0], g_gain)
        put_vec(g_refs[1], g_shift)
        mean_grad = group_total(g_shift * gain, groups) / counted
        mean_hat = group_total(g_gain * gain, groups) / counted

        def finish(start):
            hat = (read(start) - center) * scale
            grad = (other[pl.ds(start, CHUNK), :] * gain - mean_grad - hat * mean_hat) * scale
            return jnp.where(live_rows(grad.shape, live, run), grad, 0.0)

        return finish

    film = film_ref[0:1]
    lift = 1.0 + film[:, :channels]
    move = film[:, channels:]

    ready(act_two_ref)
    weight_grad(1, act_two_ref)
    conv_plans[1][0]()
    qkv_plan[2]()
    ready(inner_ref, conv_ref)
    finish = norm_back(
        1,
        lambda start: inner_ref[pl.ds(start, CHUNK), :] * lift + move,
        stat_ref[2:3],
        stat_ref[3:4],
        seg(3),
        seg(4),
        (3, 4),
        ((1, conv_plans[1][1]),),
    )

    qkv_plan[3]()

    def inner_part(i, carry):
        g_lift, g_move, g_bias = carry
        start = pl.multiple_of(i * CHUNK, CHUNK)
        moved = finish(start)
        grad = moved * lift
        put_shifted(buf, start, grad.astype(bf16).astype(f32), run)
        return (
            g_lift + col_sum(moved * inner_ref[pl.ds(start, CHUNK), :]),
            g_move + col_sum(moved),
            g_bias + col_sum(grad),
        )

    g_lift, g_move, g_bias = loop(count, inner_part, (blank, blank, blank))
    put_vec(2, g_bias)

    ready(act_one_ref)
    weight_grad(0, act_one_ref)
    conv_plans[0][0]()
    ready(time_ref, zero_ref, colsT_ref)
    pre_time = film_ref[1:2]
    embedding = film_ref[2:3]
    g_film = jnp.concatenate([g_lift, g_move], 1)
    g_embed = vec_mat(g_film, time_ref[2], True) * silu_slope(embedding)
    g_time = vec_mat(g_embed, time_ref[1], True) * silu_slope(pre_time)
    put_vec(13, g_time)
    put_vec(14, g_embed)
    put_vec(15, g_film)
    factors = jnp.concatenate(
        [
            time_wave(step_ref, embed),
            jax.nn.silu(pre_time),
            jax.nn.silu(embedding),
            g_time,
            g_embed,
            g_film,
            jnp.zeros((2, embed), f32),
        ],
        0,
    )
    factors = jnp.concatenate([factors[:, : embed // 2], factors[:, embed // 2 :]], 0)
    everyone[pl.ds(d, 1), pl.ds(z, 1), pl.ds(c, 1)] = factors.astype(bf16)[None, None, None]
    clip_plan[0]()
    conv_plans[1][2]()
    qkv_plan[4]()
    qkv_out[pl.ds(z, 1), pl.ds(c, 1)] = qkv_t[...][None, None]
    finish_zero = norm_back(
        0,
        lambda start: zero_ref[pl.ds(start, CHUNK), :],
        stat_ref[0:1],
        stat_ref[1:2],
        seg(0),
        seg(1),
        (0, 1),
        ((0, conv_plans[0][1]), (1, clip_plan[1])),
    )
    conv_plans[1][3]()

    def zero_part(i, carry):
        g_stem, g_bias = carry
        start = pl.multiple_of(i * CHUNK, CHUNK)
        rows = pl.ds(start, CHUNK)
        grad = field[rows, :] + finish_zero(start)
        return (g_stem + mm(colsT_ref[:, rows], grad.astype(bf16)), g_bias + col_sum(grad))

    taps = colsT_ref.shape[0]
    g_stem, g_bias = loop(count, zero_part, (jnp.zeros((taps, channels), f32), blank))
    put_vec(12, g_bias)
    used = taps // 8 * (channels // 128)
    put_tiles(tiles, 0, swap_taps(g_stem))
    put_tiles(tiles, used, small[...] + mid_ref[...])
    used = used + 2 * (small.shape[1] // 128)
    for i in range(used, n_z * 2 * (tiles.shape[3] // 128)):
        tiles[tile_place(tiles, i)] = jnp.zeros((8, 128), f32)
    tile_plan[0]()
    clip_plan[2]()
    conv_plans[0][2]()
    tile_plan[1]()
    spread_plan[0]()
    conv_plans[1][4]()
    mine = lane_piece(d, n_d, 2 * channels)
    rows_c = second_t.shape[0]

    def squared(value):
        return jnp.sum(value * value)

    def unfold(which, ref):
        value = ref[...].astype(f32)
        conv_out[which, 0:rows_c] = value[:, 0:channels]
        conv_out[which, rows_c:] = value[:, channels:]

    unfold(1, second_t)
    square = squared(second_t[:, mine].astype(f32)) + squared(qkv_t[:, mine].astype(f32))

    for copy in loads:
        copy.wait()
    width = 2 * channels
    early_rows = early.shape[0] * 2 * early.shape[2]
    sums = early[...].reshape(early_rows, width)
    units = down_full.shape[0]
    half = units // 2
    shared = squared(sums.astype(f32))

    def choose(rows, order):
        own = lax.broadcasted_iota(jnp.int32, (rows, order), 0) + (2 * z + c) * rows
        return jnp.where(
            own == lax.broadcasted_iota(jnp.int32, (rows, order), 1), 1.0, 0.0
        ).astype(bf16)

    pick = choose(wide_out.shape[0], channels)

    def apply(left, value, right_root):
        return mm(mm(left, value).astype(bf16), right_root.astype(bf16))

    def side_by_side(first, rows):
        return jnp.concatenate([sums[first : first + rows], sums[first + rows : first + 2 * rows]], 1)

    def stacked(first, rows):
        block = sums[first : first + rows]
        return jnp.concatenate([block[:, :channels], block[:, channels:]], 0)

    first = half + 2 * channels
    head_first = first + channels // 2
    head_out[...] = stacked(head_first, taps // 2).astype(f32)
    lefts = [mm(pick, roots_small[i].astype(bf16)).astype(bf16) for i in range(3)]
    q_end, o_end = 3 * channels, 4 * channels
    momentum = {}
    later = {}
    for index, (grad, right_root, start, end) in enumerate(
        (
            (None, root_wide, 0, q_end),
            (stacked(first, channels // 2), roots_small.at[3], q_end, o_end),
            (side_by_side(half, channels), root_large, o_end, o_end + units),
        )
    ):
        wide_dir[:, start:end] = 0.9 * apply(
            lefts[index], wide_full[:, start:end], right_root[...]
        )
        if grad is not None:
            wide_out[:, start:end] = mm(pick, grad)
            later[start, end] = apply(lefts[index], grad, right_root[...])
    grad = stacked(0, half)
    rows = root_rows[...].astype(bf16)
    down_out[...] = mm(choose(down_out.shape[0], units), grad)
    later_down = apply(rows, grad, roots_small[4])
    down_dir[...] = 0.9 * apply(rows, down_full[...], roots_small[4])

    tile_plan[2]()
    clip_plan[3]()
    clips = 2 * n_d * n_z
    depth = time_out.shape[1]
    first = (2 * z + c) * depth
    block = pl.ds(pl.multiple_of(lax.rem(first, embed // 2) // 128 * 128, 128), 128)
    offset = pl.multiple_of(lax.rem(first, 128), 8)
    upper = first >= embed // 2
    time_square = jnp.zeros((), f32)
    for i in range(3):
        sides = [
            everyone[:, :, :, :, block].astype(f32).reshape(clips, 16, 128)[:, part + i]
            for part in (0, 8)
        ]
        left = jnp.where(upper, sides[1], sides[0])
        full = everyone[...].astype(f32).reshape(clips, 16, embed // 2)
        right = jnp.concatenate([full[:, i + 3], full[:, i + 11]], 1)
        product[...] = mm(left.T.astype(bf16), right.astype(bf16))
        value = product[pl.ds(offset, depth), :]
        time_out[i] = value
        time_square = time_square + squared(value)
    square = square + time_square / n_d
    conv_plans[0][3]()
    square = square + squared(first_t[:, mine].astype(f32))
    tile_plan[3]()
    own = tile_out[pl.ds(z, 1), pl.ds(c, 1), :, mine][0, 0]
    row = lax.broadcasted_iota(jnp.int32, own.shape, 0)
    tile_number = (2 * z + c) * n_d + d
    second = tile_number - taps // 8 * (channels // 128) >= width // 128
    square = square + squared(
        jnp.where(jnp.logical_and(second, row >= 13 - 8), 0.0, own)
    )
    lane = lax.broadcasted_iota(jnp.int32, (1, 1, 128), 2)
    loss_live = mid_ref[13:15, 0:1]
    message = jnp.where(
        lane == 0, square, jnp.where(lane == 1, loss_live[0:1][None], loss_live[1:2][None])
    )
    squares[pl.ds(d * 2 * n_z + 2 * z + c, 1)] = message
    square_plan[0]()
    spread_plan[1]()
    spread_plan[2]()
    qkv_sum = qkv_out[...].reshape(channels + channels // 2, width)
    tail = qkv_sum[channels:]
    grad = jnp.concatenate(
        [qkv_sum[:channels], jnp.concatenate([tail[:, :channels], tail[:, channels:]], 0)], 1
    )
    wide_out[:, 0:q_end] = mm(pick, grad)
    later[0, q_end] = apply(lefts[0], grad, root_wide[...])
    conv_plans[0][4]()
    unfold(0, first_t)
    total = square_plan[1]()
    unit = 2.0 / (latent_ch * total[:, 2:3])
    norm = unit * jnp.sqrt(total[:, 0:1] + shared)
    factor = jnp.minimum(1.0, clip_limit / norm) * unit
    row = lax.broadcasted_iota(jnp.int32, scalar_out.shape, 0)
    loss = total[:, 1:2] * (0.5 * unit)
    scalar_out[...] = jnp.where(row == 0, loss, jnp.where(row == 1, norm, factor))
    factor = factor[0:1, 0:1]
    tile_plan[4]()
    for (start, end), value in later.items():
        wide_dir[:, start:end] += factor * value
    down_dir[...] += factor * later_down


def sized(shape, dtype=f32):
    return jax.ShapeDtypeStruct(shape, dtype)


VM = pl.BlockSpec(memory_space=pltpu.VMEM)
SM = pl.BlockSpec(memory_space=pltpu.SMEM)
ANY = pl.BlockSpec(memory_space=pl.ANY)


def params(mib):
    return pltpu.CompilerParams(vmem_limit_bytes=mib * 2**20)


def remote_params(number, mib):
    return pltpu.CompilerParams(
        collective_id=number, has_side_effects=True, vmem_limit_bytes=mib * 2**20
    )


def run_fore(run, length, step, lat, noi, stem_w, conv_w, wide_w, time_w, vec, clap):
    channels = stem_w.shape[1]
    latent_ch = stem_w.shape[0] // 9
    rows_n = lat.shape[1] * (lat.shape[0] // latent_ch)
    embed = time_w.shape[2]
    n_z = lax.axis_size("fsdp") // 2
    field = (rows_n, channels)
    land = pltpu.VMEM((n_z, 2, conv_w.shape[1] // 2, 2 * channels), bf16)
    large = [
        sized(field),
        sized(field, bf16),
        sized(field),
        sized(field, bf16),
        sized(field),
        sized(field, bf16),
        sized((3 * channels, rows_n), bf16),
    ]
    weights = [
        sized((2, 9 * channels, channels), bf16),
        sized((3, n_z, 2) + time_w.shape[1:], bf16),
        sized((n_z, 2, wide_w.shape[0], 4 * channels), bf16),
    ]
    outs = pl.pallas_call(
        functools.partial(fore_kernel, run, GROUPS),
        in_specs=[SM, SM] + [VM] * 8,
        out_specs=[ANY] * 7 + [VM] * 4 + [ANY] * 3,
        out_shape=large
        + [
            sized((9 * latent_ch, rows_n), bf16),
            sized((latent_ch, rows_n)),
            sized((8, channels)),
            sized((8, embed)),
        ]
        + weights,
        scratch_shapes=[
            pltpu.VMEM((rows_n + 2 * run, 3 * channels), bf16),
            pltpu.VMEM((rows_n, 128), bf16),
            pltpu.VMEM((128, rows_n), f32),
            land,
            land,
        ]
        + [pltpu.VMEM(item.shape, item.dtype) for item in large + weights]
        + [pltpu.SemaphoreType.DMA((8 + 3 * max(1, rows_n // CHUNK),))]
        + gather_sems(1) * 4,
        compiler_params=remote_params(1, 62),
        name="fore",
    )(length, step, lat, noi, stem_w, conv_w, wide_w, time_w, vec, clap)
    time_full = outs[12].reshape(3, -1, embed)
    first_full = outs[13].reshape(-1, 4 * channels)
    return (*outs[:12], time_full, first_full)


def run_attend(run, length, qkv_t, up, down, key_block=256):
    n_f = lax.axis_size("fsdp")
    triple, rows_n = qkv_t.shape
    channels = triple // 3
    dim = channels // HEADS
    return pl.pallas_call(
        functools.partial(attend_kernel, run, key_block),
        grid=(HEADS,),
        in_specs=[SM]
        + [pl.BlockSpec((dim, rows_n), lambda h, t=t: (t * HEADS + h, 0)) for t in range(3)]
        + [VM] * 2,
        out_specs=[
            pl.BlockSpec((dim, rows_n), lambda h: (h, 0)),
            pl.BlockSpec((1, 1, rows_n), lambda h: (h, 0, 0)),
            VM,
            VM,
        ],
        out_shape=[
            sized((channels, rows_n)),
            sized((HEADS, 1, rows_n)),
            sized((up.shape[0] * n_f, FF), bf16),
            sized((down.shape[0] * n_f, down.shape[1]), bf16),
        ],
        scratch_shapes=[
            pltpu.VMEM((rows_n, 128), bf16),
            pltpu.VMEM((128, rows_n), bf16),
            pltpu.VMEM((dim + 16, rows_n), bf16),
        ]
        + land_scratch((up.shape[0], FF), down.shape),
        compiler_params=remote_params(3, 62),
        name="attend",
    )(length, qkv_t, qkv_t, qkv_t, up, down)


def run_attend_back(
    run, length, qkv_t, lse, mixed_t, grad_t, early, wide, down, block=256
):
    n_f = lax.axis_size("fsdp")
    early = early.reshape(n_f // 2, 2, early.shape[0] // n_f, early.shape[1])
    triple, rows_n = qkv_t.shape
    channels = triple // 3
    dim = channels // HEADS
    whole = pl.BlockSpec((dim, rows_n), lambda h: (h, 0))
    return pl.pallas_call(
        functools.partial(attend_back_kernel, run, block),
        grid=(HEADS,),
        in_specs=[SM]
        + [pl.BlockSpec((dim, rows_n), lambda h, t=t: (t * HEADS + h, 0)) for t in range(3)]
        + [pl.BlockSpec((1, 1, rows_n), lambda h: (h, 0, 0)), whole, whole]
        + [VM] * 3,
        out_specs=[whole] * 3 + [VM] * 3,
        out_shape=[sized((channels, rows_n), bf16)] * 3
        + [
            sized(early.shape, bf16),
            sized((wide.shape[0] * n_f, wide.shape[1]), bf16),
            sized((down.shape[0] * n_f, down.shape[1]), bf16),
        ],
        scratch_shapes=[
            pltpu.VMEM((128, rows_n), bf16),
            pltpu.VMEM((rows_n, 128), bf16),
            pltpu.VMEM((128, rows_n), bf16),
            pltpu.VMEM((rows_n, 128), bf16),
        ]
        + total_scratch(early.shape[2], early.shape[3], bf16)
        + land_scratch(wide.shape, down.shape),
        compiler_params=remote_params(4, 62),
        name="attend_back",
    )(length, qkv_t, qkv_t, qkv_t, lse, mixed_t, grad_t, early, wide, down)


def run_middle(run, length, mixed_t, one, first, up, down, vec, head_w, noi_t):
    rows_n, channels = one.shape
    units = down.shape[0]
    latent_ch = noi_t.shape[0]
    return pl.pallas_call(
        functools.partial(middle_kernel, run),
        in_specs=[SM] + [VM] * 8,
        out_specs=[VM] * 4,
        out_shape=[
            sized((rows_n, channels)),
            sized((channels, rows_n), bf16),
            sized((units + channels, 2 * channels), bf16),
            sized((16, 2 * channels)),
        ],
        scratch_shapes=[
            pltpu.VMEM((rows_n, units), bf16),
            pltpu.VMEM((rows_n, units), f32),
            pltpu.VMEM((rows_n, channels), f32),
            pltpu.VMEM((rows_n, 128), f32),
            pltpu.VMEM((rows_n, channels), bf16),
            pltpu.VMEM((128, rows_n), f32),
            pltpu.VMEM((rows_n, 128), bf16),
            pltpu.VMEM((channels, rows_n), bf16),
            pltpu.VMEM((channels, rows_n), bf16),
            pltpu.VMEM((rows_n, units), bf16),
            pltpu.VMEM((rows_n, channels), bf16),
            pltpu.VMEM((128, channels), bf16),
        ],
        compiler_params=params(62),
        name="middle",
    )(length, mixed_t, one, first, up, down, vec, head_w, noi_t)


def run_hind(run, length, step, *arrays):
    one = arrays[5]
    rows_n, channels = one.shape
    embed = arrays[15].shape[2]
    n_d, n_f = lax.axis_size("dp"), lax.axis_size("fsdp")
    n_z = n_f // 2
    count = n_d * n_f
    rows_c = arrays[13].shape[1] // n_f
    rows_a = (channels + channels // 2) // n_f
    dma = pltpu.SemaphoreType.DMA
    return pl.pallas_call(
        functools.partial(hind_kernel, run, GROUPS),
        in_specs=[SM, SM]
        + [ANY] * 11
        + [VM] * 2
        + [ANY] * 3
        + [VM] * 2
        + [ANY] * 6,
        out_specs=[VM] * 9,
        out_shape=[
            sized((2, rows_c, channels)),
            sized((n_z, 2, 8, 2 * channels)),
            sized((3, embed // n_f, embed)),
            sized((8, 128)),
            sized((arrays[10].shape[0], channels)),
            sized((channels // n_f, 4 * channels + FF)),
            sized((channels // n_f, 4 * channels + FF)),
            sized((FF // n_f, channels)),
            sized((FF // n_f, channels)),
        ],
        scratch_shapes=[
            pltpu.VMEM((rows_n + 2 * run, 3 * channels), bf16),
            pltpu.VMEM((rows_n, channels), f32),
            pltpu.VMEM((rows_n, channels), f32),
            pltpu.VMEM((channels, rows_n), bf16),
            pltpu.VMEM((16, 2 * channels), f32),
            pltpu.VMEM((n_d, n_z, 2, 16, embed // 2), bf16),
        ]
        + small_scratch(2 * channels)
        + [
            pltpu.VMEM((count, 1, 128), f32),
            pltpu.VMEM((128, embed), f32),
        ]
        + owner_scratch(rows_c // 2, 2 * channels)
        + owner_scratch(rows_c // 2, 2 * channels)
        + owner_scratch(rows_a, 2 * channels)
        + [
            dma((n_z,)),
            dma((n_z,)),
            dma((n_d + n_z,)),
            dma((n_d + n_z,)),
            dma((count,)),
            dma((count,)),
            pltpu.VMEM((n_z, 2, rows_a, 2 * channels), bf16),
            pltpu.VMEM(arrays[-6].shape, bf16),
            pltpu.VMEM(arrays[-5].shape, bf16),
            pltpu.VMEM(arrays[-4].shape, bf16),
            pltpu.VMEM(arrays[-3].shape, f32),
            pltpu.VMEM(arrays[-2].shape, f32),
            pltpu.VMEM(arrays[-1].shape[1:], f32),
            pltpu.VMEM((FF // n_f, FF), f32),
            dma((7,)),
        ]
        + [pltpu.VMEM(arrays[i].shape, arrays[i].dtype) for i in (0, 1, 2, 4, 14, 3, 5)]
        + [pltpu.VMEM(arrays[i].shape, arrays[i].dtype) for i in (6, 7, 13, 15, 8, 9, 10)]
        + [dma((14,))],
        compiler_params=remote_params(2, 63),
        name="hind",
    )(length, step, *arrays)


def update_kernel(
    latent_ch,
    units,
    step_ref,
    scalar_ref,
    conv_g,
    time_g,
    tiles,
    head_g,
    wide_g,
    wide_dir,
    down_g,
    down_dir,
    stem_w,
    stem_m,
    stem_s,
    head_w,
    head_m,
    head_s,
    time_w,
    time_m,
    time_s,
    vec_m,
    vec_s,
    conv_w,
    conv_m,
    conv_s,
    wide_w,
    wide_m,
    down_w,
    down_m,
    stem_out,
    stem_m_out,
    stem_s_out,
    head_out,
    head_m_out,
    head_s_out,
    time_out,
    time_m_out,
    time_s_out,
    vec_out,
    vec_m_out,
    vec_s_out,
    conv_out,
    conv_m_out,
    conv_s_out,
    wide_out,
    wide_m_out,
    down_out,
    down_m_out,
):
    taps, channels = stem_w.shape
    stem_tiles = taps // 8 * (channels // 128)
    small = take_tiles(tiles, stem_tiles, 16, 2 * channels)
    factor = scalar_ref[2:3, 0:1]
    step = jnp.zeros((1, 1), f32) + step_ref[0].astype(f32)
    one_over = 1.0 / (1.0 - jnp.exp(step * math.log(0.9)))
    two_over = 1.0 / (1.0 - jnp.exp(step * math.log(0.999)))

    def adam(outs, where, weight, first, second, grad):
        grad = factor * grad
        first_new = 0.9 * first + 0.1 * grad
        second_new = 0.999 * second + 0.001 * grad * grad
        moved = first_new * one_over / (jnp.sqrt(second_new * two_over) + adam_floor)
        outs[0][where] = weight - adam_rate * (moved + decay_rate * weight)
        outs[1][where] = first_new
        outs[2][where] = second_new

    whole = slice(None)
    adam(
        (stem_out, stem_m_out, stem_s_out),
        whole,
        stem_w[...],
        stem_m[...],
        stem_s[...],
        take_tiles(tiles, 0, taps, channels),
    )
    outs = (time_out, time_m_out, time_s_out)
    for i in range(time_w.shape[0]):
        adam(outs, i, time_w[i], time_m[i], time_s[i], time_g[i])
    outs = (conv_out, conv_m_out, conv_s_out)
    for i in range(conv_w.shape[0]):
        adam(outs, i, conv_w[i], conv_m[i], conv_s[i], conv_g[i])
    outs = (head_out, head_m_out, head_s_out)
    for tap in range(9):
        where = (whole, slice(tap * channels, (tap + 1) * channels))
        grad = head_g[tap * latent_ch : (tap + 1) * latent_ch]
        adam(outs, where, head_w[where], head_m[where], head_s[where], grad)

    def vec_grad(which):
        if which < 13:
            lane = (which % 2) * channels
            return small[which // 2 : which // 2 + 1, lane : lane + channels]
        if which < 16:
            return small[which - 6 : which - 5]
        if which == 16:
            return jnp.concatenate([small[10:11], small[11:12]], 1)
        return small[12:13, 0:latent_ch]

    for which, (first, length) in enumerate(
        offsets(channels, 2 * channels, units, latent_ch)
    ):
        where = slice(first, first + length)
        grad = (factor * vec_grad(which)).reshape(length)
        vec_out[where] = grad
        vec_m_out[where] = 0.9 * vec_m[where] + 0.1 * grad
        vec_s_out[where] = 0.999 * vec_s[where] + 0.001 * grad * grad

    kept = 1.0 - shampoo_rate * decay_rate
    wide_m_out[...] = 0.9 * wide_m[...] + factor * wide_g[...]
    wide_out[...] = wide_w[...] * kept - shampoo_rate * wide_dir[...]
    down_m_out[...] = 0.9 * down_m[...] + factor * down_g[...]
    down_out[...] = down_w[...] * kept - shampoo_rate * down_dir[...]


def run_update(latent_ch, step, *arrays):
    stem_w, head_w, time_w, vec_m = arrays[9], arrays[12], arrays[15], arrays[18]
    conv_w, wide_w, down_w = arrays[20], arrays[23], arrays[25]
    shapes = [stem_w.shape] * 3 + [head_w.shape] * 3 + [time_w.shape] * 3
    shapes += [vec_m.shape] * 3 + [conv_w.shape] * 3 + [wide_w.shape] * 2 + [down_w.shape] * 2
    return pl.pallas_call(
        functools.partial(update_kernel, latent_ch, FF),
        in_specs=[SM] + [VM] * len(arrays),
        out_specs=[VM] * len(shapes),
        out_shape=[sized(shape) for shape in shapes],
        compiler_params=params(62),
        name="update",
    )(step, *arrays)


def local(
    latents,
    noises,
    clap_embed,
    timesteps,
    lengths,
    step_count,
    stem_w,
    head_w,
    time_w,
    vector,
    conv_w,
    wide_w,
    down_w,
    roots_small,
    root_wide,
    roots_large,
    stem_moment,
    stem_square,
    head_moment,
    head_square,
    time_moment,
    time_square,
    vector_moment,
    vector_square,
    conv_moment,
    conv_square,
    wide_moment,
    down_moment,
):
    frames_n, freq_bins, latent_ch = (latents.shape[1], latents.shape[2], latents.shape[3])
    channels = stem_w.shape[1]
    def by_bins(value):
        return value[0].transpose(1, 2, 0).reshape(freq_bins * latent_ch, frames_n)

    head_t = head_w.T
    (
        zero,
        act_one,
        inner,
        act_two,
        one,
        normed,
        qkv_t,
        cols_t,
        noi_t,
        stat,
        film,
        conv_full,
        time_full,
        first_full,
    ) = run_fore(
        frames_n,
        lengths,
        timesteps,
        by_bins(latents),
        by_bins(noises),
        stem_w,
        conv_w,
        wide_w,
        time_w,
        vector,
        clap_embed,
    )
    mixed_t, lse, up_full, down_full = run_attend(
        frames_n, lengths, qkv_t, wide_w, down_w
    )
    two_grad, do_t, early, small = run_middle(
        frames_n,
        lengths,
        mixed_t,
        one,
        first_full,
        up_full,
        down_full,
        vector,
        head_t,
        noi_t,
    )
    dq, dk, dv, early, wide_moment_full, down_moment_full = run_attend_back(
        frames_n, lengths, qkv_t, lse, mixed_t, do_t, early, wide_moment, down_moment
    )
    outs = run_hind(
        frames_n,
        lengths,
        timesteps,
        dq,
        dk,
        dv,
        two_grad,
        normed,
        one,
        act_two,
        inner,
        act_one,
        zero,
        cols_t,
        stat,
        film,
        conv_full,
        first_full,
        time_full,
        vector,
        small,
        early,
        wide_moment_full,
        down_moment_full,
        roots_small,
        root_wide,
        roots_large,
    )
    conv_sum, tiles, time_sum, scalars, head_sum, wide_sum, wide_dir, down_sum, down_dir = outs
    outs = run_update(
        latent_ch,
        step_count,
        scalars,
        conv_sum,
        time_sum,
        tiles,
        head_sum,
        wide_sum,
        wide_dir,
        down_sum,
        down_dir,
        stem_w,
        stem_moment,
        stem_square,
        head_t,
        head_moment.T,
        head_square.T,
        time_w,
        time_moment,
        time_square,
        vector_moment,
        vector_square,
        conv_w,
        conv_moment,
        conv_square,
        wide_w,
        wide_moment,
        down_w,
        down_moment,
    )
    outs = list(outs)
    for index in (3, 4, 5):
        outs[index] = outs[index].T
    return (scalars[0, 0], scalars[1, 0], *outs)


def solution(mesh):
    in_specs = (
        P(("dp", "fsdp"), None, None, None),
        P(("dp", "fsdp"), None, None, None),
        P(("dp", "fsdp"), None),
        P(("dp", "fsdp")),
        P(("dp", "fsdp")),
        P(),
        P(),
        P(),
        P(None, "fsdp", None),
        P(),
        P(None, "fsdp", None),
        P("fsdp", None),
        P("fsdp", None),
        P(),
        P(),
        P(),
        P(),
        P(),
        P(),
        P(),
        P(None, "fsdp", None),
        P(None, "fsdp", None),
        P(),
        P(),
        P(None, "fsdp", None),
        P(None, "fsdp", None),
        P("fsdp", None),
        P("fsdp", None),
    )
    out_specs = (
        P(),
        P(),
        P(),
        P(),
        P(),
        P(),
        P(),
        P(),
        P(None, "fsdp", None),
        P(None, "fsdp", None),
        P(None, "fsdp", None),
        P(),
        P(),
        P(),
        P(None, "fsdp", None),
        P(None, "fsdp", None),
        P(None, "fsdp", None),
        P("fsdp", None),
        P("fsdp", None),
        P("fsdp", None),
        P("fsdp", None),
    )
    return jax.shard_map(local, mesh=mesh, in_specs=in_specs, out_specs=out_specs, check_vma=False)
```

```python
import functools
import math

import jax
import jax.numpy as jnp
from jax import lax
from jax.experimental import pallas as pl
from jax.experimental.pallas import tpu as pltpu
from jax.sharding import PartitionSpec as P

HEADS = 8
FF = 1024
EMB = 512
GROUPS = 32

norm_floor = 1e-05
masked_score = -1e30
clip_limit = 0.002
adam_rate = 0.05
adam_floor = 1e-08
shampoo_rate = 0.02
decay_rate = 0.01

f32 = jnp.float32
bf16 = jnp.bfloat16
highest = lax.Precision.HIGHEST
LOG2E = math.log2(math.e)
CHUNK = 512


def mm(left_op, right_op):
    return jnp.dot(left_op, right_op, preferred_element_type=f32)


def mm_nt(left_op, right_op):
    return lax.dot_general(
        left_op, right_op, (((1,), (1,)), ((), ())), preferred_element_type=f32
    )


def col_sum(value):
    return jnp.sum(value, axis=0, keepdims=True)


def row_mean(value):
    return jnp.mean(value, axis=-1, keepdims=True)


def loop(count, body, init, hooks=()):
    if not hooks:
        return lax.fori_loop(0, count, body, init)

    def step(i, carry):
        for place, action in hooks:
            pl.when(i == place)(action)
        return body(i, carry)

    return lax.fori_loop(0, count, step, init)


def tap_shift(field, a, b, run):
    length = field.shape[1]
    step = run * (a - 1) + (b - 1)
    if step == 0:
        return field
    pos = lax.broadcasted_iota(jnp.int32, field.shape, 1)
    bin_pos = lax.rem(pos, run)
    keep = None
    for wanted, test in (
        (a == 0, lambda: pos >= run),
        (a == 2, lambda: pos < length - run),
        (b == 0, lambda: bin_pos >= 1),
        (b == 2, lambda: bin_pos < run - 1),
    ):
        if wanted:
            keep = test() if keep is None else jnp.logical_and(keep, test())
    return jnp.where(keep, pltpu.roll(field, (-step) % length, 1), 0.0)


def put_shifted(buf, start, value, run):
    rows, channels = value.shape
    bin_pos = lax.rem(lax.broadcasted_iota(jnp.int32, value.shape, 0), run)
    before = jnp.where(bin_pos == 0, 0.0, pltpu.roll(value, 1, 0))
    after = jnp.where(bin_pos == run - 1, 0.0, pltpu.roll(value, rows - 1, 0))
    where = pl.ds(start + run, rows)
    buf[where, 0:channels] = before.astype(bf16)
    buf[where, channels : 2 * channels] = value.astype(bf16)
    buf[where, 2 * channels : 3 * channels] = after.astype(bf16)


def clear_ends(buf, rows_n, run):
    blank = jnp.zeros((run, buf.shape[1]), bf16)
    buf[0:run, :] = blank
    buf[rows_n + run : rows_n + 2 * run, :] = blank


def live_rows(shape, live, run):
    return lax.rem(lax.broadcasted_iota(jnp.int32, shape, 0), run) < live


def swap_tap(tap):
    return tap % 3 * 3 + tap // 3


def swap_taps(value, axis=0):
    size = value.shape[axis] // 9
    pieces = [
        lax.slice_in_dim(value, swap_tap(t) * size, (swap_tap(t) + 1) * size, axis=axis)
        for t in range(9)
    ]
    return jnp.concatenate(pieces, axis)


def group_total(row, groups):
    channels = row.shape[1]
    size = channels // groups
    one = lax.broadcasted_iota(jnp.int32, (channels, channels), 0) // size
    two = lax.broadcasted_iota(jnp.int32, (channels, channels), 1) // size
    same = jnp.where(one == two, 1.0, 0.0).astype(f32)
    wide = jnp.broadcast_to(row, (8, channels))
    return jnp.dot(wide, same, precision=highest, preferred_element_type=f32)[0:1]


def vec_mat(row, weight, transposed=False):
    top = row.astype(bf16).astype(f32)
    rest = row - top
    mid = rest.astype(bf16).astype(f32)
    low = rest - mid
    shape = (16, row.shape[1])
    index = lax.broadcasted_iota(jnp.int32, shape, 0)
    stacked = jnp.where(
        index == 0,
        jnp.broadcast_to(top, shape),
        jnp.where(
            index == 1,
            jnp.broadcast_to(mid, shape),
            jnp.where(index == 2, jnp.broadcast_to(low, shape), 0.0),
        ),
    ).astype(bf16)
    return col_sum(mm_nt(stacked, weight) if transposed else mm(stacked, weight))


def silu_slope(value):
    gate = jax.nn.sigmoid(value)
    return gate * (1.0 + value * (1.0 - gate))


def channel_stats(read, rows_n, live, run, channels, average):
    count = rows_n // CHUNK

    def add(i, total):
        start = pl.multiple_of(i * CHUNK, CHUNK)
        value = read(start)
        return total + col_sum(jnp.where(live_rows(value.shape, live, run), value, 0.0))

    center = average(loop(count, add, jnp.zeros((1, channels), f32)))

    def add_square(i, total):
        start = pl.multiple_of(i * CHUNK, CHUNK)
        value = read(start) - center
        return total + col_sum(jnp.where(live_rows(value.shape, live, run), value * value, 0.0))

    return center, average(loop(count, add_square, jnp.zeros((1, channels), f32)))


def group_stats(read, rows_n, live, run, channels, groups, counted):
    center, spread = channel_stats(
        read, rows_n, live, run, channels, lambda row: group_total(row, groups) / counted
    )
    return center, lax.rsqrt(spread + norm_floor)


def time_wave(time_ref, embed):
    half = embed // 2
    index = lax.broadcasted_iota(jnp.int32, (1, half), 1).astype(f32)
    frequency = jnp.exp(-math.log(10000.0) * index / half)
    angles = (jnp.zeros((1, half), f32) + time_ref[0].astype(f32)) * frequency
    return jnp.concatenate([jnp.cos(angles), jnp.sin(angles)], 1)


def offsets(channels, embed_width, hidden_units, latent_ch):
    starts = []
    start = 0
    for length in [channels] * 13 + [embed_width] * 3 + [hidden_units, latent_ch]:
        starts.append((start, length))
        start = start + length
    return starts


def put_small(ref, index, value):
    if index < 13:
        half = value.shape[1]
        ref[index // 2 : index // 2 + 1, (index % 2) * half : (index % 2 + 1) * half] = value
    elif index < 16:
        ref[index - 6 : index - 5, :] = value
    elif index == 16:
        half = value.shape[1] // 2
        ref[10:11, :] = value[:, :half]
        ref[11:12, :] = value[:, half:]
    else:
        ref[index - 5 : index - 4, 0 : value.shape[1]] = value


def take_small(rows, latent_ch):
    return jnp.concatenate(
        [
            rows[0:6].reshape(-1),
            rows[6, : rows.shape[1] // 2],
            rows[7:12].reshape(-1),
            rows[12, :latent_ch],
        ]
    )


MESH = pl.DeviceIdType.MESH


def places():
    n_d, n_f = lax.axis_size("dp"), lax.axis_size("fsdp")
    me = lax.axis_index("fsdp")
    return n_d, n_f // 2, lax.axis_index("dp"), me // 2, lax.rem(me, 2)


def push(src, dst, sends, recvs, target):
    copy = pltpu.make_async_remote_copy(
        src_ref=src,
        dst_ref=dst,
        send_sem=sends,
        recv_sem=recvs,
        device_id=target,
        device_id_type=MESH,
    )
    copy.start()
    return copy


def greet(n_d, n_z, d, z, c):
    barrier = pltpu.get_barrier_semaphore()
    for j in range(1, n_d):
        pl.semaphore_signal(
            barrier, inc=1, device_id={"dp": lax.rem(d + j, n_d)}, device_id_type=MESH
        )
    for k in range(1, n_z):
        pl.semaphore_signal(
            barrier,
            inc=1,
            device_id={"fsdp": 2 * lax.rem(z + k, n_z) + c},
            device_id_type=MESH,
        )
    pl.semaphore_signal(
        barrier, inc=1, device_id={"fsdp": 2 * z + 1 - c}, device_id_type=MESH
    )


def met(n_d, n_z, d, z, c):
    pl.semaphore_wait(pltpu.get_barrier_semaphore(), n_d + n_z - 1)


def conv_piece(d, n_d, channels):
    width = 2 * channels // n_d
    return (d * width) // channels, pl.ds(
        pl.multiple_of(lax.rem(d * width, channels), 128), width
    )


def lane_piece(d, n_d, lanes):
    width = lanes // n_d
    return pl.ds(pl.multiple_of(d * width, 128), width)


def plan_gather(here, parts, wholes, sems, across=True):
    n_d, n_z, d, z, c = here
    s1, r1, s2, r2, s3, r3 = sems
    sibling = {"fsdp": 2 * z + 1 - c}

    def copy(ref, sends, recvs, target):
        return pltpu.make_async_remote_copy(
            src_ref=ref,
            dst_ref=ref,
            send_sem=sends,
            recv_sem=recvs,
            device_id=target,
            device_id_type=MESH,
        )

    def source(k):
        return lax.rem(z - k + n_z, n_z)

    def first(k):
        target = {"fsdp": 2 * lax.rem(z + k, n_z) + c}
        return [copy(r, s1.at[k, i], r1.at[k, i], target) for i, r in enumerate(parts(z))]

    def second(k, j):
        target = {"dp": lax.rem(d + j, n_d)}
        refs = parts(source(k))
        return [copy(r, s2.at[k, j, i], r2.at[k, j, i], target) for i, r in enumerate(refs)]

    def last(k):
        refs = wholes(source(k))
        return [copy(r, s3.at[k, i], r3.at[k, i], sibling) for i, r in enumerate(refs)]

    def start(group):
        for item in group:
            item.start()

    def arrive(group):
        for item in group:
            item.wait_recv()

    def leave(group):
        for item in group:
            item.wait_send()

    far = range(1, n_z)
    peers = range(1, n_d) if across else ()

    def step_one():
        for k in far:
            start(first(k))
        start(last(0))

    def step_two():
        for k in far:
            arrive(first(k))
            for j in peers:
                start(second(k, j))
            if not across:
                start(last(k))

    def step_three():
        if across:
            for k in far:
                for j in peers:
                    arrive(second(k, j))
                start(last(k))

    def step_four():
        for k in range(n_z):
            arrive(last(k))
        for k in far:
            leave(first(k))
            for j in peers:
                leave(second(k, j))
        for k in range(n_z):
            leave(last(k))

    return step_one, step_two, step_three, step_four


def gather_sems(count):
    n_d, n_z = lax.axis_size("dp"), lax.axis_size("fsdp") // 2
    dma = pltpu.SemaphoreType.DMA
    return [
        dma((n_z, count)),
        dma((n_z, count)),
        dma((n_z, n_d, count)),
        dma((n_z, n_d, count)),
        dma((n_z, count)),
        dma((n_z, count)),
    ]


def plan_total(here, value_ref, out, pair, other, from_dp, summed, from_z, sems):
    n_d, n_z, d, z, c = here
    lanes_n = out.shape[3]
    mine = lane_piece(d, n_d, lanes_n)
    sibling = {"fsdp": 2 * z + 1 - c}
    send, recv = sems

    def copy(src, dst, index, target):
        return pltpu.make_async_remote_copy(
            src_ref=src,
            dst_ref=dst,
            send_sem=send.at[index],
            recv_sem=recv.at[index],
            device_id=target,
            device_id_type=MESH,
        )

    def replica(j):
        return lax.rem(d + j, n_d)

    def chip(k):
        return lax.rem(z + k, n_z)

    def one():
        return [copy(value_ref.at[:, 1 - c], other, 0, sibling)]

    def two():
        return [
            copy(
                pair.at[:, :, lane_piece(replica(j), n_d, lanes_n)],
                from_dp.at[j],
                j,
                {"dp": replica(j)},
            )
            for j in range(1, n_d)
        ]

    def three():
        return [
            copy(summed.at[chip(k)], from_z.at[k], n_d + k, {"fsdp": 2 * chip(k) + c})
            for k in range(1, n_z)
        ]

    def four():
        ref = out.at[z, c, :, mine]
        return [
            copy(ref, ref, n_d + n_z + j, {"dp": replica(j)}) for j in range(1, n_d)
        ]

    def five():
        ref = out.at[z, c]
        return [
            copy(ref, ref, 2 * n_d + n_z + k, {"fsdp": 2 * chip(k) + c}) for k in range(1, n_z)
        ]

    def six():
        ref = out.at[:, c]
        return [copy(ref, ref, 2 * n_d + 2 * n_z, sibling)]

    def start(group):
        for item in group:
            item.start()

    def arrive(group):
        for item in group:
            item.wait_recv()

    def step_one():
        start(one())

    def step_two():
        arrive(one())
        for i in range(n_z):
            pair[i] = (
                value_ref[i, pl.ds(c, 1)][0].astype(f32) + other[i].astype(f32)
            ).astype(pair.dtype)
        start(two())

    def step_three():
        arrive(two())
        for i in range(n_z):
            value = pair[i, :, mine].astype(f32)
            for j in range(1, n_d):
                value = value + from_dp[j, i].astype(f32)
            summed[i] = value.astype(summed.dtype)
        start(three())

    def step_four():
        arrive(three())
        value = summed[pl.ds(z, 1)][0].astype(f32)
        for k in range(1, n_z):
            value = value + from_z[k].astype(f32)
        out[pl.ds(z, 1), pl.ds(c, 1), :, mine] = value.astype(out.dtype)[None, None]
        start(four())

    def step_five():
        arrive(four())
        start(five())

    def step_six():
        arrive(five())
        start(six())

    def step_seven():
        arrive(six())
        for group in (one(), two(), three(), four(), five(), six()):
            for item in group:
                item.wait_send()

    return step_one, step_two, step_three, step_four, step_five, step_six, step_seven


def starts(group):
    for item in group:
        item.start()


def arrives(group):
    for item in group:
        item.wait_recv()


def leaves(group):
    for item in group:
        item.wait_send()


def remote(src, dst, send, recv, target):
    return pltpu.make_async_remote_copy(
        src_ref=src,
        dst_ref=dst,
        send_sem=send,
        recv_sem=recv,
        device_id=target,
        device_id_type=MESH,
    )


def plan_owner(here, value, other, pair, from_dp, summed, from_z, out, sems):
    n_d, n_z, d, z, c = here
    lanes_n = out.shape[1]
    mine = lane_piece(d, n_d, lanes_n)
    send, recv = sems

    def one():
        target = {"fsdp": 2 * z + 1 - c}
        return [remote(value.at[:, 1 - c], other, send.at[0], recv.at[0], target)]

    def two():
        group = []
        for j in range(1, n_d):
            peer = lax.rem(d + j, n_d)
            ref = pair.at[:, :, lane_piece(peer, n_d, lanes_n)]
            group.append(remote(ref, from_dp.at[j], send.at[j], recv.at[j], {"dp": peer}))
        return group

    def three():
        group = []
        for k in range(1, n_z):
            chip = lax.rem(z + k, n_z)
            index = n_d + k
            target = {"fsdp": 2 * chip + c}
            group.append(
                remote(summed.at[chip], from_z.at[k], send.at[index], recv.at[index], target)
            )
        return group

    def four():
        group = []
        ref = out.at[:, mine]
        for j in range(1, n_d):
            index = n_d + n_z + j
            target = {"dp": lax.rem(d + j, n_d)}
            group.append(remote(ref, ref, send.at[index], recv.at[index], target))
        return group

    def step_one():
        starts(one())

    def step_two():
        arrives(one())
        for i in range(n_z):
            own = value[i, pl.ds(c, 1)][0].astype(f32)
            pair[i] = (own + other[i].astype(f32)).astype(bf16)
        starts(two())

    def step_three():
        arrives(two())
        for i in range(n_z):
            total = pair[i, :, mine].astype(f32)
            for j in range(1, n_d):
                total = total + from_dp[j, i].astype(f32)
            summed[i] = total.astype(bf16)
        starts(three())

    def step_four():
        arrives(three())
        total = summed[pl.ds(z, 1)][0].astype(f32)
        for k in range(1, n_z):
            total = total + from_z[k].astype(f32)
        out[:, mine] = total.astype(bf16)
        starts(four())

    def finish():
        arrives(four())
        for group in (one(), two(), three(), four()):
            leaves(group)

    return step_one, step_two, step_three, step_four, finish


def owner_scratch(rows, lanes):
    n_d, n_z = lax.axis_size("dp"), lax.axis_size("fsdp") // 2
    part = lanes // n_d
    dma = pltpu.SemaphoreType.DMA
    return [
        pltpu.VMEM((n_z, 2, rows, lanes), bf16),
        pltpu.VMEM((n_z, rows, lanes), bf16),
        pltpu.VMEM((n_z, rows, lanes), bf16),
        pltpu.VMEM((n_d, n_z, rows, part), bf16),
        pltpu.VMEM((n_z, rows, part), bf16),
        pltpu.VMEM((n_z, rows, part), bf16),
        pltpu.VMEM((rows, lanes), bf16),
        dma((2 * n_d + n_z,)),
        dma((2 * n_d + n_z,)),
    ]


def plan_spread(here, out, sems):
    n_d, n_z, d, z, c = here
    send, recv = sems

    def one():
        group = []
        for k in range(1, n_z):
            ref = out.at[z, c]
            target = {"fsdp": 2 * lax.rem(z + k, n_z) + c}
            group.append(remote(ref, ref, send.at[k], recv.at[k], target))
        return group

    def two():
        ref = out.at[:, c]
        return [remote(ref, ref, send.at[0], recv.at[0], {"fsdp": 2 * z + 1 - c})]

    def step_two():
        arrives(one())
        starts(two())

    def finish():
        arrives(two())
        leaves(one())
        leaves(two())

    return (lambda: starts(one())), step_two, finish


def plan_clips(here, everyone, sems):
    n_d, n_z, d, z, c = here
    send, recv = sems

    def one():
        group = []
        for j in range(1, n_d):
            ref = everyone.at[d, z, c]
            target = {"dp": lax.rem(d + j, n_d)}
            group.append(remote(ref, ref, send.at[j], recv.at[j], target))
        return group

    def two():
        group = []
        for k in range(1, n_z):
            ref = everyone.at[:, z, c]
            target = {"fsdp": 2 * lax.rem(z + k, n_z) + c}
            group.append(remote(ref, ref, send.at[n_d + k], recv.at[n_d + k], target))
        return group

    def three():
        ref = everyone.at[:, :, c]
        return [remote(ref, ref, send.at[0], recv.at[0], {"fsdp": 2 * z + 1 - c})]

    def step_two():
        arrives(one())
        starts(two())

    def step_three():
        arrives(two())
        starts(three())

    def finish():
        arrives(three())
        for group in (one(), two(), three()):
            leaves(group)

    return (lambda: starts(one())), step_two, step_three, finish


def all_peers(here):
    n_d, n_z, d, z, c = here
    n_f = 2 * n_z
    me = 2 * z + c
    peers = []
    for j in range(n_d):
        for k in range(n_f):
            if j or k:
                peers.append((j * n_f + k, lax.rem(d + j, n_d), lax.rem(me + k, n_f)))
    return peers


def greet_all(here):
    barrier = pltpu.get_barrier_semaphore()
    peers = all_peers(here)
    for _, other_d, other_f in peers:
        pl.semaphore_signal(
            barrier,
            inc=1,
            device_id={"dp": other_d, "fsdp": other_f},
            device_id_type=MESH,
        )


def met_all(here):
    pl.semaphore_wait(pltpu.get_barrier_semaphore(), len(all_peers(here)))


def plan_small(here, value, out, other, pair, from_dp, summed, from_z, sems):
    n_d, n_z, d, z, c = here
    lanes_n = out.shape[3]
    mine = lane_piece(d, n_d, lanes_n)
    send, recv, all_send, all_recv = sems

    def one():
        target = {"fsdp": 2 * z + 1 - c}
        return [remote(value.at[:, 1 - c], other, send.at[0], recv.at[0], target)]

    def two():
        group = []
        for j in range(1, n_d):
            peer = lax.rem(d + j, n_d)
            ref = pair.at[:, :, lane_piece(peer, n_d, lanes_n)]
            group.append(remote(ref, from_dp.at[j], send.at[j], recv.at[j], {"dp": peer}))
        return group

    def three():
        group = []
        for k in range(1, n_z):
            chip = lax.rem(z + k, n_z)
            index = n_d + k
            target = {"fsdp": 2 * chip + c}
            group.append(
                remote(summed.at[chip], from_z.at[k], send.at[index], recv.at[index], target)
            )
        return group

    def four():
        ref = out.at[z, c, :, mine]
        return [
            remote(
                ref,
                ref,
                all_send.at[index],
                all_recv.at[index],
                {"dp": other_d, "fsdp": other_f},
            )
            for index, other_d, other_f in all_peers(here)
        ]

    def step_one():
        starts(one())

    def step_two():
        arrives(one())
        for i in range(n_z):
            pair[i] = value[i, pl.ds(c, 1)][0] + other[i]
        starts(two())

    def step_three():
        arrives(two())
        for i in range(n_z):
            total = pair[i, :, mine]
            for j in range(1, n_d):
                total = total + from_dp[j, i]
            summed[i] = total
        starts(three())

    def step_four():
        arrives(three())
        total = summed[pl.ds(z, 1)][0]
        for k in range(1, n_z):
            total = total + from_z[k]
        out[pl.ds(z, 1), pl.ds(c, 1), :, mine] = total[None, None]
        starts(four())

    def finish():
        arrives(four())
        for group in (one(), two(), three(), four()):
            leaves(group)

    return step_one, step_two, step_three, step_four, finish


def small_scratch(lanes):
    n_d, n_z = lax.axis_size("dp"), lax.axis_size("fsdp") // 2
    part = lanes // n_d
    dma = pltpu.SemaphoreType.DMA
    return [
        pltpu.VMEM((n_z, 2, 8, lanes), f32),
        pltpu.VMEM((n_z, 8, lanes), f32),
        pltpu.VMEM((n_z, 8, lanes), f32),
        pltpu.VMEM((n_d, n_z, 8, part), f32),
        pltpu.VMEM((n_z, 8, part), f32),
        pltpu.VMEM((n_z, 8, part), f32),
        dma((n_d + n_z,)),
        dma((n_d + n_z,)),
        dma((n_d * n_z * 2,)),
        dma((n_d * n_z * 2,)),
    ]


def plan_scalar(here, squares, sems):
    n_d, n_z, d, z, c = here
    n_f = 2 * n_z
    mine = d * n_f + 2 * z + c
    send, recv = sems

    def one():
        ref = squares.at[mine]
        return [
            remote(
                ref, ref, send.at[index], recv.at[index], {"dp": other_d, "fsdp": other_f}
            )
            for index, other_d, other_f in all_peers(here)
        ]

    def finish():
        arrives(one())
        total = squares[0]
        for i in range(1, n_d * n_f):
            total = total + squares[i]
        leaves(one())
        return total

    return (lambda: starts(one())), finish


def store_rows(ref, first, lane, value):
    size = ref.shape[2]
    done = 0
    while done < value.shape[0]:
        shard, offset = divmod(first + done, size)
        count = min(size - offset, value.shape[0] - done)
        ref[shard // 2, shard % 2, offset : offset + count, lane : lane + value.shape[1]] = value[
            done : done + count
        ]
        done = done + count


def store_folded(ref, first, value):
    size = ref.shape[2]
    width = value.shape[1]
    done = 0
    while done < value.shape[0]:
        block, offset = divmod(first + done, size)
        shard, side = divmod(block, 2)
        count = min(size - offset, value.shape[0] - done)
        ref[
            shard // 2, shard % 2, offset : offset + count, side * width : (side + 1) * width
        ] = value[done : done + count]
        done = done + count


def tile_place(ref, tile):
    across = ref.shape[3] // 128
    shard, lane = divmod(tile, across)
    return (shard // 2, shard % 2, slice(None), slice(128 * lane, 128 * lane + 128))


def put_tiles(ref, first, value):
    across = value.shape[1] // 128
    for i in range(value.shape[0] // 8):
        for j in range(across):
            ref[tile_place(ref, first + i * across + j)] = value[
                8 * i : 8 * i + 8, 128 * j : 128 * j + 128
            ]


def take_tiles(ref, first, rows, lanes):
    across = lanes // 128
    return jnp.concatenate(
        [
            jnp.concatenate(
                [ref[tile_place(ref, first + i * across + j)] for j in range(across)], 1
            )
            for i in range(rows // 8)
        ],
        0,
    )


def total_scratch(rows, lanes, dtype):
    n_d, n_z = lax.axis_size("dp"), lax.axis_size("fsdp") // 2
    part = lanes // n_d
    dma = pltpu.SemaphoreType.DMA
    count = 2 * n_d + 2 * n_z + 1
    return [
        pltpu.VMEM((n_z, 2, rows, lanes), dtype),
        pltpu.VMEM((n_z, rows, lanes), dtype),
        pltpu.VMEM((n_z, rows, lanes), dtype),
        pltpu.VMEM((n_d, n_z, rows, part), dtype),
        pltpu.VMEM((n_z, rows, part), dtype),
        pltpu.VMEM((n_z, rows, part), dtype),
        dma((count,)),
        dma((count,)),
    ]


def fold_rows(value):
    half = value.shape[0] // 2
    return jnp.concatenate([value[:half], value[half:]], 1)


def shard_gather(here, wide_land, down_land, sems):
    n_d, n_z, d, z, c = here
    lanes_w = lane_piece(d, n_d, wide_land.shape[3])
    lanes_d = lane_piece(d, n_d, down_land.shape[3])

    def parts(source):
        return [
            wide_land.at[source, c, :, lanes_w],
            down_land.at[source, c, :, lanes_d],
        ]

    def wholes(source):
        return [wide_land.at[source, c], down_land.at[source, c]]

    return plan_gather(here, parts, wholes, sems)


def place_shards(here, wide, down, wide_land, down_land):
    z, c = here[3], here[4]
    wide_land[pl.ds(z, 1), pl.ds(c, 1)] = wide.astype(bf16)[None, None]
    down_land[pl.ds(z, 1), pl.ds(c, 1)] = fold_rows(down).astype(bf16)[None, None]


def land_out(wide_land, down_land, wide_out, down_out):
    n_z = wide_land.shape[0]
    lanes = down_out.shape[1]
    rows_w, rows_d = wide_land.shape[2], down_land.shape[2]
    for i in range(n_z):
        for j in range(2):
            shard = 2 * i + j
            wide_out[shard * rows_w : (shard + 1) * rows_w, :] = wide_land[i, j]
            first = 2 * shard * rows_d
            down_out[first : first + rows_d, :] = down_land[i, j, :, :lanes]
            down_out[first + rows_d : first + 2 * rows_d, :] = down_land[i, j, :, lanes:]


def land_scratch(wide_shape, down_shape):
    n_z = lax.axis_size("fsdp") // 2
    return [
        pltpu.VMEM((n_z, 2) + wide_shape, bf16),
        pltpu.VMEM((n_z, 2, down_shape[0] // 2, 2 * down_shape[1]), bf16),
    ] + gather_sems(2)


def land_gather(here, land, sems):
    n_d, c = here[0], here[4]
    lanes = lane_piece(here[2], n_d, land.shape[3])
    return plan_gather(
        here,
        lambda source: [land.at[source, c, :, lanes]],
        lambda source: [land.at[source, c]],
        sems,
    )


def unfold_land(land, out, which):
    n_z, _, rows, lanes = land.shape
    width = lanes // 2
    for block in range(n_z * 4):
        shard, side = divmod(block, 2)
        done = 0
        while done < rows:
            tap, offset = divmod(block * rows + done, width)
            count = min(width - offset, rows - done)
            first = swap_tap(tap) * width + offset
            out[which, first : first + count, :] = land[
                shard // 2, shard % 2, done : done + count, side * width : (side + 1) * width
            ]
            done = done + count


def fore_kernel(
    run,
    groups,
    len_ref,
    time_ref,
    lat_ref,
    noi_ref,
    stem_ref,
    conv_own,
    wide_own,
    time_own,
    vec_ref,
    clap_ref,
    zero_any,
    act_one_any,
    inner_any,
    act_two_any,
    one_any,
    normed_any,
    qkv_any,
    colsT_ref,
    noiT_ref,
    stat_ref,
    film_ref,
    conv_any,
    time_any,
    wide_any,
    buf,
    cols,
    tall,
    first_land,
    second_land,
    zero_ref,
    act_one_ref,
    inner_ref,
    act_two_ref,
    one_ref,
    normed_ref,
    qkv_ref,
    conv_ref,
    time_land,
    wide_land,
    out_sems,
    *sems,
):
    rows_n, channels = zero_ref.shape
    latent_ch = lat_ref.shape[0] * run // rows_n
    embed = time_own.shape[2]
    count = rows_n // CHUNK
    here = places()
    n_d, n_z, d, z, c = here
    greet(*here)
    first_plan = land_gather(here, first_land, sems[0:6])
    second_plan = land_gather(here, second_land, sems[6:12])
    wide_plan = plan_gather(
        here,
        lambda source: [wide_land.at[source, c]],
        lambda source: [wide_land.at[source, c]],
        sems[12:18],
        False,
    )
    t_lanes = lane_piece(d, n_d, embed)
    time_plan = plan_gather(
        here,
        lambda source: [time_land.at[:, source, c, :, t_lanes]],
        lambda source: [time_land.at[:, source, c]],
        sems[18:24],
    )
    own = (pl.ds(z, 1), pl.ds(c, 1))
    first_land[own] = fold_rows(conv_own[0]).astype(bf16)[None, None]
    second_land[own] = fold_rows(conv_own[1]).astype(bf16)[None, None]
    wide_land[own] = wide_own[:, 0 : wide_land.shape[3]].astype(bf16)[None, None]
    time_land[:, pl.ds(z, 1), pl.ds(c, 1)] = time_own[...].astype(bf16)[:, None, None]
    outs = []

    def save(src, dst):
        copy = pltpu.make_async_copy(src, dst, out_sems.at[len(outs)])
        outs.append(copy)
        copy.start()

    met(*here)
    first_plan[0]()
    time_plan[0]()
    live = len_ref[0]
    counted = (live * (rows_n // run) * (channels // groups)).astype(f32)
    segs = offsets(channels, embed, FF, latent_ch)

    def seg(index):
        start, length = segs[index]
        return vec_ref[start : start + length].reshape(1, length)

    def by_bins(value):
        return jnp.concatenate(
            [value[i * latent_ch : (i + 1) * latent_ch] for i in range(rows_n // run)], 1
        )

    noise = noi_ref[...].astype(f32)
    noiT_ref[...] = by_bins(noise)
    phase = (jnp.zeros((1, run), f32) + time_ref[0].astype(f32)) / 1000.0
    kept = jnp.cos((phase + 0.008) / 1.008 * (math.pi / 2)) ** 2
    mixed = jnp.sqrt(kept) * lat_ref[...].astype(f32) + jnp.sqrt(1.0 - kept) * noise
    pos = lax.broadcasted_iota(jnp.int32, mixed.shape, 1)
    noisy = by_bins(jnp.where(pos < live, mixed, 0.0).astype(bf16).astype(f32))
    taps = 9 * latent_ch
    for a in range(3):
        for b in range(3):
            tap = 3 * a + b
            tall[tap * latent_ch : (tap + 1) * latent_ch] = tap_shift(noisy, a, b, run)
    tall[taps:] = jnp.zeros((tall.shape[0] - taps, rows_n), f32)
    colsT_ref[...] = tall[0:taps].astype(bf16)
    cols[...] = tall[...].T.astype(bf16)
    stem_low = jnp.concatenate(
        [swap_taps(stem_ref[...]), jnp.zeros((cols.shape[1] - taps, channels), f32)], 0
    ).astype(bf16)
    stem_bias = seg(12)

    def stem_part(i, carry):
        rows = pl.ds(pl.multiple_of(i * CHUNK, CHUNK), CHUNK)
        zero_ref[rows, :] = mm(cols[rows, :], stem_low) + stem_bias
        return carry

    loop(count, stem_part, 0)
    save(zero_ref, zero_any)
    first_plan[1]()

    clear_ends(buf, rows_n, run)

    def convolve(which, start):
        total = None
        for a in range(3):
            part = mm(
                buf[pl.ds(start + run * a, CHUNK), :],
                conv_ref[which, 3 * a * channels : 3 * (a + 1) * channels, :],
            )
            total = part if total is None else total + part
        return total

    def activate(read, center, scale, gain, shift, act_ref, hooks):
        factor = scale * gain

        def part(i, carry):
            start = pl.multiple_of(i * CHUNK, CHUNK)
            value = jax.nn.silu((read(start) - center) * factor + shift)
            value = jnp.where(live_rows(value.shape, live, run), value, 0.0)
            low = value.astype(bf16)
            act_ref[pl.ds(start, CHUNK), :] = low
            put_shifted(buf, start, low.astype(f32), run)
            return carry

        loop(count, part, 0, hooks)

    def read_zero(start):
        return zero_ref[pl.ds(start, CHUNK), :]

    center, scale = group_stats(read_zero, rows_n, live, run, channels, groups, counted)
    stat_ref[0:1] = center
    stat_ref[1:2] = scale
    second_plan[0]()
    wide_plan[0]()
    activate(
        read_zero, center, scale, seg(0), seg(1), act_one_ref, ((1, time_plan[1]),)
    )
    first_plan[2]()
    second_plan[1]()
    first_plan[3]()
    unfold_land(first_land, conv_ref, 0)
    save(act_one_ref, act_one_any)
    save(conv_ref.at[0], conv_any.at[0])

    bias_one = seg(2)

    def conv_part(i, carry):
        start = pl.multiple_of(i * CHUNK, CHUNK)
        inner_ref[pl.ds(start, CHUNK), :] = convolve(0, start) + bias_one
        return carry

    loop(count, conv_part, 0)
    wide_plan[1]()
    save(inner_ref, inner_any)

    def read_inner(start):
        return inner_ref[pl.ds(start, CHUNK), :]

    pixels = (live * (rows_n // run)).astype(f32)
    middle, spread = channel_stats(
        read_inner, rows_n, live, run, channels, lambda row: row / pixels
    )
    time_plan[2]()
    time_plan[3]()
    def time_matrix(index):
        return time_land[index].reshape(embed, embed)

    wave = time_wave(time_ref, embed)
    pre_time = vec_mat(wave, time_matrix(0)) + seg(13)
    embedding = vec_mat(jax.nn.silu(pre_time), time_matrix(1)) + seg(14) + clap_ref[...]
    film = vec_mat(jax.nn.silu(embedding), time_matrix(2)) + seg(15)
    film_ref[0:1] = film
    film_ref[1:2] = pre_time
    film_ref[2:3] = embedding
    film_ref[3:8] = jnp.zeros((5, embed), f32)
    lift = 1.0 + film[:, :channels]
    move = film[:, channels:]


    def read_moved(start):
        return inner_ref[pl.ds(start, CHUNK), :] * lift + move

    size = channels // groups
    middle = middle * lift + move
    center = group_total(middle, groups) / size
    gap = middle - center
    spread = group_total(lift * lift * spread + gap * gap, groups) / size
    scale = lax.rsqrt(spread + norm_floor)
    stat_ref[2:3] = center
    stat_ref[3:4] = scale
    stat_ref[4:8] = jnp.zeros((4, channels), f32)
    second_plan[2]()
    wide_plan[2]()
    activate(read_moved, center, scale, seg(3), seg(4), act_two_ref, ())
    second_plan[3]()
    wide_plan[3]()
    unfold_land(second_land, conv_ref, 1)
    save(act_two_ref, act_two_any)
    save(conv_ref.at[1], conv_any.at[1])
    save(time_land, time_any)
    save(wide_land, wide_any)

    bias_two = seg(5)
    gain, shift = seg(6), seg(7)
    wide_full = wide_land[...].reshape(channels, wide_land.shape[3])
    wqkv_t = wide_full[:, 0 : 3 * channels].T

    def last_part(i, carry):
        start = pl.multiple_of(i * CHUNK, CHUNK)
        rows = pl.ds(start, CHUNK)
        stream = zero_ref[rows, :] + convolve(1, start) + bias_two
        one_ref[rows, :] = stream
        gap = stream - row_mean(stream)
        normed = gap * lax.rsqrt(row_mean(gap * gap) + norm_floor) * gain + shift
        low = normed.astype(bf16)
        normed_ref[rows, :] = low
        qkv_ref[:, rows] = mm_nt(wqkv_t, low).astype(bf16)
        return carry

    loop(count, last_part, 0)
    save(one_ref, one_any)
    save(normed_ref, normed_any)
    save(qkv_ref, qkv_any)
    for copy in outs:
        copy.wait()


def query_rows(query, factor, extra):
    dim, length = query.shape
    scaled = query.astype(f32) * (factor * LOG2E)
    high = scaled.astype(bf16).astype(f32)
    index = lax.broadcasted_iota(jnp.int32, (128 - 2 * dim, length), 0)
    tile = jnp.where(index == 0, 1.0, 0.0)
    for place, row in enumerate(extra):
        tile = jnp.where(index == place + 1, jnp.broadcast_to(row, tile.shape), tile)
    return jnp.concatenate([high, scaled - high, tile], 0)


def key_rows(keys, live, run):
    dim, length = keys.shape
    shape = (128 - 2 * dim, length)
    index = lax.broadcasted_iota(jnp.int32, shape, 0)
    pos = lax.broadcasted_iota(jnp.int32, shape, 1)
    mask = jnp.where(lax.rem(pos, run) < live, 0.0, masked_score)
    tile = jnp.where(index == 0, mask, jnp.where(index < 4, 1.0, 0.0))
    both = keys.astype(f32)
    return jnp.concatenate([both, both, tile], 0)


def three_parts(row):
    top = row.astype(bf16).astype(f32)
    rest = row - top
    mid = rest.astype(bf16).astype(f32)
    return top, mid, rest - mid


def attend_kernel(
    run,
    key_block,
    len_ref,
    q_ref,
    k_ref,
    v_ref,
    up_ref,
    down_ref,
    o_ref,
    lse_ref,
    up_out,
    down_out,
    kaug,
    qaug,
    vaug,
    up_land,
    down_land,
    *sems,
):
    dim, length = q_ref.shape
    here = places()
    steps = shard_gather(here, up_land, down_land, sems)
    head = pl.program_id(0)

    @pl.when(head == 0)
    def _():
        greet(*here)
        place_shards(here, up_ref[:, -up_land.shape[3] :], down_ref[...], up_land, down_land)

    @pl.when(head == 1)
    def _():
        met(*here)
        steps[0]()

    pl.when(head == 3)(steps[1])
    pl.when(head == 5)(steps[2])

    @pl.when(head == 7)
    def _():
        steps[3]()
        land_out(up_land, down_land, up_out, down_out)

    live = len_ref[0]
    qaug[...] = query_rows(q_ref[...], dim ** (-0.5), ()).astype(bf16)
    kaug[...] = key_rows(k_ref[...], live, run).T.astype(bf16)
    vaug[0:dim] = v_ref[...]
    index = lax.broadcasted_iota(jnp.int32, (16, length), 0)
    vaug[dim : dim + 16] = jnp.where(index == 0, 1.0, 0.0).astype(bf16)
    top = None
    for i in range(length // key_block):
        keys = slice(i * key_block, (i + 1) * key_block)
        scores = mm(kaug[keys, :], qaug[...])
        block_top = jnp.max(scores, axis=0, keepdims=True)
        new_top = block_top if top is None else jnp.maximum(top, block_top)
        weights = jnp.exp2(scores - new_top).astype(bf16)
        part = mm(vaug[:, keys], weights)
        total = part if top is None else total * jnp.exp2(top - new_top) + part
        top = new_top
    summed = total[dim : dim + 1]
    o_ref[...] = total[0:dim] / summed
    lse_ref[0] = top + jnp.log2(summed)


def attend_back_kernel(
    run,
    block,
    len_ref,
    q_ref,
    k_ref,
    v_ref,
    lse_ref,
    o_ref,
    do_ref,
    early_ref,
    wide_ref,
    down_ref,
    dq_ref,
    dk_ref,
    dv_ref,
    early_out,
    wide_out,
    down_out,
    kaug,
    qaug,
    vaug,
    daug,
    early_land,
    pair,
    other,
    from_dp,
    summed,
    from_z,
    send,
    recv,
    wide_land,
    down_land,
    *sems,
):
    dim, length = q_ref.shape
    here = places()
    head = pl.program_id(0)
    gathers = shard_gather(here, wide_land, down_land, sems)
    totals = plan_total(
        here, early_ref, early_land, pair, other, from_dp, summed, from_z, (send, recv)
    )

    @pl.when(head == 0)
    def _():
        greet(*here)
        place_shards(here, wide_ref[...], down_ref[...], wide_land, down_land)

    @pl.when(head == 1)
    def _():
        met(*here)
        totals[0]()

    for place in range(2, 5):

        @pl.when(head == place)
        def _(place=place):
            totals[place - 1]()
            gathers[place - 2]()

    @pl.when(head == 5)
    def _():
        totals[4]()
        gathers[3]()
        land_out(wide_land, down_land, wide_out, down_out)

    pl.when(head == 7)(totals[5])

    factor = dim ** (-0.5)
    qaug[...] = query_rows(q_ref[...], factor, three_parts(-lse_ref[0])).T.astype(bf16)
    kaug[...] = key_rows(k_ref[...], len_ref[0], run).astype(bf16)
    index = lax.broadcasted_iota(jnp.int32, (128 - dim, length), 0)
    tile = jnp.where(index < 3, -1.0, 0.0)
    vaug[...] = jnp.concatenate([v_ref[...].astype(f32), tile], 0).astype(bf16)
    back = do_ref[...].astype(f32)
    tile = jnp.zeros((128 - dim, length), f32)
    for place, row in enumerate(three_parts(col_sum(back * o_ref[...]))):
        tile = jnp.where(index == place, jnp.broadcast_to(row, tile.shape), tile)
    daug[...] = jnp.concatenate([back, tile], 0).T.astype(bf16)

    dk = dv = None
    for i in range(length // block):
        rows = slice(i * block, (i + 1) * block)
        weights = jnp.exp2(mm(qaug[rows, :], kaug[...]))
        raw = (weights * mm(daug[rows, :], vaug[...])).astype(bf16)
        dv_part = mm(do_ref[:, rows], weights.astype(bf16))
        dk_part = mm(q_ref[:, rows], raw)
        dv = dv_part if dv is None else dv + dv_part
        dk = dk_part if dk is None else dk + dk_part
        dq_ref[:, rows] = (mm_nt(k_ref[...], raw) * factor).astype(bf16)
    dk_ref[...] = (dk * factor).astype(bf16)
    dv_ref[...] = dv.astype(bf16)

    @pl.when(head == HEADS - 1)
    def _():
        totals[6]()
        early_out[...] = early_land[...]


def middle_kernel(
    run,
    len_ref,
    mixed_ref,
    one_ref,
    first_ref,
    up_ref,
    down_ref,
    vec_ref,
    headw_ref,
    noiT_ref,
    two_grad_ref,
    do_ref,
    early_ref,
    small_ref,
    hidden,
    slope,
    xhat,
    spread,
    three,
    prod,
    gcols,
    normed_t,
    three_t,
    gpre,
    glow,
    head_ref,
):
    rows_n, channels = one_ref.shape
    units = down_ref.shape[0]
    latent_ch = noiT_ref.shape[0]
    count = rows_n // CHUNK
    live = len_ref[0]
    segs = offsets(channels, EMB, units, latent_ch)

    def seg(index):
        start, length = segs[index]
        return vec_ref[start : start + length].reshape(1, length)

    w_out = first_ref[:, 3 * channels :]
    for tap in range(9):
        first = swap_tap(tap) * channels
        prod[tap * latent_ch : (tap + 1) * latent_ch, 0:channels] = headw_ref[
            :, first : first + channels
        ]
    prod[9 * latent_ch :, 0:channels] = jnp.zeros((prod.shape[0] - 9 * latent_ch, channels), f32)
    head_ref[...] = prod[:, 0:channels].astype(bf16)
    index = lax.broadcasted_iota(jnp.int32, (latent_ch, latent_ch), 0)
    same = index == lax.broadcasted_iota(jnp.int32, (latent_ch, latent_ch), 1)
    head_bias = jnp.sum(jnp.where(same, seg(17), 0.0), axis=1, keepdims=True)
    proj_bias, gain, shift, up_bias, down_bias = seg(8), seg(9), seg(10), seg(16), seg(11)

    def fore(i, carry):
        start = pl.multiple_of(i * CHUNK, CHUNK)
        rows = pl.ds(start, CHUNK)
        mixed = mixed_ref[:, rows].T.astype(bf16)
        stream = one_ref[rows, :] + mm(mixed, w_out) + proj_bias
        gap = stream - row_mean(stream)
        scale = lax.rsqrt(row_mean(gap * gap) + norm_floor)
        hat = gap * scale
        xhat[rows, :] = hat
        spread[rows, :] = jnp.broadcast_to(scale, (CHUNK, spread.shape[1]))
        normed = (hat * gain + shift).astype(bf16)
        normed_t[:, rows] = normed.T
        pre = mm(normed, up_ref[...]) + up_bias
        phi = 0.5 * lax.erf(pre * (0.5**0.5)) + 0.5
        slope[rows, :] = phi + pre * jnp.exp2(
            pre * pre * (-0.5 * LOG2E) + 0.5 * math.log2(0.5 / math.pi)
        )
        low = (pre * phi).astype(bf16)
        hidden[rows, :] = low
        stream = stream + mm(low, down_ref[...]) + down_bias
        stream = jnp.where(live_rows(stream.shape, live, run), stream, 0.0).astype(bf16)
        three[rows, :] = stream
        prod[:, rows] = mm_nt(head_ref[...], stream)
        return carry

    loop(count, fore, 0)

    taps = 9 * latent_ch
    predicted = jnp.zeros((latent_ch, rows_n), f32) + head_bias
    for a in range(3):
        for b in range(3):
            tap = 3 * a + b
            predicted = predicted + tap_shift(
                prod[tap * latent_ch : (tap + 1) * latent_ch], a, b, run
            )
    pos = lax.broadcasted_iota(jnp.int32, predicted.shape, 1)
    errors = jnp.where(lax.rem(pos, run) < live, predicted - noiT_ref[...], 0.0)
    small_ref[...] = jnp.zeros(small_ref.shape, f32)
    tile = (latent_ch, 128)
    sums = jnp.broadcast_to(jnp.sum(errors, axis=1, keepdims=True), tile)
    same = lax.broadcasted_iota(jnp.int32, tile, 0) == lax.broadcasted_iota(jnp.int32, tile, 1)
    put_small(small_ref, 17, col_sum(jnp.where(same, sums, 0.0)))
    sums = jnp.broadcast_to(jnp.sum(errors * errors, axis=1, keepdims=True), tile)
    put_small(small_ref, 18, col_sum(sums))
    put_small(small_ref, 19, jnp.zeros((1, 128), f32) + (live * (rows_n // run)).astype(f32))
    errors = errors.astype(bf16).astype(f32)
    for a in range(3):
        for b in range(3):
            tap = 3 * a + b
            prod[tap * latent_ch : (tap + 1) * latent_ch] = tap_shift(
                errors, 2 - a, 2 - b, run
            )
    prod[taps:] = jnp.zeros((prod.shape[0] - taps, rows_n), f32)
    gcols[...] = prod[...].T.astype(bf16)
    ghead = mm(prod[0:taps].astype(bf16), three[...])

    def back(i, carry):
        g_down, g_up, g_gain, g_shift, g_proj = carry
        start = pl.multiple_of(i * CHUNK, CHUNK)
        rows = pl.ds(start, CHUNK)
        grad = mm(gcols[rows, :], head_ref[...])
        grad = jnp.where(live_rows(grad.shape, live, run), grad, 0.0)
        low = grad.astype(bf16)
        three_t[:, rows] = low.T
        pre = mm_nt(low, down_ref[...]) * slope[rows, :]
        pre_low = pre.astype(bf16)
        gpre[rows, :] = pre_low
        dnormed = mm_nt(pre_low, up_ref[...])
        hat = xhat[rows, :]
        dhat = dnormed * gain
        dstream = (dhat - row_mean(dhat) - hat * row_mean(dhat * hat)) * spread[rows, 0:1]
        two = grad + dstream
        two_grad_ref[rows, :] = two
        two_low = two.astype(bf16)
        glow[rows, :] = two_low
        do_ref[:, rows] = mm_nt(w_out, two_low).astype(bf16)
        return (
            g_down + col_sum(grad),
            g_up + col_sum(pre),
            g_gain + col_sum(dnormed * hat),
            g_shift + col_sum(dnormed),
            g_proj + col_sum(two),
        )

    blank = jnp.zeros((1, channels), f32)
    sums = loop(count, back, (blank, jnp.zeros((1, units), f32), blank, blank, blank))
    for index, value in zip((11, 16, 9, 10, 8), sums):
        put_small(small_ref, index, value)
    half = units // 2
    for part in range(units // channels):
        columns = slice(part * channels, (part + 1) * channels)
        first = (part * channels) % half
        lanes = slice((part * channels) // half * channels, (part * channels) // half * channels + channels)
        early_ref[first : first + channels, lanes] = mm(three_t[...], hidden[:, columns]).T.astype(
            bf16
        )
        first = half + (part // 2) * channels
        lanes = slice((part % 2) * channels, (part % 2 + 1) * channels)
        early_ref[first : first + channels, lanes] = mm(normed_t[...], gpre[:, columns]).astype(
            bf16
        )
    gproj = mm(mixed_ref[...].astype(bf16), glow[...]).astype(bf16)
    first = half + (units // channels // 2) * channels
    middle = channels // 2
    early_ref[first : first + middle, 0:channels] = gproj[:middle]
    early_ref[first : first + middle, channels:] = gproj[middle:]
    first = first + middle
    ghead = swap_taps(ghead).astype(bf16)
    middle = taps // 2
    early_ref[first : first + middle, 0:channels] = ghead[:middle]
    early_ref[first : first + middle, channels:] = ghead[middle:]
    early_ref[first + middle :, :] = jnp.zeros(
        (early_ref.shape[0] - first - middle, 2 * channels), bf16
    )


def hind_kernel(
    run,
    groups,
    len_ref,
    step_ref,
    dq_any,
    dk_any,
    dv_any,
    two_grad_any,
    normed_any,
    one_any,
    act_two_any,
    inner_any,
    act_one_any,
    zero_any,
    colsT_any,
    stat_ref,
    film_ref,
    conv_any,
    wide_any_w,
    time_any,
    vec_ref,
    mid_ref,
    early_any,
    wide_any,
    down_any,
    small_any,
    root_any,
    large_any,
    conv_out,
    tile_out,
    time_out,
    scalar_out,
    head_out,
    wide_out,
    wide_dir,
    down_out,
    down_dir,
    buf,
    field,
    other,
    act_t,
    small,
    everyone,
    tiles,
    tile_o,
    tile_p,
    tile_d,
    tile_f,
    tile_z,
    tile_s,
    tile_r,
    tile_as,
    tile_ar,
    squares,
    product,
    first_g,
    first_o,
    first_p,
    first_d,
    first_f,
    first_z,
    first_t,
    first_s,
    first_r,
    second_g,
    second_o,
    second_p,
    second_d,
    second_f,
    second_z,
    second_t,
    second_s,
    second_r,
    qkv_g,
    qkv_o,
    qkv_p,
    qkv_d,
    qkv_f,
    qkv_z,
    qkv_t,
    qkv_s,
    qkv_r,
    spread_s,
    spread_r,
    clip_s,
    clip_r,
    square_s,
    square_r,
    qkv_out,
    early,
    wide_full,
    down_full,
    roots_small,
    root_wide,
    root_large,
    root_rows,
    local_sems,
    dq_ref,
    dk_ref,
    dv_ref,
    normed_ref,
    wide_ref,
    two_grad_ref,
    one_ref,
    act_two_ref,
    inner_ref,
    conv_ref,
    time_ref,
    act_one_ref,
    zero_ref,
    colsT_ref,
    load_sems,
):
    rows_n, channels = one_ref.shape
    embed = time_ref.shape[2]
    latent_ch = colsT_ref.shape[0] // 9
    count = rows_n // CHUNK
    live = len_ref[0]
    counted = (live * (rows_n // run) * (channels // groups)).astype(f32)
    segs = offsets(channels, embed, FF, latent_ch)
    blank = jnp.zeros((1, channels), f32)
    small[...] = jnp.zeros(small.shape, f32)
    here = places()
    n_d, n_z, d, z, c = here
    conv_plans = (
        plan_owner(here, first_g, first_o, first_p, first_d, first_f, first_z, first_t, (first_s, first_r)),
        plan_owner(here, second_g, second_o, second_p, second_d, second_f, second_z, second_t, (second_s, second_r)),
    )
    qkv_plan = plan_owner(here, qkv_g, qkv_o, qkv_p, qkv_d, qkv_f, qkv_z, qkv_t, (qkv_s, qkv_r))
    spread_plan = plan_spread(here, qkv_out, (spread_s, spread_r))
    clip_plan = plan_clips(here, everyone, (clip_s, clip_r))
    tile_plan = plan_small(
        here,
        tiles,
        tile_out,
        tile_o,
        tile_p,
        tile_d,
        tile_f,
        tile_z,
        (tile_s, tile_r, tile_as, tile_ar),
    )
    square_plan = plan_scalar(here, squares, (square_s, square_r))
    own_rows = root_rows.shape[0]
    loads = [
        pltpu.make_async_copy(src, dst, local_sems.at[index])
        for index, (src, dst) in enumerate(
            (
                (early_any, early),
                (wide_any, wide_full),
                (down_any, down_full),
                (small_any, roots_small),
                (root_any, root_wide),
                (large_any.at[0], root_large),
                (large_any.at[1, pl.ds(lax.axis_index("fsdp") * own_rows, own_rows)], root_rows),
            )
        )
    ]
    first_loads = {
        id(ref): pltpu.make_async_copy(src, ref, load_sems.at[index])
        for index, (src, ref) in enumerate(
            (
                (dq_any, dq_ref),
                (dk_any, dk_ref),
                (dv_any, dv_ref),
                (normed_any, normed_ref),
                (wide_any_w, wide_ref),
                (two_grad_any, two_grad_ref),
                (one_any, one_ref),
                (act_two_any, act_two_ref),
                (inner_any, inner_ref),
                (conv_any, conv_ref),
                (time_any, time_ref),
                (act_one_any, act_one_ref),
                (zero_any, zero_ref),
                (colsT_any, colsT_ref),
            )
        )
    }
    greet_all(here)
    starts(first_loads.values())
    starts(loads)

    def ready(*refs):
        for ref in refs:
            first_loads[id(ref)].wait()

    ready(dq_ref, dk_ref, dv_ref, normed_ref)

    def seg(index):
        start, length = segs[index]
        return vec_ref[start : start + length].reshape(1, length)

    def put_vec(index, value):
        put_small(small, index, value)

    half = channels // 2
    store_rows(qkv_g, 0, 0, mm(dq_ref[...], normed_ref[...]).T.astype(bf16))
    store_rows(qkv_g, 0, channels, mm(dk_ref[...], normed_ref[...]).T.astype(bf16))
    values_grad = mm(dv_ref[...], normed_ref[...]).T.astype(bf16)
    store_rows(qkv_g, channels, 0, values_grad[:half])
    store_rows(qkv_g, channels, channels, values_grad[half:])
    met_all(here)
    qkv_plan[0]()

    ready(wide_ref, two_grad_ref, one_ref)
    gain_one = seg(6)
    clear_ends(buf, rows_n, run)

    def norm_part(i, carry):
        g_gain, g_shift, g_bias = carry
        start = pl.multiple_of(i * CHUNK, CHUNK)
        rows = pl.ds(start, CHUNK)
        dnormed_t = None
        for part, ref in enumerate((dq_ref, dk_ref, dv_ref)):
            term = mm(wide_ref[:, part * channels : (part + 1) * channels], ref[:, rows])
            dnormed_t = term if dnormed_t is None else dnormed_t + term
        dnormed = dnormed_t.T
        stream = one_ref[rows, :]
        gap = stream - row_mean(stream)
        scale = lax.rsqrt(row_mean(gap * gap) + norm_floor)
        hat = gap * scale
        dhat = dnormed * gain_one
        grad = two_grad_ref[rows, :] + scale * (
            dhat - row_mean(dhat) - hat * row_mean(dhat * hat)
        )
        field[rows, :] = grad
        put_shifted(buf, start, grad.astype(bf16).astype(f32), run)
        return (
            g_gain + col_sum(dnormed * hat),
            g_shift + col_sum(dnormed),
            g_bias + col_sum(grad),
        )

    sums = loop(count, norm_part, (blank, blank, blank), ((1, qkv_plan[1]),))
    for index, value in zip((6, 7, 5), sums):
        put_vec(index, value)

    def weight_grad(which, act_ref):
        act_t[...] = act_ref[...].T
        for a in range(3):
            full = buf[run * (2 - a) : run * (2 - a) + rows_n, :]
            for b in range(3):
                shifted = full[:, (2 - b) * channels : (3 - b) * channels]
                first = (3 * b + a) * channels
                store_folded(
                    (first_g, second_g)[which], first, mm(act_t[...], shifted).astype(bf16)
                )

    def input_grad(which, start):
        total = None
        for a in range(3):
            for b in range(3):
                first = (3 * (2 - a) + 2 - b) * channels
                part = mm_nt(
                    buf[
                        pl.ds(start + run * a, CHUNK),
                        b * channels : (b + 1) * channels,
                    ],
                    conv_ref[which, first : first + channels, :],
                )
                total = part if total is None else total + part
        return total

    def norm_back(which, read, center, scale, gain, shift, g_refs, hooks):
        def part(i, carry):
            g_gain, g_shift = carry
            start = pl.multiple_of(i * CHUNK, CHUNK)
            rows = pl.ds(start, CHUNK)
            hat = (read(start) - center) * scale
            slope = silu_slope(hat * gain + shift)
            grad = input_grad(which, start) * slope
            grad = jnp.where(live_rows(grad.shape, live, run), grad, 0.0)
            other[rows, :] = grad
            return (g_gain + col_sum(grad * hat), g_shift + col_sum(grad))

        g_gain, g_shift = loop(count, part, (blank, blank), hooks)
        put_vec(g_refs[0], g_gain)
        put_vec(g_refs[1], g_shift)
        mean_grad = group_total(g_shift * gain, groups) / counted
        mean_hat = group_total(g_gain * gain, groups) / counted

        def finish(start):
            hat = (read(start) - center) * scale
            grad = (other[pl.ds(start, CHUNK), :] * gain - mean_grad - hat * mean_hat) * scale
            return jnp.where(live_rows(grad.shape, live, run), grad, 0.0)

        return finish

    film = film_ref[0:1]
    lift = 1.0 + film[:, :channels]
    move = film[:, channels:]

    ready(act_two_ref)
    weight_grad(1, act_two_ref)
    conv_plans[1][0]()
    qkv_plan[2]()
    ready(inner_ref, conv_ref)
    finish = norm_back(
        1,
        lambda start: inner_ref[pl.ds(start, CHUNK), :] * lift + move,
        stat_ref[2:3],
        stat_ref[3:4],
        seg(3),
        seg(4),
        (3, 4),
        ((1, conv_plans[1][1]),),
    )

    qkv_plan[3]()

    def inner_part(i, carry):
        g_lift, g_move, g_bias = carry
        start = pl.multiple_of(i * CHUNK, CHUNK)
        moved = finish(start)
        grad = moved * lift
        put_shifted(buf, start, grad.astype(bf16).astype(f32), run)
        return (
            g_lift + col_sum(moved * inner_ref[pl.ds(start, CHUNK), :]),
            g_move + col_sum(moved),
            g_bias + col_sum(grad),
        )

    g_lift, g_move, g_bias = loop(count, inner_part, (blank, blank, blank))
    put_vec(2, g_bias)

    ready(act_one_ref)
    weight_grad(0, act_one_ref)
    conv_plans[0][0]()
    ready(time_ref, zero_ref, colsT_ref)
    pre_time = film_ref[1:2]
    embedding = film_ref[2:3]
    g_film = jnp.concatenate([g_lift, g_move], 1)
    g_embed = vec_mat(g_film, time_ref[2], True) * silu_slope(embedding)
    g_time = vec_mat(g_embed, time_ref[1], True) * silu_slope(pre_time)
    put_vec(13, g_time)
    put_vec(14, g_embed)
    put_vec(15, g_film)
    factors = jnp.concatenate(
        [
            time_wave(step_ref, embed),
            jax.nn.silu(pre_time),
            jax.nn.silu(embedding),
            g_time,
            g_embed,
            g_film,
            jnp.zeros((2, embed), f32),
        ],
        0,
    )
    factors = jnp.concatenate([factors[:, : embed // 2], factors[:, embed // 2 :]], 0)
    everyone[pl.ds(d, 1), pl.ds(z, 1), pl.ds(c, 1)] = factors.astype(bf16)[None, None, None]
    clip_plan[0]()
    conv_plans[1][2]()
    qkv_plan[4]()
    qkv_out[pl.ds(z, 1), pl.ds(c, 1)] = qkv_t[...][None, None]
    finish_zero = norm_back(
        0,
        lambda start: zero_ref[pl.ds(start, CHUNK), :],
        stat_ref[0:1],
        stat_ref[1:2],
        seg(0),
        seg(1),
        (0, 1),
        ((0, conv_plans[0][1]), (1, clip_plan[1])),
    )
    conv_plans[1][3]()

    def zero_part(i, carry):
        g_stem, g_bias = carry
        start = pl.multiple_of(i * CHUNK, CHUNK)
        rows = pl.ds(start, CHUNK)
        grad = field[rows, :] + finish_zero(start)
        return (g_stem + mm(colsT_ref[:, rows], grad.astype(bf16)), g_bias + col_sum(grad))

    taps = colsT_ref.shape[0]
    g_stem, g_bias = loop(count, zero_part, (jnp.zeros((taps, channels), f32), blank))
    put_vec(12, g_bias)
    used = taps // 8 * (channels // 128)
    put_tiles(tiles, 0, swap_taps(g_stem))
    put_tiles(tiles, used, small[...] + mid_ref[...])
    used = used + 2 * (small.shape[1] // 128)
    for i in range(used, n_z * 2 * (tiles.shape[3] // 128)):
        tiles[tile_place(tiles, i)] = jnp.zeros((8, 128), f32)
    tile_plan[0]()
    clip_plan[2]()
    conv_plans[0][2]()
    tile_plan[1]()
    spread_plan[0]()
    conv_plans[1][4]()
    mine = lane_piece(d, n_d, 2 * channels)
    rows_c = second_t.shape[0]

    def squared(value):
        return jnp.sum(value * value)

    def unfold(which, ref):
        value = ref[...].astype(f32)
        conv_out[which, 0:rows_c] = value[:, 0:channels]
        conv_out[which, rows_c:] = value[:, channels:]

    unfold(1, second_t)
    square = squared(second_t[:, mine].astype(f32)) + squared(qkv_t[:, mine].astype(f32))

    for copy in loads:
        copy.wait()
    width = 2 * channels
    early_rows = early.shape[0] * 2 * early.shape[2]
    sums = early[...].reshape(early_rows, width)
    units = down_full.shape[0]
    half = units // 2
    shared = squared(sums.astype(f32))

    def choose(rows, order):
        own = lax.broadcasted_iota(jnp.int32, (rows, order), 0) + (2 * z + c) * rows
        return jnp.where(
            own == lax.broadcasted_iota(jnp.int32, (rows, order), 1), 1.0, 0.0
        ).astype(bf16)

    pick = choose(wide_out.shape[0], channels)

    def apply(left, value, right_root):
        return mm(mm(left, value).astype(bf16), right_root.astype(bf16))

    def side_by_side(first, rows):
        return jnp.concatenate([sums[first : first + rows], sums[first + rows : first + 2 * rows]], 1)

    def stacked(first, rows):
        block = sums[first : first + rows]
        return jnp.concatenate([block[:, :channels], block[:, channels:]], 0)

    first = half + 2 * channels
    head_first = first + channels // 2
    head_out[...] = stacked(head_first, taps // 2).astype(f32)
    lefts = [mm(pick, roots_small[i].astype(bf16)).astype(bf16) for i in range(3)]
    q_end, o_end = 3 * channels, 4 * channels
    momentum = {}
    later = {}
    for index, (grad, right_root, start, end) in enumerate(
        (
            (None, root_wide, 0, q_end),
            (stacked(first, channels // 2), roots_small.at[3], q_end, o_end),
            (side_by_side(half, channels), root_large, o_end, o_end + units),
        )
    ):
        wide_dir[:, start:end] = 0.9 * apply(
            lefts[index], wide_full[:, start:end], right_root[...]
        )
        if grad is not None:
            wide_out[:, start:end] = mm(pick, grad)
            later[start, end] = apply(lefts[index], grad, right_root[...])
    grad = stacked(0, half)
    rows = root_rows[...].astype(bf16)
    down_out[...] = mm(choose(down_out.shape[0], units), grad)
    later_down = apply(rows, grad, roots_small[4])
    down_dir[...] = 0.9 * apply(rows, down_full[...], roots_small[4])

    tile_plan[2]()
    clip_plan[3]()
    clips = 2 * n_d * n_z
    depth = time_out.shape[1]
    first = (2 * z + c) * depth
    block = pl.ds(pl.multiple_of(lax.rem(first, embed // 2) // 128 * 128, 128), 128)
    offset = pl.multiple_of(lax.rem(first, 128), 8)
    upper = first >= embed // 2
    time_square = jnp.zeros((), f32)
    for i in range(3):
        sides = [
            everyone[:, :, :, :, block].astype(f32).reshape(clips, 16, 128)[:, part + i]
            for part in (0, 8)
        ]
        left = jnp.where(upper, sides[1], sides[0])
        full = everyone[...].astype(f32).reshape(clips, 16, embed // 2)
        right = jnp.concatenate([full[:, i + 3], full[:, i + 11]], 1)
        product[...] = mm(left.T.astype(bf16), right.astype(bf16))
        value = product[pl.ds(offset, depth), :]
        time_out[i] = value
        time_square = time_square + squared(value)
    square = square + time_square / n_d
    conv_plans[0][3]()
    square = square + squared(first_t[:, mine].astype(f32))
    tile_plan[3]()
    own = tile_out[pl.ds(z, 1), pl.ds(c, 1), :, mine][0, 0]
    row = lax.broadcasted_iota(jnp.int32, own.shape, 0)
    tile_number = (2 * z + c) * n_d + d
    second = tile_number - taps // 8 * (channels // 128) >= width // 128
    square = square + squared(
        jnp.where(jnp.logical_and(second, row >= 13 - 8), 0.0, own)
    )
    lane = lax.broadcasted_iota(jnp.int32, (1, 1, 128), 2)
    loss_live = mid_ref[13:15, 0:1]
    message = jnp.where(
        lane == 0, square, jnp.where(lane == 1, loss_live[0:1][None], loss_live[1:2][None])
    )
    squares[pl.ds(d * 2 * n_z + 2 * z + c, 1)] = message
    square_plan[0]()
    spread_plan[1]()
    spread_plan[2]()
    qkv_sum = qkv_out[...].reshape(channels + channels // 2, width)
    tail = qkv_sum[channels:]
    grad = jnp.concatenate(
        [qkv_sum[:channels], jnp.concatenate([tail[:, :channels], tail[:, channels:]], 0)], 1
    )
    wide_out[:, 0:q_end] = mm(pick, grad)
    later[0, q_end] = apply(lefts[0], grad, root_wide[...])
    conv_plans[0][4]()
    unfold(0, first_t)
    total = square_plan[1]()
    unit = 2.0 / (latent_ch * total[:, 2:3])
    norm = unit * jnp.sqrt(total[:, 0:1] + shared)
    factor = jnp.minimum(1.0, clip_limit / norm) * unit
    row = lax.broadcasted_iota(jnp.int32, scalar_out.shape, 0)
    loss = total[:, 1:2] * (0.5 * unit)
    scalar_out[...] = jnp.where(row == 0, loss, jnp.where(row == 1, norm, factor))
    factor = factor[0:1, 0:1]
    tile_plan[4]()
    for (start, end), value in later.items():
        wide_dir[:, start:end] += factor * value
    down_dir[...] += factor * later_down


def sized(shape, dtype=f32):
    return jax.ShapeDtypeStruct(shape, dtype)


VM = pl.BlockSpec(memory_space=pltpu.VMEM)
SM = pl.BlockSpec(memory_space=pltpu.SMEM)
ANY = pl.BlockSpec(memory_space=pl.ANY)


def params(mib):
    return pltpu.CompilerParams(vmem_limit_bytes=mib * 2**20)


def remote_params(number, mib):
    return pltpu.CompilerParams(
        collective_id=number, has_side_effects=True, vmem_limit_bytes=mib * 2**20
    )


def run_fore(run, length, step, lat, noi, stem_w, conv_w, wide_w, time_w, vec, clap):
    channels = stem_w.shape[1]
    latent_ch = stem_w.shape[0] // 9
    rows_n = lat.shape[1] * (lat.shape[0] // latent_ch)
    embed = time_w.shape[2]
    n_z = lax.axis_size("fsdp") // 2
    field = (rows_n, channels)
    land = pltpu.VMEM((n_z, 2, conv_w.shape[1] // 2, 2 * channels), bf16)
    large = [
        sized(field),
        sized(field, bf16),
        sized(field),
        sized(field, bf16),
        sized(field),
        sized(field, bf16),
        sized((3 * channels, rows_n), bf16),
    ]
    weights = [
        sized((2, 9 * channels, channels), bf16),
        sized((3, n_z, 2) + time_w.shape[1:], bf16),
        sized((n_z, 2, wide_w.shape[0], 4 * channels), bf16),
    ]
    outs = pl.pallas_call(
        functools.partial(fore_kernel, run, GROUPS),
        in_specs=[SM, SM] + [VM] * 8,
        out_specs=[ANY] * 7 + [VM] * 4 + [ANY] * 3,
        out_shape=large
        + [
            sized((9 * latent_ch, rows_n), bf16),
            sized((latent_ch, rows_n)),
            sized((8, channels)),
            sized((8, embed)),
        ]
        + weights,
        scratch_shapes=[
            pltpu.VMEM((rows_n + 2 * run, 3 * channels), bf16),
            pltpu.VMEM((rows_n, 128), bf16),
            pltpu.VMEM((128, rows_n), f32),
            land,
            land,
        ]
        + [pltpu.VMEM(item.shape, item.dtype) for item in large + weights]
        + [pltpu.SemaphoreType.DMA((8 + 3 * max(1, rows_n // CHUNK),))]
        + gather_sems(1) * 4,
        compiler_params=remote_params(1, 62),
        name="fore",
    )(length, step, lat, noi, stem_w, conv_w, wide_w, time_w, vec, clap)
    time_full = outs[12].reshape(3, -1, embed)
    first_full = outs[13].reshape(-1, 4 * channels)
    return (*outs[:12], time_full, first_full)


def run_attend(run, length, qkv_t, up, down, key_block=256):
    n_f = lax.axis_size("fsdp")
    triple, rows_n = qkv_t.shape
    channels = triple // 3
    dim = channels // HEADS
    return pl.pallas_call(
        functools.partial(attend_kernel, run, key_block),
        grid=(HEADS,),
        in_specs=[SM]
        + [pl.BlockSpec((dim, rows_n), lambda h, t=t: (t * HEADS + h, 0)) for t in range(3)]
        + [VM] * 2,
        out_specs=[
            pl.BlockSpec((dim, rows_n), lambda h: (h, 0)),
            pl.BlockSpec((1, 1, rows_n), lambda h: (h, 0, 0)),
            VM,
            VM,
        ],
        out_shape=[
            sized((channels, rows_n)),
            sized((HEADS, 1, rows_n)),
            sized((up.shape[0] * n_f, FF), bf16),
            sized((down.shape[0] * n_f, down.shape[1]), bf16),
        ],
        scratch_shapes=[
            pltpu.VMEM((rows_n, 128), bf16),
            pltpu.VMEM((128, rows_n), bf16),
            pltpu.VMEM((dim + 16, rows_n), bf16),
        ]
        + land_scratch((up.shape[0], FF), down.shape),
        compiler_params=remote_params(3, 62),
        name="attend",
    )(length, qkv_t, qkv_t, qkv_t, up, down)


def run_attend_back(
    run, length, qkv_t, lse, mixed_t, grad_t, early, wide, down, block=256
):
    n_f = lax.axis_size("fsdp")
    early = early.reshape(n_f // 2, 2, early.shape[0] // n_f, early.shape[1])
    triple, rows_n = qkv_t.shape
    channels = triple // 3
    dim = channels // HEADS
    whole = pl.BlockSpec((dim, rows_n), lambda h: (h, 0))
    return pl.pallas_call(
        functools.partial(attend_back_kernel, run, block),
        grid=(HEADS,),
        in_specs=[SM]
        + [pl.BlockSpec((dim, rows_n), lambda h, t=t: (t * HEADS + h, 0)) for t in range(3)]
        + [pl.BlockSpec((1, 1, rows_n), lambda h: (h, 0, 0)), whole, whole]
        + [VM] * 3,
        out_specs=[whole] * 3 + [VM] * 3,
        out_shape=[sized((channels, rows_n), bf16)] * 3
        + [
            sized(early.shape, bf16),
            sized((wide.shape[0] * n_f, wide.shape[1]), bf16),
            sized((down.shape[0] * n_f, down.shape[1]), bf16),
        ],
        scratch_shapes=[
            pltpu.VMEM((128, rows_n), bf16),
            pltpu.VMEM((rows_n, 128), bf16),
            pltpu.VMEM((128, rows_n), bf16),
            pltpu.VMEM((rows_n, 128), bf16),
        ]
        + total_scratch(early.shape[2], early.shape[3], bf16)
        + land_scratch(wide.shape, down.shape),
        compiler_params=remote_params(4, 62),
        name="attend_back",
    )(length, qkv_t, qkv_t, qkv_t, lse, mixed_t, grad_t, early, wide, down)


def run_middle(run, length, mixed_t, one, first, up, down, vec, head_w, noi_t):
    rows_n, channels = one.shape
    units = down.shape[0]
    latent_ch = noi_t.shape[0]
    return pl.pallas_call(
        functools.partial(middle_kernel, run),
        in_specs=[SM] + [VM] * 8,
        out_specs=[VM] * 4,
        out_shape=[
            sized((rows_n, channels)),
            sized((channels, rows_n), bf16),
            sized((units + channels, 2 * channels), bf16),
            sized((16, 2 * channels)),
        ],
        scratch_shapes=[
            pltpu.VMEM((rows_n, units), bf16),
            pltpu.VMEM((rows_n, units), f32),
            pltpu.VMEM((rows_n, channels), f32),
            pltpu.VMEM((rows_n, 128), f32),
            pltpu.VMEM((rows_n, channels), bf16),
            pltpu.VMEM((128, rows_n), f32),
            pltpu.VMEM((rows_n, 128), bf16),
            pltpu.VMEM((channels, rows_n), bf16),
            pltpu.VMEM((channels, rows_n), bf16),
            pltpu.VMEM((rows_n, units), bf16),
            pltpu.VMEM((rows_n, channels), bf16),
            pltpu.VMEM((128, channels), bf16),
        ],
        compiler_params=params(62),
        name="middle",
    )(length, mixed_t, one, first, up, down, vec, head_w, noi_t)


def run_hind(run, length, step, *arrays):
    one = arrays[5]
    rows_n, channels = one.shape
    embed = arrays[15].shape[2]
    n_d, n_f = lax.axis_size("dp"), lax.axis_size("fsdp")
    n_z = n_f // 2
    count = n_d * n_f
    rows_c = arrays[13].shape[1] // n_f
    rows_a = (channels + channels // 2) // n_f
    dma = pltpu.SemaphoreType.DMA
    return pl.pallas_call(
        functools.partial(hind_kernel, run, GROUPS),
        in_specs=[SM, SM]
        + [ANY] * 11
        + [VM] * 2
        + [ANY] * 3
        + [VM] * 2
        + [ANY] * 6,
        out_specs=[VM] * 9,
        out_shape=[
            sized((2, rows_c, channels)),
            sized((n_z, 2, 8, 2 * channels)),
            sized((3, embed // n_f, embed)),
            sized((8, 128)),
            sized((arrays[10].shape[0], channels)),
            sized((channels // n_f, 4 * channels + FF)),
            sized((channels // n_f, 4 * channels + FF)),
            sized((FF // n_f, channels)),
            sized((FF // n_f, channels)),
        ],
        scratch_shapes=[
            pltpu.VMEM((rows_n + 2 * run, 3 * channels), bf16),
            pltpu.VMEM((rows_n, channels), f32),
            pltpu.VMEM((rows_n, channels), f32),
            pltpu.VMEM((channels, rows_n), bf16),
            pltpu.VMEM((16, 2 * channels), f32),
            pltpu.VMEM((n_d, n_z, 2, 16, embed // 2), bf16),
        ]
        + small_scratch(2 * channels)
        + [
            pltpu.VMEM((count, 1, 128), f32),
            pltpu.VMEM((128, embed), f32),
        ]
        + owner_scratch(rows_c // 2, 2 * channels)
        + owner_scratch(rows_c // 2, 2 * channels)
        + owner_scratch(rows_a, 2 * channels)
        + [
            dma((n_z,)),
            dma((n_z,)),
            dma((n_d + n_z,)),
            dma((n_d + n_z,)),
            dma((count,)),
            dma((count,)),
            pltpu.VMEM((n_z, 2, rows_a, 2 * channels), bf16),
            pltpu.VMEM(arrays[-6].shape, bf16),
            pltpu.VMEM(arrays[-5].shape, bf16),
            pltpu.VMEM(arrays[-4].shape, bf16),
            pltpu.VMEM(arrays[-3].shape, f32),
            pltpu.VMEM(arrays[-2].shape, f32),
            pltpu.VMEM(arrays[-1].shape[1:], f32),
            pltpu.VMEM((FF // n_f, FF), f32),
            dma((7,)),
        ]
        + [pltpu.VMEM(arrays[i].shape, arrays[i].dtype) for i in (0, 1, 2, 4, 14, 3, 5)]
        + [pltpu.VMEM(arrays[i].shape, arrays[i].dtype) for i in (6, 7, 13, 15, 8, 9, 10)]
        + [dma((14,))],
        compiler_params=remote_params(2, 63),
        name="hind",
    )(length, step, *arrays)


def update_kernel(
    latent_ch,
    units,
    step_ref,
    scalar_ref,
    conv_g,
    time_g,
    tiles,
    head_g,
    wide_g,
    wide_dir,
    down_g,
    down_dir,
    stem_w,
    stem_m,
    stem_s,
    head_w,
    head_m,
    head_s,
    time_w,
    time_m,
    time_s,
    vec_m,
    vec_s,
    conv_w,
    conv_m,
    conv_s,
    wide_w,
    wide_m,
    down_w,
    down_m,
    stem_out,
    stem_m_out,
    stem_s_out,
    head_out,
    head_m_out,
    head_s_out,
    time_out,
    time_m_out,
    time_s_out,
    vec_out,
    vec_m_out,
    vec_s_out,
    conv_out,
    conv_m_out,
    conv_s_out,
    wide_out,
    wide_m_out,
    down_out,
    down_m_out,
):
    taps, channels = stem_w.shape
    stem_tiles = taps // 8 * (channels // 128)
    small = take_tiles(tiles, stem_tiles, 16, 2 * channels)
    factor = scalar_ref[2:3, 0:1]
    step = jnp.zeros((1, 1), f32) + step_ref[0].astype(f32)
    one_over = 1.0 / (1.0 - jnp.exp(step * math.log(0.9)))
    two_over = 1.0 / (1.0 - jnp.exp(step * math.log(0.999)))

    def adam(outs, where, weight, first, second, grad):
        grad = factor * grad
        first_new = 0.9 * first + 0.1 * grad
        second_new = 0.999 * second + 0.001 * grad * grad
        moved = first_new * one_over / (jnp.sqrt(second_new * two_over) + adam_floor)
        outs[0][where] = weight - adam_rate * (moved + decay_rate * weight)
        outs[1][where] = first_new
        outs[2][where] = second_new

    whole = slice(None)
    adam(
        (stem_out, stem_m_out, stem_s_out),
        whole,
        stem_w[...],
        stem_m[...],
        stem_s[...],
        take_tiles(tiles, 0, taps, channels),
    )
    outs = (time_out, time_m_out, time_s_out)
    for i in range(time_w.shape[0]):
        adam(outs, i, time_w[i], time_m[i], time_s[i], time_g[i])
    outs = (conv_out, conv_m_out, conv_s_out)
    for i in range(conv_w.shape[0]):
        adam(outs, i, conv_w[i], conv_m[i], conv_s[i], conv_g[i])
    outs = (head_out, head_m_out, head_s_out)
    for tap in range(9):
        where = (whole, slice(tap * channels, (tap + 1) * channels))
        grad = head_g[tap * latent_ch : (tap + 1) * latent_ch]
        adam(outs, where, head_w[where], head_m[where], head_s[where], grad)

    def vec_grad(which):
        if which < 13:
            lane = (which % 2) * channels
            return small[which // 2 : which // 2 + 1, lane : lane + channels]
        if which < 16:
            return small[which - 6 : which - 5]
        if which == 16:
            return jnp.concatenate([small[10:11], small[11:12]], 1)
        return small[12:13, 0:latent_ch]

    for which, (first, length) in enumerate(
        offsets(channels, 2 * channels, units, latent_ch)
    ):
        where = slice(first, first + length)
        grad = (factor * vec_grad(which)).reshape(length)
        vec_out[where] = grad
        vec_m_out[where] = 0.9 * vec_m[where] + 0.1 * grad
        vec_s_out[where] = 0.999 * vec_s[where] + 0.001 * grad * grad

    kept = 1.0 - shampoo_rate * decay_rate
    wide_m_out[...] = 0.9 * wide_m[...] + factor * wide_g[...]
    wide_out[...] = wide_w[...] * kept - shampoo_rate * wide_dir[...]
    down_m_out[...] = 0.9 * down_m[...] + factor * down_g[...]
    down_out[...] = down_w[...] * kept - shampoo_rate * down_dir[...]


def run_update(latent_ch, step, *arrays):
    stem_w, head_w, time_w, vec_m = arrays[9], arrays[12], arrays[15], arrays[18]
    conv_w, wide_w, down_w = arrays[20], arrays[23], arrays[25]
    shapes = [stem_w.shape] * 3 + [head_w.shape] * 3 + [time_w.shape] * 3
    shapes += [vec_m.shape] * 3 + [conv_w.shape] * 3 + [wide_w.shape] * 2 + [down_w.shape] * 2
    return pl.pallas_call(
        functools.partial(update_kernel, latent_ch, FF),
        in_specs=[SM] + [VM] * len(arrays),
        out_specs=[VM] * len(shapes),
        out_shape=[sized(shape) for shape in shapes],
        compiler_params=params(62),
        name="update",
    )(step, *arrays)


def local(
    latents,
    noises,
    clap_embed,
    timesteps,
    lengths,
    step_count,
    stem_w,
    head_w,
    time_w,
    vector,
    conv_w,
    wide_w,
    down_w,
    roots_small,
    root_wide,
    roots_large,
    stem_moment,
    stem_square,
    head_moment,
    head_square,
    time_moment,
    time_square,
    vector_moment,
    vector_square,
    conv_moment,
    conv_square,
    wide_moment,
    down_moment,
):
    frames_n, freq_bins, latent_ch = (latents.shape[1], latents.shape[2], latents.shape[3])
    channels = stem_w.shape[1]
    def by_bins(value):
        return value[0].transpose(1, 2, 0).reshape(freq_bins * latent_ch, frames_n)

    head_t = head_w.T
    (
        zero,
        act_one,
        inner,
        act_two,
        one,
        normed,
        qkv_t,
        cols_t,
        noi_t,
        stat,
        film,
        conv_full,
        time_full,
        first_full,
    ) = run_fore(
        frames_n,
        lengths,
        timesteps,
        by_bins(latents),
        by_bins(noises),
        stem_w,
        conv_w,
        wide_w,
        time_w,
        vector,
        clap_embed,
    )
    mixed_t, lse, up_full, down_full = run_attend(
        frames_n, lengths, qkv_t, wide_w, down_w
    )
    two_grad, do_t, early, small = run_middle(
        frames_n,
        lengths,
        mixed_t,
        one,
        first_full,
        up_full,
        down_full,
        vector,
        head_t,
        noi_t,
    )
    dq, dk, dv, early, wide_moment_full, down_moment_full = run_attend_back(
        frames_n, lengths, qkv_t, lse, mixed_t, do_t, early, wide_moment, down_moment
    )
    outs = run_hind(
        frames_n,
        lengths,
        timesteps,
        dq,
        dk,
        dv,
        two_grad,
        normed,
        one,
        act_two,
        inner,
        act_one,
        zero,
        cols_t,
        stat,
        film,
        conv_full,
        first_full,
        time_full,
        vector,
        small,
        early,
        wide_moment_full,
        down_moment_full,
        roots_small,
        root_wide,
        roots_large,
    )
    conv_sum, tiles, time_sum, scalars, head_sum, wide_sum, wide_dir, down_sum, down_dir = outs
    outs = run_update(
        latent_ch,
        step_count,
        scalars,
        conv_sum,
        time_sum,
        tiles,
        head_sum,
        wide_sum,
        wide_dir,
        down_sum,
        down_dir,
        stem_w,
        stem_moment,
        stem_square,
        head_t,
        head_moment.T,
        head_square.T,
        time_w,
        time_moment,
        time_square,
        vector_moment,
        vector_square,
        conv_w,
        conv_moment,
        conv_square,
        wide_w,
        wide_moment,
        down_w,
        down_moment,
    )
    outs = list(outs)
    for index in (3, 4, 5):
        outs[index] = outs[index].T
    return (scalars[0, 0], scalars[1, 0], *outs)


def solution(mesh):
    in_specs = (
        P(("dp", "fsdp"), None, None, None),
        P(("dp", "fsdp"), None, None, None),
        P(("dp", "fsdp"), None),
        P(("dp", "fsdp")),
        P(("dp", "fsdp")),
        P(),
        P(),
        P(),
        P(None, "fsdp", None),
        P(),
        P(None, "fsdp", None),
        P("fsdp", None),
        P("fsdp", None),
        P(),
        P(),
        P(),
        P(),
        P(),
        P(),
        P(),
        P(None, "fsdp", None),
        P(None, "fsdp", None),
        P(),
        P(),
        P(None, "fsdp", None),
        P(None, "fsdp", None),
        P("fsdp", None),
        P("fsdp", None),
    )
    out_specs = (
        P(),
        P(),
        P(),
        P(),
        P(),
        P(),
        P(),
        P(),
        P(None, "fsdp", None),
        P(None, "fsdp", None),
        P(None, "fsdp", None),
        P(),
        P(),
        P(),
        P(None, "fsdp", None),
        P(None, "fsdp", None),
        P(None, "fsdp", None),
        P("fsdp", None),
        P("fsdp", None),
        P("fsdp", None),
        P("fsdp", None),
    )
    return jax.shard_map(local, mesh=mesh, in_specs=in_specs, out_specs=out_specs, check_vma=False)
```
